128 devices in a mesh: wide: 32 (over y_hi, z, x), tp: 4 (over y_lo, core).
Axes of the slice: x: 4, y: 4 (y_hi: 2, y_lo: 2; y = y_hi * 2 + y_lo), z: 4, core: 2. Of those that a mesh axis runs over, the one named last changes fastest.
Arguments:
- inputs: bfloat16 [16384, 2048], P(('wide', 'tp')), may hold values from -24 to 24
- positions: int32 [16384], P('wide'), may hold values from 0 to 2047, as said below
- attn_gain: bfloat16 [2048], P('wide'), may hold values from 0.5 to 1.5
- query_weight: bfloat16 [2048, 2048], P('wide', 'tp'), may hold values from -0.125 to 0.125
- key_weight: bfloat16 [2048, 256], P('wide', 'tp'), may hold values from -0.125 to 0.125
- value_weight: bfloat16 [2048, 256], P('wide', 'tp'), may hold values from -0.125 to 0.125
- out_weight: bfloat16 [2048, 2048], P('tp', 'wide'), may hold values from -2 to 2
- mlp_gain: bfloat16 [2048], P('wide'), may hold values from 0.5 to 1.5
- gate_weight: bfloat16 [2048, 5632], P('wide', 'tp'), may hold values from -0.125 to 0.125
- up_weight: bfloat16 [2048, 5632], P('wide', 'tp'), may hold values from -0.125 to 0.125
- down_weight: bfloat16 [5632, 2048], P('tp', 'wide'), may hold values from -0.078125 to 0.078125
- cotangent: bfloat16 [16384, 2048], P(('wide', 'tp')), may hold values from -24 to 24
Outputs:
- output: bfloat16 [16384, 2048], P(('wide', 'tp'))
- input_grad: float32 [16384, 2048], P(('wide', 'tp'))
- attn_gain_grad: float32 [2048], P('wide')
- query_weight_grad: float32 [2048, 2048], P('wide', 'tp')
- key_weight_grad: float32 [2048, 256], P('wide', 'tp')
- value_weight_grad: float32 [2048, 256], P('wide', 'tp')
- out_weight_grad: float32 [2048, 2048], P('tp', 'wide')
- mlp_gain_grad: float32 [2048], P('wide')
- gate_weight_grad: float32 [2048, 5632], P('wide', 'tp')
- up_weight_grad: float32 [2048, 5632], P('wide', 'tp')
- down_weight_grad: float32 [5632, 2048], P('tp', 'wide')
The draws below stay inside these ranges and needn't reach their ends.
Inputs may be any that keep to these rules, and one draw needn't show every extreme that they name: positions[t] is the index of token t within its document; every sequence of 2048 tokens begins a document at its first token and holds one to four documents; exactly one sequence, drawn from the seed, is a single document.
All inputs are finite; a program needn't handle non-finite values.
Results may differ from the reference program's by a relative error of at most 0.03.
Values may be sent and summed in bfloat16 or wider, within the bound.
No kernel may reach another device: no remote copies, remote signals or barrier semaphores. Data moves between devices by JAX's collectives and lax.ppermute only.
A program may use at most 256 MiB of HBM per device.

```python
import math
import jax
import jax.numpy as jnp
from jax import lax

D = 2048
HEADS = 32
KV = 4
HD = 64
FF = 5632
LEN = 2048
SEQS = 8
TOKENS = 16384


def draw_positions(key, part):
    key = jax.random.fold_in(key, 11)
    chosen = jax.random.randint(jax.random.fold_in(key, 1), (), 0, SEQS)
    cut_points = jax.random.randint(jax.random.fold_in(key, 2), (SEQS, 3), 1, LEN)
    token_index = jnp.arange(LEN, dtype=jnp.int32)
    boundary = jnp.any(token_index[None, :, None] == cut_points[:, None, :], -1)
    boundary = boundary & (jnp.arange(SEQS, dtype=jnp.int32)[:, None] != chosen)
    doc_starts = jnp.where(boundary, token_index[None, :], 0)
    doc_starts = lax.cummax(doc_starts, axis=1)
    return (token_index[None, :] - doc_starts).reshape(SEQS * LEN).astype(jnp.int32)


def raised(result, stream_key, source, target, blocks, factor):
    def block_of(position):
        return (jnp.arange(result.shape[position]) // (result.shape[position] // blocks)).reshape((-1,) + (1,) * (result.ndim - 1 - position))

    first = jax.random.permutation(stream_key, blocks)[block_of(target)]
    other_side = (block_of(target) + blocks // 2) % blocks
    return jnp.where((block_of(source) == first) | (block_of(source) == other_side), factor * result, result)


def levels(rng, dims, split, low, largest):
    level = 1.0
    for axis_at, shards_of in split:
        draws = jax.random.uniform(jax.random.fold_in(jax.random.fold_in(rng, 6), axis_at), (shards_of,), jnp.float32, low / len(split), largest / len(split))
        level = level * jnp.repeat(jnp.exp(draws), dims[axis_at] // shards_of).reshape((-1,) + (1,) * (len(dims) - 1 - axis_at))
    return level


def noise(stream_key, extent, width, bound, pieces=(), kind=jnp.bfloat16):
    level = levels(stream_key, extent, pieces, -0.22, 0.18) if pieces else 1.0
    drawn = jax.random.normal(stream_key, extent, jnp.float32) * width * level
    return jnp.minimum(jnp.maximum(drawn, -bound), bound).astype(kind)


def heavy_noise(stream_key, extent, spread, most, cuts, heavy, kind=jnp.bfloat16):
    result = spread * jax.random.normal(stream_key, extent, jnp.float32)
    if cuts:
        result = result * levels(stream_key, extent, cuts, -0.22, 0.18)
    return jnp.clip(raised(result, jax.random.fold_in(stream_key, 3), *heavy), -most, most).astype(kind)


def setup_inputs(seed: int = 0) -> dict:
    arg_keys = jax.random.split(jax.random.key(seed), 13)
    return {
        "inputs": heavy_noise(arg_keys[0], (TOKENS, D), 1.0, 24.0, ((0, 128),), (0, 1, 128, 5.5)),
        "positions": draw_positions(jax.random.fold_in(arg_keys[12], 71), 0),
        "attn_gain": jnp.clip(1.0 + 0.1 * jax.random.normal(arg_keys[2], (D,), jnp.float32), 0.5, 1.5).astype(jnp.bfloat16),
        "query_weight": noise(arg_keys[3], (D, HEADS * HD), D ** -0.5, 0.125, ((0, 32), (1, 4))),
        "key_weight": noise(arg_keys[4], (D, KV * HD), D ** -0.5, 0.125, ((0, 32), (1, 4))),
        "value_weight": noise(arg_keys[5], (D, KV * HD), D ** -0.5, 0.125, ((0, 32), (1, 4))),
        "out_weight": noise(arg_keys[6], (HEADS * HD, D), (max(D // 256, 1)) ** -0.5, 2.0, ((0, 4), (1, 32))),
        "mlp_gain": jnp.clip(1.0 + 0.1 * jax.random.normal(arg_keys[7], (D,), jnp.float32), 0.5, 1.5).astype(jnp.bfloat16),
        "gate_weight": noise(arg_keys[8], (D, FF), D ** -0.5, 0.125, ((0, 32), (1, 4))),
        "up_weight": noise(arg_keys[9], (D, FF), D ** -0.5, 0.125, ((0, 32), (1, 4))),
        "down_weight": noise(arg_keys[10], (FF, D), FF ** -0.5, 0.078125, ((0, 4), (1, 32))),
        "cotangent": heavy_noise(arg_keys[11], (TOKENS, D), 1.0, 24.0, ((0, 128),), (0, 1, 128, 5.5)),
    }


@jax.custom_vjp
def low(v):
    return lax.optimization_barrier(v.astype(jnp.bfloat16)).astype(jnp.float32)

@jax.custom_vjp
def low_back(v):
    return v

def low_keep(v):
    return (low(v), None)

def low_pass(kept, grad):
    return (grad,)

def back_keep(v):
    return (v, None)

def back_low(kept, grad):
    return (low(grad),)
low.defvjp(low_keep, low_pass)
low_back.defvjp(back_keep, back_low)
epsilon = 1e-05
masked_fill = -1e+30

def matmul(left, right):
    return jnp.dot(left, right, precision=lax.Precision.HIGHEST)

def normalize(values):
    return values * lax.rsqrt(lax.optimization_barrier(jnp.mean(values * values, -1, keepdims=True)) + epsilon)

def rotate(values, positions, sign):
    half = HD // 2
    heads = values.shape[1] // HD
    freqs = 10000.0 ** (-(jnp.arange(half, dtype=jnp.float32) * 2.0) / HD)
    angles = positions.astype(jnp.float32)[:, None] * freqs[None, :]
    cosine = jnp.cos(angles)[:, None, :]
    sine = sign * jnp.sin(angles)[:, None, :]
    shaped = values.reshape(values.shape[0], heads, HD)
    first = shaped[..., :half]
    second = shaped[..., half:]
    turned = jnp.concatenate([first * cosine - second * sine, second * cosine + first * sine], -1)
    return turned.reshape(values.shape)

def head_group(queries, keys, values, positions):
    raw = low_back(jnp.einsum('qgd,kd->gqk', queries, keys, precision=lax.Precision.HIGHEST))
    scores = raw * (1.0 / math.sqrt(HD))
    places = jnp.arange(LEN, dtype=jnp.int32)
    visible = (places[None, :] <= places[:, None]) & (places[:, None] - places[None, :] <= positions[:, None])
    masked = jnp.where(visible[None], scores, masked_fill)
    top = lax.optimization_barrier(jnp.max(masked, -1, keepdims=True))
    expo = jnp.exp(masked - top)
    probs = expo / lax.optimization_barrier(jnp.sum(expo, -1, keepdims=True))
    mixed = jnp.einsum('gqk,kd->qgd', low(probs), values, precision=lax.Precision.HIGHEST)
    return low(low_back(mixed))

def attention(queries, keys, values, positions):
    groups = HEADS // KV
    query_seq = queries.reshape(SEQS, LEN, KV, groups, HD)
    key_seq = keys.reshape(SEQS, LEN, KV, HD)
    value_seq = values.reshape(SEQS, LEN, KV, HD)
    place_seq = positions.reshape(SEQS, LEN)

    def one_sequence(packed):
        query_one, key_one, value_one, place_one = packed

        def one_head(inner):
            return head_group(inner[0], inner[1], inner[2], place_one)
        return lax.map(jax.checkpoint(one_head), (query_one.transpose(1, 0, 2, 3), key_one.transpose(1, 0, 2), value_one.transpose(1, 0, 2)))
    mixed = lax.map(jax.checkpoint(one_sequence), (query_seq, key_seq, value_seq, place_seq))
    return mixed.transpose(0, 2, 1, 3, 4).reshape(TOKENS, HEADS * HD)

def forward(inputs, attn_gain, query_weight, key_weight, value_weight, out_weight, mlp_gain, gate_weight, up_weight, down_weight, positions):
    first_in = low(normalize(inputs) * attn_gain)
    queries = low(rotate(low_back(matmul(first_in, query_weight)), positions, 1.0))
    keys = low(rotate(low_back(matmul(first_in, key_weight)), positions, 1.0))
    values = low(low_back(matmul(first_in, value_weight)))
    mixed = attention(queries, keys, values, positions)
    middle = inputs + low_back(matmul(mixed, out_weight))
    second_in = low(normalize(low(middle)) * mlp_gain)
    gate = low_back(matmul(second_in, gate_weight))
    up = low_back(matmul(second_in, up_weight))
    hidden = low(gate * jax.nn.sigmoid(gate) * up)
    return middle + low_back(matmul(hidden, down_weight))

def reference(inputs, positions, attn_gain, query_weight, key_weight, value_weight, out_weight, mlp_gain, gate_weight, up_weight, down_weight, cotangent):
    floats = [array.astype(jnp.float32) for array in (inputs, attn_gain, query_weight, key_weight, value_weight, out_weight, mlp_gain, gate_weight, up_weight, down_weight)]

    def wrapped(*arrays):
        return forward(*arrays, positions)
    output, pullback = jax.vjp(wrapped, *floats)
    grads = pullback(cotangent.astype(jnp.float32))
    return (output.astype(jnp.bfloat16), grads[0], grads[1], grads[2], grads[3], grads[4], grads[5], grads[6], grads[7], grads[8], grads[9])
```

```python
import functools

import jax
import jax.numpy as jnp
from jax import lax
from jax.experimental import pallas as pl
from jax.experimental.pallas import tpu as pltpu
from jax.sharding import Mesh, PartitionSpec as P

HEADS = 32
KV = 4
HD = 64
SEQ_DEVS = 4
WIDE = ("yh", "z", "x")
TP = ("yl", "core")
BF = jnp.bfloat16
F32 = jnp.float32

epsilon = 1e-05
masked_fill = -1e30
VMEM_LIMIT = 56 * 1024 * 1024


def after(value, *earlier):
    return lax.optimization_barrier((value, earlier))[0]


def shift(block, axis, distance):
    n = lax.axis_size(axis)
    return lax.ppermute(block, axis, [(i, (i + distance) % n) for i in range(n)])


def swap(block, axis):
    return shift(block, axis, 1)


def place(axis, step=0):
    n = lax.axis_size(axis)
    return ((lax.axis_index(axis) + (step + n)) & (n - 1)).astype(jnp.uint32)


def pick(array, index, dim):
    return lax.dynamic_index_in_dim(array, index, dim, keepdims=False)


def gather_stage(block, axis, dim, hold=()):
    n = lax.axis_size(axis)
    order = (0, 1, n - 1, *range(2, n - 1))
    arrived = [block] + [after(shift(block, axis, d), *hold) for d in order[1:]]
    out = jnp.zeros(block.shape[:dim] + (n,) + block.shape[dim:], block.dtype)
    for d, piece in zip(order, arrived):
        out = lax.dynamic_update_index_in_dim(out, piece, place(axis, -d), dim)
    return out


def join_sides(shard, other):
    first = lax.axis_index("yh") == 0
    return jnp.concatenate([jnp.where(first, shard, other), jnp.where(first, other, shard)], 0)


def flat(blocks):
    return blocks.reshape(-1, blocks.shape[-1])


def to_inner(rows):
    t, d = rows.shape
    return rows.reshape(t, 2, 16, d // 32).transpose(0, 2, 1, 3).reshape(t, d)


def from_inner(rows):
    t, d = rows.shape
    return rows.reshape(t, 16, 2, d // 32).transpose(0, 2, 1, 3).reshape(t, d)


def gather_rows(rows):
    across = swap(rows, "yl")
    return [rows, swap(rows, "core"), across, swap(across, "core")]


def scatter_rows(partial):
    n = partial.shape[0] // 4
    low = partial.astype(BF)
    far = swap(low[3 * n :], "core").astype(F32)
    near = swap(low[n : 2 * n], "core").astype(F32)
    other = partial[2 * n : 3 * n].astype(F32) + far
    mine = partial[:n].astype(F32) + near
    return mine + swap(other.astype(BF), "yl").astype(F32)


def contract_last(left, right):
    return lax.dot_general(left, right, (((1,), (1,)), ((), ())), preferred_element_type=F32)


def contract_first(left, right):
    return lax.dot_general(left, right, (((0,), (0,)), ((), ())), preferred_element_type=F32)


def columns_of(rows, axis, index):
    t, d = rows.shape
    blocks = rows.reshape(t, 4, 4, d // 16)
    return pick(blocks, index, {"z": 1, "x": 2}[axis]).reshape(t, d // 4)


def exchange_sum(parts, axis, hold=()):
    n = len(parts)
    total = parts[0].astype(F32)
    for d in (1, n - 1, *range(2, n - 1))[: n - 1]:
        total = total + after(shift(parts[d].astype(BF), axis, d), *hold).astype(F32)
    return total


def sides_sum(part, hold=()):
    half = part.reshape(2, part.shape[0] // 2, part.shape[1])
    return exchange_sum([pick(half, place("yh"), 0), pick(half, place("yh", 1), 0)], "yh", hold)


def wide_parts(left, right, axis):
    return [
        contract_first(columns_of(left, axis, place(axis, d)), right).astype(BF)
        for d in range(lax.axis_size(axis))
    ]


def wide_sum_next(part, axis, hold=()):
    n = lax.axis_size(axis)
    part = part.reshape(n, part.shape[0] // n, part.shape[1])
    pieces = [pick(part, place(axis, d), 0) for d in range(n)]
    return exchange_sum(pieces, axis, hold).astype(BF)


def mm(left, right):
    return jnp.dot(left, right, preferred_element_type=F32)


def mm_last(left, right):
    return lax.dot_general(left, right, (((1,), (1,)), ((), ())), preferred_element_type=F32)


def normed_rows(piece):
    values = piece.astype(F32)
    factor = lax.rsqrt(jnp.mean(values * values, -1, keepdims=True) + epsilon)
    return values * factor, factor


def scale_rows(piece_refs, gain, scaled_ref):
    for n, ref in enumerate(piece_refs):
        for at in range(0, ref.shape[0], 32):
            normed, _ = normed_rows(ref[at : at + 32, :])
            rows = n * ref.shape[0] + at
            scaled_ref[rows : rows + 32, :] = (normed * gain).astype(BF)


def project_kernel(*refs):
    piece_refs, (w_ref, last_ref, cos_ref, sin_ref, q_ref, kv_ref, scaled_ref, gains_ref) = refs[:4], refs[4:]
    width_q = q_ref.shape[0]
    half = HD // 2
    cos, sin = cos_ref[...], sin_ref[...]
    tiles = [(w, at) for w in (w_ref, last_ref) for at in range(0, w.shape[1], 128)]

    def turned(block):
        a, b = block[:half], block[half:]
        return jnp.concatenate([a * cos - b * sin, b * cos + a * sin], 0)

    w, at = tiles[-1]
    gains_ref[...] = w[:, at : at + 128].T[:8].astype(F32)
    scale_rows(piece_refs, gains_ref[0:1, :], scaled_ref)
    x = scaled_ref[...]
    for n in range(width_q // 128):
        w, at = tiles[n]
        piece = mm(x, w[:, at : at + 128]).T
        for sub in range(0, 128, HD):
            low = turned(piece[sub : sub + HD]).astype(BF)
            q_ref[n * 128 + sub : n * 128 + sub + HD, :] = low * 0.125
    w, at = tiles[width_q // 128]
    piece = mm(x, w[:, at : at + 128]).T
    kv = jnp.concatenate([turned(piece[:HD]), piece[HD:]], 0)
    kv_ref[...] = kv.T.astype(BF)


def hidden_kernel(*refs):
    pieces, cots, (gain_ref, gate_ref, up_ref, down_ref, hidden_ref, dgate_ref, dup_ref, scaled_ref, cot_ref) = (
        refs[:4], refs[4:8], refs[8:],
    )

    @pl.when(pl.program_id(0) == 0)
    def _():
        scale_rows(pieces, gain_ref[1:2, :], scaled_ref)
        for n, ref in enumerate(cots):
            cot_ref[n * ref.shape[0] : (n + 1) * ref.shape[0], :] = ref[...]

    tile = gate_ref.shape[1]
    both = mm(scaled_ref[...], jnp.concatenate([gate_ref[...], up_ref[...]], 1))
    grad = mm(cot_ref[...], down_ref[...])
    gate, up = both[:, :tile], both[:, tile:]
    sigmoid = 1.0 / (1.0 + jnp.exp(-gate))
    gated = gate * sigmoid
    hidden_ref[...] = (gated * up).astype(BF)
    dgate_ref[...] = (grad * up * sigmoid * (1.0 + gate * (1.0 - sigmoid))).astype(BF)
    dup_ref[...] = (grad * gated).astype(BF)


def rows_grad_kernel(count, gain_row, *refs):
    grads, weights, pieces = refs[:count], refs[count : 2 * count], refs[2 * count : 2 * count + 4]
    gain_ref, out_ref, sum_ref = refs[2 * count + 4 :]
    step = pl.program_id(0)
    tile = weights[0].shape[0]
    total = None
    for g_ref, w_ref in zip(grads, weights):
        part = mm_last(g_ref[...], w_ref[...])
        total = part if total is None else total + part
    columns = pl.ds(pl.multiple_of(step * tile, tile), tile)
    sum_ref[:, columns] = total * gain_ref[gain_row : gain_row + 1, columns]

    @pl.when(step == pl.num_programs(0) - 1)
    def _():
        for n, ref in enumerate(pieces):
            for at in range(0, ref.shape[0], 32):
                normed, factor = normed_rows(ref[at : at + 32, :])
                rows = slice(n * ref.shape[0] + at, n * ref.shape[0] + at + 32)
                scaled = sum_ref[rows, :]
                inner = jnp.mean(scaled * normed, -1, keepdims=True)
                out_ref[rows, :] = (factor * (scaled - normed * inner)).astype(BF)


def fill_bias(bias_ref, me_ref, pos_ref, span, distances):
    step = 64
    quarter = span // 4
    me = me_ref[0, 0]
    at = lax.broadcasted_iota(jnp.int32, (1, span), 1)
    query = (((at // quarter) ^ me) * quarter) + (at & (quarter - 1))
    first = query - pos_ref[...]

    @pl.loop(0, span // step)
    def _(i):
        block = (i * step) // quarter
        start = (block ^ me) * quarter + i * step - block * quarter
        key = start + lax.broadcasted_iota(jnp.int32, (step, span), 0)
        for n, d in enumerate(distances):
            seen = (key - d * span <= query) & (key - d * span >= first)
            bias_ref[pl.ds(pl.multiple_of(n * span + i * step, step), step), :] = jnp.where(
                seen, 0.0, masked_fill
            ).astype(F32)


def attend_kernel(q_ref, *refs):
    blocks = len(refs) - 7
    kv_refs = refs[:blocks]
    me_ref, pos_ref, mix_ref, lse_ref, bias_ref, s_ref, vt_ref = refs[blocks:]
    span = q_ref.shape[1]
    fill_bias(bias_ref, me_ref, pos_ref, span, range(blocks))
    for d in range(blocks):
        vt_ref[:, d * span : (d + 1) * span] = kv_refs[d][...].T[HD:]

    @pl.loop(0, q_ref.shape[0] // 128)
    def _(pair):
        outs = []
        for sub in range(2):
            q = q_ref[pl.ds(pl.multiple_of(pair * 128 + sub * HD, HD), HD), :]
            top = None
            for d in range(blocks):
                rows = slice(d * span, (d + 1) * span)
                s = mm(kv_refs[d][:, :HD], q) + bias_ref[rows, :]
                s_ref[rows, :] = s
                high = jnp.max(s, 0, keepdims=True)
                top = high if top is None else jnp.maximum(top, high)
            total = jnp.zeros_like(top)
            out = jnp.zeros((HD, span), F32)
            for d in range(blocks):
                rows = slice(d * span, (d + 1) * span)
                p = jnp.exp(s_ref[rows, :] - top)
                total = total + jnp.sum(p, 0, keepdims=True)
                out = out + mm(vt_ref[:, rows], p.astype(BF))
            outs.append(out / total)
            lse_ref[pl.ds(pair * 2 + sub, 1), :] = top + jnp.log(total)
        mix_ref[:, pl.ds(pl.multiple_of(pair * 128, 128), 128)] = (
            jnp.concatenate(outs, 0).T.astype(BF)
        )


def attend_back_kernel(distances, first, last, q_ref, *refs):
    blocks = len(distances)
    refs = list(refs)

    def take(count):
        got, refs[:count] = refs[:count], []
        return got

    kv_refs = take(blocks)
    me_ref, pos_ref, lse_ref = take(3)
    if first:
        mix_ref, grad_ref = take(2)
    else:
        gt_ref, delta_ref, part_ref = take(3)
    if last:
        cos_ref, sin_ref = take(2)
        (dq_ref,) = take(1)
    else:
        (sum_ref,) = take(1)
    (dkv_ref,) = take(1)
    if first:
        gt_ref, delta_ref = take(2)
    bias_ref, v_ref, kt_ref, dk_ref, dv_ref = take(5)
    span = q_ref.shape[1]
    half = HD // 2
    heads = q_ref.shape[0] // HD
    fill_bias(bias_ref, me_ref, pos_ref, span, distances)
    for n in range(blocks):
        rows = slice(n * span, (n + 1) * span)
        both = kv_refs[n][...].T
        kt_ref[:, rows] = both[:HD]
        v_ref[rows, :] = both[HD:].T
    dk_ref[...] = jnp.zeros_like(dk_ref)
    dv_ref[...] = jnp.zeros_like(dv_ref)
    if first:
        for at in range(0, heads * HD, 128):
            gt = grad_ref[:, at : at + 128].T
            mt = mix_ref[:, at : at + 128].T
            gt_ref[at : at + 128, :] = gt
            prod = gt.astype(F32) * mt.astype(F32)
            for sub in range(2):
                h = at // HD + sub
                delta_ref[h : h + 1, :] = jnp.sum(prod[sub * HD : (sub + 1) * HD], 0, keepdims=True)

    @pl.loop(0, heads // 2)
    def _(pair):
        outs = []
        for sub in range(2):
            rows_h = pl.ds(pl.multiple_of(pair * 128 + sub * HD, HD), HD)
            q, g = q_ref[rows_h, :], gt_ref[rows_h, :]
            lse = lse_ref[pl.ds(pair * 2 + sub, 1), :]
            delta = delta_ref[pl.ds(pair * 2 + sub, 1), :]
            dq = jnp.zeros((HD, span), F32) if first else part_ref[rows_h, :]
            for n in range(blocks):
                rows = slice(n * span, (n + 1) * span)
                s = mm(kv_refs[n][:, :HD], q) + bias_ref[rows, :]
                p = jnp.exp(s - lse)
                ds = (p * (mm(v_ref[rows, :], g) - delta)).astype(BF)
                dv_ref[rows, :] += mm_last(p.astype(BF), g)
                dk_ref[rows, :] += mm_last(ds, q)
                dq = dq + mm(kt_ref[:, rows], ds)
            if last:
                dq = dq * 0.125
                a, b = dq[:half], dq[half:]
                cos, sin = cos_ref[...], sin_ref[...]
                outs += [a * cos + b * sin, b * cos - a * sin]
            else:
                sum_ref[rows_h, :] = dq
        if last:
            dq_ref[:, pl.ds(pl.multiple_of(pair * 128, 128), 128)] = (
                jnp.concatenate(outs, 0).T.astype(BF)
            )

    for n in range(blocks):
        rows = slice(n * span, (n + 1) * span)
        dkv_ref[rows, :] = jnp.concatenate([dk_ref[rows, :], dv_ref[rows, :]], 1).astype(dkv_ref.dtype)


def weight_grads_kernel(left_ref, *refs):
    out_ref = refs[-1]
    turned = left_ref[...].T
    at = 0
    for ref in refs[:-1]:
        for c in range(0, ref.shape[1], 256):
            size = min(256, ref.shape[1] - c)
            out_ref[:, at + c : at + c + size] = mm(turned, ref[:, c : c + size]).astype(BF)
        at += ref.shape[1]


def params():
    return pltpu.CompilerParams(vmem_limit_bytes=VMEM_LIMIT)


def whole(count):
    return [pl.BlockSpec(memory_space=pltpu.VMEM)] * count


def cost(products, moved):
    return pl.CostEstimate(flops=2 * products, bytes_accessed=moved, transcendentals=0)


def project(pieces, w, last, cos, sin, width_q):
    span, d = 4 * pieces[0].shape[0], pieces[0].shape[1]
    return pl.pallas_call(
        project_kernel,
        out_shape=(
            jax.ShapeDtypeStruct((width_q, span), BF),
            jax.ShapeDtypeStruct((span, 2 * HD), BF),
            jax.ShapeDtypeStruct((span, d), BF),
            jax.ShapeDtypeStruct((8, d), F32),
        ),
        in_specs=whole(8),
        out_specs=tuple(whole(4)),
        compiler_params=params(),
        cost_estimate=cost(span * d * (width_q + 2 * HD), 8 << 20),
        name="project",
    )(*pieces, w, last, cos, sin)


def hidden_units(pieces, cots, gains, weights, width):
    span, d = 4 * pieces[0].shape[0], pieces[0].shape[1]
    tile = 128
    tiles = width // tile

    def fixed(array):
        return pl.BlockSpec(array.shape, lambda i: (0, 0))

    def columns(base):
        return pl.BlockSpec((d, tile), lambda i: (0, i + base))

    out = pl.BlockSpec((span, tile), lambda i: (0, i))
    return pl.pallas_call(
        hidden_kernel,
        grid=(tiles,),
        out_shape=(jax.ShapeDtypeStruct((span, width), BF),) * 3
        + (jax.ShapeDtypeStruct((span, d), BF),) * 2,
        in_specs=[fixed(a) for a in (*pieces, *cots, gains)]
        + [columns(0), columns(tiles), columns(2 * tiles)],
        out_specs=(out,) * 3 + (pl.BlockSpec((span, d), lambda i: (0, 0)),) * 2,
        compiler_params=params(),
        cost_estimate=cost(3 * span * d * width, 6 * d * width),
        name="hidden_units",
    )(*pieces, *cots, gains, weights, weights, weights)


def rows_grad(grads, weights, pieces, gains, gain_row):
    span, d = 4 * pieces[0].shape[0], pieces[0].shape[1]
    tile = 256

    def fixed(array):
        return pl.BlockSpec(array.shape, lambda i: (0, 0))

    def rows(grad, index):
        return pl.BlockSpec((tile, grad.shape[1]), lambda i: (i, index))

    return pl.pallas_call(
        functools.partial(rows_grad_kernel, len(grads), gain_row),
        grid=(d // tile,),
        out_shape=jax.ShapeDtypeStruct((span, d), BF),
        in_specs=[fixed(g) for g in grads]
        + [rows(g, w[1]) for g, w in zip(grads, weights)]
        + [fixed(a) for a in (*pieces, gains)],
        out_specs=pl.BlockSpec((span, d), lambda i: (0, 0)),
        scratch_shapes=[pltpu.VMEM((span, d), F32)],
        compiler_params=params(),
        cost_estimate=cost(sum(span * d * g.shape[1] for g in grads), 8 << 20),
        name="rows_grad",
    )(*grads, *[w[0] for w in weights], *pieces, gains)


def window_specs():
    return [pl.BlockSpec(memory_space=pltpu.SMEM)] + whole(1)


def attend(q, kvs, window):
    n = len(kvs)
    width, span = q.shape
    heads = width // HD
    return pl.pallas_call(
        attend_kernel,
        out_shape=(
            jax.ShapeDtypeStruct((span, width), BF),
            jax.ShapeDtypeStruct((heads, span), F32),
        ),
        in_specs=whole(n + 1) + window_specs(),
        out_specs=tuple(whole(2)),
        scratch_shapes=[
            pltpu.VMEM((n * span, span), F32),
            pltpu.VMEM((n * span, span), F32),
            pltpu.VMEM((HD, n * span), BF),
        ],
        compiler_params=params(),
        cost_estimate=pl.CostEstimate(flops=16 * span * width * n * span, bytes_accessed=2 << 20, transcendentals=heads * n * span * span),
        name="attend",
    )(q, *kvs, *window)


def attend_back(distances, q, kvs, window, lse, prepared, mixed=None, grad=None, turn=None):
    n = len(kvs)
    width, span = q.shape
    heads = width // HD
    first, last = prepared is None, turn is not None
    operands = [q, *kvs, *window, lse]
    operands += [mixed, grad] if first else list(prepared)
    shapes = []
    if last:
        operands += turn
        shapes.append(jax.ShapeDtypeStruct((span, width), BF))
    else:
        shapes.append(jax.ShapeDtypeStruct((width, span), F32))
    shapes.append(jax.ShapeDtypeStruct((n * span, 2 * HD), F32 if last else BF))
    if first:
        shapes.append(jax.ShapeDtypeStruct((width, span), BF))
        shapes.append(jax.ShapeDtypeStruct((heads, span), F32))
    return pl.pallas_call(
        functools.partial(attend_back_kernel, distances, first, last),
        out_shape=tuple(shapes),
        in_specs=whole(n + 1) + window_specs() + whole(len(operands) - n - 3),
        out_specs=tuple(whole(len(shapes))),
        scratch_shapes=[
            pltpu.VMEM((n * span, span), F32),
            pltpu.VMEM((n * span, HD), BF),
            pltpu.VMEM((HD, n * span), BF),
            pltpu.VMEM((n * span, HD), F32),
            pltpu.VMEM((n * span, HD), F32),
        ],
        compiler_params=params(),
        cost_estimate=pl.CostEstimate(flops=40 * span * width * n * span, bytes_accessed=4 << 20, transcendentals=heads * n * span * span),
        name="attend_back",
    )(*operands)


def weight_grads(left, *rights):
    t, d = left.shape
    tile = 256
    width = sum(right.shape[1] for right in rights)
    return pl.pallas_call(
        weight_grads_kernel,
        grid=(d // tile,),
        out_shape=jax.ShapeDtypeStruct((d, width), BF),
        in_specs=[pl.BlockSpec((t, tile), lambda i: (0, i))]
        + [pl.BlockSpec(right.shape, lambda i: (0, 0)) for right in rights],
        out_specs=pl.BlockSpec((tile, width), lambda i: (i, 0)),
        compiler_params=params(),
        cost_estimate=cost(t * d * width, 2 * d * width + 4 * t * d),
        name="weight_grads",
    )(left, *rights)


def per_device(
    inputs,
    positions,
    attn_gain,
    query_weight,
    key_weight,
    value_weight,
    out_weight,
    mlp_gain,
    gate_weight,
    up_weight,
    down_weight,
    cotangent,
):
    width_q = query_weight.shape[1]
    width_k = key_weight.shape[1]
    hidden_width = gate_weight.shape[1]
    span = positions.shape[0]
    quarter = span // 4
    cut = 3 * width_q // 4

    inputs = to_inner(inputs)
    cotangent = to_inner(cotangent)

    pad = jnp.zeros((attn_gain.shape[0], 126), BF)
    shard_a = query_weight[:, :cut]
    shard_b = jnp.concatenate(
        [query_weight[:, cut:], key_weight, value_weight, attn_gain[:, None], mlp_gain[:, None], pad], 1
    )
    width_b = width_q - cut + 2 * width_k
    shard_mlp = jnp.concatenate([gate_weight, up_weight, down_weight.T], 1)
    other_a, other_b = swap(shard_a, "yh"), swap(shard_b, "yh")
    other_mlp = swap(shard_mlp, "yh")
    rows_in = gather_rows(inputs)

    part_b = gather_stage(join_sides(shard_b, other_b), "x", 0)
    part_a = gather_stage(join_sides(shard_a, other_a), "z", 0)
    out_turned = after(out_weight.T, part_a, part_b)
    other_out = swap(out_turned, "yh")
    mlp_pair = join_sides(shard_mlp, after(other_mlp, other_out))
    mlp_whole = lax.all_gather(mlp_pair, ("z", "x"), axis=0, tiled=True)
    whole_b = flat(gather_stage(part_b, "z", 0))
    whole_a = flat(gather_stage(part_a, "x", 1))
    pair_out = join_sides(out_turned, other_out)

    me = (lax.axis_index("yl") * 2 + lax.axis_index("core")).astype(jnp.int32)
    blocked = jnp.arange(4, dtype=jnp.int32) ^ me
    positions = jnp.take(positions.reshape(4, quarter), blocked, axis=0, mode="clip").reshape(1, span)
    freqs = 10000.0 ** (-(jnp.arange(HD // 2, dtype=F32) * 2.0) / HD)
    angles = freqs[:, None] * positions.astype(F32)
    cos, sin = jnp.cos(angles), jnp.sin(angles)
    window = (me.reshape(1, 1), positions)

    queries, kv_block, scaled_in, gains = project(rows_in, whole_a, whole_b, cos, sin, width_q)
    blocks = [kv_block] + [shift(kv_block, "x", d) for d in range(1, SEQ_DEVS)]
    part_out = gather_stage(pair_out, "x", 0, hold=[kv_block])
    cotangents = gather_rows(after(cotangent, kv_block))
    mixed, log_total = attend(queries, blocks, window)
    out_whole = flat(gather_stage(part_out, "z", 0, hold=[log_total]))

    middle = inputs.astype(F32) + scatter_rows(contract_last(mixed, out_whole))
    rows_mid = gather_rows(middle.astype(BF))
    hidden, grad_gate, grad_up, scaled_mid, cotangent_all = hidden_units(
        rows_mid, cotangents, gains, mlp_whole, hidden_width
    )
    mid_partial = rows_grad(
        [grad_gate, grad_up], [(mlp_whole, 0), (mlp_whole, 1)], rows_mid, gains, 1
    )
    mid_part = scatter_rows(mid_partial)
    grad_middle = cotangent.astype(F32) + mid_part
    grad_middle_all = jnp.concatenate(gather_rows(grad_middle.astype(BF)), 0)

    gate_up_sum = weight_grads(after(scaled_mid, mid_partial), grad_gate, grad_up)
    gate_up_sum = lax.psum_scatter(gate_up_sum, ("z", "x"), scatter_dimension=0, tiled=True)
    down_parts = wide_parts(after(cotangent_all, mid_partial), hidden, "z")
    mlp_partial = contract_last(after(hidden, down_parts), mlp_whole[:, 2 * hidden_width :])

    grad_mixed = jnp.dot(grad_middle_all, out_whole, preferred_element_type=F32).astype(BF)
    out_parts = wide_parts(grad_middle_all, mixed, "x")
    down_sum = exchange_sum(down_parts, "z", hold=[grad_middle_all]).astype(BF)
    query_part, far_grads, grad_turned, delta = attend_back(
        (1, 2, 3), queries, blocks[1:], window, log_total, None, mixed, after(grad_mixed, out_parts)
    )
    mlp_rows = scatter_rows(after(mlp_partial, grad_middle_all))
    output = (middle + mlp_rows).astype(BF)
    arriving = [
        shift(far_grads[(d - 1) * span : d * span], "x", -d) for d in range(1, SEQ_DEVS)
    ]
    out_sum = exchange_sum(out_parts, "x", hold=[query_part]).astype(BF)
    down_sum = wide_sum_next(down_sum, "x", hold=[query_part])
    query_raw_grad, carried = attend_back(
        (0,), queries, blocks[:1], window, log_total, (grad_turned, delta, query_part), turn=[cos, sin]
    )
    out_sum = wide_sum_next(out_sum, "z", hold=[query_raw_grad])
    outer = jnp.concatenate([down_sum, out_sum], 1)
    for piece in arriving:
        carried = carried + piece.astype(F32)

    a_sum = exchange_sum(wide_parts(scaled_in, query_raw_grad[:, :cut], "x"), "x").astype(BF)
    turned = carried[:, :width_k]
    first, second = turned[:, : HD // 2], turned[:, HD // 2 :]
    key_raw_grad = jnp.concatenate(
        [first * cos.T + second * sin.T, second * cos.T - first * sin.T], 1
    ).astype(BF)
    grad_b = jnp.concatenate(
        [query_raw_grad[:, cut:], key_raw_grad, carried[:, width_k:].astype(BF)], 1
    )
    in_part = scatter_rows(
        rows_grad([query_raw_grad[:, :cut], grad_b], [(whole_a, 0), (whole_b, 0)], rows_in, gains, 0)
    )
    input_grad = grad_middle + in_part
    b_sum = exchange_sum(wide_parts(scaled_in, grad_b, "z"), "z").astype(BF)
    a_sum, b_sum = wide_sum_next(a_sum, "z"), wide_sum_next(b_sum, "x")
    attn_sum = sides_sum(jnp.concatenate([a_sum, b_sum], 1))
    a_grad, b_grad = attn_sum[:, :cut], attn_sum[:, cut:]
    outer_grad = sides_sum(outer, hold=[b_sum]).T
    down_grad, out_grad = outer_grad[:hidden_width], outer_grad[hidden_width:]
    mlp_grad = sides_sum(after(gate_up_sum, query_raw_grad))
    gate_grad, up_grad = mlp_grad[:, :hidden_width], mlp_grad[:, hidden_width:]

    attn_gain_part = jnp.sum(shard_a.astype(F32) * a_grad, 1) + jnp.sum(
        shard_b[:, :width_b].astype(F32) * b_grad, 1
    )
    mlp_gain_part = jnp.sum(
        gate_weight.astype(F32) * gate_grad + up_weight.astype(F32) * up_grad, 1
    )
    attn_gain_grad, mlp_gain_grad = lax.psum((attn_gain_part, mlp_gain_part), TP)
    own = width_q - cut
    return (
        from_inner(output),
        from_inner(input_grad),
        attn_gain_grad / attn_gain.astype(F32),
        jnp.concatenate([a_grad, b_grad[:, :own]], 1),
        b_grad[:, own : own + width_k],
        b_grad[:, own + width_k :],
        out_grad,
        mlp_gain_grad / mlp_gain.astype(F32),
        gate_grad,
        up_grad,
        down_grad,
    )


def solution(mesh):
    split = Mesh(mesh.devices.reshape(2, 4, 4, 2, 2), WIDE + TP)
    rows = P(WIDE + TP, None)
    inward = P(WIDE, TP)
    outward = P(TP, WIDE)
    gain = P(WIDE)
    return jax.shard_map(
        per_device,
        mesh=split,
        in_specs=(
            rows, gain, gain, inward, inward, inward, outward, gain, inward, inward, outward, rows,
        ),
        out_specs=(
            rows, rows, gain, inward, inward, inward, outward, gain, inward, inward, outward,
        ),
        check_vma=False,
    )
```

```python
import functools

import jax
import jax.numpy as jnp
from jax import lax
from jax.experimental import pallas as pl
from jax.experimental.pallas import tpu as pltpu
from jax.sharding import Mesh, PartitionSpec as P

HEADS = 32
KV = 4
HD = 64
SEQ_DEVS = 4
WIDE = ("yh", "z", "x")
TP = ("yl", "core")
BF = jnp.bfloat16
F32 = jnp.float32

epsilon = 1e-05
masked_fill = -1e30
VMEM_LIMIT = 56 * 1024 * 1024


def after(value, *earlier):
    return lax.optimization_barrier((value, earlier))[0]


def shift(block, axis, distance):
    n = lax.axis_size(axis)
    return lax.ppermute(block, axis, [(i, (i + distance) % n) for i in range(n)])


def swap(block, axis):
    return shift(block, axis, 1)


def place(axis, step=0):
    n = lax.axis_size(axis)
    return ((lax.axis_index(axis) + (step + n)) & (n - 1)).astype(jnp.uint32)


def pick(array, index, dim):
    return lax.dynamic_index_in_dim(array, index, dim, keepdims=False)


def send_stage(block, axis):
    n = lax.axis_size(axis)
    return [block] + [shift(block, axis, d) for d in (1, n - 1, *range(2, n - 1))]


def stack_stage(arrived, axis, dim):
    n = len(arrived)
    block = arrived[0]
    out = jnp.zeros(block.shape[:dim] + (n,) + block.shape[dim:], block.dtype)
    for d, piece in zip((0, 1, n - 1, *range(2, n - 1)), arrived):
        out = lax.dynamic_update_index_in_dim(out, piece, place(axis, -d), dim)
    return out


def gather_ring(block, axis, dim):
    half = block.shape[0] // 2
    left, right = shift(block, axis, 1), shift(block, axis, -1)
    upper, lower = shift(left[:half], axis, 1), shift(right[half:], axis, -1)
    out = jnp.zeros(block.shape[:dim] + (4,) + block.shape[dim:], block.dtype)
    out = lax.dynamic_update_index_in_dim(out, block, place(axis), dim)
    out = lax.dynamic_update_index_in_dim(out, left, place(axis, -1), dim)
    out = lax.dynamic_update_index_in_dim(out, right, place(axis, 1), dim)
    return lax.dynamic_update_index_in_dim(
        out, jnp.concatenate([upper, lower], 0), place(axis, 2), dim
    )


def join_sides(shard, other):
    first = lax.axis_index("yh") == 0
    return jnp.concatenate([jnp.where(first, shard, other), jnp.where(first, other, shard)], 0)


def flat(blocks):
    return blocks.reshape(-1, blocks.shape[-1])


def to_inner(rows):
    t, d = rows.shape
    return rows.reshape(t, 2, 16, d // 32).transpose(0, 2, 1, 3).reshape(t, d)


def gather_rows(rows):
    across = swap(rows, "yl")
    return [rows, swap(rows, "core"), across, swap(across, "core")]


def scatter_cores(partial):
    n = partial.shape[0] // 4
    far = swap(partial[3 * n :], "core").astype(F32)
    near = swap(partial[n : 2 * n], "core")
    return partial[:n], near, (partial[2 * n : 3 * n].astype(F32) + far).astype(BF)


def scatter_rows(partial):
    own, near, other = scatter_cores(partial)
    return [own, near, swap(other, "yl")]


def total(first, parts):
    for part in parts:
        first = first + part.astype(F32)
    return first


def exchange_sum(parts, axis, hold=()):
    n = len(parts)
    total = parts[0].astype(F32)
    for d in (1, n - 1, *range(2, n - 1))[: n - 1]:
        total = total + after(shift(parts[d].astype(BF), axis, d), *hold).astype(F32)
    return total


def sides_sum(part, hold=()):
    half = part.reshape(2, part.shape[0] // 2, part.shape[1])
    return exchange_sum([pick(half, place("yh"), 0), pick(half, place("yh", 1), 0)], "yh", hold)


def wide_sum_next(part, axis, hold=()):
    n = lax.axis_size(axis)
    part = part.reshape(n, part.shape[0] // n, part.shape[1])
    pieces = [pick(part, place(axis, d), 0) for d in range(n)]
    return exchange_sum(pieces, axis, hold).astype(BF)


def mm(left, right):
    return jnp.dot(left, right, preferred_element_type=F32)


def mm_last(left, right):
    return lax.dot_general(left, right, (((1,), (1,)), ((), ())), preferred_element_type=F32)


def normed_rows(piece):
    values = piece.astype(F32)
    factor = lax.rsqrt(jnp.mean(values * values, -1, keepdims=True) + epsilon)
    return values * factor, factor


def scale_rows(piece_refs, gain, scaled_ref):
    for n, ref in enumerate(piece_refs):
        for at in range(0, ref.shape[0], 32):
            normed, _ = normed_rows(ref[at : at + 32, :])
            rows = n * ref.shape[0] + at
            scaled_ref[rows : rows + 32, :] = (normed * gain).astype(BF)


def project_kernel(skip, *refs):
    piece_refs, (w_ref, last_ref, cos_ref, sin_ref, q_ref, kv_ref, scaled_ref, gains_ref) = refs[:4], refs[4:]
    width_q = q_ref.shape[0]
    half = HD // 2
    cos, sin = cos_ref[...], sin_ref[...]
    tiles = [(w, at) for w in (w_ref, last_ref) for at in range(skip, w.shape[1], 128)]

    def turned(block):
        a, b = block[:half], block[half:]
        return jnp.concatenate([a * cos - b * sin, b * cos + a * sin], 0)

    w, at = tiles[-1]
    gains_ref[...] = w[:, at : at + 128].T[:8].astype(F32)
    scale_rows(piece_refs, gains_ref[0:1, :], scaled_ref)
    x = scaled_ref[...]
    for n in range(width_q // 128):
        w, at = tiles[n]
        piece = mm(x, w[:, at : at + 128]).T
        for sub in range(0, 128, HD):
            low = turned(piece[sub : sub + HD]).astype(BF)
            q_ref[n * 128 + sub : n * 128 + sub + HD, :] = low * 0.125
    w, at = tiles[width_q // 128]
    piece = mm(x, w[:, at : at + 128]).T
    kv = jnp.concatenate([turned(piece[:HD]), piece[HD:]], 0)
    kv_ref[...] = kv.T.astype(BF)


def hidden_kernel(*refs):
    pieces, cots, (gain_ref, gate_ref, up_ref, down_ref, hidden_ref, dgate_ref, dup_ref, scaled_ref, cot_ref) = (
        refs[:4], refs[4:8], refs[8:],
    )

    @pl.when(pl.program_id(0) == 0)
    def _():
        scale_rows(pieces, gain_ref[1:2, :], scaled_ref)
        for n, ref in enumerate(cots):
            cot_ref[n * ref.shape[0] : (n + 1) * ref.shape[0], :] = ref[...]

    tile = gate_ref.shape[1]
    both = mm(scaled_ref[...], jnp.concatenate([gate_ref[...], up_ref[...]], 1))
    grad = mm(cot_ref[...], down_ref[...])
    gate, up = both[:, :tile], both[:, tile:]
    sigmoid = 1.0 / (1.0 + jnp.exp(-gate))
    gated = gate * sigmoid
    hidden_ref[...] = (gated * up).astype(BF)
    dgate_ref[...] = (grad * up * sigmoid * (1.0 + gate * (1.0 - sigmoid))).astype(BF)
    dup_ref[...] = (grad * gated).astype(BF)


def sum_of_products(terms, refs):
    total = None
    for left, (low, high), right, (first, last) in terms:
        part = mm_last(refs[left][:, low:high], refs[right][:, first:last])
        total = part if total is None else total + part
    return total


def rows_grad_kernel(terms, count, gain_row, *refs):
    pieces = refs[count : count + 4]
    gain_ref, out_ref, sum_ref = refs[count + 4 :]
    step = pl.program_id(0)
    tile = sum_ref.shape[1] // pl.num_programs(0)
    columns = pl.ds(pl.multiple_of(step * tile, tile), tile)
    sum_ref[:, columns] = sum_of_products(terms, refs) * gain_ref[gain_row : gain_row + 1, columns]

    @pl.when(step == pl.num_programs(0) - 1)
    def _():
        for n, ref in enumerate(pieces):
            for at in range(0, ref.shape[0], 32):
                normed, factor = normed_rows(ref[at : at + 32, :])
                rows = slice(n * ref.shape[0] + at, n * ref.shape[0] + at + 32)
                scaled = sum_ref[rows, :]
                inner = jnp.mean(scaled * normed, -1, keepdims=True)
                out_ref[rows, :] = (factor * (scaled - normed * inner)).astype(BF)


def rows_out_kernel(terms, *refs):
    refs[-1][...] = sum_of_products(terms, refs).astype(BF)


def write_parts(outs, turned_of, axis, me, right, base):
    for d, out in enumerate(outs):
        index = (me + d) & 3
        if axis == "z":
            turned = turned_of(pl.multiple_of(index * 512, 512), 512)
        else:
            turned = jnp.concatenate(
                [turned_of(pl.multiple_of(z * 512 + index * 128, 128), 128) for z in range(4)], 0
            )
        out[:, base : base + right.shape[1]] = mm(turned, right).astype(BF)


def parts_kernel(axis, columns, count, me_ref, *refs):
    lefts, right_ref, outs = refs[:count], refs[count], refs[count + 1 :]

    def turned_of(at, size):
        return jnp.concatenate([left[:, pl.ds(at, size)] for left in lefts], 0).T

    write_parts(outs, turned_of, axis, me_ref[0, 0], right_ref[:, columns[0] : columns[1]], 0)


def last_parts_kernel(axis, cut, me_ref, left_ref, dq_ref, own_ref, one_ref, two_ref, three_ref,
                      cos_ref, sin_ref, *outs):
    half = HD // 2
    cos, sin = cos_ref[...], sin_ref[...]
    kv = own_ref[...]
    for ref in (one_ref, two_ref, three_ref):
        kv = kv + ref[...].astype(F32)
    kv = kv.T
    a, b = kv[:half], kv[half:HD]
    kv = jnp.concatenate([a * cos + b * sin, b * cos - a * sin, kv[HD:]], 0).T.astype(BF)
    outs[0][...] = kv
    right = jnp.concatenate([dq_ref[:, cut:], kv], 1)

    def turned_of(at, size):
        return left_ref[:, pl.ds(at, size)].T

    write_parts(outs[1:], turned_of, axis, me_ref[0, 0], right, 0)


def settle_kernel(base_ref, *refs):
    out_ref = refs[-1]
    width = base_ref.shape[1]

    def block(at):
        value = base_ref[:, at : at + 128].astype(F32)
        for ref in refs[:-1]:
            value = value + ref[:, at : at + 128].astype(F32)
        return value

    for n in range(width // 256):
        one, two = block(256 * n), block(256 * n + 128)
        low = jnp.concatenate([one[:, :HD], two[:, :HD]], 1)
        high = jnp.concatenate([one[:, HD:], two[:, HD:]], 1)
        out_ref[:, 128 * n : 128 * n + 128] = low.astype(out_ref.dtype)
        out_ref[:, width // 2 + 128 * n : width // 2 + 128 * n + 128] = high.astype(out_ref.dtype)


def fill_bias(bias_ref, me_ref, pos_ref, span, distances):
    step = 64
    quarter = span // 4
    me = me_ref[0, 0]
    at = lax.broadcasted_iota(jnp.int32, (1, span), 1)
    query = (((at // quarter) ^ me) * quarter) + (at & (quarter - 1))
    first = query - pos_ref[...]

    @pl.loop(0, span // step)
    def _(i):
        block = (i * step) // quarter
        start = (block ^ me) * quarter + i * step - block * quarter
        key = start + lax.broadcasted_iota(jnp.int32, (step, span), 0)
        for n, d in enumerate(distances):
            seen = (key - d * span <= query) & (key - d * span >= first)
            bias_ref[pl.ds(pl.multiple_of(n * span + i * step, step), step), :] = jnp.where(
                seen, 0.0, masked_fill
            ).astype(F32)


def attend_kernel(q_ref, *refs):
    blocks = len(refs) - 7
    kv_refs = refs[:blocks]
    me_ref, pos_ref, mix_ref, lse_ref, bias_ref, s_ref, vt_ref = refs[blocks:]
    span = q_ref.shape[1]
    fill_bias(bias_ref, me_ref, pos_ref, span, range(blocks))
    for d in range(blocks):
        vt_ref[:, d * span : (d + 1) * span] = kv_refs[d][...].T[HD:]

    @pl.loop(0, q_ref.shape[0] // 128)
    def _(pair):
        outs = []
        for sub in range(2):
            q = q_ref[pl.ds(pl.multiple_of(pair * 128 + sub * HD, HD), HD), :]
            top = None
            for d in range(blocks):
                rows = slice(d * span, (d + 1) * span)
                s = mm(kv_refs[d][:, :HD], q) + bias_ref[rows, :]
                s_ref[rows, :] = s
                high = jnp.max(s, 0, keepdims=True)
                top = high if top is None else jnp.maximum(top, high)
            total = jnp.zeros_like(top)
            out = jnp.zeros((HD, span), F32)
            for d in range(blocks):
                rows = slice(d * span, (d + 1) * span)
                p = jnp.exp(s_ref[rows, :] - top)
                total = total + jnp.sum(p, 0, keepdims=True)
                out = out + mm(vt_ref[:, rows], p.astype(BF))
            outs.append(out / total)
            lse_ref[pl.ds(pair * 2 + sub, 1), :] = top + jnp.log(total)
        mix_ref[:, pl.ds(pl.multiple_of(pair * 128, 128), 128)] = (
            jnp.concatenate(outs, 0).T.astype(BF)
        )


def attend_back_kernel(distances, first, last, q_ref, *refs):
    blocks = len(distances)
    refs = list(refs)

    def take(count):
        got, refs[:count] = refs[:count], []
        return got

    kv_refs = take(blocks)
    me_ref, pos_ref, lse_ref = take(3)
    if first:
        mix_ref, wa_ref, wb_ref, *piece_refs = take(7)
    else:
        gt_ref, delta_ref, part_ref = take(3)
    if last:
        cos_ref, sin_ref = take(2)
        (dq_ref,) = take(1)
    else:
        (sum_ref,) = take(1)
    (dkv_ref,) = take(1)
    if first:
        gt_ref, delta_ref = take(2)
    bias_ref, v_ref, kt_ref, dk_ref, dv_ref = take(5)
    span = q_ref.shape[1]
    half = HD // 2
    heads = q_ref.shape[0] // HD
    fill_bias(bias_ref, me_ref, pos_ref, span, distances)
    for n in range(blocks):
        rows = slice(n * span, (n + 1) * span)
        both = kv_refs[n][...].T
        kt_ref[:, rows] = both[:HD]
        v_ref[rows, :] = both[HD:].T
    dk_ref[...] = jnp.zeros_like(dk_ref)
    dv_ref[...] = jnp.zeros_like(dv_ref)
    if first:
        rows_all = jnp.concatenate([ref[...] for ref in piece_refs], 0)
        grads = [mm(rows_all, w_ref[:, : heads * HD // 2]).astype(BF) for w_ref in (wa_ref, wb_ref)]
        for at in range(0, heads * HD, 128):
            where = at % (heads * HD // 2)
            gt = grads[2 * at // (heads * HD)][:, where : where + 128].T
            mt = mix_ref[:, at : at + 128].T
            gt_ref[at : at + 128, :] = gt
            prod = gt.astype(F32) * mt.astype(F32)
            for sub in range(2):
                h = at // HD + sub
                delta_ref[h : h + 1, :] = jnp.sum(prod[sub * HD : (sub + 1) * HD], 0, keepdims=True)

    @pl.loop(0, heads // 2)
    def _(pair):
        outs = []
        for sub in range(2):
            rows_h = pl.ds(pl.multiple_of(pair * 128 + sub * HD, HD), HD)
            q, g = q_ref[rows_h, :], gt_ref[rows_h, :]
            lse = lse_ref[pl.ds(pair * 2 + sub, 1), :]
            delta = delta_ref[pl.ds(pair * 2 + sub, 1), :]
            dq = jnp.zeros((HD, span), F32) if first else part_ref[rows_h, :]
            for n in range(blocks):
                rows = slice(n * span, (n + 1) * span)
                s = mm(kv_refs[n][:, :HD], q) + bias_ref[rows, :]
                p = jnp.exp(s - lse)
                ds = (p * (mm(v_ref[rows, :], g) - delta)).astype(BF)
                dv_ref[rows, :] += mm_last(p.astype(BF), g)
                dk_ref[rows, :] += mm_last(ds, q)
                dq = dq + mm(kt_ref[:, rows], ds)
            if last:
                dq = dq * 0.125
                a, b = dq[:half], dq[half:]
                cos, sin = cos_ref[...], sin_ref[...]
                outs += [a * cos + b * sin, b * cos - a * sin]
            else:
                sum_ref[rows_h, :] = dq
        if last:
            dq_ref[:, pl.ds(pl.multiple_of(pair * 128, 128), 128)] = (
                jnp.concatenate(outs, 0).T.astype(BF)
            )

    for n in range(blocks):
        rows = slice(n * span, (n + 1) * span)
        dkv_ref[rows, :] = jnp.concatenate([dk_ref[rows, :], dv_ref[rows, :]], 1).astype(dkv_ref.dtype)


def weight_grads_kernel(left_ref, one_ref, two_ref, other_left_ref, other_ref, out_ref):
    at = 0
    for lefts, rights in ((left_ref, (one_ref, two_ref)), (other_left_ref, (other_ref,))):
        turned = lefts[...].T
        for ref in rights:
            for c in range(0, ref.shape[1], 256):
                size = min(256, ref.shape[1] - c)
                out_ref[:, at + c : at + c + size] = mm(turned, ref[:, c : c + size]).astype(BF)
            at += ref.shape[1]


def params():
    return pltpu.CompilerParams(vmem_limit_bytes=VMEM_LIMIT)


def whole(count):
    return [pl.BlockSpec(memory_space=pltpu.VMEM)] * count


def cost(products, moved):
    return pl.CostEstimate(flops=2 * products, bytes_accessed=moved, transcendentals=0)


def project(pieces, w, last, skip, cos, sin, width_q):
    span, d = 4 * pieces[0].shape[0], pieces[0].shape[1]
    return pl.pallas_call(
        functools.partial(project_kernel, skip),
        out_shape=(
            jax.ShapeDtypeStruct((width_q, span), BF),
            jax.ShapeDtypeStruct((span, 2 * HD), BF),
            jax.ShapeDtypeStruct((span, d), BF),
            jax.ShapeDtypeStruct((8, d), F32),
        ),
        in_specs=whole(8),
        out_specs=tuple(whole(4)),
        compiler_params=params(),
        cost_estimate=cost(span * d * (width_q + 2 * HD), 8 << 20),
        name="project",
    )(*pieces, w, last, cos, sin)


def hidden_units(pieces, cots, gains, weights, width):
    span, d = 4 * pieces[0].shape[0], pieces[0].shape[1]
    tile = 128
    tiles = width // tile

    def columns(base):
        return pl.BlockSpec((d, tile), lambda i: (0, i + base))

    out = pl.BlockSpec((span, tile), lambda i: (0, i))
    return pl.pallas_call(
        hidden_kernel,
        grid=(tiles,),
        out_shape=(jax.ShapeDtypeStruct((span, width), BF),) * 3
        + (jax.ShapeDtypeStruct((span, d), BF),) * 2,
        in_specs=[fixed(a) for a in (*pieces, *cots, gains)]
        + [columns(0), columns(tiles), columns(2 * tiles)],
        out_specs=(out,) * 3 + (pl.BlockSpec((span, d), lambda i: (0, 0)),) * 2,
        compiler_params=params(),
        cost_estimate=cost(3 * span * d * width, 6 * d * width),
        name="hidden_units",
    )(*pieces, *cots, gains, weights, weights, weights)


def feature_rows(weight, tile):
    if not isinstance(weight, tuple):
        return pl.BlockSpec((tile, weight.shape[1]), lambda i: (i, 0))
    return pl.BlockSpec((tile, weight[2]), lambda i: (i, weight[1]))


def array_of(weight):
    return weight[0] if isinstance(weight, tuple) else weight


def fixed(array):
    return pl.BlockSpec(array.shape, lambda i: (0, 0))


def rows_grad(grads, weights, terms, pieces, gains, gain_row):
    span, d = 4 * pieces[0].shape[0], pieces[0].shape[1]
    tile = 256
    n = len(grads)
    terms = [(g, c, n + w, e) for g, c, w, e in terms]
    return pl.pallas_call(
        functools.partial(rows_grad_kernel, terms, n + len(weights), gain_row),
        grid=(d // tile,),
        out_shape=jax.ShapeDtypeStruct((span, d), BF),
        in_specs=[fixed(g) for g in grads]
        + [feature_rows(w, tile) for w in weights]
        + [fixed(a) for a in (*pieces, gains)],
        out_specs=pl.BlockSpec((span, d), lambda i: (0, 0)),
        scratch_shapes=[pltpu.VMEM((span, d), F32)],
        compiler_params=params(),
        cost_estimate=cost(sum(span * d * (c[1] - c[0]) for _, c, _, _ in terms), 8 << 20),
        name="rows_grad",
    )(*grads, *map(array_of, weights), *pieces, gains)


def rows_out(lefts, weights, terms):
    span, d = lefts[0].shape[0], array_of(weights[0]).shape[0]
    tile = 256
    n = len(lefts)
    terms = [(g, c, n + w, e) for g, c, w, e in terms]
    return pl.pallas_call(
        functools.partial(rows_out_kernel, terms),
        grid=(d // tile,),
        out_shape=jax.ShapeDtypeStruct((span, d), BF),
        in_specs=[fixed(g) for g in lefts] + [feature_rows(w, tile) for w in weights],
        out_specs=pl.BlockSpec((span, tile), lambda i: (0, i)),
        compiler_params=params(),
        cost_estimate=cost(sum(span * d * (c[1] - c[0]) for _, c, _, _ in terms), 6 << 20),
        name="rows_out",
    )(*lefts, *map(array_of, weights))


def scalar():
    return [pl.BlockSpec(memory_space=pltpu.SMEM)]


def at_place(axis):
    return place(axis).astype(jnp.int32).reshape(1, 1)


def wide_parts(lefts, right, columns, axis):
    span, d = right.shape[0], lefts[0].shape[1]
    width = columns[1] - columns[0]
    return pl.pallas_call(
        functools.partial(parts_kernel, axis, columns, len(lefts)),
        out_shape=(jax.ShapeDtypeStruct((d // 4, width), BF),) * 4,
        in_specs=scalar() + whole(len(lefts) + 1),
        out_specs=tuple(whole(4)),
        compiler_params=params(),
        cost_estimate=cost(span * d * width, 8 << 20),
        name="wide_parts",
    )(at_place(axis), *lefts, right)


def last_parts(left, dq, cut, own, arrived, cos, sin, axis):
    span, d = left.shape
    width = dq.shape[1] - cut + 2 * HD
    return pl.pallas_call(
        functools.partial(last_parts_kernel, axis, cut),
        out_shape=(jax.ShapeDtypeStruct((span, 2 * HD), BF),)
        + (jax.ShapeDtypeStruct((d // 4, width), BF),) * 4,
        in_specs=scalar() + whole(8),
        out_specs=tuple(whole(5)),
        compiler_params=params(),
        cost_estimate=cost(span * d * width, 8 << 20),
        name="last_parts",
    )(at_place(axis), left, dq, own, *arrived, cos, sin)


def settle(base, parts, kind):
    return pl.pallas_call(
        settle_kernel,
        out_shape=jax.ShapeDtypeStruct(base.shape, kind),
        in_specs=whole(1 + len(parts)),
        out_specs=whole(1)[0],
        compiler_params=params(),
        cost_estimate=cost(0, 4 << 20),
        name="settle",
    )(base, *parts)


def window_specs():
    return [pl.BlockSpec(memory_space=pltpu.SMEM)] + whole(1)


def attend(q, kvs, window):
    n = len(kvs)
    width, span = q.shape
    heads = width // HD
    return pl.pallas_call(
        attend_kernel,
        out_shape=(
            jax.ShapeDtypeStruct((span, width), BF),
            jax.ShapeDtypeStruct((heads, span), F32),
        ),
        in_specs=whole(n + 1) + window_specs(),
        out_specs=tuple(whole(2)),
        scratch_shapes=[
            pltpu.VMEM((n * span, span), F32),
            pltpu.VMEM((n * span, span), F32),
            pltpu.VMEM((HD, n * span), BF),
        ],
        compiler_params=params(),
        cost_estimate=pl.CostEstimate(flops=16 * span * width * n * span, bytes_accessed=2 << 20, transcendentals=heads * n * span * span),
        name="attend",
    )(q, *kvs, *window)


def attend_back(distances, q, kvs, window, lse, prepared, mixed=None, out=None, turn=None):
    n = len(kvs)
    width, span = q.shape
    heads = width // HD
    first, last = prepared is None, turn is not None
    operands = [q, *kvs, *window, lse]
    operands += [mixed, *out] if first else list(prepared)
    shapes = []
    if last:
        operands += turn
        shapes.append(jax.ShapeDtypeStruct((span, width), BF))
    else:
        shapes.append(jax.ShapeDtypeStruct((width, span), F32))
    shapes.append(jax.ShapeDtypeStruct((n * span, 2 * HD), F32 if last else BF))
    if first:
        shapes.append(jax.ShapeDtypeStruct((width, span), BF))
        shapes.append(jax.ShapeDtypeStruct((heads, span), F32))
    return pl.pallas_call(
        functools.partial(attend_back_kernel, distances, first, last),
        out_shape=tuple(shapes),
        in_specs=whole(n + 1) + window_specs() + whole(len(operands) - n - 3),
        out_specs=tuple(whole(len(shapes))),
        scratch_shapes=[
            pltpu.VMEM((n * span, span), F32),
            pltpu.VMEM((n * span, HD), BF),
            pltpu.VMEM((HD, n * span), BF),
            pltpu.VMEM((n * span, HD), F32),
            pltpu.VMEM((n * span, HD), F32),
        ],
        compiler_params=params(),
        cost_estimate=pl.CostEstimate(flops=40 * span * width * n * span, bytes_accessed=4 << 20, transcendentals=heads * n * span * span),
        name="attend_back",
    )(*operands)


def weight_grads(left, one, two, other_left, other):
    t, d = left.shape
    tile = 256
    rows = pl.BlockSpec((t, tile), lambda i: (0, i))
    width = one.shape[1] + two.shape[1] + other.shape[1]
    return pl.pallas_call(
        weight_grads_kernel,
        grid=(d // tile,),
        out_shape=jax.ShapeDtypeStruct((d, width), BF),
        in_specs=[rows, fixed(one), fixed(two), rows, fixed(other)],
        out_specs=pl.BlockSpec((tile, width), lambda i: (i, 0)),
        compiler_params=params(),
        cost_estimate=cost(t * d * width, 2 * d * width + 4 * t * d),
        name="weight_grads",
    )(left, one, two, other_left, other)


def per_device(
    inputs,
    positions,
    attn_gain,
    query_weight,
    key_weight,
    value_weight,
    out_weight,
    mlp_gain,
    gate_weight,
    up_weight,
    down_weight,
    cotangent,
):
    width_q = query_weight.shape[1]
    width_k = key_weight.shape[1]
    hidden_width = gate_weight.shape[1]
    span = positions.shape[0]
    quarter = span // 4
    cut = 3 * width_q // 4
    skip = width_q // 2

    inputs = to_inner(inputs)
    cotangent = to_inner(cotangent)

    pad = jnp.zeros((attn_gain.shape[0], 126), BF)
    out_turned = out_weight.T
    shard_a = jnp.concatenate([out_turned[:, :skip], query_weight[:, :cut]], 1)
    shard_b = jnp.concatenate(
        [out_turned[:, skip:], query_weight[:, cut:], key_weight, value_weight,
         attn_gain[:, None], mlp_gain[:, None], pad], 1
    )
    width_b = width_q - cut + 2 * width_k
    shard_mlp = jnp.concatenate([gate_weight, up_weight, down_weight.T], 1)
    other_a, other_b = swap(shard_a, "yh"), swap(shard_b, "yh")
    other_mlp = swap(shard_mlp, "yh")
    rows_in = gather_rows(inputs)
    along_b = send_stage(join_sides(shard_b, other_b), "x")
    along_a = send_stage(join_sides(shard_a, other_a), "z")
    mlp_pair = join_sides(shard_mlp, after(other_mlp, along_a[1:], along_b[1:]))
    mlp_whole = lax.all_gather(mlp_pair, ("z", "x"), axis=0, tiled=True)
    part_b = stack_stage(along_b, "x", 0)
    part_a = stack_stage(along_a, "z", 0)
    whole_b = flat(gather_ring(part_b, "z", 0))
    whole_a = flat(gather_ring(part_a, "x", 1))

    me = (lax.axis_index("yl") * 2 + lax.axis_index("core")).astype(jnp.int32)
    blocked = jnp.arange(4, dtype=jnp.int32) ^ me
    positions = jnp.take(positions.reshape(4, quarter), blocked, axis=0, mode="clip").reshape(1, span)
    freqs = 10000.0 ** (-(jnp.arange(HD // 2, dtype=F32) * 2.0) / HD)
    angles = freqs[:, None] * positions.astype(F32)
    cos, sin = jnp.cos(angles), jnp.sin(angles)
    window = (me.reshape(1, 1), positions)

    queries, kv_block, scaled_in, gains = project(
        rows_in, whole_a, whole_b, skip, cos, sin, width_q
    )
    blocks = [kv_block] + [shift(kv_block, "x", d) for d in range(1, SEQ_DEVS)]
    cotangents = gather_rows(after(cotangent, kv_block))
    mixed, log_total = attend(queries, blocks, window)

    attn_rows = rows_out(
        [mixed], [whole_a, whole_b],
        [(0, (0, skip), 0, (0, skip)), (0, (skip, width_q), 1, (0, skip))],
    )
    middle = total(inputs.astype(F32), scatter_rows(attn_rows))
    rows_mid = gather_rows(middle.astype(BF))
    hidden, grad_gate, grad_up, scaled_mid, cotangent_all = hidden_units(
        rows_mid, cotangents, gains, mlp_whole, hidden_width
    )
    every = (0, hidden_width)
    mid_partial = rows_grad(
        [grad_gate, grad_up],
        [(mlp_whole, 0, hidden_width), (mlp_whole, 1, hidden_width)],
        [(0, every, 0, every), (1, every, 1, every)],
        rows_mid, gains, 1,
    )
    grad_middle = total(cotangent.astype(F32), scatter_rows(mid_partial))
    rows_grad_middle = gather_rows(grad_middle.astype(BF))

    mlp_sum = weight_grads(
        after(scaled_mid, mid_partial), grad_gate, grad_up, cotangent_all, hidden
    )
    mlp_rows = rows_out(
        [after(hidden, mlp_sum)], [(mlp_whole, 2, hidden_width)], [(0, every, 0, every)]
    )
    mlp_sum = lax.psum_scatter(mlp_sum, ("z", "x"), scatter_dimension=0, tiled=True)

    out_parts = wide_parts(rows_grad_middle, mixed, (0, width_q), "z")
    mlp_own, mlp_near, mlp_other = scatter_cores(mlp_rows)
    query_part, far_grads, grad_turned, delta = attend_back(
        (1, 2, 3), queries, blocks[1:], window, log_total, None, after(mixed, out_parts, mlp_other),
        [whole_a, whole_b, *rows_grad_middle],
    )
    mlp_across = swap(after(mlp_other, rows_grad_middle), "yl")
    output = settle(middle, [mlp_own, mlp_near, after(mlp_across, query_part)], BF)
    arriving = [
        shift(far_grads[(d - 1) * span : d * span], "x", -d) for d in range(1, SEQ_DEVS)
    ]
    out_sum = exchange_sum(out_parts, "z", hold=[query_part]).astype(BF)
    query_raw_grad, own_grads = attend_back(
        (0,), after(queries, out_sum, output), blocks[:1], window, log_total, (grad_turned, delta, query_part), turn=[cos, sin]
    )

    a_parts = wide_parts([scaled_in], query_raw_grad, (0, cut), "x")
    kv_raw_grad, *b_parts = last_parts(
        scaled_in, after(query_raw_grad, a_parts), cut, own_grads, arriving, cos, sin, "z"
    )
    in_partial = rows_grad(
        [query_raw_grad, kv_raw_grad],
        [whole_a, whole_b],
        [
            (0, (0, cut), 0, (skip, skip + cut)),
            (0, (cut, width_q), 1, (skip, skip + width_q - cut)),
            (1, (0, 2 * width_k), 1, (skip + width_q - cut, skip + width_b)),
        ],
        rows_in, gains, 0,
    )
    input_grad = settle(grad_middle, scatter_rows(in_partial), F32)
    a_sum = wide_sum_next(exchange_sum(a_parts, "x").astype(BF), "z")
    b_sum = exchange_sum(b_parts, "z").astype(BF)
    b_sum = wide_sum_next(jnp.concatenate([b_sum, out_sum], 1), "x")
    attn_sum = sides_sum(jnp.concatenate([a_sum, b_sum], 1))
    a_grad, b_grad = attn_sum[:, :cut], attn_sum[:, cut : cut + width_b]
    out_grad = attn_sum[:, cut + width_b :].T
    mlp_grad = sides_sum(after(mlp_sum, query_raw_grad))
    gate_grad, up_grad = mlp_grad[:, :hidden_width], mlp_grad[:, hidden_width : 2 * hidden_width]
    down_grad = mlp_grad[:, 2 * hidden_width :].T

    attn_gain_part = jnp.sum(shard_a[:, skip:].astype(F32) * a_grad, 1) + jnp.sum(
        shard_b[:, skip : skip + width_b].astype(F32) * b_grad, 1
    )
    mlp_gain_part = jnp.sum(
        gate_weight.astype(F32) * gate_grad + up_weight.astype(F32) * up_grad, 1
    )
    attn_gain_grad, mlp_gain_grad = lax.psum((attn_gain_part, mlp_gain_part), TP)
    own = width_q - cut
    return (
        output,
        input_grad,
        attn_gain_grad / attn_gain.astype(F32),
        jnp.concatenate([a_grad, b_grad[:, :own]], 1),
        b_grad[:, own : own + width_k],
        b_grad[:, own + width_k :],
        out_grad,
        mlp_gain_grad / mlp_gain.astype(F32),
        gate_grad,
        up_grad,
        down_grad,
    )


def solution(mesh):
    split = Mesh(mesh.devices.reshape(2, 4, 4, 2, 2), WIDE + TP)
    rows = P(WIDE + TP, None)
    inward = P(WIDE, TP)
    outward = P(TP, WIDE)
    gain = P(WIDE)
    return jax.shard_map(
        per_device,
        mesh=split,
        in_specs=(
            rows, gain, gain, inward, inward, inward, outward, gain, inward, inward, outward, rows,
        ),
        out_specs=(
            rows, rows, gain, inward, inward, inward, outward, gain, inward, inward, outward,
        ),
        check_vma=False,
    )
```

```python
import functools

import jax
import jax.numpy as jnp
from jax import lax
from jax.experimental import pallas as pl
from jax.experimental.pallas import tpu as pltpu
from jax.sharding import Mesh, PartitionSpec as P

HEADS = 32
KV = 4
HD = 64
SEQ_DEVS = 4
WIDE = ("yh", "z", "x")
TP = ("yl", "core")
BF = jnp.bfloat16
F32 = jnp.float32

epsilon = 1e-05
masked_fill = -1e30
VMEM_LIMIT = 56 * 1024 * 1024


def after(value, *earlier):
    return lax.optimization_barrier((value, earlier))[0]


def shift(block, axis, distance):
    n = lax.axis_size(axis)
    return lax.ppermute(block, axis, [(i, (i + distance) % n) for i in range(n)])


def swap(block, axis):
    return shift(block, axis, 1)


def place(axis, step=0):
    n = lax.axis_size(axis)
    return ((lax.axis_index(axis) + (step + n)) & (n - 1)).astype(jnp.uint32)


def pick(array, index, dim):
    return lax.dynamic_index_in_dim(array, index, dim, keepdims=False)


def send_stage(block, axis):
    n = lax.axis_size(axis)
    return [block] + [shift(block, axis, d) for d in (1, n - 1, *range(2, n - 1))]


def stack_stage(arrived, axis, dim):
    n = len(arrived)
    block = arrived[0]
    out = jnp.zeros(block.shape[:dim] + (n,) + block.shape[dim:], block.dtype)
    for d, piece in zip((0, 1, n - 1, *range(2, n - 1)), arrived):
        out = lax.dynamic_update_index_in_dim(out, piece, place(axis, -d), dim)
    return out


def gather_ring(block, axis, dim):
    half = block.shape[0] // 2
    left, right = shift(block, axis, 1), shift(block, axis, -1)
    upper, lower = shift(left[:half], axis, 1), shift(right[half:], axis, -1)
    out = jnp.zeros(block.shape[:dim] + (4,) + block.shape[dim:], block.dtype)
    out = lax.dynamic_update_index_in_dim(out, block, place(axis), dim)
    out = lax.dynamic_update_index_in_dim(out, left, place(axis, -1), dim)
    out = lax.dynamic_update_index_in_dim(out, right, place(axis, 1), dim)
    return lax.dynamic_update_index_in_dim(
        out, jnp.concatenate([upper, lower], 0), place(axis, 2), dim
    )


def join_sides(shard, other):
    first = lax.axis_index("yh") == 0
    return jnp.concatenate([jnp.where(first, shard, other), jnp.where(first, other, shard)], 0)


def flat(blocks):
    return blocks.reshape(-1, blocks.shape[-1])


def gather_rows(rows):
    across = swap(rows, "yl")
    return [rows, swap(rows, "core"), across, swap(across, "core")]


def scatter_cores(partial):
    own, beside, across, corner = partial
    far = swap(corner, "core").astype(F32)
    return own, swap(beside, "core"), (across.astype(F32) + far).astype(BF)


def scatter_rows(partial):
    own, near, other = scatter_cores(partial)
    return [own, near, swap(other, "yl")]


def total(first, parts):
    for part in parts:
        first = first + part.astype(F32)
    return first


def exchange_sum(parts, axis, hold=()):
    n = len(parts)
    total = parts[0].astype(F32)
    for d in (1, n - 1, *range(2, n - 1))[: n - 1]:
        total = total + after(shift(parts[d], axis, d), *hold).astype(F32)
    return total


def wide_sum_next(part, axis, hold=()):
    n = lax.axis_size(axis)
    part = part.reshape(n, part.shape[0] // n, part.shape[1])
    pieces = [pick(part, place(axis, d), 0) for d in range(n)]
    return exchange_sum(pieces, axis, hold).astype(BF)


def mm(left, right):
    return jnp.dot(left, right, preferred_element_type=F32)


def mm_last(left, right):
    return lax.dot_general(left, right, (((1,), (1,)), ((), ())), preferred_element_type=F32)


def normed_rows(piece):
    values = piece.astype(F32)
    factor = lax.rsqrt(jnp.mean(values * values, -1, keepdims=True) + epsilon)
    return values * factor, factor


def scale_rows(piece_refs, gain, scaled_ref):
    for n, ref in enumerate(piece_refs):
        for at in range(0, ref.shape[0], 32):
            normed, _ = normed_rows(ref[at : at + 32, :])
            rows = n * ref.shape[0] + at
            scaled_ref[rows : rows + 32, :] = (normed * gain).astype(BF)


def turned(block, cos, sin):
    a, b = block[: HD // 2], block[HD // 2 :]
    return jnp.concatenate([a * cos - b * sin, b * cos + a * sin], 0)


def keys_values_kernel(skip, *refs):
    piece_refs, (w_ref, cos_ref, sin_ref, kv_ref, scaled_ref, gains_ref) = refs[:4], refs[4:]
    gains_ref[...] = w_ref[:, skip + 128 : skip + 256].T[:8].astype(F32)
    scale_rows(piece_refs, gains_ref[0:1, :], scaled_ref)
    both = mm(scaled_ref[...], w_ref[:, skip : skip + 128]).T
    keys = turned(both[:HD], cos_ref[...], sin_ref[...])
    kv_ref[...] = jnp.concatenate([keys, both[HD:]], 0).T.astype(BF)


def queries_kernel(skip, x_ref, w_ref, cos_ref, sin_ref, q_ref):
    for at in range(0, q_ref.shape[0], 256):
        piece = mm(x_ref[...], w_ref[:, skip + at : skip + at + 256]).T
        for sub in range(0, 256, HD):
            low = turned(piece[sub : sub + HD], cos_ref[...], sin_ref[...]).astype(BF)
            q_ref[at + sub : at + sub + HD, :] = low * 0.125


def to_inner(ref, out_ref):
    half = ref.shape[1] // 2
    for at in range(0, half, 128):
        low, high = ref[:, at : at + 128], ref[:, half + at : half + at + 128]
        out_ref[:, 2 * at : 2 * at + 128] = jnp.concatenate([low[:, :HD], high[:, :HD]], 1)
        out_ref[:, 2 * at + 128 : 2 * at + 256] = jnp.concatenate([low[:, HD:], high[:, HD:]], 1)


def pack_kernel(inputs_ref, cot_ref, again_ref, mgain_ref, q_ref, k_ref, v_ref, o_ref, g_ref, u_ref, d_ref,
                rows_ref, cots_ref, a_ref, b_ref, mlp_ref):
    to_inner(inputs_ref, rows_ref)
    to_inner(cot_ref, cots_ref)
    out = o_ref[...].T
    half = out.shape[1] // 2
    a_ref[:, :half] = out[:, :half]
    a_ref[:, half:] = q_ref[...]
    b_ref[:, :half] = out[:, half:]
    b_ref[:, half : half + 128] = jnp.concatenate([k_ref[...], v_ref[...]], 1)
    gains = jnp.concatenate(
        [again_ref[...].astype(F32), mgain_ref[...].astype(F32), jnp.zeros((126, HD), F32)], 0
    )
    b_ref[:, half + 128 :] = gains.T.astype(BF)
    width = g_ref.shape[1]
    mlp_ref[:, :width] = g_ref[...]
    mlp_ref[:, width : 2 * width] = u_ref[...]
    mlp_ref[:, 2 * width :] = d_ref[...].T


def finish_mlp_kernel(side_ref, pair_ref, other_ref, gate_ref, up_ref, down_ref):
    rows = pl.ds(pl.multiple_of(side_ref[0, 0] * HD, HD), HD)
    width = gate_ref.shape[1]

    def summed(at):
        columns = slice(at, at + width)
        return pair_ref[rows, columns].astype(F32) + other_ref[:, columns].astype(F32)

    gate_ref[...] = summed(0)
    up_ref[...] = summed(width)
    down_ref[...] = summed(2 * width).T


def finish_attn_kernel(side_ref, pair_ref, other_ref, q_ref, k_ref, v_ref, o_ref):
    rows = pl.ds(pl.multiple_of(side_ref[0, 0] * HD, HD), HD)
    both = pair_ref[rows, :].astype(F32) + other_ref[...].astype(F32)
    width = q_ref.shape[1]
    q_ref[...] = both[:, :width]
    k_ref[...] = both[:, width : width + HD]
    v_ref[...] = both[:, width + HD : width + 2 * HD]
    o_ref[...] = both[:, width + 2 * HD :].T


def hidden_kernel(*refs):
    pieces, cots, (gain_ref, gate_ref, up_ref, down_ref, hidden_ref, dgate_ref, dup_ref, scaled_ref, cot_ref) = (
        refs[:4], refs[4:8], refs[8:],
    )

    @pl.when(pl.program_id(0) == 0)
    def _():
        scale_rows(pieces, gain_ref[1:2, :], scaled_ref)
        for n, ref in enumerate(cots):
            cot_ref[n * ref.shape[0] : (n + 1) * ref.shape[0], :] = ref[...]

    tile = gate_ref.shape[1]
    gate = mm(scaled_ref[...], gate_ref[...])
    up = mm(scaled_ref[...], up_ref[...])
    grad = mm(cot_ref[...], down_ref[...])
    sigmoid = 1.0 / (1.0 + jnp.exp(-gate))
    gated = gate * sigmoid
    last = hidden_ref.shape[1] - tile
    columns = pl.ds(pl.multiple_of(jnp.minimum(pl.program_id(0) * tile, last), 128), tile)
    hidden_ref[:, columns] = (gated * up).astype(BF)
    dgate_ref[:, columns] = (grad * up * sigmoid * (1.0 + gate * (1.0 - sigmoid))).astype(BF)
    dup_ref[:, columns] = (grad * gated).astype(BF)


def sum_of_products(terms, refs):
    total = None
    for left, (low, high), right, (first, last) in terms:
        part = mm_last(refs[left][:, low:high], refs[right][:, first:last])
        total = part if total is None else total + part
    return total


def rows_grad_kernel(terms, count, gain_row, *refs):
    pieces, gain_ref, outs, sum_ref = refs[count : count + 4], refs[count + 4], refs[count + 5 : -1], refs[-1]
    step = pl.program_id(0)
    tile = sum_ref.shape[1] // pl.num_programs(0)
    columns = pl.ds(pl.multiple_of(step * tile, tile), tile)
    sum_ref[:, columns] = sum_of_products(terms, refs) * gain_ref[gain_row : gain_row + 1, columns]

    @pl.when(step == pl.num_programs(0) - 1)
    def _():
        for n, ref in enumerate(pieces):
            for at in range(0, ref.shape[0], 32):
                normed, factor = normed_rows(ref[at : at + 32, :])
                scaled = sum_ref[n * ref.shape[0] + at : n * ref.shape[0] + at + 32, :]
                inner = jnp.mean(scaled * normed, -1, keepdims=True)
                outs[n][at : at + 32, :] = (factor * (scaled - normed * inner)).astype(BF)


def rows_out_kernel(terms, *refs):
    value = sum_of_products(terms, refs).astype(BF)
    for n, ref in enumerate(refs[-4:]):
        ref[...] = value[n * ref.shape[0] : (n + 1) * ref.shape[0]]


def write_parts(outs, turned_of, axis, me, right, base):
    for d, out in enumerate(outs):
        index = (me + d) & 3
        if axis == "z":
            turned = turned_of(pl.multiple_of(index * 512, 512), 512)
        else:
            turned = jnp.concatenate(
                [turned_of(pl.multiple_of(z * 512 + index * 128, 128), 128) for z in range(4)], 0
            )
        out[:, base : base + right.shape[1]] = mm(turned, right).astype(BF)


def parts_kernel(axis, columns, count, me_ref, *refs):
    lefts, right_ref, outs = refs[:count], refs[count], refs[count + 1 :]

    def turned_of(at, size):
        return jnp.concatenate([left[:, pl.ds(at, size)] for left in lefts], 0).T

    write_parts(outs, turned_of, axis, me_ref[0, 0], right_ref[:, columns[0] : columns[1]], 0)


def last_parts_kernel(axis, cut, me_ref, left_ref, dq_ref, own_ref, one_ref, two_ref, three_ref,
                      cos_ref, sin_ref, *outs):
    half = HD // 2
    cos, sin = cos_ref[...], sin_ref[...]
    kv = own_ref[...]
    for ref in (one_ref, two_ref, three_ref):
        kv = kv + ref[...].astype(F32)
    kv = kv.T
    a, b = kv[:half], kv[half:HD]
    kv = jnp.concatenate([a * cos + b * sin, b * cos - a * sin, kv[HD:]], 0).T.astype(BF)
    outs[0][...] = kv
    right = jnp.concatenate([dq_ref[:, cut:], kv], 1)

    def turned_of(at, size):
        return left_ref[:, pl.ds(at, size)].T

    write_parts(outs[1:], turned_of, axis, me_ref[0, 0], right, 0)


def settle_kernel(base_ref, *refs):
    out_ref = refs[-1]
    width = base_ref.shape[1]

    def block(at):
        value = base_ref[:, at : at + 128].astype(F32)
        for ref in refs[:-1]:
            value = value + ref[:, at : at + 128].astype(F32)
        return value

    for n in range(width // 256):
        one, two = block(256 * n), block(256 * n + 128)
        low = jnp.concatenate([one[:, :HD], two[:, :HD]], 1)
        high = jnp.concatenate([one[:, HD:], two[:, HD:]], 1)
        out_ref[:, 128 * n : 128 * n + 128] = low.astype(out_ref.dtype)
        out_ref[:, width // 2 + 128 * n : width // 2 + 128 * n + 128] = high.astype(out_ref.dtype)


def fill_bias(bias_ref, me_ref, pos_ref, span, distances):
    step = 64
    quarter = span // 4
    me = me_ref[0, 0]
    at = lax.broadcasted_iota(jnp.int32, (1, span), 1)
    query = (((at // quarter) ^ me) * quarter) + (at & (quarter - 1))
    first = query - pos_ref[...]

    @pl.loop(0, span // step)
    def _(i):
        block = (i * step) // quarter
        start = (block ^ me) * quarter + i * step - block * quarter
        key = start + lax.broadcasted_iota(jnp.int32, (step, span), 0)
        for n, d in enumerate(distances):
            seen = (key - d * span <= query) & (key - d * span >= first)
            bias_ref[pl.ds(pl.multiple_of(n * span + i * step, step), step), :] = jnp.where(
                seen, 0.0, masked_fill
            ).astype(F32)


def attend_kernel(q_ref, *refs):
    blocks = len(refs) - 7
    kv_refs = refs[:blocks]
    me_ref, pos_ref, mix_ref, lse_ref, bias_ref, s_ref, vt_ref = refs[blocks:]
    span = q_ref.shape[1]
    fill_bias(bias_ref, me_ref, pos_ref, span, range(blocks))
    for d in range(blocks):
        vt_ref[:, d * span : (d + 1) * span] = kv_refs[d][...].T[HD:]

    @pl.loop(0, q_ref.shape[0] // 128)
    def _(pair):
        outs = []
        for sub in range(2):
            q = q_ref[pl.ds(pl.multiple_of(pair * 128 + sub * HD, HD), HD), :]
            top = None
            for d in range(blocks):
                rows = slice(d * span, (d + 1) * span)
                s = mm(kv_refs[d][:, :HD], q) + bias_ref[rows, :]
                s_ref[rows, :] = s
                high = jnp.max(s, 0, keepdims=True)
                top = high if top is None else jnp.maximum(top, high)
            total = jnp.zeros_like(top)
            out = jnp.zeros((HD, span), F32)
            for d in range(blocks):
                rows = slice(d * span, (d + 1) * span)
                p = jnp.exp(s_ref[rows, :] - top)
                total = total + jnp.sum(p, 0, keepdims=True)
                out = out + mm(vt_ref[:, rows], p.astype(BF))
            outs.append(out / total)
            lse_ref[pl.ds(pair * 2 + sub, 1), :] = top + jnp.log(total)
        mix_ref[:, pl.ds(pl.multiple_of(pair * 128, 128), 128)] = (
            jnp.concatenate(outs, 0).T.astype(BF)
        )


def attend_back_kernel(distances, first, last, q_ref, *refs):
    blocks = len(distances)
    refs = list(refs)

    def take(count):
        got, refs[:count] = refs[:count], []
        return got

    kv_refs = take(blocks)
    me_ref, pos_ref, lse_ref = take(3)
    if first:
        mix_ref, wa_ref, wb_ref, *piece_refs = take(7)
    else:
        gt_ref, delta_ref, part_ref = take(3)
    if last:
        cos_ref, sin_ref = take(2)
        (dq_ref,) = take(1)
    else:
        (sum_ref,) = take(1)
    (dkv_ref,) = take(1)
    if first:
        gt_ref, delta_ref = take(2)
    bias_ref, v_ref, kt_ref, dk_ref, dv_ref = take(5)
    span = q_ref.shape[1]
    half = HD // 2
    heads = q_ref.shape[0] // HD
    fill_bias(bias_ref, me_ref, pos_ref, span, distances)
    for n in range(blocks):
        rows = slice(n * span, (n + 1) * span)
        both = kv_refs[n][...].T
        kt_ref[:, rows] = both[:HD]
        v_ref[rows, :] = both[HD:].T
    dk_ref[...] = jnp.zeros_like(dk_ref)
    dv_ref[...] = jnp.zeros_like(dv_ref)
    if first:
        rows_all = jnp.concatenate([ref[...] for ref in piece_refs], 0)
        grads = [mm(rows_all, w_ref[:, : heads * HD // 2]).astype(BF) for w_ref in (wa_ref, wb_ref)]
        for at in range(0, heads * HD, 128):
            where = at % (heads * HD // 2)
            gt = grads[2 * at // (heads * HD)][:, where : where + 128].T
            mt = mix_ref[:, at : at + 128].T
            gt_ref[at : at + 128, :] = gt
            prod = gt.astype(F32) * mt.astype(F32)
            for sub in range(2):
                h = at // HD + sub
                delta_ref[h : h + 1, :] = jnp.sum(prod[sub * HD : (sub + 1) * HD], 0, keepdims=True)

    @pl.loop(0, heads // 2)
    def _(pair):
        outs = []
        for sub in range(2):
            rows_h = pl.ds(pl.multiple_of(pair * 128 + sub * HD, HD), HD)
            q, g = q_ref[rows_h, :], gt_ref[rows_h, :]
            lse = lse_ref[pl.ds(pair * 2 + sub, 1), :]
            delta = delta_ref[pl.ds(pair * 2 + sub, 1), :]
            dq = jnp.zeros((HD, span), F32) if first else part_ref[rows_h, :]
            for n in range(blocks):
                rows = slice(n * span, (n + 1) * span)
                s = mm(kv_refs[n][:, :HD], q) + bias_ref[rows, :]
                p = jnp.exp(s - lse)
                ds = (p * (mm(v_ref[rows, :], g) - delta)).astype(BF)
                dv_ref[rows, :] += mm_last(p.astype(BF), g)
                dk_ref[rows, :] += mm_last(ds, q)
                dq = dq + mm(kt_ref[:, rows], ds)
            if last:
                dq = dq * 0.125
                a, b = dq[:half], dq[half:]
                cos, sin = cos_ref[...], sin_ref[...]
                outs += [a * cos + b * sin, b * cos - a * sin]
            else:
                sum_ref[rows_h, :] = dq
        if last:
            dq_ref[:, pl.ds(pl.multiple_of(pair * 128, 128), 128)] = (
                jnp.concatenate(outs, 0).T.astype(BF)
            )

    for n in range(blocks):
        rows = slice(n * span, (n + 1) * span)
        dkv_ref[rows, :] = jnp.concatenate([dk_ref[rows, :], dv_ref[rows, :]], 1).astype(dkv_ref.dtype)


def weight_grads_kernel(left_ref, one_ref, two_ref, other_left_ref, other_ref, out_ref):
    at = 0
    for lefts, rights in ((left_ref, (one_ref, two_ref)), (other_left_ref, (other_ref,))):
        turned = lefts[...].T
        for ref in rights:
            for c in range(0, ref.shape[1], 256):
                size = min(256, ref.shape[1] - c)
                out_ref[:, at + c : at + c + size] = mm(turned, ref[:, c : c + size]).astype(BF)
            at += ref.shape[1]


def params():
    return pltpu.CompilerParams(vmem_limit_bytes=VMEM_LIMIT)


def whole(count):
    return [pl.BlockSpec(memory_space=pltpu.VMEM)] * count


def cost(products, moved):
    return pl.CostEstimate(flops=2 * products, bytes_accessed=moved, transcendentals=0)


def call(kernel, name, shapes, operands, scalars=0, products=0):
    return pl.pallas_call(
        kernel,
        out_shape=tuple(jax.ShapeDtypeStruct(*shape) for shape in shapes),
        in_specs=[pl.BlockSpec(memory_space=pltpu.SMEM)] * scalars + whole(len(operands) - scalars),
        out_specs=tuple(whole(len(shapes))),
        compiler_params=params(),
        cost_estimate=cost(products, 4 << 20),
        name=name,
    )(*operands)


def hidden_units(pieces, cots, gains, weights, width):
    span, d = 4 * pieces[0].shape[0], pieces[0].shape[1]
    tile = 256

    def columns(base):
        def start(i):
            return (0, pl.multiple_of(base * width + jnp.minimum(i * tile, width - tile), 128))

        return pl.BlockSpec((pl.Element(d), pl.Element(tile)), start)

    out = pl.BlockSpec((span, width), lambda i: (0, 0))
    return pl.pallas_call(
        hidden_kernel,
        grid=(-(-width // tile),),
        out_shape=(jax.ShapeDtypeStruct((span, width), BF),) * 3
        + (jax.ShapeDtypeStruct((span, d), BF),) * 2,
        in_specs=[fixed(a) for a in (*pieces, *cots, gains)]
        + [columns(0), columns(1), columns(2)],
        out_specs=(out,) * 3 + (pl.BlockSpec((span, d), lambda i: (0, 0)),) * 2,
        compiler_params=params(),
        cost_estimate=cost(3 * span * d * width, 6 * d * width),
        name="hidden_units",
    )(*pieces, *cots, gains, weights, weights, weights)


def feature_rows(weight, tile):
    if not isinstance(weight, tuple):
        return pl.BlockSpec((tile, weight.shape[1]), lambda i: (i, 0))
    return pl.BlockSpec((tile, weight[2]), lambda i: (i, weight[1]))


def array_of(weight):
    return weight[0] if isinstance(weight, tuple) else weight


def fixed(array):
    return pl.BlockSpec(array.shape, lambda i: (0, 0))


def rows_grad(grads, weights, terms, pieces, gains, gain_row):
    span, d = 4 * pieces[0].shape[0], pieces[0].shape[1]
    tile = 512
    n = len(grads)
    terms = [(g, c, n + w, e) for g, c, w, e in terms]
    return pl.pallas_call(
        functools.partial(rows_grad_kernel, terms, n + len(weights), gain_row),
        grid=(d // tile,),
        out_shape=(jax.ShapeDtypeStruct((span // 4, d), BF),) * 4,
        in_specs=[fixed(g) for g in grads]
        + [feature_rows(w, tile) for w in weights]
        + [fixed(a) for a in (*pieces, gains)],
        out_specs=(pl.BlockSpec((span // 4, d), lambda i: (0, 0)),) * 4,
        scratch_shapes=[pltpu.VMEM((span, d), F32)],
        compiler_params=params(),
        cost_estimate=cost(sum(span * d * (c[1] - c[0]) for _, c, _, _ in terms), 8 << 20),
        name="rows_grad",
    )(*grads, *map(array_of, weights), *pieces, gains)


def rows_out(lefts, weights, terms, tile):
    span, d = lefts[0].shape[0], array_of(weights[0]).shape[0]
    n = len(lefts)
    terms = [(g, c, n + w, e) for g, c, w, e in terms]
    return pl.pallas_call(
        functools.partial(rows_out_kernel, terms),
        grid=(d // tile,),
        out_shape=(jax.ShapeDtypeStruct((span // 4, d), BF),) * 4,
        in_specs=[fixed(g) for g in lefts] + [feature_rows(w, tile) for w in weights],
        out_specs=(pl.BlockSpec((span // 4, tile), lambda i: (0, i)),) * 4,
        compiler_params=params(),
        cost_estimate=cost(sum(span * d * (c[1] - c[0]) for _, c, _, _ in terms), 6 << 20),
        name="rows_out",
    )(*lefts, *map(array_of, weights))


def scalar():
    return [pl.BlockSpec(memory_space=pltpu.SMEM)]


def at_place(axis):
    return place(axis).astype(jnp.int32).reshape(1, 1)


def wide_parts(lefts, right, columns, axis):
    span, d = right.shape[0], lefts[0].shape[1]
    width = columns[1] - columns[0]
    return pl.pallas_call(
        functools.partial(parts_kernel, axis, columns, len(lefts)),
        out_shape=(jax.ShapeDtypeStruct((d // 4, width), BF),) * 4,
        in_specs=scalar() + whole(len(lefts) + 1),
        out_specs=tuple(whole(4)),
        compiler_params=params(),
        cost_estimate=cost(span * d * width, 8 << 20),
        name="wide_parts",
    )(at_place(axis), *lefts, right)


def last_parts(left, dq, cut, own, arrived, cos, sin, axis):
    span, d = left.shape
    width = dq.shape[1] - cut + 2 * HD
    return pl.pallas_call(
        functools.partial(last_parts_kernel, axis, cut),
        out_shape=(jax.ShapeDtypeStruct((span, 2 * HD), BF),)
        + (jax.ShapeDtypeStruct((d // 4, width), BF),) * 4,
        in_specs=scalar() + whole(8),
        out_specs=tuple(whole(5)),
        compiler_params=params(),
        cost_estimate=cost(span * d * width, 8 << 20),
        name="last_parts",
    )(at_place(axis), left, dq, own, *arrived, cos, sin)


def settle(base, parts, kind):
    return pl.pallas_call(
        settle_kernel,
        out_shape=jax.ShapeDtypeStruct(base.shape, kind),
        in_specs=whole(1 + len(parts)),
        out_specs=whole(1)[0],
        compiler_params=params(),
        cost_estimate=cost(0, 4 << 20),
        name="settle",
    )(base, *parts)


def window_specs():
    return [pl.BlockSpec(memory_space=pltpu.SMEM)] + whole(1)


def attend(q, kvs, window):
    n = len(kvs)
    width, span = q.shape
    heads = width // HD
    return pl.pallas_call(
        attend_kernel,
        out_shape=(
            jax.ShapeDtypeStruct((span, width), BF),
            jax.ShapeDtypeStruct((heads, span), F32),
        ),
        in_specs=whole(n + 1) + window_specs(),
        out_specs=tuple(whole(2)),
        scratch_shapes=[
            pltpu.VMEM((n * span, span), F32),
            pltpu.VMEM((n * span, span), F32),
            pltpu.VMEM((HD, n * span), BF),
        ],
        compiler_params=params(),
        cost_estimate=pl.CostEstimate(flops=16 * span * width * n * span, bytes_accessed=2 << 20, transcendentals=heads * n * span * span),
        name="attend",
    )(q, *kvs, *window)


def attend_back(distances, q, kvs, window, lse, prepared, mixed=None, out=None, turn=None):
    n = len(kvs)
    width, span = q.shape
    heads = width // HD
    first, last = prepared is None, turn is not None
    operands = [q, *kvs, *window, lse]
    operands += [mixed, *out] if first else list(prepared)
    shapes = []
    if last:
        operands += turn
        shapes.append(jax.ShapeDtypeStruct((span, width), BF))
    else:
        shapes.append(jax.ShapeDtypeStruct((width, span), F32))
    shapes.append(jax.ShapeDtypeStruct((n * span, 2 * HD), F32 if last else BF))
    if first:
        shapes.append(jax.ShapeDtypeStruct((width, span), BF))
        shapes.append(jax.ShapeDtypeStruct((heads, span), F32))
    return pl.pallas_call(
        functools.partial(attend_back_kernel, distances, first, last),
        out_shape=tuple(shapes),
        in_specs=whole(n + 1) + window_specs() + whole(len(operands) - n - 3),
        out_specs=tuple(whole(len(shapes))),
        scratch_shapes=[
            pltpu.VMEM((n * span, span), F32),
            pltpu.VMEM((n * span, HD), BF),
            pltpu.VMEM((HD, n * span), BF),
            pltpu.VMEM((n * span, HD), F32),
            pltpu.VMEM((n * span, HD), F32),
        ],
        compiler_params=params(),
        cost_estimate=pl.CostEstimate(flops=40 * span * width * n * span, bytes_accessed=4 << 20, transcendentals=heads * n * span * span),
        name="attend_back",
    )(*operands)


def weight_grads(left, one, two, other_left, other):
    t, d = left.shape
    tile = 256
    rows = pl.BlockSpec((t, tile), lambda i: (0, i))
    width = one.shape[1] + two.shape[1] + other.shape[1]
    return pl.pallas_call(
        weight_grads_kernel,
        grid=(d // tile,),
        out_shape=jax.ShapeDtypeStruct((d, width), BF),
        in_specs=[rows, fixed(one), fixed(two), rows, fixed(other)],
        out_specs=pl.BlockSpec((tile, width), lambda i: (i, 0)),
        compiler_params=params(),
        cost_estimate=cost(t * d * width, 2 * d * width + 4 * t * d),
        name="weight_grads",
    )(left, one, two, other_left, other)


def per_device(
    inputs,
    positions,
    attn_gain,
    query_weight,
    key_weight,
    value_weight,
    out_weight,
    mlp_gain,
    gate_weight,
    up_weight,
    down_weight,
    cotangent,
):
    width_q = query_weight.shape[1]
    width_k = key_weight.shape[1]
    hidden_width = gate_weight.shape[1]
    span = positions.shape[0]
    quarter = span // 4
    cut = 3 * width_q // 4
    skip = width_q // 2
    d = inputs.shape[1]
    shard = query_weight.shape[0]
    side = place("yh").astype(jnp.int32).reshape(1, 1)

    inputs, cotangent, shard_a, shard_b, shard_mlp = call(
        pack_kernel, "pack",
        [(inputs.shape, BF), (inputs.shape, BF), ((shard, skip + width_q), BF),
         ((shard, skip + 256), BF), ((shard, 3 * hidden_width), BF)],
        [inputs, cotangent, attn_gain[None], mlp_gain[None], query_weight, key_weight, value_weight,
         out_weight, gate_weight, up_weight, down_weight],
    )
    other_b, other_a = swap(shard_b, "yh"), swap(shard_a, "yh")
    other_mlp = swap(shard_mlp, "yh")
    rows_in = gather_rows(inputs)
    pair_b, pair_a = join_sides(shard_b, other_b), join_sides(shard_a, other_a)
    along_b, along_a = send_stage(pair_b, "x"), send_stage(pair_a, "z")
    mlp_pair = join_sides(shard_mlp, after(other_mlp, along_a[1:], along_b[1:]))
    mlp_whole = lax.all_gather(mlp_pair, ("z", "x"), axis=0, tiled=True)
    whole_b = flat(gather_ring(stack_stage(along_b, "x", 0), "z", 0))
    whole_a = flat(gather_ring(stack_stage(along_a, "z", 0), "x", 1))
    cotangents = gather_rows(after(cotangent, rows_in[2]))

    me = (lax.axis_index("yl") * 2 + lax.axis_index("core")).astype(jnp.int32)
    blocked = jnp.arange(4, dtype=jnp.int32) ^ me
    positions = jnp.take(positions.reshape(4, quarter), blocked, axis=0, mode="clip").reshape(1, span)
    freqs = 10000.0 ** (-(jnp.arange(HD // 2, dtype=F32) * 2.0) / HD)
    angles = freqs[:, None] * positions.astype(F32)
    cos, sin = jnp.cos(angles), jnp.sin(angles)
    window = (me.reshape(1, 1), positions)

    kv_block, scaled_in, gains = call(
        functools.partial(keys_values_kernel, skip), "keys_values",
        [((span, 2 * width_k), BF), ((span, d), BF), ((8, d), F32)],
        [*rows_in, whole_b, cos, sin], products=span * d * 2 * width_k,
    )
    (queries,) = call(
        functools.partial(queries_kernel, skip), "queries",
        [((width_q, span), BF)],
        [scaled_in, after(whole_a, kv_block, cotangents), cos, sin], products=span * d * width_q,
    )
    blocks = [kv_block] + [shift(kv_block, "x", d) for d in range(1, SEQ_DEVS)]
    mixed, log_total = attend(queries, blocks, window)

    out_a, out_b = (whole_a, 0, skip), (whole_b, 0, skip)
    attn_rows = rows_out(
        [mixed], [out_a, out_b],
        [(0, (0, skip), 0, (0, skip)), (0, (skip, width_q), 1, (0, skip))], 1024,
    )
    middle = total(inputs.astype(F32), scatter_rows(attn_rows))
    rows_mid = gather_rows(middle.astype(BF))
    hidden, grad_gate, grad_up, scaled_mid, cotangent_all = hidden_units(
        rows_mid, cotangents, gains, mlp_whole, hidden_width
    )
    every = (0, hidden_width)
    mid_partial = rows_grad(
        [grad_gate, grad_up],
        [(mlp_whole, 0, hidden_width), (mlp_whole, 1, hidden_width)],
        [(0, every, 0, every), (1, every, 1, every)],
        rows_mid, gains, 1,
    )
    grad_middle = total(cotangent.astype(F32), scatter_rows(mid_partial))
    rows_grad_middle = gather_rows(grad_middle.astype(BF))

    mlp_sum = weight_grads(
        after(scaled_mid, mid_partial), grad_gate, grad_up, cotangent_all, hidden
    )
    mlp_rows = rows_out(
        [after(hidden, mlp_sum)], [(mlp_whole, 2, hidden_width)], [(0, every, 0, every)], 512
    )
    mlp_sum = lax.psum_scatter(mlp_sum, ("z", "x"), scatter_dimension=0, tiled=True)

    out_parts = wide_parts(rows_grad_middle, mixed, (0, width_q), "z")
    mlp_own, mlp_near, mlp_other = scatter_cores(mlp_rows)
    query_part, far_grads, grad_turned, delta = attend_back(
        (1, 2, 3), queries, blocks[1:], window, log_total, None, after(mixed, out_parts, mlp_other),
        [whole_a, whole_b, *rows_grad_middle],
    )
    mlp_across = swap(after(mlp_other, rows_grad_middle), "yl")
    output = settle(middle, [mlp_own, mlp_near, after(mlp_across, query_part)], BF)
    arriving = [
        shift(far_grads[(d - 1) * span : d * span], "x", -d) for d in range(1, SEQ_DEVS)
    ]
    out_sum = exchange_sum(out_parts, "z", hold=[query_part]).astype(BF)
    query_raw_grad, own_grads = attend_back(
        (0,), after(queries, out_sum, output), blocks[:1], window, log_total, (grad_turned, delta, query_part), turn=[cos, sin]
    )

    a_parts = wide_parts([scaled_in], query_raw_grad, (0, cut), "x")
    kv_raw_grad, *b_parts = last_parts(
        scaled_in, after(query_raw_grad, a_parts), cut, own_grads, arriving, cos, sin, "z"
    )
    in_partial = rows_grad(
        [query_raw_grad, kv_raw_grad],
        [whole_a, whole_b],
        [
            (0, (0, width_q), 0, (skip, skip + width_q)),
            (1, (0, 2 * width_k), 1, (skip, skip + 2 * width_k)),
        ],
        rows_in, gains, 0,
    )
    input_grad = settle(grad_middle, scatter_rows(in_partial), F32)

    mlp_send = pick(mlp_sum.reshape(2, shard, -1), place("yh", 1), 0)
    a_sum = wide_sum_next(exchange_sum(a_parts, "x").astype(BF), "z")
    b_sum = exchange_sum(b_parts, "z").astype(BF)
    b_sum = wide_sum_next(jnp.concatenate([b_sum, out_sum], 1), "x", hold=[mlp_send])
    sides = jnp.concatenate([a_sum, b_sum], 1)
    other_sides = swap(pick(sides.reshape(2, shard, -1), place("yh", 1), 0), "yh")
    query_grad, key_grad, value_grad, out_grad = call(
        finish_attn_kernel, "finish_attn",
        [(query_weight.shape, F32), (key_weight.shape, F32), (value_weight.shape, F32),
         (out_weight.shape, F32)],
        [side, sides, other_sides], scalars=1,
    )
    gate_grad, up_grad, down_grad = call(
        finish_mlp_kernel, "finish_mlp",
        [(gate_weight.shape, F32), (up_weight.shape, F32), (down_weight.shape, F32)],
        [side, mlp_sum, swap(mlp_send, "yh")], scalars=1,
    )

    ends = width_q - cut
    attn_weights = jnp.concatenate(
        [pair_a[:, skip:], pair_b[:, skip : skip + 2 * width_k]], 1
    ).astype(F32)
    gain_parts = jnp.stack(
        [
            jnp.sum(attn_weights * sides[:, : cut + ends + 2 * width_k].astype(F32), 1),
            jnp.sum(
                mlp_pair[:, : 2 * hidden_width].astype(F32)
                * mlp_sum[:, : 2 * hidden_width].astype(F32),
                1,
            ),
        ]
    )
    gain_parts = lax.psum(gain_parts, ("yh",) + TP)
    own_gains = pick(gain_parts.reshape(2, 2, shard), place("yh"), 1)
    return (
        output,
        input_grad,
        own_gains[0] / attn_gain.astype(F32),
        query_grad,
        key_grad,
        value_grad,
        out_grad,
        own_gains[1] / mlp_gain.astype(F32),
        gate_grad,
        up_grad,
        down_grad,
    )


def solution(mesh):
    split = Mesh(mesh.devices.reshape(2, 4, 4, 2, 2), WIDE + TP)
    rows = P(WIDE + TP, None)
    inward = P(WIDE, TP)
    outward = P(TP, WIDE)
    gain = P(WIDE)
    return jax.shard_map(
        per_device,
        mesh=split,
        in_specs=(
            rows, gain, gain, inward, inward, inward, outward, gain, inward, inward, outward, rows,
        ),
        out_specs=(
            rows, rows, gain, inward, inward, inward, outward, gain, inward, inward, outward,
        ),
        check_vma=False,
    )
```

```python
import functools

import jax
import jax.numpy as jnp
from jax import lax
from jax.experimental import pallas as pl
from jax.experimental.pallas import tpu as pltpu
from jax.sharding import Mesh, PartitionSpec as P

HEADS = 32
KV = 4
HD = 64
SEQ_DEVS = 4
WIDE = ("yh", "z", "x")
TP = ("yl", "core")
RING = ("yh", "yl")
BF = jnp.bfloat16
F32 = jnp.float32

epsilon = 1e-05
masked_fill = -1e30
VMEM_LIMIT = 56 * 1024 * 1024


def after(value, *earlier):
    return lax.optimization_barrier((value, earlier))[0]


def shift(block, axis, distance):
    n = 4 if axis == RING else lax.axis_size(axis)
    return lax.ppermute(block, axis, [(i, (i + distance) % n) for i in range(n)])


def swap(block, axis):
    return shift(block, axis, 1)


def place(axis, step=0):
    n = lax.axis_size(axis)
    return ((lax.axis_index(axis) + (step + n)) & (n - 1)).astype(jnp.uint32)


def pick(array, index, dim):
    return lax.dynamic_index_in_dim(array, index, dim, keepdims=False)


def send_stage(block, axis):
    n = lax.axis_size(axis)
    return [block] + [shift(block, axis, d) for d in (1, n - 1, *range(2, n - 1))]


def stack_stage(arrived, axis, dim):
    n = len(arrived)
    block = arrived[0]
    out = jnp.zeros(block.shape[:dim] + (n,) + block.shape[dim:], block.dtype)
    for d, piece in zip((0, 1, n - 1, *range(2, n - 1)), arrived):
        out = lax.dynamic_update_index_in_dim(out, piece, place(axis, -d), dim)
    return out


def gather_ring(block, axis, dim):
    half = block.shape[0] // 2
    left, right = shift(block, axis, 1), shift(block, axis, -1)
    upper, lower = shift(left[:half], axis, 1), shift(right[half:], axis, -1)
    out = jnp.zeros(block.shape[:dim] + (4,) + block.shape[dim:], block.dtype)
    out = lax.dynamic_update_index_in_dim(out, block, place(axis), dim)
    out = lax.dynamic_update_index_in_dim(out, left, place(axis, -1), dim)
    out = lax.dynamic_update_index_in_dim(out, right, place(axis, 1), dim)
    across = jnp.concatenate([upper, lower], 0)
    return lax.dynamic_update_index_in_dim(out, across, place(axis, 2), dim), (left, right)


def join_sides(shard, other):
    first = lax.axis_index("yh") == 0
    return jnp.concatenate([jnp.where(first, shard, other), jnp.where(first, other, shard)], 0)


def flat(blocks):
    return blocks.reshape(-1, blocks.shape[-1])


def gather_rows(rows):
    across = swap(rows, "yl")
    return [rows, swap(rows, "core"), across, swap(across, "core")]


def gather_eight(rows):
    near = [rows, shift(rows, RING, 1), shift(rows, RING, 2), shift(rows, RING, -1)]
    return near + [swap(piece, "core") for piece in near]


def scatter_eight(own_core, other_core):
    quarter, d = own_core.shape[0] // 4, own_core.shape[1]
    own, *others = call(
        add_pieces_kernel, "add_pieces",
        [((quarter, d), F32)] + [((quarter, d), BF)] * 3, [own_core, swap(other_core, "core")],
    )
    return own, others


def send_back(others):
    one, two, three = others
    return [shift(one, RING, -1), shift(three, RING, 1), shift(two, RING, 2)]


def scatter_cores(partial):
    own, beside, across, corner = partial
    far = swap(corner, "core").astype(F32)
    return own, swap(beside, "core"), (across.astype(F32) + far).astype(BF)


def scatter_rows(partial):
    own, near, other = scatter_cores(partial)
    return [own, near, swap(other, "yl")]


def total(first, parts):
    for part in parts:
        first = first + part.astype(F32)
    return first


def exchange_sum(parts, axis, hold=()):
    near = parts[0].astype(F32)
    for d in (1, 3):
        near = near + after(shift(parts[d], axis, d), *hold).astype(F32)
    return near + after(shift(parts[2], axis, 2), *hold).astype(F32)


def wide_sum_next(part, axis, hold=()):
    n = lax.axis_size(axis)
    part = part.reshape(n, part.shape[0] // n, part.shape[1])
    pieces = [pick(part, place(axis, d), 0) for d in range(n)]
    return exchange_sum(pieces, axis, hold).astype(BF)


def mm(left, right):
    return jnp.dot(left, right, preferred_element_type=F32)


def mm_last(left, right):
    return lax.dot_general(left, right, (((1,), (1,)), ((), ())), preferred_element_type=F32)


def normed_rows(piece):
    values = piece.astype(F32)
    factor = lax.rsqrt(jnp.mean(values * values, -1, keepdims=True) + epsilon)
    return values * factor, factor


def scale_rows(piece_refs, gain, scaled_ref):
    for n, ref in enumerate(piece_refs):
        for at in range(0, ref.shape[0], 32):
            normed, _ = normed_rows(ref[at : at + 32, :])
            rows = n * ref.shape[0] + at
            scaled_ref[rows : rows + 32, :] = (normed * gain).astype(BF)


def turned(block, cos, sin):
    a, b = block[: HD // 2], block[HD // 2 :]
    return jnp.concatenate([a * cos - b * sin, b * cos + a * sin], 0)


def keys_values_kernel(skip, *refs):
    piece_refs, (w_ref, cos_ref, sin_ref, kv_ref, scaled_ref, gains_ref) = refs[:4], refs[4:]
    gains_ref[...] = w_ref[:, skip + 128 : skip + 256].T[:8].astype(F32)
    scale_rows(piece_refs, gains_ref[0:1, :], scaled_ref)
    both = mm(scaled_ref[...], w_ref[:, skip : skip + 128]).T
    keys = turned(both[:HD], cos_ref[...], sin_ref[...])
    kv_ref[...] = jnp.concatenate([keys, both[HD:]], 0).T.astype(BF)


def queries_kernel(skip, x_ref, w_ref, cos_ref, sin_ref, q_ref):
    for at in range(0, q_ref.shape[0], 256):
        piece = mm(x_ref[...], w_ref[:, skip + at : skip + at + 256]).T
        for sub in range(0, 256, HD):
            low = turned(piece[sub : sub + HD], cos_ref[...], sin_ref[...]).astype(BF)
            q_ref[at + sub : at + sub + HD, :] = low * 0.125


def to_inner(ref, out_ref):
    half = ref.shape[1] // 2
    for at in range(0, half, 128):
        low, high = ref[:, at : at + 128], ref[:, half + at : half + at + 128]
        out_ref[:, 2 * at : 2 * at + 128] = jnp.concatenate([low[:, :HD], high[:, :HD]], 1)
        out_ref[:, 2 * at + 128 : 2 * at + 256] = jnp.concatenate([low[:, HD:], high[:, HD:]], 1)


def pack_kernel(inputs_ref, cot_ref, again_ref, mgain_ref, q_ref, k_ref, v_ref, o_ref, g_ref, u_ref, d_ref,
                rows_ref, cots_ref, a_ref, b_ref, mlp_ref):
    to_inner(inputs_ref, rows_ref)
    to_inner(cot_ref, cots_ref)
    out = o_ref[...].T
    half = out.shape[1] // 2
    a_ref[:, :half] = out[:, :half]
    a_ref[:, half:] = q_ref[...]
    b_ref[:, :half] = out[:, half:]
    b_ref[:, half : half + 128] = jnp.concatenate([k_ref[...], v_ref[...]], 1)
    gains = jnp.concatenate(
        [again_ref[...].astype(F32), mgain_ref[...].astype(F32), jnp.zeros((126, HD), F32)], 0
    )
    b_ref[:, half + 128 :] = gains.T.astype(BF)
    width = g_ref.shape[1]
    down = d_ref[...].T
    whole_units = 128 * (width // 256)
    tail = 2 * whole_units
    for side in range(2):
        units = slice(side * whole_units, (side + 1) * whole_units)
        ends = slice(tail + 64 * side, tail + 64 * side + 64)
        mlp_ref[side, :, :whole_units] = g_ref[:, units]
        mlp_ref[side, :, whole_units:tail] = u_ref[:, units]
        mlp_ref[side, :, tail : tail + 128] = jnp.concatenate([g_ref[:, ends], u_ref[:, ends]], 1)
        mlp_ref[side, :, tail + 128 : tail + 128 + whole_units] = down[:, units]
        mlp_ref[side, :, tail + 128 + whole_units :] = jnp.concatenate(
            [down[:, ends], jnp.zeros_like(down[:, ends])], 1
        )


def finish_mlp_kernel(side_ref, pair_ref, other_ref, gate_ref, up_ref, down_ref):
    rows = pl.ds(pl.multiple_of(side_ref[0, 0] * HD, HD), HD)
    own, other = pair_ref[rows, :].astype(F32), other_ref[...].astype(F32)
    here = side_ref[0, 0] == 0
    halves = jnp.where(here, own, other), jnp.where(here, other, own)
    units = 128 * (gate_ref.shape[1] // 256)
    tail = 2 * units
    down = []
    for n, half in enumerate(halves):
        gate_ref[:, n * units : (n + 1) * units] = half[:, :units]
        up_ref[:, n * units : (n + 1) * units] = half[:, units:tail]
        down.append(half[:, tail + 128 : tail + 128 + units])
    ends = [half[:, tail : tail + 128] for half in halves]
    gate_ref[:, tail:] = jnp.concatenate([end[:, :64] for end in ends], 1)
    up_ref[:, tail:] = jnp.concatenate([end[:, 64:] for end in ends], 1)
    down += [half[:, tail + 128 + units : tail + 192 + units] for half in halves]
    for n in range(2):
        down_ref[n * units : (n + 1) * units, :] = down[n].T
    down_ref[tail:, :] = jnp.concatenate(down[2:], 1).T


def finish_attn_kernel(side_ref, pair_ref, other_ref, q_ref, k_ref, v_ref, o_ref):
    rows = pl.ds(pl.multiple_of(side_ref[0, 0] * HD, HD), HD)
    both = pair_ref[rows, :].astype(F32) + other_ref[...].astype(F32)
    width = q_ref.shape[1]
    q_ref[...] = both[:, :width]
    k_ref[...] = both[:, width : width + HD]
    v_ref[...] = both[:, width + HD : width + 2 * HD]
    o_ref[...] = both[:, width + 2 * HD :].T


def add_pieces_kernel(one_ref, two_ref, *outs):
    for n, out in enumerate(outs):
        rows = slice(n * out.shape[0], (n + 1) * out.shape[0])
        out[...] = (one_ref[rows, :].astype(F32) + two_ref[rows, :].astype(F32)).astype(out.dtype)


def middle_kernel(base_ref, *refs):
    parts, (gain_ref, sum_ref, scaled_ref) = refs[:-3], refs[-3:]
    for at in range(0, base_ref.shape[0], 32):
        rows = slice(at, at + 32)
        value = base_ref[rows, :].astype(F32)
        for ref in parts:
            value = value + ref[rows, :].astype(F32)
        sum_ref[rows, :] = value
        normed, _ = normed_rows(value.astype(BF))
        scaled_ref[rows, :] = (normed * gain_ref[1:2, :]).astype(BF)


def middle_grad_kernel(base_ref, *refs):
    parts, (middle_ref, gain_ref, sum_ref, low_ref) = refs[:-4], refs[-4:]
    for at in range(0, base_ref.shape[0], 32):
        rows = slice(at, at + 32)
        value = parts[0][rows, :].astype(F32)
        for ref in parts[1:]:
            value = value + ref[rows, :].astype(F32)
        normed, factor = normed_rows(middle_ref[rows, :].astype(BF))
        value = value * gain_ref[1:2, :]
        inner = jnp.mean(value * normed, -1, keepdims=True)
        value = base_ref[rows, :].astype(F32) + factor * (value - normed * inner)
        sum_ref[rows, :] = value
        low_ref[rows, :] = value.astype(BF)


def hidden_kernel(width, *refs):
    (w_ref, hidden_ref, both_ref, x_ref, c_ref, gate_up_ref, down_ref, sems) = refs[16:]
    first = gate_up_ref.shape[1]
    copies = [
        pltpu.make_async_copy(w_ref.at[:, pl.ds(0, first)], gate_up_ref, sems.at[0]),
        pltpu.make_async_copy(w_ref.at[:, pl.ds(first, down_ref.shape[1])], down_ref, sems.at[1]),
    ]
    count = x_ref.shape[0] // 8
    for n in range(8):
        rows = pl.ds(n * count, count)
        copies.append(pltpu.make_async_copy(refs[n], x_ref.at[rows, :], sems.at[2 + n]))
        copies.append(pltpu.make_async_copy(refs[8 + n], c_ref.at[rows, :], sems.at[10 + n]))
    weights_up, weights_down, *pieces = copies
    xs, cots = pieces[::2], pieces[1::2]
    for copy in (*xs[:4], weights_up, *xs[4:], weights_down, *cots):
        copy.start()

    def units(gate, up, grad):
        sigmoid = 1.0 / (1.0 + jnp.exp(-gate))
        gated = gate * sigmoid
        return (
            (gated * up).astype(BF),
            (grad * up * sigmoid * (1.0 + gate * (1.0 - sigmoid))).astype(BF),
            (grad * gated).astype(BF),
        )

    half = 4 * count
    for part in range(2):
        rows = slice(part * half, (part + 1) * half)
        for copy in xs[4 * part : 4 * part + 4]:
            copy.wait()
        if part == 0:
            weights_up.wait()
        x = x_ref[rows, :]
        gate = mm(x, gate_up_ref[:, :width])
        up = mm(x, gate_up_ref[:, width : 2 * width])
        ends = mm(x, gate_up_ref[:, 2 * width :])
        for copy in cots[4 * part : 4 * part + 4]:
            copy.wait()
        if part == 0:
            weights_down.wait()
        c = c_ref[rows, :]
        value, dgate, dup = units(gate, up, mm(c, down_ref[:, :width]))
        hidden_ref[rows, :width] = value
        both_ref[rows, :width] = dgate
        both_ref[rows, width : 2 * width] = dup
        value, dgate, dup = units(ends[:, :64], ends[:, 64:], mm(c, down_ref[:, width:])[:, :64])
        hidden_ref[rows, width:] = jnp.concatenate([value, jnp.zeros_like(value)], 1)
        both_ref[rows, 2 * width :] = jnp.concatenate([dgate, dup], 1)


def sum_of_products(terms, refs):
    total = None
    for left, (low, high), right, (first, last) in terms:
        part = mm_last(refs[left][:, low:high], refs[right][:, first:last])
        total = part if total is None else total + part
    return total


def rows_grad_kernel(terms, count, gain_row, *refs):
    pieces, gain_ref, outs, sum_ref = refs[count : count + 4], refs[count + 4], refs[count + 5 : -1], refs[-1]
    step = pl.program_id(0)
    tile = sum_ref.shape[1] // pl.num_programs(0)
    columns = pl.ds(pl.multiple_of(step * tile, tile), tile)
    sum_ref[:, columns] = sum_of_products(terms, refs) * gain_ref[gain_row : gain_row + 1, columns]

    @pl.when(step == pl.num_programs(0) - 1)
    def _():
        for n, ref in enumerate(pieces):
            for at in range(0, ref.shape[0], 32):
                normed, factor = normed_rows(ref[at : at + 32, :])
                scaled = sum_ref[n * ref.shape[0] + at : n * ref.shape[0] + at + 32, :]
                inner = jnp.mean(scaled * normed, -1, keepdims=True)
                outs[n][at : at + 32, :] = (factor * (scaled - normed * inner)).astype(BF)


def rows_out_kernel(terms, *refs):
    value = sum_of_products(terms, refs).astype(BF)
    for n in range(value.shape[0] // refs[-1].shape[0]):
        ref = refs[n - value.shape[0] // refs[-1].shape[0]]
        ref[...] = value[n * ref.shape[0] : (n + 1) * ref.shape[0]]


def write_parts(outs, turned_of, axis, me, right, base):
    for d, out in enumerate(outs):
        index = (me + d) & 3
        if axis == "z":
            turned = turned_of(pl.multiple_of(index * 512, 512), 512)
        else:
            turned = jnp.concatenate(
                [turned_of(pl.multiple_of(z * 512 + index * 128, 128), 128) for z in range(4)], 0
            )
        out[:, base : base + right.shape[1]] = mm(turned, right).astype(BF)


def parts_kernel(axis, columns, count, me_ref, *refs):
    lefts, right_ref, outs = refs[:count], refs[count], refs[count + 1 :]

    def turned_of(at, size):
        return jnp.concatenate([left[:, pl.ds(at, size)] for left in lefts], 0).T

    write_parts(outs, turned_of, axis, me_ref[0, 0], right_ref[:, columns[0] : columns[1]], 0)


def last_parts_kernel(axis, cut, me_ref, left_ref, dq_ref, own_ref, one_ref, two_ref, three_ref,
                      cos_ref, sin_ref, *outs):
    half = HD // 2
    cos, sin = cos_ref[...], sin_ref[...]
    kv = own_ref[...]
    for ref in (one_ref, two_ref, three_ref):
        kv = kv + ref[...].astype(F32)
    kv = kv.T
    a, b = kv[:half], kv[half:HD]
    kv = jnp.concatenate([a * cos + b * sin, b * cos - a * sin, kv[HD:]], 0).T.astype(BF)
    outs[0][...] = kv
    right = jnp.concatenate([dq_ref[:, cut:], kv], 1)

    def turned_of(at, size):
        return left_ref[:, pl.ds(at, size)].T

    write_parts(outs[1:], turned_of, axis, me_ref[0, 0], right, 0)


def settle_kernel(base_ref, *refs):
    out_ref = refs[-1]
    width = base_ref.shape[1]

    def block(at):
        value = base_ref[:, at : at + 128].astype(F32)
        for ref in refs[:-1]:
            value = value + ref[:, at : at + 128].astype(F32)
        return value

    for n in range(width // 256):
        one, two = block(256 * n), block(256 * n + 128)
        low = jnp.concatenate([one[:, :HD], two[:, :HD]], 1)
        high = jnp.concatenate([one[:, HD:], two[:, HD:]], 1)
        out_ref[:, 128 * n : 128 * n + 128] = low.astype(out_ref.dtype)
        out_ref[:, width // 2 + 128 * n : width // 2 + 128 * n + 128] = high.astype(out_ref.dtype)


def fill_bias(bias_ref, me_ref, pos_ref, span, distances):
    step = 64
    quarter = span // 4
    me = me_ref[0, 0]
    at = lax.broadcasted_iota(jnp.int32, (1, span), 1)
    query = (((at // quarter) ^ me) * quarter) + (at & (quarter - 1))
    first = query - pos_ref[...]

    @pl.loop(0, span // step)
    def _(i):
        block = (i * step) // quarter
        start = (block ^ me) * quarter + i * step - block * quarter
        key = start + lax.broadcasted_iota(jnp.int32, (step, span), 0)
        for n, d in enumerate(distances):
            seen = (key - d * span <= query) & (key - d * span >= first)
            bias_ref[pl.ds(pl.multiple_of(n * span + i * step, step), step), :] = jnp.where(
                seen, 0.0, masked_fill
            ).astype(F32)


def attend_kernel(q_ref, *refs):
    blocks = len(refs) - 7
    kv_refs = refs[:blocks]
    me_ref, pos_ref, mix_ref, lse_ref, bias_ref, s_ref, vt_ref = refs[blocks:]
    span = q_ref.shape[1]
    fill_bias(bias_ref, me_ref, pos_ref, span, range(blocks))
    for d in range(blocks):
        vt_ref[:, d * span : (d + 1) * span] = kv_refs[d][...].T[HD:]

    @pl.loop(0, q_ref.shape[0] // 128)
    def _(pair):
        outs = []
        for sub in range(2):
            q = q_ref[pl.ds(pl.multiple_of(pair * 128 + sub * HD, HD), HD), :]
            top = None
            for d in range(blocks):
                rows = slice(d * span, (d + 1) * span)
                s = mm(kv_refs[d][:, :HD], q) + bias_ref[rows, :]
                s_ref[rows, :] = s
                high = jnp.max(s, 0, keepdims=True)
                top = high if top is None else jnp.maximum(top, high)
            total = jnp.zeros_like(top)
            out = jnp.zeros((HD, span), F32)
            for d in range(blocks):
                rows = slice(d * span, (d + 1) * span)
                p = jnp.exp(s_ref[rows, :] - top)
                total = total + jnp.sum(p, 0, keepdims=True)
                out = out + mm(vt_ref[:, rows], p.astype(BF))
            outs.append(out / total)
            lse_ref[pl.ds(pair * 2 + sub, 1), :] = top + jnp.log(total)
        mix_ref[:, pl.ds(pl.multiple_of(pair * 128, 128), 128)] = (
            jnp.concatenate(outs, 0).T.astype(BF)
        )


def attend_back_kernel(distances, first, last, q_ref, *refs):
    blocks = len(distances)
    refs = list(refs)

    def take(count):
        got, refs[:count] = refs[:count], []
        return got

    kv_refs = take(blocks)
    me_ref, pos_ref, lse_ref = take(3)
    if first:
        mix_ref, wa_ref, wb_ref, *piece_refs = take(7)
    else:
        gt_ref, delta_ref, part_ref = take(3)
    if last:
        cos_ref, sin_ref = take(2)
        (dq_ref,) = take(1)
    else:
        (sum_ref,) = take(1)
    (dkv_ref,) = take(1)
    if first:
        gt_ref, delta_ref = take(2)
    bias_ref, v_ref, kt_ref, dk_ref, dv_ref = take(5)
    span = q_ref.shape[1]
    half = HD // 2
    heads = q_ref.shape[0] // HD
    fill_bias(bias_ref, me_ref, pos_ref, span, distances)
    for n in range(blocks):
        rows = slice(n * span, (n + 1) * span)
        both = kv_refs[n][...].T
        kt_ref[:, rows] = both[:HD]
        v_ref[rows, :] = both[HD:].T
    dk_ref[...] = jnp.zeros_like(dk_ref)
    dv_ref[...] = jnp.zeros_like(dv_ref)
    if first:
        rows_all = jnp.concatenate([ref[...] for ref in piece_refs], 0)
        grads = [mm(rows_all, w_ref[:, : heads * HD // 2]).astype(BF) for w_ref in (wa_ref, wb_ref)]
        for at in range(0, heads * HD, 128):
            where = at % (heads * HD // 2)
            gt = grads[2 * at // (heads * HD)][:, where : where + 128].T
            mt = mix_ref[:, at : at + 128].T
            gt_ref[at : at + 128, :] = gt
            prod = gt.astype(F32) * mt.astype(F32)
            for sub in range(2):
                h = at // HD + sub
                delta_ref[h : h + 1, :] = jnp.sum(prod[sub * HD : (sub + 1) * HD], 0, keepdims=True)

    @pl.loop(0, heads // 2)
    def _(pair):
        outs = []
        for sub in range(2):
            rows_h = pl.ds(pl.multiple_of(pair * 128 + sub * HD, HD), HD)
            q, g = q_ref[rows_h, :], gt_ref[rows_h, :]
            lse = lse_ref[pl.ds(pair * 2 + sub, 1), :]
            delta = delta_ref[pl.ds(pair * 2 + sub, 1), :]
            dq = jnp.zeros((HD, span), F32) if first else part_ref[rows_h, :]
            for n in range(blocks):
                rows = slice(n * span, (n + 1) * span)
                s = mm(kv_refs[n][:, :HD], q) + bias_ref[rows, :]
                p = jnp.exp(s - lse)
                ds = (p * (mm(v_ref[rows, :], g) - delta)).astype(BF)
                dv_ref[rows, :] += mm_last(p.astype(BF), g)
                dk_ref[rows, :] += mm_last(ds, q)
                dq = dq + mm(kt_ref[:, rows], ds)
            if last:
                dq = dq * 0.125
                a, b = dq[:half], dq[half:]
                cos, sin = cos_ref[...], sin_ref[...]
                outs += [a * cos + b * sin, b * cos - a * sin]
            else:
                sum_ref[rows_h, :] = dq
        if last:
            dq_ref[:, pl.ds(pl.multiple_of(pair * 128, 128), 128)] = (
                jnp.concatenate(outs, 0).T.astype(BF)
            )

    for n in range(blocks):
        rows = slice(n * span, (n + 1) * span)
        dkv_ref[rows, :] = jnp.concatenate([dk_ref[rows, :], dv_ref[rows, :]], 1).astype(dkv_ref.dtype)


def weight_grads_kernel(*refs):
    one_ref, two_ref, out_ref = refs[16:]
    at = 0
    for lefts, ref in ((refs[:8], one_ref), (refs[8:16], two_ref)):
        turned = jnp.concatenate([left[...] for left in lefts], 0).T
        for c in range(0, ref.shape[1], 256):
            size = min(256, ref.shape[1] - c)
            out_ref[:, at + c : at + c + size] = mm(turned, ref[:, c : c + size]).astype(BF)
        at += ref.shape[1]


def params():
    return pltpu.CompilerParams(vmem_limit_bytes=VMEM_LIMIT)


def whole(count):
    return [pl.BlockSpec(memory_space=pltpu.VMEM)] * count


def cost(products, moved):
    return pl.CostEstimate(flops=2 * products, bytes_accessed=moved, transcendentals=0)


def call(kernel, name, shapes, operands, scalars=0, products=0):
    return pl.pallas_call(
        kernel,
        out_shape=tuple(jax.ShapeDtypeStruct(*shape) for shape in shapes),
        in_specs=[pl.BlockSpec(memory_space=pltpu.SMEM)] * scalars + whole(len(operands) - scalars),
        out_specs=tuple(whole(len(shapes))),
        compiler_params=params(),
        cost_estimate=cost(products, 4 << 20),
        name=name,
    )(*operands)


def hidden_units(pieces, cots, weights, width):
    count, d = pieces[0].shape
    span = 8 * count
    both, down = 2 * width + 128, width + 128
    return pl.pallas_call(
        functools.partial(hidden_kernel, width),
        out_shape=(jax.ShapeDtypeStruct((span, down), BF), jax.ShapeDtypeStruct((span, both), BF)),
        in_specs=[pl.BlockSpec(memory_space=pl.ANY)] * 17,
        out_specs=tuple(whole(2)),
        scratch_shapes=[
            pltpu.VMEM((span, d), BF),
            pltpu.VMEM((span, d), BF),
            pltpu.VMEM((d, both), BF),
            pltpu.VMEM((d, down), BF),
            pltpu.SemaphoreType.DMA((18,)),
        ],
        compiler_params=params(),
        cost_estimate=cost(3 * span * d * width, 6 * d * width),
        name="hidden_units",
    )(*pieces, *cots, weights)


def feature_rows(weight, tile):
    if not isinstance(weight, tuple):
        return pl.BlockSpec((tile, weight.shape[1]), lambda i: (i, 0))
    return pl.BlockSpec((pl.Element(tile), pl.Element(weight[2])), lambda i: (i * tile, weight[1]))


def array_of(weight):
    return weight[0] if isinstance(weight, tuple) else weight


def fixed(array):
    return pl.BlockSpec(array.shape, lambda i: (0, 0))


def rows_grad(grads, weights, terms, pieces, gains, gain_row):
    span, d = 4 * pieces[0].shape[0], pieces[0].shape[1]
    tile = 512
    n = len(grads)
    terms = [(g, c, n + w, e) for g, c, w, e in terms]
    return pl.pallas_call(
        functools.partial(rows_grad_kernel, terms, n + len(weights), gain_row),
        grid=(d // tile,),
        out_shape=(jax.ShapeDtypeStruct((span // 4, d), BF),) * 4,
        in_specs=[fixed(g) for g in grads]
        + [feature_rows(w, tile) for w in weights]
        + [fixed(a) for a in (*pieces, gains)],
        out_specs=(pl.BlockSpec((span // 4, d), lambda i: (0, 0)),) * 4,
        scratch_shapes=[pltpu.VMEM((span, d), F32)],
        compiler_params=params(),
        cost_estimate=cost(sum(span * d * (c[1] - c[0]) for _, c, _, _ in terms), 8 << 20),
        name="rows_grad",
    )(*grads, *map(array_of, weights), *pieces, gains)


def rows_out(lefts, weights, terms, tile, pieces):
    span, d = lefts[0].shape[0], array_of(weights[0]).shape[0]
    n = len(lefts)
    terms = [(g, c, n + w, e) for g, c, w, e in terms]
    return pl.pallas_call(
        functools.partial(rows_out_kernel, terms),
        grid=(d // tile,),
        out_shape=(jax.ShapeDtypeStruct((span // pieces, d), BF),) * pieces,
        in_specs=[fixed(g) for g in lefts] + [feature_rows(w, tile) for w in weights],
        out_specs=(pl.BlockSpec((span // pieces, tile), lambda i: (0, i)),) * pieces,
        compiler_params=params(),
        cost_estimate=cost(sum(span * d * (c[1] - c[0]) for _, c, _, _ in terms), 6 << 20),
        name="rows_out",
    )(*lefts, *map(array_of, weights))


def scalar():
    return [pl.BlockSpec(memory_space=pltpu.SMEM)]


def at_place(axis):
    return place(axis).astype(jnp.int32).reshape(1, 1)


def wide_parts(lefts, right, columns, axis):
    span, d = right.shape[0], lefts[0].shape[1]
    width = columns[1] - columns[0]
    return pl.pallas_call(
        functools.partial(parts_kernel, axis, columns, len(lefts)),
        out_shape=(jax.ShapeDtypeStruct((d // 4, width), BF),) * 4,
        in_specs=scalar() + whole(len(lefts) + 1),
        out_specs=tuple(whole(4)),
        compiler_params=params(),
        cost_estimate=cost(span * d * width, 8 << 20),
        name="wide_parts",
    )(at_place(axis), *lefts, right)


def last_parts(left, dq, cut, own, arrived, cos, sin, axis):
    span, d = left.shape
    width = dq.shape[1] - cut + 2 * HD
    return pl.pallas_call(
        functools.partial(last_parts_kernel, axis, cut),
        out_shape=(jax.ShapeDtypeStruct((span, 2 * HD), BF),)
        + (jax.ShapeDtypeStruct((d // 4, width), BF),) * 4,
        in_specs=scalar() + whole(8),
        out_specs=tuple(whole(5)),
        compiler_params=params(),
        cost_estimate=cost(span * d * width, 8 << 20),
        name="last_parts",
    )(at_place(axis), left, dq, own, *arrived, cos, sin)


def settle(base, parts, kind):
    return pl.pallas_call(
        settle_kernel,
        out_shape=jax.ShapeDtypeStruct(base.shape, kind),
        in_specs=whole(1 + len(parts)),
        out_specs=whole(1)[0],
        compiler_params=params(),
        cost_estimate=cost(0, 4 << 20),
        name="settle",
    )(base, *parts)


def window_specs():
    return [pl.BlockSpec(memory_space=pltpu.SMEM)] + whole(1)


def attend(q, kvs, window):
    n = len(kvs)
    width, span = q.shape
    heads = width // HD
    return pl.pallas_call(
        attend_kernel,
        out_shape=(
            jax.ShapeDtypeStruct((span, width), BF),
            jax.ShapeDtypeStruct((heads, span), F32),
        ),
        in_specs=whole(n + 1) + window_specs(),
        out_specs=tuple(whole(2)),
        scratch_shapes=[
            pltpu.VMEM((n * span, span), F32),
            pltpu.VMEM((n * span, span), F32),
            pltpu.VMEM((HD, n * span), BF),
        ],
        compiler_params=params(),
        cost_estimate=pl.CostEstimate(flops=16 * span * width * n * span, bytes_accessed=2 << 20, transcendentals=heads * n * span * span),
        name="attend",
    )(q, *kvs, *window)


def attend_back(distances, q, kvs, window, lse, prepared, mixed=None, out=None, turn=None):
    n = len(kvs)
    width, span = q.shape
    heads = width // HD
    first, last = prepared is None, turn is not None
    operands = [q, *kvs, *window, lse]
    operands += [mixed, *out] if first else list(prepared)
    shapes = []
    if last:
        operands += turn
        shapes.append(jax.ShapeDtypeStruct((span, width), BF))
    else:
        shapes.append(jax.ShapeDtypeStruct((width, span), F32))
    shapes.append(jax.ShapeDtypeStruct((n * span, 2 * HD), F32 if last else BF))
    if first:
        shapes.append(jax.ShapeDtypeStruct((width, span), BF))
        shapes.append(jax.ShapeDtypeStruct((heads, span), F32))
    return pl.pallas_call(
        functools.partial(attend_back_kernel, distances, first, last),
        out_shape=tuple(shapes),
        in_specs=whole(n + 1) + window_specs() + whole(len(operands) - n - 3),
        out_specs=tuple(whole(len(shapes))),
        scratch_shapes=[
            pltpu.VMEM((n * span, span), F32),
            pltpu.VMEM((n * span, HD), BF),
            pltpu.VMEM((HD, n * span), BF),
            pltpu.VMEM((n * span, HD), F32),
            pltpu.VMEM((n * span, HD), F32),
        ],
        compiler_params=params(),
        cost_estimate=cost((1000 if first else 20) * span * width * n * span, 4 << 20),
        name="attend_back",
    )(*operands)


def weight_grads(xs, cots, one, two):
    t, d = xs[0].shape
    tile = 256
    rows = pl.BlockSpec((t, tile), lambda i: (0, i))
    width = one.shape[1] + two.shape[1]
    return pl.pallas_call(
        weight_grads_kernel,
        grid=(d // tile,),
        out_shape=jax.ShapeDtypeStruct((d, width), BF),
        in_specs=[rows] * 16 + [fixed(one), fixed(two)],
        out_specs=pl.BlockSpec((tile, width), lambda i: (i, 0)),
        compiler_params=params(),
        cost_estimate=cost(8 * t * d * width, 2 * d * width + 32 * t * d),
        name="weight_grads",
    )(*xs, *cots, one, two)


def per_device(
    inputs,
    positions,
    attn_gain,
    query_weight,
    key_weight,
    value_weight,
    out_weight,
    mlp_gain,
    gate_weight,
    up_weight,
    down_weight,
    cotangent,
):
    width_q = query_weight.shape[1]
    width_k = key_weight.shape[1]
    hidden_width = gate_weight.shape[1]
    span = positions.shape[0]
    quarter = span // 4
    cut = 3 * width_q // 4
    skip = width_q // 2
    d = inputs.shape[1]
    shard = query_weight.shape[0]
    side = place("yh").astype(jnp.int32).reshape(1, 1)

    units = 128 * (hidden_width // 256)
    both_width, down_width = 2 * units + 128, units + 128
    inputs, cotangent, shard_a, shard_b, shard_mlp = call(
        pack_kernel, "pack",
        [(inputs.shape, BF), (inputs.shape, BF), ((shard, skip + width_q), BF),
         ((shard, skip + 256), BF), ((2, shard, both_width + down_width), BF)],
        [inputs, cotangent, attn_gain[None], mlp_gain[None], query_weight, key_weight, value_weight,
         out_weight, gate_weight, up_weight, down_weight],
    )
    other_b, other_a = swap(shard_b, "yh"), swap(shard_a, "yh")
    other_mlp = swap(pick(shard_mlp, place("yh", 1), 0), "yh")
    rows_in = gather_rows(inputs)
    pair_b, pair_a = join_sides(shard_b, other_b), join_sides(shard_a, other_a)
    along_b, along_a = send_stage(pair_b, "x"), send_stage(pair_a, "z")
    whole_b, came_b = gather_ring(stack_stage(along_b, "x", 0), "z", 0)
    whole_a, came_a = gather_ring(stack_stage(along_a, "z", 0), "x", 1)
    whole_a, whole_b = flat(whole_a), flat(whole_b)
    mlp_pair = join_sides(pick(shard_mlp, place("yh"), 0), after(other_mlp, came_a, came_b))
    mlp_whole = lax.all_gather(mlp_pair, ("z", "x"), axis=0, tiled=True)
    cotangents = gather_eight(after(cotangent, rows_in[2]))

    me = (lax.axis_index("yl") * 2 + lax.axis_index("core")).astype(jnp.int32)
    blocked = jnp.arange(4, dtype=jnp.int32) ^ me
    positions = jnp.take(positions.reshape(4, quarter), blocked, axis=0, mode="clip").reshape(1, span)
    freqs = 10000.0 ** (-(jnp.arange(HD // 2, dtype=F32) * 2.0) / HD)
    angles = freqs[:, None] * positions.astype(F32)
    cos, sin = jnp.cos(angles), jnp.sin(angles)
    window = (me.reshape(1, 1), positions)

    kv_block, scaled_in, gains = call(
        functools.partial(keys_values_kernel, skip), "keys_values",
        [((span, 2 * width_k), BF), ((span, d), BF), ((8, d), F32)],
        [*rows_in, whole_b, cos, sin], products=span * d * 2 * width_k,
    )
    (queries,) = call(
        functools.partial(queries_kernel, skip), "queries",
        [((width_q, span), BF)],
        [scaled_in, after(whole_a, kv_block, cotangents), cos, sin], products=span * d * width_q,
    )
    blocks = [kv_block] + [shift(kv_block, "x", d) for d in range(1, SEQ_DEVS)]
    mixed, log_total = attend(queries, blocks, window)

    out_a, out_b = (whole_a, 0, skip), (whole_b, 0, skip)
    attn_rows = rows_out(
        [mixed], [out_a, out_b],
        [(0, (0, skip), 0, (0, skip)), (0, (skip, width_q), 1, (0, skip))], 1024, 4,
    )
    middle, scaled_mid = call(
        middle_kernel, "middle", [(inputs.shape, F32), (inputs.shape, BF)],
        [inputs, *scatter_rows(attn_rows), gains],
    )
    scaled_all = gather_eight(scaled_mid)
    hidden, grad_both = hidden_units(scaled_all, cotangents, mlp_whole, units)
    mid_partial = rows_out(
        [grad_both], [(mlp_whole, 0, both_width)], [(0, (0, both_width), 0, (0, both_width))], 512, 2
    )
    mid_own, mid_others = scatter_eight(*mid_partial)
    mid_arrived = send_back(mid_others)
    mlp_rows = rows_out(
        [after(hidden, mid_others)], [(mlp_whole, both_width, down_width)],
        [(0, (0, down_width), 0, (0, down_width))], 512, 2,
    )
    grad_middle, grad_middle_low = call(
        middle_grad_kernel, "middle_grad", [(inputs.shape, F32), (inputs.shape, BF)],
        [cotangent, mid_own, *after(mid_arrived, mlp_rows), middle, gains],
    )
    mlp_sum = weight_grads(
        [after(scaled_all[0], grad_middle_low), *scaled_all[1:]], cotangents, grad_both, hidden
    )
    across = after(swap(grad_middle_low, "yl"), mlp_sum)
    rows_grad_middle = [grad_middle_low, swap(grad_middle_low, "core"), across, swap(across, "core")]
    mlp_sum = lax.psum_scatter(mlp_sum, ("z", "x"), scatter_dimension=0, tiled=True)

    out_parts = wide_parts(rows_grad_middle, mixed, (0, width_q), "z")
    mlp_own, mlp_others = scatter_eight(mlp_rows[0], after(mlp_rows[1], grad_middle_low))
    query_part, far_grads, grad_turned, delta = attend_back(
        (1, 2, 3), queries, blocks[1:], window, log_total, None, after(mixed, out_parts, mlp_others),
        [whole_a, whole_b, *rows_grad_middle],
    )
    mlp_arrived = send_back(after(mlp_others, rows_grad_middle))
    mlp_near = [after(piece, query_part) for piece in mlp_arrived[:2]]
    arriving = [
        shift(far_grads[(d - 1) * span : d * span], "x", -d) for d in range(1, SEQ_DEVS)
    ]
    out_near = out_parts[0].astype(F32)
    for distance in (1, 3):
        out_near = out_near + after(shift(out_parts[distance], "z", distance), query_part).astype(F32)
    out_far = shift(out_parts[2], "z", 2)
    query_raw_grad, own_grads = attend_back(
        (0,), after(queries, out_near, mlp_near), blocks[:1], window, log_total, (grad_turned, delta, query_part), turn=[cos, sin]
    )

    out_sum = (out_near + after(out_far, query_raw_grad).astype(F32)).astype(BF)
    output = settle(middle, [mlp_own, *mlp_near, after(mlp_arrived[2], query_raw_grad)], BF)
    a_parts = wide_parts([scaled_in], query_raw_grad, (0, cut), "x")
    kv_raw_grad, *b_parts = last_parts(
        scaled_in, after(query_raw_grad, a_parts), cut, own_grads, arriving, cos, sin, "z"
    )
    in_partial = rows_grad(
        [query_raw_grad, kv_raw_grad],
        [whole_a, whole_b],
        [
            (0, (0, width_q), 0, (skip, skip + width_q)),
            (1, (0, 2 * width_k), 1, (skip, skip + 2 * width_k)),
        ],
        rows_in, gains, 0,
    )
    input_grad = settle(grad_middle, scatter_rows(in_partial), F32)

    mlp_send = pick(mlp_sum.reshape(2, shard, -1), place("yh", 1), 0)
    a_sum = wide_sum_next(exchange_sum(a_parts, "x").astype(BF), "z")
    b_sum = exchange_sum(b_parts, "z").astype(BF)
    b_sum = wide_sum_next(jnp.concatenate([b_sum, out_sum], 1), "x", hold=[mlp_send])
    sides = jnp.concatenate([a_sum, b_sum], 1)
    other_sides = swap(pick(sides.reshape(2, shard, -1), place("yh", 1), 0), "yh")
    query_grad, key_grad, value_grad, out_grad = call(
        finish_attn_kernel, "finish_attn",
        [(query_weight.shape, F32), (key_weight.shape, F32), (value_weight.shape, F32),
         (out_weight.shape, F32)],
        [side, sides, other_sides], scalars=1,
    )
    gate_grad, up_grad, down_grad = call(
        finish_mlp_kernel, "finish_mlp",
        [(gate_weight.shape, F32), (up_weight.shape, F32), (down_weight.shape, F32)],
        [side, mlp_sum, swap(mlp_send, "yh")], scalars=1,
    )

    ends = width_q - cut
    attn_weights = jnp.concatenate(
        [pair_a[:, skip:], pair_b[:, skip : skip + 2 * width_k]], 1
    ).astype(F32)
    gain_parts = jnp.stack(
        [
            jnp.sum(attn_weights * sides[:, : cut + ends + 2 * width_k].astype(F32), 1),
            jnp.sum(
                mlp_pair[:, :both_width].astype(F32) * mlp_sum[:, :both_width].astype(F32),
                1,
            ),
        ]
    )
    gain_parts = lax.psum(gain_parts, ("yh",) + TP)
    own_gains = pick(gain_parts.reshape(2, 2, shard), place("yh"), 1)
    return (
        output,
        input_grad,
        own_gains[0] / attn_gain.astype(F32),
        query_grad,
        key_grad,
        value_grad,
        out_grad,
        own_gains[1] / mlp_gain.astype(F32),
        gate_grad,
        up_grad,
        down_grad,
    )


def solution(mesh):
    split = Mesh(mesh.devices.reshape(2, 4, 4, 2, 2), WIDE + TP)
    rows = P(WIDE + TP, None)
    inward = P(WIDE, TP)
    outward = P(TP, WIDE)
    gain = P(WIDE)
    return jax.shard_map(
        per_device,
        mesh=split,
        in_specs=(
            rows, gain, gain, inward, inward, inward, outward, gain, inward, inward, outward, rows,
        ),
        out_specs=(
            rows, rows, gain, inward, inward, inward, outward, gain, inward, inward, outward,
        ),
        check_vma=False,
    )
```

```python
import functools

import jax
import jax.numpy as jnp
from jax import lax
from jax.experimental import pallas as pl
from jax.experimental.pallas import tpu as pltpu
from jax.sharding import Mesh, PartitionSpec as P

HEADS = 32
KV = 4
HD = 64
SEQ_DEVS = 4
WIDE = ("yh", "z", "x")
TP = ("yl", "core")
RING = ("yh", "yl")
BF = jnp.bfloat16
F32 = jnp.float32

epsilon = 1e-05
masked_fill = -1e30
MIB = 1024 * 1024


def after(value, *earlier):
    return lax.optimization_barrier((value, earlier))[0]


def shift(block, axis, distance):
    n = 4 if axis == RING else lax.axis_size(axis)
    return lax.ppermute(block, axis, [(i, (i + distance) % n) for i in range(n)])


def swap(block, axis):
    return shift(block, axis, 1)


def place(axis, step=0):
    n = lax.axis_size(axis)
    return ((lax.axis_index(axis) + (step + n)) & (n - 1)).astype(jnp.uint32)


def pick(array, index, dim):
    return lax.dynamic_index_in_dim(array, index, dim, keepdims=False)


def send_stage(block, axis):
    n = lax.axis_size(axis)
    return [block] + [shift(block, axis, d) for d in (1, n - 1, *range(2, n - 1))]


def stack_stage(arrived, axis, dim):
    n = len(arrived)
    block = arrived[0]
    out = jnp.zeros(block.shape[:dim] + (n,) + block.shape[dim:], block.dtype)
    for d, piece in zip((0, 1, n - 1, *range(2, n - 1)), arrived):
        out = lax.dynamic_update_index_in_dim(out, piece, place(axis, -d), dim)
    return out


def gather_ring(block, axis, dim):
    half = block.shape[0] // 2
    left, right = shift(block, axis, 1), shift(block, axis, -1)
    upper, lower = shift(left[:half], axis, 1), shift(right[half:], axis, -1)
    out = jnp.zeros(block.shape[:dim] + (4,) + block.shape[dim:], block.dtype)
    out = lax.dynamic_update_index_in_dim(out, block, place(axis), dim)
    out = lax.dynamic_update_index_in_dim(out, left, place(axis, -1), dim)
    out = lax.dynamic_update_index_in_dim(out, right, place(axis, 1), dim)
    across = jnp.concatenate([upper, lower], 0)
    return lax.dynamic_update_index_in_dim(out, across, place(axis, 2), dim)


def join_sides(shard, other):
    first = lax.axis_index("yh") == 0
    return jnp.concatenate([jnp.where(first, shard, other), jnp.where(first, other, shard)], 0)


def flat(blocks):
    return blocks.reshape(-1, blocks.shape[-1])


def gather_rows(rows):
    across = swap(rows, "yl")
    return [rows, swap(rows, "core"), across, swap(across, "core")]


def gather_eight(rows):
    near = [rows, shift(rows, RING, 1), shift(rows, RING, 2), shift(rows, RING, -1)]
    return near + [swap(piece, "core") for piece in near]


def scatter_eight(own_core, other_core):
    quarter, d = own_core.shape[0] // 4, own_core.shape[1]
    own, *others = call(
        add_pieces_kernel, "add_pieces",
        [((quarter, d), F32)] + [((quarter, d), BF)] * 3, [own_core, swap(other_core, "core")],
    )
    return own, others


def send_back(others):
    one, two, three = others
    return [shift(one, RING, -1), shift(three, RING, 1), shift(two, RING, 2)]


def scatter_rows(partial):
    own, across, cores = partial
    n = own.shape[0]
    arrived = swap(cores, "core")
    other = (across.astype(F32) + arrived[n:].astype(F32)).astype(BF)
    return [own, arrived[:n], swap(other, "yl")]


def total(first, parts):
    for part in parts:
        first = first + part.astype(F32)
    return first


def exchange_sum(parts, axis, hold=()):
    near = parts[0].astype(F32)
    for d in (1, 3):
        near = near + after(shift(parts[d], axis, d), *hold).astype(F32)
    return near + after(shift(parts[2], axis, 2), *hold).astype(F32)


def wide_sum_next(part, axis, hold=()):
    n = lax.axis_size(axis)
    part = part.reshape(n, part.shape[0] // n, part.shape[1])
    pieces = [pick(part, place(axis, d), 0) for d in range(n)]
    return exchange_sum(pieces, axis, hold).astype(BF)


def mm(left, right):
    return jnp.dot(left, right, preferred_element_type=F32)


def mm_last(left, right):
    return lax.dot_general(left, right, (((1,), (1,)), ((), ())), preferred_element_type=F32)


def normed_rows(piece):
    values = piece.astype(F32)
    factor = lax.rsqrt(jnp.mean(values * values, -1, keepdims=True) + epsilon)
    return values * factor, factor


def scale_rows(piece_refs, gain, scaled_ref):
    for n, ref in enumerate(piece_refs):
        for at in range(0, ref.shape[0], 32):
            normed, _ = normed_rows(ref[at : at + 32, :])
            rows = n * ref.shape[0] + at
            scaled_ref[rows : rows + 32, :] = (normed * gain).astype(BF)


def turned(block, cos, sin):
    a, b = block[: HD // 2], block[HD // 2 :]
    return jnp.concatenate([a * cos - b * sin, b * cos + a * sin], 0)


def keys_values_kernel(skip, *refs):
    piece_refs, (w_ref, cos_ref, sin_ref, kv_ref, scaled_ref, gains_ref) = refs[:4], refs[4:]
    gains_ref[...] = w_ref[:, skip + 128 : skip + 256].T[:8].astype(F32)
    scale_rows(piece_refs, gains_ref[0:1, :], scaled_ref)
    both = mm(scaled_ref[...], w_ref[:, skip : skip + 128]).T
    keys = turned(both[:HD], cos_ref[...], sin_ref[...])
    kv_ref[...] = jnp.concatenate([keys, both[HD:]], 0).T.astype(BF)


def queries_kernel(skip, x_ref, w_ref, cos_ref, sin_ref, q_ref):
    for at in range(0, q_ref.shape[0], 256):
        piece = mm(x_ref[...], w_ref[:, skip + at : skip + at + 256]).T
        for sub in range(0, 256, HD):
            low = turned(piece[sub : sub + HD], cos_ref[...], sin_ref[...]).astype(BF)
            q_ref[at + sub : at + sub + HD, :] = low * 0.125


def to_inner(ref, out_ref):
    half = ref.shape[1] // 2
    for at in range(0, half, 128):
        low, high = ref[:, at : at + 128], ref[:, half + at : half + at + 128]
        out_ref[:, 2 * at : 2 * at + 128] = jnp.concatenate([low[:, :HD], high[:, :HD]], 1)
        out_ref[:, 2 * at + 128 : 2 * at + 256] = jnp.concatenate([low[:, HD:], high[:, HD:]], 1)


def pack_kernel(inputs_ref, cot_ref, again_ref, mgain_ref, q_ref, k_ref, v_ref, o_ref, g_ref, u_ref, d_ref,
                rows_ref, cots_ref, a_ref, b_ref, mlp_ref):
    to_inner(inputs_ref, rows_ref)
    to_inner(cot_ref, cots_ref)
    half = o_ref.shape[1] // 2
    a_ref[:, :half] = o_ref[:, :half]
    a_ref[:, half:] = q_ref[...]
    b_ref[:, :half] = o_ref[:, half:]
    b_ref[:, half : half + 128] = jnp.concatenate([k_ref[...], v_ref[...]], 1)
    gains = jnp.concatenate(
        [again_ref[...].astype(F32), mgain_ref[...].astype(F32), jnp.zeros((126, HD), F32)], 0
    )
    b_ref[:, half + 128 :] = gains.T.astype(BF)
    width = g_ref.shape[1]
    down = d_ref[...]
    whole_units = 128 * (width // 256)
    tail = 2 * whole_units
    for side in range(2):
        units = slice(side * whole_units, (side + 1) * whole_units)
        ends = slice(tail + 64 * side, tail + 64 * side + 64)
        mlp_ref[side, :, :whole_units] = g_ref[:, units]
        mlp_ref[side, :, whole_units:tail] = u_ref[:, units]
        mlp_ref[side, :, tail : tail + 128] = jnp.concatenate([g_ref[:, ends], u_ref[:, ends]], 1)
        mlp_ref[side, :, tail + 128 : tail + 128 + whole_units] = down[:, units]
        mlp_ref[side, :, tail + 128 + whole_units :] = jnp.concatenate(
            [down[:, ends], jnp.zeros_like(down[:, ends])], 1
        )


def finish_mlp_kernel(side_ref, pair_ref, other_ref, gate_ref, up_ref, down_ref):
    rows = pl.ds(pl.multiple_of(side_ref[0, 0] * HD, HD), HD)
    own, other = pair_ref[rows, :].astype(F32), other_ref[...].astype(F32)
    here = side_ref[0, 0] == 0
    halves = jnp.where(here, own, other), jnp.where(here, other, own)
    units = 128 * (gate_ref.shape[1] // 256)
    tail = 2 * units
    down = []
    for n, half in enumerate(halves):
        gate_ref[:, n * units : (n + 1) * units] = half[:, :units]
        up_ref[:, n * units : (n + 1) * units] = half[:, units:tail]
        down.append(half[:, tail + 128 : tail + 128 + units])
    ends = [half[:, tail : tail + 128] for half in halves]
    gate_ref[:, tail:] = jnp.concatenate([end[:, :64] for end in ends], 1)
    up_ref[:, tail:] = jnp.concatenate([end[:, 64:] for end in ends], 1)
    down += [half[:, tail + 128 + units : tail + 192 + units] for half in halves]
    for n in range(2):
        down_ref[:, n * units : (n + 1) * units] = down[n]
    down_ref[:, tail:] = jnp.concatenate(down[2:], 1)


def finish_attn_kernel(side_ref, pair_ref, other_ref, q_ref, k_ref, v_ref, o_ref):
    rows = pl.ds(pl.multiple_of(side_ref[0, 0] * HD, HD), HD)
    both = pair_ref[rows, :].astype(F32) + other_ref[...].astype(F32)
    width = q_ref.shape[1]
    q_ref[...] = both[:, :width]
    k_ref[...] = both[:, width : width + HD]
    v_ref[...] = both[:, width + HD : width + 2 * HD]
    o_ref[...] = both[:, width + 2 * HD :]


def add_pieces_kernel(one_ref, two_ref, *outs):
    for n, out in enumerate(outs):
        rows = slice(n * out.shape[0], (n + 1) * out.shape[0])
        out[...] = (one_ref[rows, :].astype(F32) + two_ref[rows, :].astype(F32)).astype(out.dtype)


def pair_pieces_kernel(odd_ref, one_ref, two_ref, own_ref, beside_ref, far_ref):
    size = own_ref.shape[0]
    back = 3 - 2 * odd_ref[0, 0]
    for out, at, step in (
        (own_ref, 0, 0), (beside_ref, 0, back), (beside_ref, size, 4 - back), (far_ref, 0, 2)
    ):
        rows = pl.ds(pl.multiple_of(step * size, size), size)
        value = one_ref[rows, :].astype(F32) + two_ref[rows, :].astype(F32)
        out[at : at + size, :] = value.astype(out.dtype)


def middle_kernel(base_ref, *refs):
    parts, (gain_ref, sum_ref, scaled_ref) = refs[:-3], refs[-3:]
    for at in range(0, base_ref.shape[0], 32):
        rows = slice(at, at + 32)
        value = base_ref[rows, :].astype(F32)
        for ref in parts:
            value = value + ref[rows, :].astype(F32)
        sum_ref[rows, :] = value
        normed, _ = normed_rows(value.astype(BF))
        scaled_ref[rows, :] = (normed * gain_ref[1:2, :]).astype(BF)


def middle_grad_kernel(base_ref, *refs):
    parts, (middle_ref, gain_ref, sum_ref, low_ref) = refs[:-4], refs[-4:]
    for at in range(0, base_ref.shape[0], 32):
        rows = slice(at, at + 32)
        value = parts[0][rows, :].astype(F32)
        for ref in parts[1:]:
            value = value + ref[rows, :].astype(F32)
        normed, factor = normed_rows(middle_ref[rows, :].astype(BF))
        value = value * gain_ref[1:2, :]
        inner = jnp.mean(value * normed, -1, keepdims=True)
        value = base_ref[rows, :].astype(F32) + factor * (value - normed * inner)
        sum_ref[rows, :] = value
        low_ref[rows, :] = value.astype(BF)


def place_of_piece(where_ref, n):
    return (((where_ref[0, 0] - n % 4) & 3) * 2) + (where_ref[0, 1] ^ (n // 4))


def hidden_kernel(width, where_ref, *refs):
    (cots_ref, w_ref, hidden_ref, both_ref, x_ref, c_ref, gate_up_ref, down_ref, sems) = refs[8:]
    first = gate_up_ref.shape[1]
    copies = [
        pltpu.make_async_copy(w_ref.at[:, pl.ds(0, first)], gate_up_ref, sems.at[0]),
        pltpu.make_async_copy(w_ref.at[:, pl.ds(first, down_ref.shape[1])], down_ref, sems.at[1]),
    ]
    count = x_ref.shape[0] // 8
    for n in range(8):
        rows = pl.ds(n * count, count)
        copies.append(pltpu.make_async_copy(refs[n], x_ref.at[rows, :], sems.at[2 + n]))
        at = pl.ds(pl.multiple_of(place_of_piece(where_ref, n) * count, count), count)
        copies.append(pltpu.make_async_copy(cots_ref.at[at, :], c_ref.at[rows, :], sems.at[10 + n]))
    weights_up, weights_down, *pieces = copies
    xs, cots = pieces[::2], pieces[1::2]
    for copy in (*xs[:4], weights_up, *xs[4:], weights_down, *cots):
        copy.start()

    def units(gate, up, grad):
        sigmoid = 1.0 / (1.0 + jnp.exp(-gate))
        gated = gate * sigmoid
        return (
            (gated * up).astype(BF),
            (grad * up * sigmoid * (1.0 + gate * (1.0 - sigmoid))).astype(BF),
            (grad * gated).astype(BF),
        )

    half = 4 * count
    for part in range(2):
        rows = slice(part * half, (part + 1) * half)
        for copy in xs[4 * part : 4 * part + 4]:
            copy.wait()
        if part == 0:
            weights_up.wait()
        x = x_ref[rows, :]
        gate = mm(x, gate_up_ref[:, :width])
        up = mm(x, gate_up_ref[:, width : 2 * width])
        ends = mm(x, gate_up_ref[:, 2 * width :])
        for copy in cots[4 * part : 4 * part + 4]:
            copy.wait()
        if part == 0:
            weights_down.wait()
        c = c_ref[rows, :]
        value, dgate, dup = units(gate, up, mm(c, down_ref[:, :width]))
        hidden_ref[rows, :width] = value
        both_ref[rows, :width] = dgate
        both_ref[rows, width : 2 * width] = dup
        value, dgate, dup = units(ends[:, :64], ends[:, 64:], mm(c, down_ref[:, width:])[:, :64])
        hidden_ref[rows, width:] = jnp.concatenate([value, jnp.zeros_like(value)], 1)
        both_ref[rows, 2 * width :] = jnp.concatenate([dgate, dup], 1)


def sum_of_products(terms, refs):
    total = None
    for left, (low, high), right, (first, last) in terms:
        part = mm_last(refs[left][:, low:high], refs[right][:, first:last])
        total = part if total is None else total + part
    return total


def rows_grad_kernel(terms, count, gain_row, *refs):
    pieces, gain_ref, outs, sum_ref = refs[count : count + 4], refs[count + 4], refs[count + 5 : -1], refs[-1]
    own_ref, across_ref, cores_ref = outs
    size = own_ref.shape[0]
    outs = [own_ref, cores_ref.at[pl.ds(0, size), :], across_ref, cores_ref.at[pl.ds(size, size), :]]
    step = pl.program_id(0)
    tile = sum_ref.shape[1] // pl.num_programs(0)
    columns = pl.ds(pl.multiple_of(step * tile, tile), tile)
    sum_ref[:, columns] = sum_of_products(terms, refs) * gain_ref[gain_row : gain_row + 1, columns]

    @pl.when(step == pl.num_programs(0) - 1)
    def _():
        for n, ref in enumerate(pieces):
            for at in range(0, ref.shape[0], 32):
                normed, factor = normed_rows(ref[at : at + 32, :])
                scaled = sum_ref[n * ref.shape[0] + at : n * ref.shape[0] + at + 32, :]
                inner = jnp.mean(scaled * normed, -1, keepdims=True)
                outs[n][at : at + 32, :] = (factor * (scaled - normed * inner)).astype(BF)


def rows_out_kernel(terms, places, *refs):
    value = sum_of_products(terms, refs).astype(BF)
    outs = refs[len(refs) - len(places) :]
    size = value.shape[0] // sum(len(held) for held in places)
    for out, held in zip(outs, places):
        for n, piece in enumerate(held):
            out[n * size : (n + 1) * size, :] = value[piece * size : (piece + 1) * size]


def write_parts(outs, turned_of, axis, me, right, base):
    for d, out in enumerate(outs):
        index = (me + d) & 3
        if axis == "z":
            turned = turned_of(pl.multiple_of(index * 512, 512), 512)
        else:
            turned = jnp.concatenate(
                [turned_of(pl.multiple_of(z * 512 + index * 128, 128), 128) for z in range(4)], 0
            )
        out[:, base : base + right.shape[1]] = mm(turned, right).astype(BF)


def parts_kernel(axis, columns, count, me_ref, *refs):
    lefts, right_ref, outs = refs[:count], refs[count], refs[count + 1 :]

    def turned_of(at, size):
        return jnp.concatenate([left[:, pl.ds(at, size)] for left in lefts], 0).T

    write_parts(outs, turned_of, axis, me_ref[0, 0], right_ref[:, columns[0] : columns[1]], 0)


def last_parts_kernel(axis, cut, me_ref, left_ref, dq_ref, own_ref, one_ref, two_ref, three_ref,
                      cos_ref, sin_ref, *outs):
    half = HD // 2
    cos, sin = cos_ref[...], sin_ref[...]
    kv = own_ref[...]
    for ref in (one_ref, two_ref, three_ref):
        kv = kv + ref[...].astype(F32)
    kv = kv.T
    a, b = kv[:half], kv[half:HD]
    kv = jnp.concatenate([a * cos + b * sin, b * cos - a * sin, kv[HD:]], 0).T.astype(BF)
    outs[0][...] = kv
    right = jnp.concatenate([dq_ref[:, cut:], kv], 1)

    def turned_of(at, size):
        return left_ref[:, pl.ds(at, size)].T

    write_parts(outs[1:], turned_of, axis, me_ref[0, 0], right, 0)


def settle_kernel(base_ref, *refs):
    out_ref = refs[-1]
    width = base_ref.shape[1]

    def block(at):
        value = base_ref[:, at : at + 128].astype(F32)
        for ref in refs[:-1]:
            value = value + ref[:, at : at + 128].astype(F32)
        return value

    for n in range(width // 256):
        one, two = block(256 * n), block(256 * n + 128)
        low = jnp.concatenate([one[:, :HD], two[:, :HD]], 1)
        high = jnp.concatenate([one[:, HD:], two[:, HD:]], 1)
        out_ref[:, 128 * n : 128 * n + 128] = low.astype(out_ref.dtype)
        out_ref[:, width // 2 + 128 * n : width // 2 + 128 * n + 128] = high.astype(out_ref.dtype)


def fill_bias(bias_ref, me_ref, pos_ref, span, distances):
    step = 64
    quarter = span // 4
    me = me_ref[0, 0]
    at = lax.broadcasted_iota(jnp.int32, (1, span), 1)
    query = (((at // quarter) ^ me) * quarter) + (at & (quarter - 1))
    first = query - pos_ref[...]

    @pl.loop(0, span // step)
    def _(i):
        block = (i * step) // quarter
        start = (block ^ me) * quarter + i * step - block * quarter
        key = start + lax.broadcasted_iota(jnp.int32, (step, span), 0)
        for n, d in enumerate(distances):
            seen = (key - d * span <= query) & (key - d * span >= first)
            bias_ref[pl.ds(pl.multiple_of(n * span + i * step, step), step), :] = jnp.where(
                seen, 0.0, masked_fill
            ).astype(F32)


def attend_kernel(q_ref, *refs):
    blocks = len(refs) - 7
    kv_refs = refs[:blocks]
    me_ref, pos_ref, mix_ref, lse_ref, bias_ref, s_ref, vt_ref = refs[blocks:]
    span = q_ref.shape[1]
    fill_bias(bias_ref, me_ref, pos_ref, span, range(blocks))
    for d in range(blocks):
        vt_ref[:, d * span : (d + 1) * span] = kv_refs[d][...].T[HD:]

    @pl.loop(0, q_ref.shape[0] // 128)
    def _(pair):
        outs = []
        for sub in range(2):
            q = q_ref[pl.ds(pl.multiple_of(pair * 128 + sub * HD, HD), HD), :]
            top = None
            for d in range(blocks):
                rows = slice(d * span, (d + 1) * span)
                s = mm(kv_refs[d][:, :HD], q) + bias_ref[rows, :]
                s_ref[rows, :] = s
                high = jnp.max(s, 0, keepdims=True)
                top = high if top is None else jnp.maximum(top, high)
            total = jnp.zeros_like(top)
            out = jnp.zeros((HD, span), F32)
            for d in range(blocks):
                rows = slice(d * span, (d + 1) * span)
                p = jnp.exp(s_ref[rows, :] - top)
                total = total + jnp.sum(p, 0, keepdims=True)
                out = out + mm(vt_ref[:, rows], p.astype(BF))
            outs.append(out / total)
            lse_ref[pl.ds(pair * 2 + sub, 1), :] = top + jnp.log(total)
        mix_ref[:, pl.ds(pl.multiple_of(pair * 128, 128), 128)] = (
            jnp.concatenate(outs, 0).T.astype(BF)
        )


def attend_back_kernel(distances, first, last, q_ref, *refs):
    blocks = len(distances)
    refs = list(refs)

    def take(count):
        got, refs[:count] = refs[:count], []
        return got

    kv_refs = take(blocks)
    me_ref, pos_ref, lse_ref = take(3)
    if first:
        mix_ref, wa_ref, wb_ref, *piece_refs = take(7)
    else:
        gt_ref, delta_ref, part_ref = take(3)
    if last:
        cos_ref, sin_ref = take(2)
        (dq_ref,) = take(1)
    else:
        (sum_ref,) = take(1)
    (dkv_ref,) = take(1)
    if first:
        gt_ref, delta_ref = take(2)
    bias_ref, v_ref, kt_ref, dk_ref, dv_ref = take(5)
    span = q_ref.shape[1]
    half = HD // 2
    heads = q_ref.shape[0] // HD
    fill_bias(bias_ref, me_ref, pos_ref, span, distances)
    for n in range(blocks):
        rows = slice(n * span, (n + 1) * span)
        both = kv_refs[n][...].T
        kt_ref[:, rows] = both[:HD]
        v_ref[rows, :] = both[HD:].T
    dk_ref[...] = jnp.zeros_like(dk_ref)
    dv_ref[...] = jnp.zeros_like(dv_ref)
    if first:
        rows_all = jnp.concatenate([ref[...] for ref in piece_refs], 0)
        grads = [mm(rows_all, w_ref[:, : heads * HD // 2]).astype(BF) for w_ref in (wa_ref, wb_ref)]
        for at in range(0, heads * HD, 128):
            where = at % (heads * HD // 2)
            gt = grads[2 * at // (heads * HD)][:, where : where + 128].T
            mt = mix_ref[:, at : at + 128].T
            gt_ref[at : at + 128, :] = gt
            prod = gt.astype(F32) * mt.astype(F32)
            for sub in range(2):
                h = at // HD + sub
                delta_ref[h : h + 1, :] = jnp.sum(prod[sub * HD : (sub + 1) * HD], 0, keepdims=True)

    @pl.loop(0, heads // 2)
    def _(pair):
        outs = []
        for sub in range(2):
            rows_h = pl.ds(pl.multiple_of(pair * 128 + sub * HD, HD), HD)
            q, g = q_ref[rows_h, :], gt_ref[rows_h, :]
            lse = lse_ref[pl.ds(pair * 2 + sub, 1), :]
            delta = delta_ref[pl.ds(pair * 2 + sub, 1), :]
            dq = jnp.zeros((HD, span), F32) if first else part_ref[rows_h, :]
            for n in range(blocks):
                rows = slice(n * span, (n + 1) * span)
                s = mm(kv_refs[n][:, :HD], q) + bias_ref[rows, :]
                p = jnp.exp(s - lse)
                ds = (p * (mm(v_ref[rows, :], g) - delta)).astype(BF)
                dv_ref[rows, :] += mm_last(p.astype(BF), g)
                dk_ref[rows, :] += mm_last(ds, q)
                dq = dq + mm(kt_ref[:, rows], ds)
            if last:
                dq = dq * 0.125
                a, b = dq[:half], dq[half:]
                cos, sin = cos_ref[...], sin_ref[...]
                outs += [a * cos + b * sin, b * cos - a * sin]
            else:
                sum_ref[rows_h, :] = dq
        if last:
            dq_ref[:, pl.ds(pl.multiple_of(pair * 128, 128), 128)] = (
                jnp.concatenate(outs, 0).T.astype(BF)
            )

    for n in range(blocks):
        rows = slice(n * span, (n + 1) * span)
        dkv_ref[rows, :] = jnp.concatenate([dk_ref[rows, :], dv_ref[rows, :]], 1).astype(dkv_ref.dtype)


def weight_grads_kernel(where_ref, *refs):
    cots_ref, one_ref, two_ref, out_ref = refs[8:]
    count = refs[0].shape[0]

    def piece(n):
        return cots_ref[pl.ds(pl.multiple_of(place_of_piece(where_ref, n) * count, count), count), :]

    at = 0
    for lefts, ref in (
        ([left[...] for left in refs[:8]], one_ref), ([piece(n) for n in range(8)], two_ref)
    ):
        turned = jnp.concatenate(lefts, 0).T
        for c in range(0, ref.shape[1], 256):
            size = min(256, ref.shape[1] - c)
            out_ref[:, at + c : at + c + size] = mm(turned, ref[:, c : c + size]).astype(BF)
        at += ref.shape[1]


def params(mib):
    return pltpu.CompilerParams(vmem_limit_bytes=mib * MIB)


def whole(count):
    return [pl.BlockSpec(memory_space=pltpu.VMEM)] * count


def cost(products, moved):
    return pl.CostEstimate(flops=2 * products, bytes_accessed=moved, transcendentals=0)


def call(kernel, name, shapes, operands, scalars=0, products=0, mib=16):
    return pl.pallas_call(
        kernel,
        out_shape=tuple(jax.ShapeDtypeStruct(*shape) for shape in shapes),
        in_specs=[pl.BlockSpec(memory_space=pltpu.SMEM)] * scalars + whole(len(operands) - scalars),
        out_specs=tuple(whole(len(shapes))),
        compiler_params=params(mib),
        cost_estimate=cost(products, 4 << 20),
        name=name,
    )(*operands)


def hidden_units(where, pieces, cots, weights, width):
    count, d = pieces[0].shape
    span = 8 * count
    both, down = 2 * width + 128, width + 128
    return pl.pallas_call(
        functools.partial(hidden_kernel, width),
        out_shape=(jax.ShapeDtypeStruct((span, down), BF), jax.ShapeDtypeStruct((span, both), BF)),
        in_specs=scalar() + [pl.BlockSpec(memory_space=pl.ANY)] * 10,
        out_specs=tuple(whole(2)),
        scratch_shapes=[
            pltpu.VMEM((span, d), BF),
            pltpu.VMEM((span, d), BF),
            pltpu.VMEM((d, both), BF),
            pltpu.VMEM((d, down), BF),
            pltpu.SemaphoreType.DMA((18,)),
        ],
        compiler_params=params(40),
        cost_estimate=cost(3 * span * d * width, 6 * d * width),
        name="hidden_units",
    )(where, *pieces, cots, weights)


def feature_rows(weight, tile):
    if not isinstance(weight, tuple):
        return pl.BlockSpec((tile, weight.shape[1]), lambda i: (i, 0))
    return pl.BlockSpec((pl.Element(tile), pl.Element(weight[2])), lambda i: (i * tile, weight[1]))


def array_of(weight):
    return weight[0] if isinstance(weight, tuple) else weight


def fixed(array):
    return pl.BlockSpec(array.shape, lambda i: (0, 0))


def rows_grad(grads, weights, terms, pieces, gains, gain_row):
    span, d = 4 * pieces[0].shape[0], pieces[0].shape[1]
    tile = 512
    n = len(grads)
    terms = [(g, c, n + w, e) for g, c, w, e in terms]
    return pl.pallas_call(
        functools.partial(rows_grad_kernel, terms, n + len(weights), gain_row),
        grid=(d // tile,),
        out_shape=tuple(jax.ShapeDtypeStruct((span // n, d), BF) for n in (4, 4, 2)),
        in_specs=[fixed(g) for g in grads]
        + [feature_rows(w, tile) for w in weights]
        + [fixed(a) for a in (*pieces, gains)],
        out_specs=tuple(pl.BlockSpec((span // n, d), lambda i: (0, 0)) for n in (4, 4, 2)),
        scratch_shapes=[pltpu.VMEM((span, d), F32)],
        compiler_params=params(32),
        cost_estimate=cost(0, 0),
        name="rows_grad",
    )(*grads, *map(array_of, weights), *pieces, gains)


def rows_out(lefts, weights, terms, tile, places):
    span, d = lefts[0].shape[0], array_of(weights[0]).shape[0]
    n = len(lefts)
    terms = [(g, c, n + w, e) for g, c, w, e in terms]
    size = span // sum(len(held) for held in places)
    return pl.pallas_call(
        functools.partial(rows_out_kernel, terms, places),
        grid=(d // tile,),
        out_shape=tuple(jax.ShapeDtypeStruct((len(held) * size, d), BF) for held in places),
        in_specs=[fixed(g) for g in lefts] + [feature_rows(w, tile) for w in weights],
        out_specs=tuple(pl.BlockSpec((len(held) * size, tile), lambda i: (0, i)) for held in places),
        compiler_params=params(28),
        cost_estimate=cost(sum(span * d * (c[1] - c[0]) for _, c, _, _ in terms), 6 << 20),
        name="rows_out",
    )(*lefts, *map(array_of, weights))


def scalar():
    return [pl.BlockSpec(memory_space=pltpu.SMEM)]


def at_place(axis):
    return place(axis).astype(jnp.int32).reshape(1, 1)


def wide_parts(lefts, right, columns, axis):
    span, d = right.shape[0], lefts[0].shape[1]
    width = columns[1] - columns[0]
    return pl.pallas_call(
        functools.partial(parts_kernel, axis, columns, len(lefts)),
        out_shape=(jax.ShapeDtypeStruct((d // 4, width), BF),) * 4,
        in_specs=scalar() + whole(len(lefts) + 1),
        out_specs=tuple(whole(4)),
        compiler_params=params(20),
        cost_estimate=cost(span * d * width, 8 << 20),
        name="wide_parts",
    )(at_place(axis), *lefts, right)


def last_parts(left, dq, cut, own, arrived, cos, sin, axis):
    span, d = left.shape
    width = dq.shape[1] - cut + 2 * HD
    return pl.pallas_call(
        functools.partial(last_parts_kernel, axis, cut),
        out_shape=(jax.ShapeDtypeStruct((span, 2 * HD), BF),)
        + (jax.ShapeDtypeStruct((d // 4, width), BF),) * 4,
        in_specs=scalar() + whole(8),
        out_specs=tuple(whole(5)),
        compiler_params=params(20),
        cost_estimate=cost(0, 0),
        name="last_parts",
    )(at_place(axis), left, dq, own, *arrived, cos, sin)


def settle(base, parts, kind):
    return pl.pallas_call(
        settle_kernel,
        out_shape=jax.ShapeDtypeStruct(base.shape, kind),
        in_specs=whole(1 + len(parts)),
        out_specs=whole(1)[0],
        compiler_params=params(12),
        cost_estimate=cost(0, 4 << 20),
        name="settle",
    )(base, *parts)


def window_specs():
    return [pl.BlockSpec(memory_space=pltpu.SMEM)] + whole(1)


def attend(q, kvs, window):
    n = len(kvs)
    width, span = q.shape
    heads = width // HD
    return pl.pallas_call(
        attend_kernel,
        out_shape=(
            jax.ShapeDtypeStruct((span, width), BF),
            jax.ShapeDtypeStruct((heads, span), F32),
        ),
        in_specs=whole(n + 1) + window_specs(),
        out_specs=tuple(whole(2)),
        scratch_shapes=[
            pltpu.VMEM((n * span, span), F32),
            pltpu.VMEM((n * span, span), F32),
            pltpu.VMEM((HD, n * span), BF),
        ],
        compiler_params=params(32),
        cost_estimate=cost(span * span * width, 2 << 20),
        name="attend",
    )(q, *kvs, *window)


def attend_back(distances, q, kvs, window, lse, prepared, mixed=None, out=None, turn=None):
    n = len(kvs)
    width, span = q.shape
    heads = width // HD
    first, last = prepared is None, turn is not None
    operands = [q, *kvs, *window, lse]
    operands += [mixed, *out] if first else list(prepared)
    shapes = []
    if last:
        operands += turn
        shapes.append(jax.ShapeDtypeStruct((span, width), BF))
    else:
        shapes.append(jax.ShapeDtypeStruct((width, span), F32))
    shapes.append(jax.ShapeDtypeStruct((n * span, 2 * HD), F32 if last else BF))
    if first:
        shapes.append(jax.ShapeDtypeStruct((width, span), BF))
        shapes.append(jax.ShapeDtypeStruct((heads, span), F32))
    return pl.pallas_call(
        functools.partial(attend_back_kernel, distances, first, last),
        out_shape=tuple(shapes),
        in_specs=whole(n + 1) + window_specs() + whole(len(operands) - n - 3),
        out_specs=tuple(whole(len(shapes))),
        scratch_shapes=[
            pltpu.VMEM((n * span, span), F32),
            pltpu.VMEM((n * span, HD), BF),
            pltpu.VMEM((HD, n * span), BF),
            pltpu.VMEM((n * span, HD), F32),
            pltpu.VMEM((n * span, HD), F32),
        ],
        compiler_params=params(40),
        cost_estimate=cost(30 * 580_000_000 if first else 0, 1 << 20),
        name="attend_back",
    )(*operands)


def weight_grads(where, xs, cots, one, two):
    t, d = xs[0].shape
    tile = 256
    rows = pl.BlockSpec((t, tile), lambda i: (0, i))
    width = one.shape[1] + two.shape[1]
    return pl.pallas_call(
        weight_grads_kernel,
        grid=(d // tile,),
        out_shape=jax.ShapeDtypeStruct((d, width), BF),
        in_specs=scalar() + [rows] * 8 + [pl.BlockSpec((8 * t, tile), lambda i: (0, i)), fixed(one), fixed(two)],
        out_specs=pl.BlockSpec((tile, width), lambda i: (i, 0)),
        compiler_params=params(28),
        cost_estimate=cost(8 * t * d * width, 2 * d * width + 32 * t * d),
        name="weight_grads",
    )(where, *xs, cots, one, two)


def per_device(
    inputs,
    positions,
    attn_gain,
    query_weight,
    key_weight,
    value_weight,
    out_weight,
    mlp_gain,
    gate_weight,
    up_weight,
    down_weight,
    cotangent,
):
    width_q = query_weight.shape[1]
    width_k = key_weight.shape[1]
    hidden_width = gate_weight.shape[1]
    span = positions.shape[0]
    quarter = span // 4
    cut = 3 * width_q // 4
    skip = width_q // 2
    d = inputs.shape[1]
    shard = query_weight.shape[0]
    side = place("yh").astype(jnp.int32).reshape(1, 1)

    units = 128 * (hidden_width // 256)
    both_width, down_width = 2 * units + 128, units + 128
    inputs, cotangent, shard_a, shard_b, shard_mlp = call(
        pack_kernel, "pack",
        [(inputs.shape, BF), (inputs.shape, BF), ((shard, skip + width_q), BF),
         ((shard, skip + 256), BF), ((2, shard, both_width + down_width), BF)],
        [inputs, cotangent, attn_gain[None], mlp_gain[None], query_weight, key_weight, value_weight,
         out_weight.T, gate_weight, up_weight, down_weight.T],
    )
    cotangents = lax.all_gather(cotangent, RING + ("core",), axis=0, tiled=True)
    where = jnp.stack([lax.axis_index("yh") * 2 + lax.axis_index("yl"), lax.axis_index("core")])
    where = where.astype(jnp.int32).reshape(1, 2)
    other_b, other_a = swap(shard_b, "yh"), swap(shard_a, "yh")
    other_mlp = swap(pick(shard_mlp, place("yh", 1), 0), "yh")
    rows_in = gather_rows(inputs)
    pair_b, pair_a = join_sides(shard_b, other_b), join_sides(shard_a, other_a)
    along_b, along_a = send_stage(pair_b, "x"), send_stage(pair_a, "z")
    whole_b = flat(gather_ring(stack_stage(along_b, "x", 0), "z", 0))
    whole_a = flat(gather_ring(after(stack_stage(along_a, "z", 0), rows_in), "x", 1))
    mlp_pair = join_sides(pick(shard_mlp, place("yh"), 0), after(other_mlp, whole_a, whole_b))
    mlp_whole = lax.all_gather(mlp_pair, ("z", "x"), axis=0, tiled=True)

    me = (lax.axis_index("yl") * 2 + lax.axis_index("core")).astype(jnp.int32)
    blocked = jnp.arange(4, dtype=jnp.int32) ^ me
    positions = jnp.take(positions.reshape(4, quarter), blocked, axis=0, mode="clip").reshape(1, span)
    freqs = 10000.0 ** (-(jnp.arange(HD // 2, dtype=F32) * 2.0) / HD)
    angles = freqs[:, None] * positions.astype(F32)
    cos, sin = jnp.cos(angles), jnp.sin(angles)
    window = (me.reshape(1, 1), positions)

    kv_block, scaled_in, gains = call(
        functools.partial(keys_values_kernel, skip), "keys_values",
        [((span, 2 * width_k), BF), ((span, d), BF), ((8, d), F32)],
        [*rows_in, whole_b, cos, sin], products=span * d * 2 * width_k,
    )
    (queries,) = call(
        functools.partial(queries_kernel, skip), "queries",
        [((width_q, span), BF)],
        [scaled_in, after(whole_a, kv_block), cos, sin], products=span * d * width_q,
    )
    blocks = [kv_block] + [shift(kv_block, "x", d) for d in range(1, SEQ_DEVS)]
    mixed, log_total = attend(queries, blocks, window)

    out_a, out_b = (whole_a, 0, skip), (whole_b, 0, skip)
    attn_rows = rows_out(
        [mixed], [out_a, out_b],
        [(0, (0, skip), 0, (0, skip)), (0, (skip, width_q), 1, (0, skip))], 1024, [(0,), (2,), (1, 3)],
    )
    middle, scaled_mid = call(
        middle_kernel, "middle", [(inputs.shape, F32), (inputs.shape, BF)],
        [inputs, *scatter_rows(attn_rows), gains],
    )
    scaled_all = gather_eight(scaled_mid)
    hidden, grad_both = hidden_units(where, scaled_all, cotangents, mlp_whole, units)
    mid_partial = rows_out(
        [grad_both], [(mlp_whole, 0, both_width)], [(0, (0, both_width), 0, (0, both_width))], 512, [(0, 1, 2, 3), (4, 5, 6, 7)]
    )
    mid_own, mid_others = scatter_eight(*mid_partial)
    mid_arrived = send_back(mid_others)
    mlp_sum = weight_grads(
        where, [after(scaled_all[0], mid_others), *scaled_all[1:]], cotangents, grad_both, hidden
    )
    mlp_rows = rows_out(
        [after(hidden, mlp_sum)], [(mlp_whole, both_width, down_width)],
        [(0, (0, down_width), 0, (0, down_width))], 512, [(0, 1, 2, 3), (4, 5, 6, 7)],
    )
    grad_middle, grad_middle_low = call(
        middle_grad_kernel, "middle_grad", [(inputs.shape, F32), (inputs.shape, BF)],
        [cotangent, mid_own, *after(mid_arrived, mlp_rows), middle, gains],
    )
    rows_grad_middle = gather_rows(grad_middle_low)
    mlp_sum = lax.psum_scatter(mlp_sum, ("z", "x"), scatter_dimension=0, tiled=True)

    out_parts = wide_parts(rows_grad_middle, mixed, (0, width_q), "z")
    mlp_cores = swap(after(mlp_rows[1], grad_middle_low), "core")
    mlp_own, mlp_beside, mlp_far = call(
        pair_pieces_kernel, "pair_pieces",
        [(inputs.shape, F32), ((2 * quarter, d), BF), (inputs.shape, BF)],
        [place("yl").astype(jnp.int32).reshape(1, 1), mlp_rows[0], mlp_cores], scalars=1,
    )
    query_part, far_grads, grad_turned, delta = attend_back(
        (1, 2, 3), queries, blocks[1:], window, log_total, None, after(mixed, out_parts, mlp_beside),
        [whole_a, whole_b, *rows_grad_middle],
    )
    mlp_arrived = after(swap(after(mlp_beside, rows_grad_middle), "yl"), query_part)
    mlp_far = (mlp_far.astype(F32) + mlp_arrived[quarter:].astype(F32)).astype(BF)
    arriving = [
        shift(far_grads[(d - 1) * span : d * span], "x", -d) for d in range(1, SEQ_DEVS)
    ]
    out_arrived = [after(shift(out_parts[n], "z", n), query_part) for n in (1, 2, 3)]
    query_raw_grad, own_grads = attend_back(
        (0,), after(queries, mlp_far, out_arrived), blocks[:1], window, log_total, (grad_turned, delta, query_part), turn=[cos, sin]
    )

    out_sum = total(out_parts[0].astype(F32), out_arrived).astype(BF)
    output = settle(
        middle, [mlp_own, mlp_arrived[:quarter], after(swap(mlp_far, "yh"), query_raw_grad)], BF
    )
    a_parts = wide_parts([scaled_in], after(query_raw_grad, arriving), (0, cut), "x")
    a_arrived = [shift(a_parts[n], "x", n) for n in (2, 1, 3)]
    kv_raw_grad, *b_parts = last_parts(
        scaled_in, after(query_raw_grad, a_parts), cut, own_grads, arriving, cos, sin, "z"
    )
    b_arrived = [shift(b_parts[n], "z", n) for n in (2, 1, 3)]
    in_partial = rows_grad(
        [after(query_raw_grad, a_arrived[:2], b_arrived[:2]), kv_raw_grad],
        [whole_a, whole_b],
        [
            (0, (0, width_q), 0, (skip, skip + width_q)),
            (1, (0, 2 * width_k), 1, (skip, skip + 2 * width_k)),
        ],
        rows_in, gains, 0,
    )
    input_grad = settle(grad_middle, scatter_rows(in_partial), F32)

    mlp_send = pick(mlp_sum.reshape(2, shard, -1), place("yh", 1), 0)
    a_sum = wide_sum_next(total(a_parts[0].astype(F32), a_arrived).astype(BF), "z")
    b_sum = total(b_parts[0].astype(F32), b_arrived).astype(BF)
    b_sum = wide_sum_next(jnp.concatenate([b_sum, out_sum], 1), "x", hold=[mlp_send])
    sides = jnp.concatenate([a_sum, b_sum], 1)
    other_sides = swap(pick(sides.reshape(2, shard, -1), place("yh", 1), 0), "yh")
    query_grad, key_grad, value_grad, out_grad = call(
        finish_attn_kernel, "finish_attn",
        [(query_weight.shape, F32), (key_weight.shape, F32), (value_weight.shape, F32),
         (out_weight.shape[::-1], F32)],
        [side, sides, other_sides], scalars=1,
    )
    gate_grad, up_grad, down_grad = call(
        finish_mlp_kernel, "finish_mlp",
        [(gate_weight.shape, F32), (up_weight.shape, F32), (down_weight.shape[::-1], F32)],
        [side, mlp_sum, swap(mlp_send, "yh")], scalars=1,
    )

    ends = width_q - cut
    attn_weights = jnp.concatenate(
        [pair_a[:, skip:], pair_b[:, skip : skip + 2 * width_k]], 1
    ).astype(F32)
    gain_parts = jnp.stack(
        [
            jnp.sum(attn_weights * sides[:, : cut + ends + 2 * width_k].astype(F32), 1),
            jnp.sum(
                mlp_pair[:, :both_width].astype(F32) * mlp_sum[:, :both_width].astype(F32),
                1,
            ),
        ]
    )
    gain_parts = lax.psum(gain_parts, ("yh",) + TP)
    own_gains = pick(gain_parts.reshape(2, 2, shard), place("yh"), 1)
    return (
        output,
        input_grad,
        own_gains[0] / attn_gain.astype(F32),
        query_grad,
        key_grad,
        value_grad,
        out_grad.T,
        own_gains[1] / mlp_gain.astype(F32),
        gate_grad,
        up_grad,
        down_grad.T,
    )


def solution(mesh):
    split = Mesh(mesh.devices.reshape(2, 4, 4, 2, 2), WIDE + TP)
    rows = P(WIDE + TP, None)
    inward = P(WIDE, TP)
    outward = P(TP, WIDE)
    gain = P(WIDE)
    return jax.shard_map(
        per_device,
        mesh=split,
        in_specs=(
            rows, gain, gain, inward, inward, inward, outward, gain, inward, inward, outward, rows,
        ),
        out_specs=(
            rows, rows, gain, inward, inward, inward, outward, gain, inward, inward, outward,
        ),
        check_vma=False,
    )
```

```python
import functools

import jax
import jax.numpy as jnp
from jax import lax
from jax.experimental import pallas as pl
from jax.experimental.pallas import tpu as pltpu
from jax.sharding import Mesh, PartitionSpec as P

HEADS = 32
KV = 4
HD = 64
SEQ_DEVS = 4
WIDE = ("yh", "z", "x")
TP = ("yl", "core")
RING = ("yh", "yl")
BF = jnp.bfloat16
F32 = jnp.float32

epsilon = 1e-05
masked_fill = -1e30
MIB = 1024 * 1024


def after(value, *earlier):
    return lax.optimization_barrier((value, earlier))[0]


def shift(block, axis, distance):
    n = 4 if axis == RING else lax.axis_size(axis)
    return lax.ppermute(block, axis, [(i, (i + distance) % n) for i in range(n)])


def swap(block, axis):
    return shift(block, axis, 1)


def place(axis, step=0):
    n = lax.axis_size(axis)
    return ((lax.axis_index(axis) + (step + n)) & (n - 1)).astype(jnp.uint32)


def pick(array, index, dim):
    return lax.dynamic_index_in_dim(array, index, dim, keepdims=False)


def send_stage(block, axis):
    n = lax.axis_size(axis)
    return [block] + [shift(block, axis, d) for d in (1, n - 1, *range(2, n - 1))]


def stack_stage(arrived, axis, dim):
    n = len(arrived)
    block = arrived[0]
    out = jnp.zeros(block.shape[:dim] + (n,) + block.shape[dim:], block.dtype)
    for d, piece in zip((0, 1, n - 1, *range(2, n - 1)), arrived):
        out = lax.dynamic_update_index_in_dim(out, piece, place(axis, -d), dim)
    return out


def gather_ring(block, axis, dim):
    half = block.shape[0] // 2
    left, right = shift(block, axis, 1), shift(block, axis, -1)
    upper, lower = shift(left[:half], axis, 1), shift(right[half:], axis, -1)
    out = jnp.zeros(block.shape[:dim] + (4,) + block.shape[dim:], block.dtype)
    out = lax.dynamic_update_index_in_dim(out, block, place(axis), dim)
    out = lax.dynamic_update_index_in_dim(out, left, place(axis, -1), dim)
    out = lax.dynamic_update_index_in_dim(out, right, place(axis, 1), dim)
    across = jnp.concatenate([upper, lower], 0)
    return lax.dynamic_update_index_in_dim(out, across, place(axis, 2), dim)


def join_sides(shard, other):
    first = lax.axis_index("yh") == 0
    return jnp.concatenate([jnp.where(first, shard, other), jnp.where(first, other, shard)], 0)


def flat(blocks):
    return blocks.reshape(-1, blocks.shape[-1])


def gather_rows(rows):
    across = swap(rows, "yl")
    return [rows, swap(rows, "core"), across, swap(across, "core")]


def gather_eight(rows):
    near = [rows, shift(rows, RING, 1), shift(rows, RING, 2), shift(rows, RING, -1)]
    return near + [swap(piece, "core") for piece in near]


def scatter_eight(own_core, other_core):
    quarter, d = own_core.shape[0] // 4, own_core.shape[1]
    own, *others = call(
        add_pieces_kernel, "add_pieces",
        [((quarter, d), F32)] + [((quarter, d), BF)] * 3, [own_core, swap(other_core, "core")],
    )
    return own, others


def send_back(others):
    one, two, three = others
    return [shift(one, RING, -1), shift(three, RING, 1), shift(two, RING, 2)]


def scatter_rows(partial):
    own, across, cores = partial
    n = own.shape[0]
    arrived = swap(cores, "core")
    other = (across.astype(F32) + arrived[n:].astype(F32)).astype(BF)
    return [own, arrived[:n], swap(other, "yl")]


def total(first, parts):
    for part in parts:
        first = first + part.astype(F32)
    return first


def exchange_sum(parts, axis, hold=()):
    near = parts[0].astype(F32)
    for d in (1, 3):
        near = near + after(shift(parts[d], axis, d), *hold).astype(F32)
    return near + after(shift(parts[2], axis, 2), *hold).astype(F32)


def wide_sum_next(part, axis, hold=()):
    n = lax.axis_size(axis)
    part = part.reshape(n, part.shape[0] // n, part.shape[1])
    pieces = [pick(part, place(axis, d), 0) for d in range(n)]
    return exchange_sum(pieces, axis, hold).astype(BF)


def mm(left, right):
    return jnp.dot(left, right, preferred_element_type=F32)


def mm_last(left, right):
    return lax.dot_general(left, right, (((1,), (1,)), ((), ())), preferred_element_type=F32)


def normed_rows(piece):
    values = piece.astype(F32)
    factor = lax.rsqrt(jnp.mean(values * values, -1, keepdims=True) + epsilon)
    return values * factor, factor


def scale_rows(piece_refs, gain, scaled_ref):
    for n, ref in enumerate(piece_refs):
        for at in range(0, ref.shape[0], 32):
            normed, _ = normed_rows(ref[at : at + 32, :])
            rows = n * ref.shape[0] + at
            scaled_ref[rows : rows + 32, :] = (normed * gain).astype(BF)


def turned(block, cos, sin):
    a, b = block[: HD // 2], block[HD // 2 :]
    return jnp.concatenate([a * cos - b * sin, b * cos + a * sin], 0)


def keys_values_kernel(skip, *refs):
    piece_refs, (w_ref, cos_ref, sin_ref, kv_ref, scaled_ref, gains_ref) = refs[:4], refs[4:]
    gains_ref[...] = w_ref[:, skip + 128 : skip + 256].T[:8].astype(F32)
    scale_rows(piece_refs, gains_ref[0:1, :], scaled_ref)
    both = mm(scaled_ref[...], w_ref[:, skip : skip + 128]).T
    keys = turned(both[:HD], cos_ref[...], sin_ref[...])
    kv_ref[...] = jnp.concatenate([keys, both[HD:]], 0).T.astype(BF)


def queries_kernel(x_ref, w_ref, cos_ref, sin_ref, q_ref):
    for at in range(0, q_ref.shape[0], 256):
        piece = mm(x_ref[...], w_ref[:, at : at + 256]).T
        for sub in range(0, 256, HD):
            low = turned(piece[sub : sub + HD], cos_ref[...], sin_ref[...]).astype(BF)
            q_ref[at + sub : at + sub + HD, :] = low * 0.125


def to_inner(ref, out_ref):
    half = ref.shape[1] // 2
    for at in range(0, half, 128):
        low, high = ref[:, at : at + 128], ref[:, half + at : half + at + 128]
        out_ref[:, 2 * at : 2 * at + 128] = jnp.concatenate([low[:, :HD], high[:, :HD]], 1)
        out_ref[:, 2 * at + 128 : 2 * at + 256] = jnp.concatenate([low[:, HD:], high[:, HD:]], 1)


def pack_kernel(inputs_ref, cot_ref, again_ref, mgain_ref, q_ref, k_ref, v_ref, g_ref, u_ref, d_ref,
                rows_ref, cots_ref, first_ref, mlp_ref):
    to_inner(inputs_ref, rows_ref)
    to_inner(cot_ref, cots_ref)
    width = q_ref.shape[1]
    first_ref[:, :width] = q_ref[...]
    first_ref[:, width : width + 128] = jnp.concatenate([k_ref[...], v_ref[...]], 1)
    gains = jnp.concatenate(
        [again_ref[...].astype(F32), mgain_ref[...].astype(F32), jnp.zeros((126, HD), F32)], 0
    )
    first_ref[:, width + 128 :] = gains.T.astype(BF)
    width = g_ref.shape[1]
    down = d_ref[...]
    whole_units = 128 * (width // 256)
    tail = 2 * whole_units
    for side in range(2):
        units = slice(side * whole_units, (side + 1) * whole_units)
        ends = slice(tail + 64 * side, tail + 64 * side + 64)
        mlp_ref[side, :, :whole_units] = g_ref[:, units]
        mlp_ref[side, :, whole_units:tail] = u_ref[:, units]
        mlp_ref[side, :, tail : tail + 128] = jnp.concatenate([g_ref[:, ends], u_ref[:, ends]], 1)
        mlp_ref[side, :, tail + 128 : tail + 128 + whole_units] = down[:, units]
        mlp_ref[side, :, tail + 128 + whole_units :] = jnp.concatenate(
            [down[:, ends], jnp.zeros_like(down[:, ends])], 1
        )


def finish_mlp_kernel(side_ref, pair_ref, other_ref, gate_ref, up_ref, down_ref):
    rows = pl.ds(pl.multiple_of(side_ref[0, 0] * HD, HD), HD)
    own, other = pair_ref[rows, :].astype(F32), other_ref[...].astype(F32)
    here = side_ref[0, 0] == 0
    halves = jnp.where(here, own, other), jnp.where(here, other, own)
    units = 128 * (gate_ref.shape[1] // 256)
    tail = 2 * units
    down = []
    for n, half in enumerate(halves):
        gate_ref[:, n * units : (n + 1) * units] = half[:, :units]
        up_ref[:, n * units : (n + 1) * units] = half[:, units:tail]
        down.append(half[:, tail + 128 : tail + 128 + units])
    ends = [half[:, tail : tail + 128] for half in halves]
    gate_ref[:, tail:] = jnp.concatenate([end[:, :64] for end in ends], 1)
    up_ref[:, tail:] = jnp.concatenate([end[:, 64:] for end in ends], 1)
    down += [half[:, tail + 128 + units : tail + 192 + units] for half in halves]
    for n in range(2):
        down_ref[:, n * units : (n + 1) * units] = down[n]
    down_ref[:, tail:] = jnp.concatenate(down[2:], 1)


def finish_attn_kernel(side_ref, pair_ref, other_ref, q_ref, k_ref, v_ref, o_ref):
    rows = pl.ds(pl.multiple_of(side_ref[0, 0] * HD, HD), HD)
    both = pair_ref[rows, :].astype(F32) + other_ref[...].astype(F32)
    width = q_ref.shape[1]
    q_ref[...] = both[:, :width]
    k_ref[...] = both[:, width : width + HD]
    v_ref[...] = both[:, width + HD : width + 2 * HD]
    o_ref[...] = both[:, width + 2 * HD :]


def add_pieces_kernel(one_ref, two_ref, *outs):
    for n, out in enumerate(outs):
        rows = slice(n * out.shape[0], (n + 1) * out.shape[0])
        out[...] = (one_ref[rows, :].astype(F32) + two_ref[rows, :].astype(F32)).astype(out.dtype)


def pair_pieces_kernel(odd_ref, one_ref, two_ref, own_ref, beside_ref, far_ref):
    size = own_ref.shape[0]
    back = 3 - 2 * odd_ref[0, 0]
    for out, at, step in (
        (own_ref, 0, 0), (beside_ref, 0, back), (beside_ref, size, 4 - back), (far_ref, 0, 2)
    ):
        rows = pl.ds(pl.multiple_of(step * size, size), size)
        value = one_ref[rows, :].astype(F32) + two_ref[rows, :].astype(F32)
        out[at : at + size, :] = value.astype(out.dtype)


def middle_kernel(base_ref, *refs):
    parts, (gain_ref, sum_ref, scaled_ref) = refs[:-3], refs[-3:]
    for at in range(0, base_ref.shape[0], 32):
        rows = slice(at, at + 32)
        value = base_ref[rows, :].astype(F32)
        for ref in parts:
            value = value + ref[rows, :].astype(F32)
        sum_ref[rows, :] = value
        normed, _ = normed_rows(value.astype(BF))
        scaled_ref[rows, :] = (normed * gain_ref[1:2, :]).astype(BF)


def middle_grad_kernel(base_ref, *refs):
    parts, (middle_ref, gain_ref, sum_ref, low_ref) = refs[:-4], refs[-4:]
    for at in range(0, base_ref.shape[0], 32):
        rows = slice(at, at + 32)
        value = parts[0][rows, :].astype(F32)
        for ref in parts[1:]:
            value = value + ref[rows, :].astype(F32)
        normed, factor = normed_rows(middle_ref[rows, :].astype(BF))
        value = value * gain_ref[1:2, :]
        inner = jnp.mean(value * normed, -1, keepdims=True)
        value = base_ref[rows, :].astype(F32) + factor * (value - normed * inner)
        sum_ref[rows, :] = value
        low_ref[rows, :] = value.astype(BF)


def hidden_kernel(width, *refs):
    (w_ref, hidden_ref, both_ref, x_ref, c_ref, gate_up_ref, down_ref, sems) = refs[16:]
    first = gate_up_ref.shape[1]
    copies = [
        pltpu.make_async_copy(w_ref.at[:, pl.ds(0, first)], gate_up_ref, sems.at[0]),
        pltpu.make_async_copy(w_ref.at[:, pl.ds(first, down_ref.shape[1])], down_ref, sems.at[1]),
    ]
    count = x_ref.shape[0] // 8
    for n in range(8):
        rows = pl.ds(n * count, count)
        copies.append(pltpu.make_async_copy(refs[n], x_ref.at[rows, :], sems.at[2 + n]))
        copies.append(pltpu.make_async_copy(refs[8 + n], c_ref.at[rows, :], sems.at[10 + n]))
    weights_up, weights_down, *pieces = copies
    xs, cots = pieces[::2], pieces[1::2]
    for copy in (*xs[:4], weights_up, *xs[4:], weights_down, *cots):
        copy.start()

    def units(gate, up, grad):
        sigmoid = 1.0 / (1.0 + jnp.exp(-gate))
        gated = gate * sigmoid
        return (
            (gated * up).astype(BF),
            (grad * up * sigmoid * (1.0 + gate * (1.0 - sigmoid))).astype(BF),
            (grad * gated).astype(BF),
        )

    half = 4 * count
    for part in range(2):
        rows = slice(part * half, (part + 1) * half)
        for copy in xs[4 * part : 4 * part + 4]:
            copy.wait()
        if part == 0:
            weights_up.wait()
        x = x_ref[rows, :]
        gate = mm(x, gate_up_ref[:, :width])
        up = mm(x, gate_up_ref[:, width : 2 * width])
        ends = mm(x, gate_up_ref[:, 2 * width :])
        for copy in cots[4 * part : 4 * part + 4]:
            copy.wait()
        if part == 0:
            weights_down.wait()
        c = c_ref[rows, :]
        value, dgate, dup = units(gate, up, mm(c, down_ref[:, :width]))
        hidden_ref[rows, :width] = value
        both_ref[rows, :width] = dgate
        both_ref[rows, width : 2 * width] = dup
        value, dgate, dup = units(ends[:, :64], ends[:, 64:], mm(c, down_ref[:, width:])[:, :64])
        hidden_ref[rows, width:] = jnp.concatenate([value, jnp.zeros_like(value)], 1)
        both_ref[rows, 2 * width :] = jnp.concatenate([dgate, dup], 1)


def sum_of_products(terms, refs):
    total = None
    for left, (low, high), right, (first, last) in terms:
        part = mm_last(refs[left][:, low:high], refs[right][:, first:last])
        total = part if total is None else total + part
    return total


def rows_grad_kernel(terms, count, gain_row, *refs):
    pieces, gain_ref, outs, sum_ref = refs[count : count + 4], refs[count + 4], refs[count + 5 : -1], refs[-1]
    own_ref, across_ref, cores_ref = outs
    size = own_ref.shape[0]
    outs = [own_ref, cores_ref.at[pl.ds(0, size), :], across_ref, cores_ref.at[pl.ds(size, size), :]]
    step = pl.program_id(0)
    tile = sum_ref.shape[1] // pl.num_programs(0)
    columns = pl.ds(pl.multiple_of(step * tile, tile), tile)
    sum_ref[:, columns] = sum_of_products(terms, refs) * gain_ref[gain_row : gain_row + 1, columns]

    @pl.when(step == pl.num_programs(0) - 1)
    def _():
        for n, ref in enumerate(pieces):
            for at in range(0, ref.shape[0], 32):
                normed, factor = normed_rows(ref[at : at + 32, :])
                scaled = sum_ref[n * ref.shape[0] + at : n * ref.shape[0] + at + 32, :]
                inner = jnp.mean(scaled * normed, -1, keepdims=True)
                outs[n][at : at + 32, :] = (factor * (scaled - normed * inner)).astype(BF)


def rows_out_kernel(terms, places, *refs):
    value = sum_of_products(terms, refs).astype(BF)
    outs = refs[len(refs) - len(places) :]
    size = value.shape[0] // sum(len(held) for held in places)
    for out, held in zip(outs, places):
        for n, piece in enumerate(held):
            out[n * size : (n + 1) * size, :] = value[piece * size : (piece + 1) * size]


def write_parts(outs, turned_of, axis, me, right, base):
    for d, out in enumerate(outs):
        index = (me + d) & 3
        if axis == "z":
            turned = turned_of(pl.multiple_of(index * 512, 512), 512)
        else:
            turned = jnp.concatenate(
                [turned_of(pl.multiple_of(z * 512 + index * 128, 128), 128) for z in range(4)], 0
            )
        out[:, base : base + right.shape[1]] = mm(turned, right).astype(BF)


def parts_kernel(axis, columns, count, me_ref, *refs):
    lefts, right_ref, outs = refs[:count], refs[count], refs[count + 1 :]

    def turned_of(at, size):
        return jnp.concatenate([left[:, pl.ds(at, size)] for left in lefts], 0).T

    write_parts(outs, turned_of, axis, me_ref[0, 0], right_ref[:, columns[0] : columns[1]], 0)


def last_parts_kernel(axis, cut, me_ref, left_ref, dq_ref, own_ref, one_ref, two_ref, three_ref,
                      cos_ref, sin_ref, *outs):
    half = HD // 2
    cos, sin = cos_ref[...], sin_ref[...]
    kv = own_ref[...]
    for ref in (one_ref, two_ref, three_ref):
        kv = kv + ref[...].astype(F32)
    kv = kv.T
    a, b = kv[:half], kv[half:HD]
    kv = jnp.concatenate([a * cos + b * sin, b * cos - a * sin, kv[HD:]], 0).T.astype(BF)
    outs[0][...] = kv
    right = jnp.concatenate([dq_ref[:, cut:], kv], 1)

    def turned_of(at, size):
        return left_ref[:, pl.ds(at, size)].T

    write_parts(outs[1:], turned_of, axis, me_ref[0, 0], right, 0)


def settle_kernel(base_ref, *refs):
    out_ref = refs[-1]
    width = base_ref.shape[1]

    def block(at):
        value = base_ref[:, at : at + 128].astype(F32)
        for ref in refs[:-1]:
            value = value + ref[:, at : at + 128].astype(F32)
        return value

    for n in range(width // 256):
        one, two = block(256 * n), block(256 * n + 128)
        low = jnp.concatenate([one[:, :HD], two[:, :HD]], 1)
        high = jnp.concatenate([one[:, HD:], two[:, HD:]], 1)
        out_ref[:, 128 * n : 128 * n + 128] = low.astype(out_ref.dtype)
        out_ref[:, width // 2 + 128 * n : width // 2 + 128 * n + 128] = high.astype(out_ref.dtype)


def fill_bias(bias_ref, me_ref, pos_ref, span, distances):
    step = 64
    quarter = span // 4
    me = me_ref[0, 0]
    at = lax.broadcasted_iota(jnp.int32, (1, span), 1)
    query = (((at // quarter) ^ me) * quarter) + (at & (quarter - 1))
    first = query - pos_ref[...]

    @pl.loop(0, span // step)
    def _(i):
        block = (i * step) // quarter
        start = (block ^ me) * quarter + i * step - block * quarter
        key = start + lax.broadcasted_iota(jnp.int32, (step, span), 0)
        for n, d in enumerate(distances):
            seen = (key - d * span <= query) & (key - d * span >= first)
            bias_ref[pl.ds(pl.multiple_of(n * span + i * step, step), step), :] = jnp.where(
                seen, 0.0, masked_fill
            ).astype(F32)


def attend_kernel(q_ref, *refs):
    blocks = len(refs) - 7
    kv_refs = refs[:blocks]
    me_ref, pos_ref, mix_ref, lse_ref, bias_ref, s_ref, vt_ref = refs[blocks:]
    span = q_ref.shape[1]
    fill_bias(bias_ref, me_ref, pos_ref, span, range(blocks))
    for d in range(blocks):
        vt_ref[:, d * span : (d + 1) * span] = kv_refs[d][...].T[HD:]

    @pl.loop(0, q_ref.shape[0] // 128)
    def _(pair):
        outs = []
        for sub in range(2):
            q = q_ref[pl.ds(pl.multiple_of(pair * 128 + sub * HD, HD), HD), :]
            top = None
            for d in range(blocks):
                rows = slice(d * span, (d + 1) * span)
                s = mm(kv_refs[d][:, :HD], q) + bias_ref[rows, :]
                s_ref[rows, :] = s
                high = jnp.max(s, 0, keepdims=True)
                top = high if top is None else jnp.maximum(top, high)
            total = jnp.zeros_like(top)
            out = jnp.zeros((HD, span), F32)
            for d in range(blocks):
                rows = slice(d * span, (d + 1) * span)
                p = jnp.exp(s_ref[rows, :] - top)
                total = total + jnp.sum(p, 0, keepdims=True)
                out = out + mm(vt_ref[:, rows], p.astype(BF))
            outs.append(out / total)
            lse_ref[pl.ds(pair * 2 + sub, 1), :] = top + jnp.log(total)
        mix_ref[:, pl.ds(pl.multiple_of(pair * 128, 128), 128)] = (
            jnp.concatenate(outs, 0).T.astype(BF)
        )


def attend_back_kernel(distances, first, last, q_ref, *refs):
    blocks = len(distances)
    refs = list(refs)

    def take(count):
        got, refs[:count] = refs[:count], []
        return got

    kv_refs = take(blocks)
    me_ref, pos_ref, lse_ref = take(3)
    if first:
        mix_ref, w_ref, *piece_refs = take(6)
    else:
        gt_ref, delta_ref, part_ref = take(3)
    if last:
        cos_ref, sin_ref = take(2)
        (dq_ref,) = take(1)
    else:
        (sum_ref,) = take(1)
    (dkv_ref,) = take(1)
    if first:
        gt_ref, delta_ref = take(2)
    bias_ref, v_ref, kt_ref, dk_ref, dv_ref = take(5)
    span = q_ref.shape[1]
    half = HD // 2
    heads = q_ref.shape[0] // HD
    fill_bias(bias_ref, me_ref, pos_ref, span, distances)
    for n in range(blocks):
        rows = slice(n * span, (n + 1) * span)
        both = kv_refs[n][...].T
        kt_ref[:, rows] = both[:HD]
        v_ref[rows, :] = both[HD:].T
    dk_ref[...] = jnp.zeros_like(dk_ref)
    dv_ref[...] = jnp.zeros_like(dv_ref)
    if first:
        rows_all = jnp.concatenate([ref[...] for ref in piece_refs], 0)
        for at in range(0, heads * HD, 256):
            grads = mm(rows_all, w_ref[:, at : at + 256]).astype(BF).T
            gt_ref[at : at + 256, :] = grads
        for at in range(0, heads * HD, 128):
            gt = gt_ref[at : at + 128, :]
            mt = mix_ref[:, at : at + 128].T
            prod = gt.astype(F32) * mt.astype(F32)
            for sub in range(2):
                h = at // HD + sub
                delta_ref[h : h + 1, :] = jnp.sum(prod[sub * HD : (sub + 1) * HD], 0, keepdims=True)

    @pl.loop(0, heads // 2)
    def _(pair):
        outs = []
        for sub in range(2):
            rows_h = pl.ds(pl.multiple_of(pair * 128 + sub * HD, HD), HD)
            q, g = q_ref[rows_h, :], gt_ref[rows_h, :]
            lse = lse_ref[pl.ds(pair * 2 + sub, 1), :]
            delta = delta_ref[pl.ds(pair * 2 + sub, 1), :]
            dq = jnp.zeros((HD, span), F32) if first else part_ref[rows_h, :]
            for n in range(blocks):
                rows = slice(n * span, (n + 1) * span)
                s = mm(kv_refs[n][:, :HD], q) + bias_ref[rows, :]
                p = jnp.exp(s - lse)
                ds = (p * (mm(v_ref[rows, :], g) - delta)).astype(BF)
                dv_ref[rows, :] += mm_last(p.astype(BF), g)
                dk_ref[rows, :] += mm_last(ds, q)
                dq = dq + mm(kt_ref[:, rows], ds)
            if last:
                dq = dq * 0.125
                a, b = dq[:half], dq[half:]
                cos, sin = cos_ref[...], sin_ref[...]
                outs += [a * cos + b * sin, b * cos - a * sin]
            else:
                sum_ref[rows_h, :] = dq
        if last:
            dq_ref[:, pl.ds(pl.multiple_of(pair * 128, 128), 128)] = (
                jnp.concatenate(outs, 0).T.astype(BF)
            )

    for n in range(blocks):
        rows = slice(n * span, (n + 1) * span)
        dkv_ref[rows, :] = jnp.concatenate([dk_ref[rows, :], dv_ref[rows, :]], 1).astype(dkv_ref.dtype)


def weight_grads_kernel(*refs):
    one_ref, two_ref, out_ref = refs[16:]
    at = 0
    for lefts, ref in ((refs[:8], one_ref), (refs[8:16], two_ref)):
        turned = jnp.concatenate([left[...] for left in lefts], 0).T
        for c in range(0, ref.shape[1], 256):
            size = min(256, ref.shape[1] - c)
            out_ref[:, at + c : at + c + size] = mm(turned, ref[:, c : c + size]).astype(BF)
        at += ref.shape[1]


def params(mib):
    return pltpu.CompilerParams(vmem_limit_bytes=mib * MIB)


def whole(count):
    return [pl.BlockSpec(memory_space=pltpu.VMEM)] * count


def cost(products, moved):
    return pl.CostEstimate(flops=2 * products, bytes_accessed=moved, transcendentals=0)


def call(kernel, name, shapes, operands, scalars=0, products=0, mib=16):
    return pl.pallas_call(
        kernel,
        out_shape=tuple(jax.ShapeDtypeStruct(*shape) for shape in shapes),
        in_specs=[pl.BlockSpec(memory_space=pltpu.SMEM)] * scalars + whole(len(operands) - scalars),
        out_specs=tuple(whole(len(shapes))),
        compiler_params=params(mib),
        cost_estimate=cost(products, 4 << 20),
        name=name,
    )(*operands)


def hidden_units(pieces, cots, weights, width):
    count, d = pieces[0].shape
    span = 8 * count
    both, down = 2 * width + 128, width + 128
    return pl.pallas_call(
        functools.partial(hidden_kernel, width),
        out_shape=(jax.ShapeDtypeStruct((span, down), BF), jax.ShapeDtypeStruct((span, both), BF)),
        in_specs=[pl.BlockSpec(memory_space=pl.ANY)] * 17,
        out_specs=tuple(whole(2)),
        scratch_shapes=[
            pltpu.VMEM((span, d), BF),
            pltpu.VMEM((span, d), BF),
            pltpu.VMEM((d, both), BF),
            pltpu.VMEM((d, down), BF),
            pltpu.SemaphoreType.DMA((18,)),
        ],
        compiler_params=params(56),
        cost_estimate=cost(3 * span * d * width, 6 * d * width),
        name="hidden_units",
    )(*pieces, *cots, weights)


def feature_rows(weight, tile):
    if not isinstance(weight, tuple):
        return pl.BlockSpec((tile, weight.shape[1]), lambda i: (i, 0))
    return pl.BlockSpec((pl.Element(tile), pl.Element(weight[2])), lambda i: (i * tile, weight[1]))


def array_of(weight):
    return weight[0] if isinstance(weight, tuple) else weight


def fixed(array):
    return pl.BlockSpec(array.shape, lambda i: (0, 0))


def rows_grad(grads, weights, terms, pieces, gains, gain_row):
    span, d = 4 * pieces[0].shape[0], pieces[0].shape[1]
    tile = 512
    n = len(grads)
    terms = [(g, c, n + w, e) for g, c, w, e in terms]
    return pl.pallas_call(
        functools.partial(rows_grad_kernel, terms, n + len(weights), gain_row),
        grid=(d // tile,),
        out_shape=tuple(jax.ShapeDtypeStruct((span // n, d), BF) for n in (4, 4, 2)),
        in_specs=[fixed(g) for g in grads]
        + [feature_rows(w, tile) for w in weights]
        + [fixed(a) for a in (*pieces, gains)],
        out_specs=tuple(pl.BlockSpec((span // n, d), lambda i: (0, 0)) for n in (4, 4, 2)),
        scratch_shapes=[pltpu.VMEM((span, d), F32)],
        compiler_params=params(32),
        cost_estimate=cost(0, 0),
        name="rows_grad",
    )(*grads, *map(array_of, weights), *pieces, gains)


def rows_out(lefts, weights, terms, tile, places, mib):
    span, d = lefts[0].shape[0], array_of(weights[0]).shape[0]
    n = len(lefts)
    terms = [(g, c, n + w, e) for g, c, w, e in terms]
    size = span // sum(len(held) for held in places)
    return pl.pallas_call(
        functools.partial(rows_out_kernel, terms, places),
        grid=(d // tile,),
        out_shape=tuple(jax.ShapeDtypeStruct((len(held) * size, d), BF) for held in places),
        in_specs=[fixed(g) for g in lefts] + [feature_rows(w, tile) for w in weights],
        out_specs=tuple(pl.BlockSpec((len(held) * size, tile), lambda i: (0, i)) for held in places),
        compiler_params=params(mib),
        cost_estimate=cost(sum(span * d * (c[1] - c[0]) for _, c, _, _ in terms), 6 << 20),
        name="rows_out",
    )(*lefts, *map(array_of, weights))


def scalar():
    return [pl.BlockSpec(memory_space=pltpu.SMEM)]


def at_place(axis):
    return place(axis).astype(jnp.int32).reshape(1, 1)


def wide_parts(lefts, right, columns, axis):
    span, d = right.shape[0], lefts[0].shape[1]
    width = columns[1] - columns[0]
    return pl.pallas_call(
        functools.partial(parts_kernel, axis, columns, len(lefts)),
        out_shape=(jax.ShapeDtypeStruct((d // 4, width), BF),) * 4,
        in_specs=scalar() + whole(len(lefts) + 1),
        out_specs=tuple(whole(4)),
        compiler_params=params(20),
        cost_estimate=cost(span * d * width, 8 << 20),
        name="wide_parts",
    )(at_place(axis), *lefts, right)


def last_parts(left, dq, cut, own, arrived, cos, sin, axis):
    span, d = left.shape
    width = dq.shape[1] - cut + 2 * HD
    return pl.pallas_call(
        functools.partial(last_parts_kernel, axis, cut),
        out_shape=(jax.ShapeDtypeStruct((span, 2 * HD), BF),)
        + (jax.ShapeDtypeStruct((d // 4, width), BF),) * 4,
        in_specs=scalar() + whole(8),
        out_specs=tuple(whole(5)),
        compiler_params=params(20),
        cost_estimate=cost(0, 0),
        name="last_parts",
    )(at_place(axis), left, dq, own, *arrived, cos, sin)


def settle(base, parts, kind):
    return pl.pallas_call(
        settle_kernel,
        out_shape=jax.ShapeDtypeStruct(base.shape, kind),
        in_specs=whole(1 + len(parts)),
        out_specs=whole(1)[0],
        compiler_params=params(12),
        cost_estimate=cost(0, 4 << 20),
        name="settle",
    )(base, *parts)


def window_specs():
    return [pl.BlockSpec(memory_space=pltpu.SMEM)] + whole(1)


def attend(q, kvs, window):
    n = len(kvs)
    width, span = q.shape
    heads = width // HD
    return pl.pallas_call(
        attend_kernel,
        out_shape=(
            jax.ShapeDtypeStruct((span, width), BF),
            jax.ShapeDtypeStruct((heads, span), F32),
        ),
        in_specs=whole(n + 1) + window_specs(),
        out_specs=tuple(whole(2)),
        scratch_shapes=[
            pltpu.VMEM((n * span, span), F32),
            pltpu.VMEM((n * span, span), F32),
            pltpu.VMEM((HD, n * span), BF),
        ],
        compiler_params=params(32),
        cost_estimate=cost(span * span * width, 2 << 20),
        name="attend",
    )(q, *kvs, *window)


def attend_back(distances, q, kvs, window, lse, prepared, mixed=None, out=None, turn=None):
    n = len(kvs)
    width, span = q.shape
    heads = width // HD
    first, last = prepared is None, turn is not None
    operands = [q, *kvs, *window, lse]
    operands += [mixed, *out] if first else list(prepared)
    shapes = []
    if last:
        operands += turn
        shapes.append(jax.ShapeDtypeStruct((span, width), BF))
    else:
        shapes.append(jax.ShapeDtypeStruct((width, span), F32))
    shapes.append(jax.ShapeDtypeStruct((n * span, 2 * HD), F32 if last else BF))
    if first:
        shapes.append(jax.ShapeDtypeStruct((width, span), BF))
        shapes.append(jax.ShapeDtypeStruct((heads, span), F32))
    return pl.pallas_call(
        functools.partial(attend_back_kernel, distances, first, last),
        out_shape=tuple(shapes),
        in_specs=whole(n + 1) + window_specs() + whole(len(operands) - n - 3),
        out_specs=tuple(whole(len(shapes))),
        scratch_shapes=[
            pltpu.VMEM((n * span, span), F32),
            pltpu.VMEM((n * span, HD), BF),
            pltpu.VMEM((HD, n * span), BF),
            pltpu.VMEM((n * span, HD), F32),
            pltpu.VMEM((n * span, HD), F32),
        ],
        compiler_params=params(40),
        cost_estimate=cost(100 * 580_000_000 if first else 0, 1 << 20),
        name="attend_back",
    )(*operands)


def weight_grads(xs, cots, one, two):
    t, d = xs[0].shape
    tile = 256
    rows = pl.BlockSpec((t, tile), lambda i: (0, i))
    width = one.shape[1] + two.shape[1]
    return pl.pallas_call(
        weight_grads_kernel,
        grid=(d // tile,),
        out_shape=jax.ShapeDtypeStruct((d, width), BF),
        in_specs=[rows] * 16 + [fixed(one), fixed(two)],
        out_specs=pl.BlockSpec((tile, width), lambda i: (i, 0)),
        compiler_params=params(56),
        cost_estimate=cost(8 * t * d * width, 2 * d * width + 32 * t * d),
        name="weight_grads",
    )(*xs, *cots, one, two)


def per_device(
    inputs,
    positions,
    attn_gain,
    query_weight,
    key_weight,
    value_weight,
    out_weight,
    mlp_gain,
    gate_weight,
    up_weight,
    down_weight,
    cotangent,
):
    width_q = query_weight.shape[1]
    width_k = key_weight.shape[1]
    hidden_width = gate_weight.shape[1]
    span = positions.shape[0]
    quarter = span // 4
    cut = 3 * width_q // 4
    d = inputs.shape[1]
    shard = query_weight.shape[0]
    side = place("yh").astype(jnp.int32).reshape(1, 1)

    units = 128 * (hidden_width // 256)
    both_width, down_width = 2 * units + 128, units + 128
    inputs, cotangent, shard_first, shard_mlp = call(
        pack_kernel, "pack",
        [(inputs.shape, BF), (inputs.shape, BF), ((shard, width_q + 256), BF),
         ((2, shard, both_width + down_width), BF)],
        [inputs, cotangent, attn_gain[None], mlp_gain[None], query_weight, key_weight, value_weight,
         gate_weight, up_weight, down_weight.T],
        mib=56,
    )
    pair_first = join_sides(shard_first, swap(shard_first, "yh"))
    first_whole = lax.all_gather(pair_first, ("z", "x"), axis=0, tiled=True)

    rows_in = gather_rows(after(inputs, pair_first))
    out_turned = after(out_weight.T, pair_first)
    pair_out = join_sides(out_turned, swap(out_turned, "yh"))
    out_whole = flat(gather_ring(stack_stage(send_stage(pair_out, "x"), "x", 0), "z", 0))
    cotangents = gather_eight(after(cotangent, rows_in[2]))
    other_mlp = swap(after(pick(shard_mlp, place("yh", 1), 0), pair_first), "yh")
    first_whole = after(first_whole, out_whole, cotangents, rows_in, other_mlp)
    mlp_pair = join_sides(pick(shard_mlp, place("yh"), 0), after(other_mlp, first_whole))
    mlp_whole = lax.all_gather(mlp_pair, ("z", "x"), axis=0, tiled=True)

    me = (lax.axis_index("yl") * 2 + lax.axis_index("core")).astype(jnp.int32)
    blocked = jnp.arange(4, dtype=jnp.int32) ^ me
    positions = jnp.take(positions.reshape(4, quarter), blocked, axis=0, mode="clip").reshape(1, span)
    freqs = 10000.0 ** (-(jnp.arange(HD // 2, dtype=F32) * 2.0) / HD)
    angles = freqs[:, None] * positions.astype(F32)
    cos, sin = jnp.cos(angles), jnp.sin(angles)
    window = (me.reshape(1, 1), positions)

    kv_block, scaled_in, gains = call(
        functools.partial(keys_values_kernel, width_q), "keys_values",
        [((span, 2 * width_k), BF), ((span, d), BF), ((8, d), F32)],
        [*rows_in, first_whole, cos, sin], products=span * d * 2 * width_k,
    )
    (queries,) = call(
        queries_kernel, "queries",
        [((width_q, span), BF)],
        [scaled_in, after(first_whole, kv_block), cos, sin], products=span * d * width_q,
    )
    blocks = [kv_block] + [shift(kv_block, "x", d) for d in range(1, SEQ_DEVS)]
    mixed, log_total = attend(queries, blocks, window)

    all_heads = (0, width_q)
    attn_rows = rows_out(
        [mixed], [out_whole], [(0, all_heads, 0, all_heads)], 1024, [(0,), (2,), (1, 3)], 24
    )
    middle, scaled_mid = call(
        middle_kernel, "middle", [(inputs.shape, F32), (inputs.shape, BF)],
        [inputs, *scatter_rows(attn_rows), gains],
    )
    scaled_all = gather_eight(scaled_mid)
    hidden, grad_both = hidden_units(scaled_all, cotangents, mlp_whole, units)
    mid_partial = rows_out(
        [grad_both], [(mlp_whole, 0, both_width)], [(0, (0, both_width), 0, (0, both_width))], 512, [(0, 1, 2, 3), (4, 5, 6, 7)], 56,
    )
    mid_own, mid_others = scatter_eight(*mid_partial)
    mid_arrived = send_back(mid_others)
    mlp_sum = weight_grads(
        [after(scaled_all[0], mid_others), *scaled_all[1:]], cotangents, grad_both, hidden
    )
    mlp_rows = rows_out(
        [after(hidden, mlp_sum)], [(mlp_whole, both_width, down_width)],
        [(0, (0, down_width), 0, (0, down_width))], 512, [(0, 1, 2, 3), (4, 5, 6, 7)], 56,
    )
    grad_middle, grad_middle_low = call(
        middle_grad_kernel, "middle_grad", [(inputs.shape, F32), (inputs.shape, BF)],
        [cotangent, mid_own, *after(mid_arrived, mlp_rows), middle, gains],
    )
    rows_grad_middle = gather_rows(grad_middle_low)
    mlp_sum = lax.psum_scatter(mlp_sum, ("z", "x"), scatter_dimension=0, tiled=True)

    out_parts = wide_parts(rows_grad_middle, mixed, (0, width_q), "z")
    mlp_cores = swap(after(mlp_rows[1], grad_middle_low), "core")
    mlp_own, mlp_beside, mlp_far = call(
        pair_pieces_kernel, "pair_pieces",
        [(inputs.shape, F32), ((2 * quarter, d), BF), (inputs.shape, BF)],
        [place("yl").astype(jnp.int32).reshape(1, 1), mlp_rows[0], mlp_cores], scalars=1,
    )
    query_part, far_grads, grad_turned, delta = attend_back(
        (1, 2, 3), queries, blocks[1:], window, log_total, None, after(mixed, out_parts, mlp_beside),
        [out_whole, *rows_grad_middle],
    )
    mlp_arrived = after(swap(after(mlp_beside, rows_grad_middle), "yl"), query_part)
    mlp_far = (mlp_far.astype(F32) + mlp_arrived[quarter:].astype(F32)).astype(BF)
    arriving = [
        shift(far_grads[(d - 1) * span : d * span], "x", -d) for d in range(1, SEQ_DEVS)
    ]
    out_arrived = [after(shift(out_parts[n], "z", n), query_part) for n in (1, 2, 3)]
    query_raw_grad, own_grads = attend_back(
        (0,), after(queries, mlp_far, out_arrived), blocks[:1], window, log_total, (grad_turned, delta, query_part), turn=[cos, sin]
    )

    out_sum = total(out_parts[0].astype(F32), out_arrived).astype(BF)
    output = settle(
        middle, [mlp_own, mlp_arrived[:quarter], after(swap(mlp_far, "yh"), query_raw_grad)], BF
    )
    a_parts = wide_parts([scaled_in], after(query_raw_grad, arriving), (0, cut), "x")
    a_arrived = [shift(a_parts[n], "x", n) for n in (2, 1, 3)]
    kv_raw_grad, *b_parts = last_parts(
        scaled_in, after(query_raw_grad, a_parts), cut, own_grads, arriving, cos, sin, "z"
    )
    b_arrived = [shift(b_parts[n], "z", n) for n in (2, 1, 3)]
    in_partial = rows_grad(
        [query_raw_grad, kv_raw_grad],
        [first_whole],
        [
            (0, all_heads, 0, all_heads),
            (1, (0, 2 * width_k), 0, (width_q, width_q + 2 * width_k)),
        ],
        rows_in, gains, 0,
    )
    input_grad = settle(grad_middle, scatter_rows(in_partial), F32)

    mlp_send = pick(mlp_sum.reshape(2, shard, -1), place("yh", 1), 0)
    a_sum = wide_sum_next(total(a_parts[0].astype(F32), after(a_arrived, in_partial)).astype(BF), "z")
    b_sum = total(b_parts[0].astype(F32), after(b_arrived, in_partial)).astype(BF)
    b_sum = wide_sum_next(jnp.concatenate([b_sum, out_sum], 1), "x", hold=[mlp_send])
    sides = jnp.concatenate([a_sum, b_sum], 1)
    other_sides = swap(pick(sides.reshape(2, shard, -1), place("yh", 1), 0), "yh")
    query_grad, key_grad, value_grad, out_grad = call(
        finish_attn_kernel, "finish_attn",
        [(query_weight.shape, F32), (key_weight.shape, F32), (value_weight.shape, F32),
         (out_weight.shape[::-1], F32)],
        [side, sides, other_sides], scalars=1,
    )
    gate_grad, up_grad, down_grad = call(
        finish_mlp_kernel, "finish_mlp",
        [(gate_weight.shape, F32), (up_weight.shape, F32), (down_weight.shape[::-1], F32)],
        [side, mlp_sum, swap(mlp_send, "yh")], scalars=1,
    )

    ends = width_q - cut
    attn_weights = pair_first[:, : width_q + 2 * width_k].astype(F32)
    gain_parts = jnp.stack(
        [
            jnp.sum(attn_weights * sides[:, : cut + ends + 2 * width_k].astype(F32), 1),
            jnp.sum(
                mlp_pair[:, :both_width].astype(F32) * mlp_sum[:, :both_width].astype(F32),
                1,
            ),
        ]
    )
    gain_parts = lax.psum(gain_parts, ("yh",) + TP)
    own_gains = pick(gain_parts.reshape(2, 2, shard), place("yh"), 1)
    return (
        output,
        input_grad,
        own_gains[0] / attn_gain.astype(F32),
        query_grad,
        key_grad,
        value_grad,
        out_grad.T,
        own_gains[1] / mlp_gain.astype(F32),
        gate_grad,
        up_grad,
        down_grad.T,
    )


def solution(mesh):
    split = Mesh(mesh.devices.reshape(2, 4, 4, 2, 2), WIDE + TP)
    rows = P(WIDE + TP, None)
    inward = P(WIDE, TP)
    outward = P(TP, WIDE)
    gain = P(WIDE)
    return jax.shard_map(
        per_device,
        mesh=split,
        in_specs=(
            rows, gain, gain, inward, inward, inward, outward, gain, inward, inward, outward, rows,
        ),
        out_specs=(
            rows, rows, gain, inward, inward, inward, outward, gain, inward, inward, outward,
        ),
        check_vma=False,
    )
```

```python
import functools

import jax
import jax.numpy as jnp
from jax import lax
from jax.experimental import pallas as pl
from jax.experimental.pallas import tpu as pltpu
from jax.sharding import Mesh, PartitionSpec as P

HEADS = 32
KV = 4
HD = 64
SEQ_DEVS = 4
WIDE = ("yh", "z", "x")
TP = ("yl", "core")
RING = ("yh", "yl")
BF = jnp.bfloat16
F32 = jnp.float32

epsilon = 1e-05
masked_fill = -1e30
MIB = 1024 * 1024


def after(value, *earlier):
    return lax.optimization_barrier((value, earlier))[0]


def shift(block, axis, distance):
    n = 4 if axis == RING else lax.axis_size(axis)
    return lax.ppermute(block, axis, [(i, (i + distance) % n) for i in range(n)])


def swap(block, axis):
    return shift(block, axis, 1)


def place(axis, step=0):
    n = lax.axis_size(axis)
    return ((lax.axis_index(axis) + (step + n)) & (n - 1)).astype(jnp.uint32)


def pick(array, index, dim):
    return lax.dynamic_index_in_dim(array, index, dim, keepdims=False)


def send_stage(block, axis):
    n = lax.axis_size(axis)
    return [block] + [shift(block, axis, d) for d in (1, n - 1, *range(2, n - 1))]


def stack_stage(arrived, axis, dim):
    n = len(arrived)
    block = arrived[0]
    out = jnp.zeros(block.shape[:dim] + (n,) + block.shape[dim:], block.dtype)
    for d, piece in zip((0, 1, n - 1, *range(2, n - 1)), arrived):
        out = lax.dynamic_update_index_in_dim(out, piece, place(axis, -d), dim)
    return out


def send_ring(block, axis):
    half = block.shape[0] // 2
    left, right = shift(block, axis, 1), shift(block, axis, -1)
    return [block, left, right, shift(left[:half], axis, 1), shift(right[half:], axis, -1)]


def stack_ring(arrived, axis, dim):
    block, left, right, upper, lower = arrived
    return stack_stage([block, left, right, jnp.concatenate([upper, lower], 0)], axis, dim)


def join_sides(shard, other):
    first = lax.axis_index("yh") == 0
    return jnp.concatenate([jnp.where(first, shard, other), jnp.where(first, other, shard)], 0)


def flat(blocks):
    return blocks.reshape(-1, blocks.shape[-1])


def gather_rows(rows):
    across = swap(rows, "yl")
    return [rows, swap(rows, "core"), across, swap(across, "core")]


def gather_eight(rows):
    near = [rows, shift(rows, RING, 1), shift(rows, RING, 2), shift(rows, RING, -1)]
    return near + [swap(piece, "core") for piece in near]


def scatter_eight(own_core, other_core):
    quarter, d = own_core.shape[0] // 4, own_core.shape[1]
    own, *others = call(
        add_pieces_kernel, "add_pieces",
        [((quarter, d), F32)] + [((quarter, d), BF)] * 3, [own_core, swap(other_core, "core")],
    )
    return own, others


def send_back(others):
    one, two, three = others
    return [shift(one, RING, -1), shift(three, RING, 1), shift(two, RING, 2)]


def scatter_rows(partial):
    own, across, cores = partial
    n = own.shape[0]
    arrived = swap(cores, "core")
    other = (across.astype(F32) + arrived[n:].astype(F32)).astype(BF)
    return [own, arrived[:n], swap(other, "yl")]


def total(first, parts):
    for part in parts:
        first = first + part.astype(F32)
    return first


def exchange_sum(parts, axis, hold=()):
    near = parts[0].astype(F32)
    for d in (1, 3):
        near = near + after(shift(parts[d], axis, d), *hold).astype(F32)
    return near + after(shift(parts[2], axis, 2), *hold).astype(F32)


def wide_sum_next(part, axis, hold=()):
    n = lax.axis_size(axis)
    part = part.reshape(n, part.shape[0] // n, part.shape[1])
    pieces = [pick(part, place(axis, d), 0) for d in range(n)]
    return exchange_sum(pieces, axis, hold).astype(BF)


def mm(left, right):
    return jnp.dot(left, right, preferred_element_type=F32)


def mm_last(left, right):
    return lax.dot_general(left, right, (((1,), (1,)), ((), ())), preferred_element_type=F32)


def normed_rows(piece):
    values = piece.astype(F32)
    factor = lax.rsqrt(jnp.mean(values * values, -1, keepdims=True) + epsilon)
    return values * factor, factor


def scale_rows(piece_refs, gain, scaled_ref):
    for n, ref in enumerate(piece_refs):
        for at in range(0, ref.shape[0], 32):
            normed, _ = normed_rows(ref[at : at + 32, :])
            rows = n * ref.shape[0] + at
            scaled_ref[rows : rows + 32, :] = (normed * gain).astype(BF)


def turned(block, cos, sin):
    a, b = block[: HD // 2], block[HD // 2 :]
    return jnp.concatenate([a * cos - b * sin, b * cos + a * sin], 0)


def keys_values_kernel(*refs):
    piece_refs, (w_ref, cos_ref, sin_ref, kv_ref, scaled_ref, gains_ref) = refs[:4], refs[4:]
    gains_ref[...] = w_ref[:, 128:].T[:8].astype(F32)
    scale_rows(piece_refs, gains_ref[0:1, :], scaled_ref)
    both = mm(scaled_ref[...], w_ref[:, :128]).T
    keys = turned(both[:HD], cos_ref[...], sin_ref[...])
    kv_ref[...] = jnp.concatenate([keys, both[HD:]], 0).T.astype(BF)


def queries_kernel(x_ref, w_ref, cos_ref, sin_ref, q_ref):
    for at in range(0, q_ref.shape[0], 256):
        piece = mm(x_ref[...], w_ref[:, at : at + 256]).T
        for sub in range(0, 256, HD):
            low = turned(piece[sub : sub + HD], cos_ref[...], sin_ref[...]).astype(BF)
            q_ref[at + sub : at + sub + HD, :] = low * 0.125


def to_inner(ref, out_ref):
    half = ref.shape[1] // 2
    for at in range(0, half, 128):
        low, high = ref[:, at : at + 128], ref[:, half + at : half + at + 128]
        out_ref[:, 2 * at : 2 * at + 128] = jnp.concatenate([low[:, :HD], high[:, :HD]], 1)
        out_ref[:, 2 * at + 128 : 2 * at + 256] = jnp.concatenate([low[:, HD:], high[:, HD:]], 1)


def pack_kernel(inputs_ref, cot_ref, again_ref, mgain_ref, k_ref, v_ref, g_ref, u_ref, d_ref,
                rows_ref, cots_ref, kv_ref, mlp_ref):
    to_inner(inputs_ref, rows_ref)
    to_inner(cot_ref, cots_ref)
    kv_ref[:, :128] = jnp.concatenate([k_ref[...], v_ref[...]], 1)
    gains = jnp.concatenate(
        [again_ref[...].astype(F32), mgain_ref[...].astype(F32), jnp.zeros((126, HD), F32)], 0
    )
    kv_ref[:, 128:] = gains.T.astype(BF)
    width = g_ref.shape[1]
    down = d_ref[...]
    whole_units = 128 * (width // 256)
    tail = 2 * whole_units
    for side in range(2):
        units = slice(side * whole_units, (side + 1) * whole_units)
        ends = slice(tail + 64 * side, tail + 64 * side + 64)
        mlp_ref[side, :, :whole_units] = g_ref[:, units]
        mlp_ref[side, :, whole_units:tail] = u_ref[:, units]
        mlp_ref[side, :, tail : tail + 128] = jnp.concatenate([g_ref[:, ends], u_ref[:, ends]], 1)
        mlp_ref[side, :, tail + 128 : tail + 128 + whole_units] = down[:, units]
        mlp_ref[side, :, tail + 128 + whole_units :] = jnp.concatenate(
            [down[:, ends], jnp.zeros_like(down[:, ends])], 1
        )


def finish_mlp_kernel(side_ref, pair_ref, other_ref, gate_ref, up_ref, down_ref):
    rows = pl.ds(pl.multiple_of(side_ref[0, 0] * HD, HD), HD)
    own, other = pair_ref[rows, :].astype(F32), other_ref[...].astype(F32)
    here = side_ref[0, 0] == 0
    halves = jnp.where(here, own, other), jnp.where(here, other, own)
    units = 128 * (gate_ref.shape[1] // 256)
    tail = 2 * units
    down = []
    for n, half in enumerate(halves):
        gate_ref[:, n * units : (n + 1) * units] = half[:, :units]
        up_ref[:, n * units : (n + 1) * units] = half[:, units:tail]
        down.append(half[:, tail + 128 : tail + 128 + units])
    ends = [half[:, tail : tail + 128] for half in halves]
    gate_ref[:, tail:] = jnp.concatenate([end[:, :64] for end in ends], 1)
    up_ref[:, tail:] = jnp.concatenate([end[:, 64:] for end in ends], 1)
    down += [half[:, tail + 128 + units : tail + 192 + units] for half in halves]
    for n in range(2):
        down_ref[:, n * units : (n + 1) * units] = down[n]
    down_ref[:, tail:] = jnp.concatenate(down[2:], 1)


def finish_attn_kernel(side_ref, pair_ref, other_ref, q_ref, k_ref, v_ref, o_ref):
    rows = pl.ds(pl.multiple_of(side_ref[0, 0] * HD, HD), HD)
    both = pair_ref[rows, :].astype(F32) + other_ref[...].astype(F32)
    width = q_ref.shape[1]
    q_ref[...] = both[:, :width]
    k_ref[...] = both[:, width : width + HD]
    v_ref[...] = both[:, width + HD : width + 2 * HD]
    o_ref[...] = both[:, width + 2 * HD :]


def add_pieces_kernel(one_ref, two_ref, *outs):
    for n, out in enumerate(outs):
        rows = slice(n * out.shape[0], (n + 1) * out.shape[0])
        out[...] = (one_ref[rows, :].astype(F32) + two_ref[rows, :].astype(F32)).astype(out.dtype)


def pair_pieces_kernel(odd_ref, one_ref, two_ref, own_ref, beside_ref, far_ref):
    size = own_ref.shape[0]
    back = 3 - 2 * odd_ref[0, 0]
    for out, at, step in (
        (own_ref, 0, 0), (beside_ref, 0, back), (beside_ref, size, 4 - back), (far_ref, 0, 2)
    ):
        rows = pl.ds(pl.multiple_of(step * size, size), size)
        value = one_ref[rows, :].astype(F32) + two_ref[rows, :].astype(F32)
        out[at : at + size, :] = value.astype(out.dtype)


def middle_kernel(base_ref, *refs):
    parts, (gain_ref, sum_ref, scaled_ref) = refs[:-3], refs[-3:]
    for at in range(0, base_ref.shape[0], 32):
        rows = slice(at, at + 32)
        value = base_ref[rows, :].astype(F32)
        for ref in parts:
            value = value + ref[rows, :].astype(F32)
        sum_ref[rows, :] = value
        normed, _ = normed_rows(value.astype(BF))
        scaled_ref[rows, :] = (normed * gain_ref[1:2, :]).astype(BF)


def middle_grad_kernel(base_ref, *refs):
    parts, (middle_ref, gain_ref, sum_ref, low_ref) = refs[:-4], refs[-4:]
    for at in range(0, base_ref.shape[0], 32):
        rows = slice(at, at + 32)
        value = parts[0][rows, :].astype(F32)
        for ref in parts[1:]:
            value = value + ref[rows, :].astype(F32)
        normed, factor = normed_rows(middle_ref[rows, :].astype(BF))
        value = value * gain_ref[1:2, :]
        inner = jnp.mean(value * normed, -1, keepdims=True)
        value = base_ref[rows, :].astype(F32) + factor * (value - normed * inner)
        sum_ref[rows, :] = value
        low_ref[rows, :] = value.astype(BF)


def cotangent_at(odd_ref, n):
    return (0, 3 - 2 * odd_ref[0, 0], 2, 1 + 2 * odd_ref[0, 0])[n % 4]


def hidden_kernel(width, odd_ref, *refs):
    (w_ref, hidden_ref, both_ref, x_ref, c_ref, gate_up_ref, down_ref, sems) = refs[10:]
    first = gate_up_ref.shape[1]
    copies = [
        pltpu.make_async_copy(w_ref.at[:, pl.ds(0, first)], gate_up_ref, sems.at[0]),
        pltpu.make_async_copy(w_ref.at[:, pl.ds(first, down_ref.shape[1])], down_ref, sems.at[1]),
    ]
    count = x_ref.shape[0] // 8
    for n in range(8):
        rows = pl.ds(n * count, count)
        copies.append(pltpu.make_async_copy(refs[n], x_ref.at[rows, :], sems.at[2 + n]))
        at = pl.ds(pl.multiple_of(cotangent_at(odd_ref, n) * count, count), count)
        copies.append(
            pltpu.make_async_copy(refs[8 + n // 4].at[at, :], c_ref.at[rows, :], sems.at[10 + n])
        )
    weights_up, weights_down, *pieces = copies
    xs, cots = pieces[::2], pieces[1::2]
    for copy in (*xs[:4], weights_up, *xs[4:], weights_down, *cots):
        copy.start()

    def units(gate, up, grad):
        sigmoid = 1.0 / (1.0 + jnp.exp(-gate))
        gated = gate * sigmoid
        return (
            (gated * up).astype(BF),
            (grad * up * sigmoid * (1.0 + gate * (1.0 - sigmoid))).astype(BF),
            (grad * gated).astype(BF),
        )

    half = 4 * count
    for part in range(2):
        rows = slice(part * half, (part + 1) * half)
        for copy in xs[4 * part : 4 * part + 4]:
            copy.wait()
        if part == 0:
            weights_up.wait()
        x = x_ref[rows, :]
        gate = mm(x, gate_up_ref[:, :width])
        up = mm(x, gate_up_ref[:, width : 2 * width])
        ends = mm(x, gate_up_ref[:, 2 * width :])
        for copy in cots[4 * part : 4 * part + 4]:
            copy.wait()
        if part == 0:
            weights_down.wait()
        c = c_ref[rows, :]
        value, dgate, dup = units(gate, up, mm(c, down_ref[:, :width]))
        hidden_ref[rows, :width] = value
        both_ref[rows, :width] = dgate
        both_ref[rows, width : 2 * width] = dup
        value, dgate, dup = units(ends[:, :64], ends[:, 64:], mm(c, down_ref[:, width:])[:, :64])
        hidden_ref[rows, width:] = jnp.concatenate([value, jnp.zeros_like(value)], 1)
        both_ref[rows, 2 * width :] = jnp.concatenate([dgate, dup], 1)


def sum_of_products(terms, refs):
    total = None
    for left, (low, high), right, (first, last) in terms:
        part = mm_last(refs[left][:, low:high], refs[right][:, first:last])
        total = part if total is None else total + part
    return total


def rows_grad_kernel(terms, count, gain_row, *refs):
    pieces, gain_ref, outs, sum_ref = refs[count : count + 4], refs[count + 4], refs[count + 5 : -1], refs[-1]
    own_ref, across_ref, cores_ref = outs
    size = own_ref.shape[0]
    outs = [own_ref, cores_ref.at[pl.ds(0, size), :], across_ref, cores_ref.at[pl.ds(size, size), :]]
    step = pl.program_id(0)
    tile = sum_ref.shape[1] // pl.num_programs(0)
    columns = pl.ds(pl.multiple_of(step * tile, tile), tile)
    sum_ref[:, columns] = sum_of_products(terms, refs) * gain_ref[gain_row : gain_row + 1, columns]

    @pl.when(step == pl.num_programs(0) - 1)
    def _():
        for n, ref in enumerate(pieces):
            for at in range(0, ref.shape[0], 32):
                normed, factor = normed_rows(ref[at : at + 32, :])
                scaled = sum_ref[n * ref.shape[0] + at : n * ref.shape[0] + at + 32, :]
                inner = jnp.mean(scaled * normed, -1, keepdims=True)
                outs[n][at : at + 32, :] = (factor * (scaled - normed * inner)).astype(BF)


def rows_out_kernel(terms, places, *refs):
    value = sum_of_products(terms, refs).astype(BF)
    outs = refs[len(refs) - len(places) :]
    size = value.shape[0] // sum(len(held) for held in places)
    for out, held in zip(outs, places):
        for n, piece in enumerate(held):
            out[n * size : (n + 1) * size, :] = value[piece * size : (piece + 1) * size]


def write_parts(outs, turned_of, axis, me, right, base):
    for d, out in enumerate(outs):
        index = (me + d) & 3
        if axis == "z":
            turned = turned_of(pl.multiple_of(index * 512, 512), 512)
        else:
            turned = jnp.concatenate(
                [turned_of(pl.multiple_of(z * 512 + index * 128, 128), 128) for z in range(4)], 0
            )
        out[:, base : base + right.shape[1]] = mm(turned, right).astype(BF)


def parts_kernel(axis, columns, count, me_ref, *refs):
    lefts, right_ref, outs = refs[:count], refs[count], refs[count + 1 :]

    def turned_of(at, size):
        return jnp.concatenate([left[:, pl.ds(at, size)] for left in lefts], 0).T

    write_parts(outs, turned_of, axis, me_ref[0, 0], right_ref[:, columns[0] : columns[1]], 0)


def last_parts_kernel(axis, cut, me_ref, left_ref, dq_ref, own_ref, one_ref, two_ref, three_ref,
                      cos_ref, sin_ref, *outs):
    half = HD // 2
    cos, sin = cos_ref[...], sin_ref[...]
    kv = own_ref[...]
    for ref in (one_ref, two_ref, three_ref):
        kv = kv + ref[...].astype(F32)
    kv = kv.T
    a, b = kv[:half], kv[half:HD]
    kv = jnp.concatenate([a * cos + b * sin, b * cos - a * sin, kv[HD:]], 0).T.astype(BF)
    outs[0][...] = kv
    right = jnp.concatenate([dq_ref[:, cut:], kv], 1)

    def turned_of(at, size):
        return left_ref[:, pl.ds(at, size)].T

    write_parts(outs[1:], turned_of, axis, me_ref[0, 0], right, 0)


def settle_kernel(base_ref, *refs):
    out_ref = refs[-1]
    width = base_ref.shape[1]

    def block(at):
        value = base_ref[:, at : at + 128].astype(F32)
        for ref in refs[:-1]:
            value = value + ref[:, at : at + 128].astype(F32)
        return value

    for n in range(width // 256):
        one, two = block(256 * n), block(256 * n + 128)
        low = jnp.concatenate([one[:, :HD], two[:, :HD]], 1)
        high = jnp.concatenate([one[:, HD:], two[:, HD:]], 1)
        out_ref[:, 128 * n : 128 * n + 128] = low.astype(out_ref.dtype)
        out_ref[:, width // 2 + 128 * n : width // 2 + 128 * n + 128] = high.astype(out_ref.dtype)


def fill_bias(bias_ref, me_ref, pos_ref, span, distances):
    step = 64
    quarter = span // 4
    me = me_ref[0, 0]
    at = lax.broadcasted_iota(jnp.int32, (1, span), 1)
    query = (((at // quarter) ^ me) * quarter) + (at & (quarter - 1))
    first = query - pos_ref[...]

    @pl.loop(0, span // step)
    def _(i):
        block = (i * step) // quarter
        start = (block ^ me) * quarter + i * step - block * quarter
        key = start + lax.broadcasted_iota(jnp.int32, (step, span), 0)
        for n, d in enumerate(distances):
            seen = (key - d * span <= query) & (key - d * span >= first)
            bias_ref[pl.ds(pl.multiple_of(n * span + i * step, step), step), :] = jnp.where(
                seen, 0.0, masked_fill
            ).astype(F32)


def attend_kernel(q_ref, *refs):
    blocks = len(refs) - 7
    kv_refs = refs[:blocks]
    me_ref, pos_ref, mix_ref, lse_ref, bias_ref, s_ref, vt_ref = refs[blocks:]
    span = q_ref.shape[1]
    fill_bias(bias_ref, me_ref, pos_ref, span, range(blocks))
    for d in range(blocks):
        vt_ref[:, d * span : (d + 1) * span] = kv_refs[d][...].T[HD:]

    @pl.loop(0, q_ref.shape[0] // 128)
    def _(pair):
        outs = []
        for sub in range(2):
            q = q_ref[pl.ds(pl.multiple_of(pair * 128 + sub * HD, HD), HD), :]
            top = None
            for d in range(blocks):
                rows = slice(d * span, (d + 1) * span)
                s = mm(kv_refs[d][:, :HD], q) + bias_ref[rows, :]
                s_ref[rows, :] = s
                high = jnp.max(s, 0, keepdims=True)
                top = high if top is None else jnp.maximum(top, high)
            total = jnp.zeros_like(top)
            out = jnp.zeros((HD, span), F32)
            for d in range(blocks):
                rows = slice(d * span, (d + 1) * span)
                p = jnp.exp(s_ref[rows, :] - top)
                total = total + jnp.sum(p, 0, keepdims=True)
                out = out + mm(vt_ref[:, rows], p.astype(BF))
            outs.append(out / total)
            lse_ref[pl.ds(pair * 2 + sub, 1), :] = top + jnp.log(total)
        mix_ref[:, pl.ds(pl.multiple_of(pair * 128, 128), 128)] = (
            jnp.concatenate(outs, 0).T.astype(BF)
        )


def attend_back_kernel(distances, first, last, q_ref, *refs):
    blocks = len(distances)
    refs = list(refs)

    def take(count):
        got, refs[:count] = refs[:count], []
        return got

    kv_refs = take(blocks)
    me_ref, pos_ref, lse_ref = take(3)
    if first:
        mix_ref, w_ref, *piece_refs = take(6)
    else:
        gt_ref, delta_ref, part_ref = take(3)
    if last:
        cos_ref, sin_ref = take(2)
        (dq_ref,) = take(1)
    else:
        (sum_ref,) = take(1)
    (dkv_ref,) = take(1)
    if first:
        gt_ref, delta_ref = take(2)
    bias_ref, v_ref, kt_ref, dk_ref, dv_ref = take(5)
    span = q_ref.shape[1]
    half = HD // 2
    heads = q_ref.shape[0] // HD
    fill_bias(bias_ref, me_ref, pos_ref, span, distances)
    for n in range(blocks):
        rows = slice(n * span, (n + 1) * span)
        both = kv_refs[n][...].T
        kt_ref[:, rows] = both[:HD]
        v_ref[rows, :] = both[HD:].T
    dk_ref[...] = jnp.zeros_like(dk_ref)
    dv_ref[...] = jnp.zeros_like(dv_ref)
    if first:
        rows_all = jnp.concatenate([ref[...] for ref in piece_refs], 0)
        for at in range(0, heads * HD, 256):
            grads = mm(rows_all, w_ref[:, at : at + 256]).astype(BF).T
            gt_ref[at : at + 256, :] = grads
        for at in range(0, heads * HD, 128):
            gt = gt_ref[at : at + 128, :]
            mt = mix_ref[:, at : at + 128].T
            prod = gt.astype(F32) * mt.astype(F32)
            for sub in range(2):
                h = at // HD + sub
                delta_ref[h : h + 1, :] = jnp.sum(prod[sub * HD : (sub + 1) * HD], 0, keepdims=True)

    @pl.loop(0, heads // 2)
    def _(pair):
        outs = []
        for sub in range(2):
            rows_h = pl.ds(pl.multiple_of(pair * 128 + sub * HD, HD), HD)
            q, g = q_ref[rows_h, :], gt_ref[rows_h, :]
            lse = lse_ref[pl.ds(pair * 2 + sub, 1), :]
            delta = delta_ref[pl.ds(pair * 2 + sub, 1), :]
            dq = jnp.zeros((HD, span), F32) if first else part_ref[rows_h, :]
            for n in range(blocks):
                rows = slice(n * span, (n + 1) * span)
                s = mm(kv_refs[n][:, :HD], q) + bias_ref[rows, :]
                p = jnp.exp(s - lse)
                ds = (p * (mm(v_ref[rows, :], g) - delta)).astype(BF)
                dv_ref[rows, :] += mm_last(p.astype(BF), g)
                dk_ref[rows, :] += mm_last(ds, q)
                dq = dq + mm(kt_ref[:, rows], ds)
            if last:
                dq = dq * 0.125
                a, b = dq[:half], dq[half:]
                cos, sin = cos_ref[...], sin_ref[...]
                outs += [a * cos + b * sin, b * cos - a * sin]
            else:
                sum_ref[rows_h, :] = dq
        if last:
            dq_ref[:, pl.ds(pl.multiple_of(pair * 128, 128), 128)] = (
                jnp.concatenate(outs, 0).T.astype(BF)
            )

    for n in range(blocks):
        rows = slice(n * span, (n + 1) * span)
        dkv_ref[rows, :] = jnp.concatenate([dk_ref[rows, :], dv_ref[rows, :]], 1).astype(dkv_ref.dtype)


def weight_grads_kernel(odd_ref, *refs):
    one_ref, two_ref, out_ref = refs[10:]
    count = refs[0].shape[0]

    def cotangent(n):
        at = pl.multiple_of(cotangent_at(odd_ref, n) * count, count)
        return refs[8 + n // 4][pl.ds(at, count), :]

    at = 0
    for lefts, ref in (
        ([left[...] for left in refs[:8]], one_ref), ([cotangent(n) for n in range(8)], two_ref)
    ):
        turned = jnp.concatenate(lefts, 0).T
        for c in range(0, ref.shape[1], 256):
            size = min(256, ref.shape[1] - c)
            out_ref[:, at + c : at + c + size] = mm(turned, ref[:, c : c + size]).astype(BF)
        at += ref.shape[1]


def params(mib):
    return pltpu.CompilerParams(vmem_limit_bytes=mib * MIB)


def whole(count):
    return [pl.BlockSpec(memory_space=pltpu.VMEM)] * count


def cost(products, moved):
    return pl.CostEstimate(flops=2 * products, bytes_accessed=moved, transcendentals=0)


def call(kernel, name, shapes, operands, scalars=0, products=0, mib=16):
    return pl.pallas_call(
        kernel,
        out_shape=tuple(jax.ShapeDtypeStruct(*shape) for shape in shapes),
        in_specs=[pl.BlockSpec(memory_space=pltpu.SMEM)] * scalars + whole(len(operands) - scalars),
        out_specs=tuple(whole(len(shapes))),
        compiler_params=params(mib),
        cost_estimate=cost(products, 4 << 20),
        name=name,
    )(*operands)


def hidden_units(odd, pieces, cots, weights, width):
    count, d = pieces[0].shape
    span = 8 * count
    both, down = 2 * width + 128, width + 128
    return pl.pallas_call(
        functools.partial(hidden_kernel, width),
        out_shape=(jax.ShapeDtypeStruct((span, down), BF), jax.ShapeDtypeStruct((span, both), BF)),
        in_specs=scalar() + [pl.BlockSpec(memory_space=pl.ANY)] * 11,
        out_specs=tuple(whole(2)),
        scratch_shapes=[
            pltpu.VMEM((span, d), BF),
            pltpu.VMEM((span, d), BF),
            pltpu.VMEM((d, both), BF),
            pltpu.VMEM((d, down), BF),
            pltpu.SemaphoreType.DMA((18,)),
        ],
        compiler_params=params(56),
        cost_estimate=cost(3 * span * d * width, 6 * d * width),
        name="hidden_units",
    )(odd, *pieces, *cots, weights)


def feature_rows(weight, tile):
    if not isinstance(weight, tuple):
        return pl.BlockSpec((tile, weight.shape[1]), lambda i: (i, 0))
    return pl.BlockSpec((pl.Element(tile), pl.Element(weight[2])), lambda i: (i * tile, weight[1]))


def array_of(weight):
    return weight[0] if isinstance(weight, tuple) else weight


def fixed(array):
    return pl.BlockSpec(array.shape, lambda i: (0, 0))


def rows_grad(grads, weights, terms, pieces, gains, gain_row):
    span, d = 4 * pieces[0].shape[0], pieces[0].shape[1]
    tile = 512
    n = len(grads)
    terms = [(g, c, n + w, e) for g, c, w, e in terms]
    return pl.pallas_call(
        functools.partial(rows_grad_kernel, terms, n + len(weights), gain_row),
        grid=(d // tile,),
        out_shape=tuple(jax.ShapeDtypeStruct((span // n, d), BF) for n in (4, 4, 2)),
        in_specs=[fixed(g) for g in grads]
        + [feature_rows(w, tile) for w in weights]
        + [fixed(a) for a in (*pieces, gains)],
        out_specs=tuple(pl.BlockSpec((span // n, d), lambda i: (0, 0)) for n in (4, 4, 2)),
        scratch_shapes=[pltpu.VMEM((span, d), F32)],
        compiler_params=params(32),
        cost_estimate=cost(0, 0),
        name="rows_grad",
    )(*grads, *map(array_of, weights), *pieces, gains)


def rows_out(lefts, weights, terms, tile, places, mib):
    span, d = lefts[0].shape[0], array_of(weights[0]).shape[0]
    n = len(lefts)
    terms = [(g, c, n + w, e) for g, c, w, e in terms]
    size = span // sum(len(held) for held in places)
    return pl.pallas_call(
        functools.partial(rows_out_kernel, terms, places),
        grid=(d // tile,),
        out_shape=tuple(jax.ShapeDtypeStruct((len(held) * size, d), BF) for held in places),
        in_specs=[fixed(g) for g in lefts] + [feature_rows(w, tile) for w in weights],
        out_specs=tuple(pl.BlockSpec((len(held) * size, tile), lambda i: (0, i)) for held in places),
        compiler_params=params(mib),
        cost_estimate=cost(sum(span * d * (c[1] - c[0]) for _, c, _, _ in terms), 6 << 20),
        name="rows_out",
    )(*lefts, *map(array_of, weights))


def scalar():
    return [pl.BlockSpec(memory_space=pltpu.SMEM)]


def at_place(axis):
    return place(axis).astype(jnp.int32).reshape(1, 1)


def wide_parts(lefts, right, columns, axis):
    span, d = right.shape[0], lefts[0].shape[1]
    width = columns[1] - columns[0]
    return pl.pallas_call(
        functools.partial(parts_kernel, axis, columns, len(lefts)),
        out_shape=(jax.ShapeDtypeStruct((d // 4, width), BF),) * 4,
        in_specs=scalar() + whole(len(lefts) + 1),
        out_specs=tuple(whole(4)),
        compiler_params=params(20),
        cost_estimate=cost(span * d * width, 8 << 20),
        name="wide_parts",
    )(at_place(axis), *lefts, right)


def last_parts(left, dq, cut, own, arrived, cos, sin, axis):
    span, d = left.shape
    width = dq.shape[1] - cut + 2 * HD
    return pl.pallas_call(
        functools.partial(last_parts_kernel, axis, cut),
        out_shape=(jax.ShapeDtypeStruct((span, 2 * HD), BF),)
        + (jax.ShapeDtypeStruct((d // 4, width), BF),) * 4,
        in_specs=scalar() + whole(8),
        out_specs=tuple(whole(5)),
        compiler_params=params(20),
        cost_estimate=cost(0, 0),
        name="last_parts",
    )(at_place(axis), left, dq, own, *arrived, cos, sin)


def settle(base, parts, kind):
    return pl.pallas_call(
        settle_kernel,
        out_shape=jax.ShapeDtypeStruct(base.shape, kind),
        in_specs=whole(1 + len(parts)),
        out_specs=whole(1)[0],
        compiler_params=params(12),
        cost_estimate=cost(0, 4 << 20),
        name="settle",
    )(base, *parts)


def window_specs():
    return [pl.BlockSpec(memory_space=pltpu.SMEM)] + whole(1)


def attend(q, kvs, window):
    n = len(kvs)
    width, span = q.shape
    heads = width // HD
    return pl.pallas_call(
        attend_kernel,
        out_shape=(
            jax.ShapeDtypeStruct((span, width), BF),
            jax.ShapeDtypeStruct((heads, span), F32),
        ),
        in_specs=whole(n + 1) + window_specs(),
        out_specs=tuple(whole(2)),
        scratch_shapes=[
            pltpu.VMEM((n * span, span), F32),
            pltpu.VMEM((n * span, span), F32),
            pltpu.VMEM((HD, n * span), BF),
        ],
        compiler_params=params(32),
        cost_estimate=cost(30 * 580_000_000, 2 << 20),
        name="attend",
    )(q, *kvs, *window)


def attend_back(distances, q, kvs, window, lse, prepared, mixed=None, out=None, turn=None):
    n = len(kvs)
    width, span = q.shape
    heads = width // HD
    first, last = prepared is None, turn is not None
    operands = [q, *kvs, *window, lse]
    operands += [mixed, *out] if first else list(prepared)
    shapes = []
    if last:
        operands += turn
        shapes.append(jax.ShapeDtypeStruct((span, width), BF))
    else:
        shapes.append(jax.ShapeDtypeStruct((width, span), F32))
    shapes.append(jax.ShapeDtypeStruct((n * span, 2 * HD), F32 if last else BF))
    if first:
        shapes.append(jax.ShapeDtypeStruct((width, span), BF))
        shapes.append(jax.ShapeDtypeStruct((heads, span), F32))
    return pl.pallas_call(
        functools.partial(attend_back_kernel, distances, first, last),
        out_shape=tuple(shapes),
        in_specs=whole(n + 1) + window_specs() + whole(len(operands) - n - 3),
        out_specs=tuple(whole(len(shapes))),
        scratch_shapes=[
            pltpu.VMEM((n * span, span), F32),
            pltpu.VMEM((n * span, HD), BF),
            pltpu.VMEM((HD, n * span), BF),
            pltpu.VMEM((n * span, HD), F32),
            pltpu.VMEM((n * span, HD), F32),
        ],
        compiler_params=params(40),
        cost_estimate=cost(1000 * 580_000_000 if first else 0, 1 << 20),
        name="attend_back",
    )(*operands)


def weight_grads(odd, xs, cots, one, two):
    t, d = xs[0].shape
    tile = 256
    rows = pl.BlockSpec((t, tile), lambda i: (0, i))
    width = one.shape[1] + two.shape[1]
    return pl.pallas_call(
        weight_grads_kernel,
        grid=(d // tile,),
        out_shape=jax.ShapeDtypeStruct((d, width), BF),
        in_specs=scalar()
        + [rows] * 8
        + [pl.BlockSpec((4 * t, tile), lambda i: (0, i))] * 2
        + [fixed(one), fixed(two)],
        out_specs=pl.BlockSpec((tile, width), lambda i: (i, 0)),
        compiler_params=params(56),
        cost_estimate=cost(8 * t * d * width, 2 * d * width + 32 * t * d),
        name="weight_grads",
    )(odd, *xs, *cots, one, two)


def per_device(
    inputs,
    positions,
    attn_gain,
    query_weight,
    key_weight,
    value_weight,
    out_weight,
    mlp_gain,
    gate_weight,
    up_weight,
    down_weight,
    cotangent,
):
    width_q = query_weight.shape[1]
    width_k = key_weight.shape[1]
    hidden_width = gate_weight.shape[1]
    span = positions.shape[0]
    quarter = span // 4
    cut = 3 * width_q // 4
    d = inputs.shape[1]
    shard = query_weight.shape[0]
    side = place("yh").astype(jnp.int32).reshape(1, 1)

    units = 128 * (hidden_width // 256)
    both_width, down_width = 2 * units + 128, units + 128
    inputs, cotangent, shard_kv, shard_mlp = call(
        pack_kernel, "pack",
        [(inputs.shape, BF), (inputs.shape, BF), ((shard, 256), BF),
         ((2, shard, both_width + down_width), BF)],
        [inputs, cotangent, attn_gain[None], mlp_gain[None], key_weight, value_weight,
         gate_weight, up_weight, down_weight.T],
        mib=56,
    )
    other_kv, other_q = swap(shard_kv, "yh"), swap(query_weight, "yh")
    pair_kv, pair_q = join_sides(shard_kv, other_kv), join_sides(query_weight, after(other_q, shard_kv))
    q_whole = lax.all_gather(pair_q, ("z", "x"), axis=0, tiled=True)
    along_kv = send_stage(pair_kv, "x")
    rows_in = gather_rows(after(inputs, other_kv))
    across_kv = send_stage(stack_stage(along_kv, "x", 0), "z")
    kv_whole = flat(stack_stage(across_kv, "z", 0))
    out_turned = after(out_weight.T, other_kv)
    pair_out = join_sides(out_turned, swap(out_turned, "yh"))
    part_out = stack_stage(send_stage(after(pair_out, across_kv[1]), "x"), "x", 0)
    cot_yl = swap(after(cotangent, rows_in[2]), "yl")
    other_mlp = swap(after(pick(shard_mlp, place("yh", 1), 0), along_kv[1]), "yh")
    kv_whole = after(kv_whole, cot_yl, other_mlp)

    me = (lax.axis_index("yl") * 2 + lax.axis_index("core")).astype(jnp.int32)
    blocked = jnp.arange(4, dtype=jnp.int32) ^ me
    positions = jnp.take(positions.reshape(4, quarter), blocked, axis=0, mode="clip").reshape(1, span)
    freqs = 10000.0 ** (-(jnp.arange(HD // 2, dtype=F32) * 2.0) / HD)
    angles = freqs[:, None] * positions.astype(F32)
    cos, sin = jnp.cos(angles), jnp.sin(angles)
    window = (me.reshape(1, 1), positions)

    kv_block, scaled_in, gains = call(
        keys_values_kernel, "keys_values",
        [((span, 2 * width_k), BF), ((span, d), BF), ((8, d), F32)],
        [*rows_in, kv_whole, cos, sin], products=span * d * 2 * width_k,
    )
    (queries,) = call(
        queries_kernel, "queries",
        [((width_q, span), BF)],
        [scaled_in, after(q_whole, kv_block), cos, sin], products=span * d * width_q,
    )
    blocks = [kv_block] + [shift(kv_block, "x", d) for d in range(1, SEQ_DEVS)]
    along_out = send_ring(after(part_out, kv_block), "z")
    cot_near = after(jnp.concatenate([cotangent, cot_yl], 0), kv_block)
    cotangents = jnp.concatenate([cot_near, swap(cot_near, "yh")], 0)
    cotangents = [cotangents, swap(cotangents, "core")]
    mlp_pair = join_sides(pick(shard_mlp, place("yh"), 0), after(other_mlp, q_whole, blocks[1:], along_out[:3]))
    mlp_whole = lax.all_gather(mlp_pair, ("z", "x"), axis=0, tiled=True)
    odd = place("yl").astype(jnp.int32).reshape(1, 1)
    mixed, log_total = attend(queries, blocks, window)

    out_whole = flat(stack_ring(along_out[:3] + after(along_out[3:], log_total), "z", 0))
    all_heads = (0, width_q)
    attn_rows = rows_out(
        [after(mixed, cotangents[0])], [out_whole], [(0, all_heads, 0, all_heads)], 1024, [(0,), (2,), (1, 3)], 24
    )
    middle, scaled_mid = call(
        middle_kernel, "middle", [(inputs.shape, F32), (inputs.shape, BF)],
        [inputs, *scatter_rows(attn_rows), gains],
    )
    scaled_all = gather_eight(scaled_mid)
    hidden, grad_both = hidden_units(odd, scaled_all, cotangents, mlp_whole, units)
    mid_partial = rows_out(
        [grad_both], [(mlp_whole, 0, both_width)], [(0, (0, both_width), 0, (0, both_width))], 512, [(0, 1, 2, 3), (4, 5, 6, 7)], 56,
    )
    mid_own, mid_others = scatter_eight(*mid_partial)
    mid_arrived = send_back(mid_others)
    mlp_sum = weight_grads(
        odd, [after(scaled_all[0], mid_others), *scaled_all[1:]], cotangents, grad_both, hidden
    )
    mlp_rows = rows_out(
        [after(hidden, mlp_sum)], [(mlp_whole, both_width, down_width)],
        [(0, (0, down_width), 0, (0, down_width))], 512, [(0, 1, 2, 3), (4, 5, 6, 7)], 56,
    )
    grad_middle, grad_middle_low = call(
        middle_grad_kernel, "middle_grad", [(inputs.shape, F32), (inputs.shape, BF)],
        [cotangent, mid_own, *after(mid_arrived, mlp_rows), middle, gains],
    )
    rows_grad_middle = gather_rows(grad_middle_low)
    mlp_sum = lax.psum_scatter(mlp_sum, ("z", "x"), scatter_dimension=0, tiled=True)

    out_parts = wide_parts(rows_grad_middle, mixed, (0, width_q), "z")
    mlp_cores = swap(after(mlp_rows[1], grad_middle_low), "core")
    mlp_own, mlp_beside, mlp_far = call(
        pair_pieces_kernel, "pair_pieces",
        [(inputs.shape, F32), ((2 * quarter, d), BF), (inputs.shape, BF)],
        [odd, mlp_rows[0], mlp_cores], scalars=1,
    )
    query_part, far_grads, grad_turned, delta = attend_back(
        (1, 2, 3), queries, blocks[1:], window, log_total, None, after(mixed, out_parts, mlp_beside),
        [out_whole, *rows_grad_middle],
    )
    mlp_arrived = after(swap(after(mlp_beside, rows_grad_middle), "yl"), query_part)
    mlp_far = (mlp_far.astype(F32) + mlp_arrived[quarter:].astype(F32)).astype(BF)
    arriving = [
        shift(far_grads[(d - 1) * span : d * span], "x", -d) for d in range(1, SEQ_DEVS)
    ]
    out_arrived = [after(shift(out_parts[n], "z", n), query_part) for n in (1, 2, 3)]
    query_raw_grad, own_grads = attend_back(
        (0,), after(queries, mlp_far, out_arrived), blocks[:1], window, log_total, (grad_turned, delta, query_part), turn=[cos, sin]
    )

    out_sum = total(out_parts[0].astype(F32), out_arrived).astype(BF)
    output = settle(
        middle, [mlp_own, mlp_arrived[:quarter], after(swap(mlp_far, "yh"), query_raw_grad)], BF
    )
    a_parts = wide_parts([scaled_in], after(query_raw_grad, arriving), (0, cut), "x")
    a_arrived = [shift(a_parts[n], "x", n) for n in (2, 1, 3)]
    kv_raw_grad, *b_parts = last_parts(
        scaled_in, after(query_raw_grad, a_parts), cut, own_grads, arriving, cos, sin, "z"
    )
    b_arrived = [shift(b_parts[n], "z", n) for n in (2, 1, 3)]
    in_partial = rows_grad(
        [after(query_raw_grad, a_arrived, b_arrived), kv_raw_grad],
        [q_whole, kv_whole],
        [(0, all_heads, 0, all_heads), (1, (0, 2 * width_k), 1, (0, 2 * width_k))],
        rows_in, gains, 0,
    )
    input_grad = settle(grad_middle, scatter_rows(in_partial), F32)

    mlp_send = pick(mlp_sum.reshape(2, shard, -1), place("yh", 1), 0)
    a_sum = wide_sum_next(total(a_parts[0].astype(F32), a_arrived).astype(BF), "z")
    b_sum = total(b_parts[0].astype(F32), b_arrived).astype(BF)
    b_sum = wide_sum_next(jnp.concatenate([b_sum, out_sum], 1), "x", hold=[mlp_send])
    sides = jnp.concatenate([a_sum, b_sum], 1)
    other_sides = swap(pick(sides.reshape(2, shard, -1), place("yh", 1), 0), "yh")
    query_grad, key_grad, value_grad, out_grad = call(
        finish_attn_kernel, "finish_attn",
        [(query_weight.shape, F32), (key_weight.shape, F32), (value_weight.shape, F32),
         (out_weight.shape[::-1], F32)],
        [side, sides, other_sides], scalars=1,
    )
    gate_grad, up_grad, down_grad = call(
        finish_mlp_kernel, "finish_mlp",
        [(gate_weight.shape, F32), (up_weight.shape, F32), (down_weight.shape[::-1], F32)],
        [side, mlp_sum, swap(mlp_send, "yh")], scalars=1,
    )

    ends = width_q - cut
    attn_weights = jnp.concatenate([pair_q, pair_kv[:, : 2 * width_k]], 1).astype(F32)
    gain_parts = jnp.stack(
        [
            jnp.sum(attn_weights * sides[:, : cut + ends + 2 * width_k].astype(F32), 1),
            jnp.sum(
                mlp_pair[:, :both_width].astype(F32) * mlp_sum[:, :both_width].astype(F32),
                1,
            ),
        ]
    )
    gain_parts = lax.psum(gain_parts, ("yh",) + TP)
    own_gains = pick(gain_parts.reshape(2, 2, shard), place("yh"), 1)
    return (
        output,
        input_grad,
        own_gains[0] / attn_gain.astype(F32),
        query_grad,
        key_grad,
        value_grad,
        out_grad.T,
        own_gains[1] / mlp_gain.astype(F32),
        gate_grad,
        up_grad,
        down_grad.T,
    )


def solution(mesh):
    split = Mesh(mesh.devices.reshape(2, 4, 4, 2, 2), WIDE + TP)
    rows = P(WIDE + TP, None)
    inward = P(WIDE, TP)
    outward = P(TP, WIDE)
    gain = P(WIDE)
    return jax.shard_map(
        per_device,
        mesh=split,
        in_specs=(
            rows, gain, gain, inward, inward, inward, outward, gain, inward, inward, outward, rows,
        ),
        out_specs=(
            rows, rows, gain, inward, inward, inward, outward, gain, inward, inward, outward,
        ),
        check_vma=False,
    )
```

```python
import functools

import jax
import jax.numpy as jnp
from jax import lax
from jax.experimental import pallas as pl
from jax.experimental.pallas import tpu as pltpu
from jax.sharding import Mesh, PartitionSpec as P

HEADS = 32
KV = 4
HD = 64
SEQ_DEVS = 4
WIDE = ("yh", "z", "x")
TP = ("yl", "core")
RING = ("yh", "yl")
BF = jnp.bfloat16
F32 = jnp.float32

epsilon = 1e-05
masked_fill = -1e30
MIB = 1024 * 1024


def after(value, *earlier):
    return lax.optimization_barrier((value, earlier))[0]


def shift(block, axis, distance):
    n = 4 if axis == RING else lax.axis_size(axis)
    return lax.ppermute(block, axis, [(i, (i + distance) % n) for i in range(n)])


def swap(block, axis):
    return shift(block, axis, 1)


def place(axis, step=0):
    n = lax.axis_size(axis)
    return ((lax.axis_index(axis) + (step + n)) & (n - 1)).astype(jnp.uint32)


def pick(array, index, dim):
    return lax.dynamic_index_in_dim(array, index, dim, keepdims=False)


def send_stage(block, axis):
    n = lax.axis_size(axis)
    return [block] + [shift(block, axis, d) for d in (1, n - 1, *range(2, n - 1))]


def stack_stage(arrived, axis, dim):
    n = len(arrived)
    block = arrived[0]
    out = jnp.zeros(block.shape[:dim] + (n,) + block.shape[dim:], block.dtype)
    for d, piece in zip((0, 1, n - 1, *range(2, n - 1)), arrived):
        out = lax.dynamic_update_index_in_dim(out, piece, place(axis, -d), dim)
    return out


def join_sides(shard, other):
    first = lax.axis_index("yh") == 0
    return jnp.concatenate([jnp.where(first, shard, other), jnp.where(first, other, shard)], 0)


def flat(blocks):
    return blocks.reshape(-1, blocks.shape[-1])


def gather_rows(rows):
    across = swap(rows, "yl")
    return [rows, swap(rows, "core"), across, swap(across, "core")]


def gather_eight(rows):
    near = [rows, shift(rows, RING, 1), shift(rows, RING, 2), shift(rows, RING, -1)]
    return near + [swap(piece, "core") for piece in near]


def scatter_eight(own_core, other_core):
    quarter, d = own_core.shape[0] // 4, own_core.shape[1]
    own, *others = call(
        add_pieces_kernel, "add_pieces",
        [((quarter, d), F32)] + [((quarter, d), BF)] * 3, [own_core, swap(other_core, "core")],
    )
    return own, others


def send_back(others):
    one, two, three = others
    return [shift(one, RING, -1), shift(three, RING, 1), shift(two, RING, 2)]


def scatter_rows(partial):
    own, across, cores = partial
    n = own.shape[0]
    arrived = swap(cores, "core")
    other = (across.astype(F32) + arrived[n:].astype(F32)).astype(BF)
    return [own, arrived[:n], swap(other, "yl")]


def total(first, parts):
    for part in parts:
        first = first + part.astype(F32)
    return first


def exchange_sum(parts, axis, hold=()):
    near = parts[0].astype(F32)
    for d in (1, 3):
        near = near + after(shift(parts[d], axis, d), *hold).astype(F32)
    return near + after(shift(parts[2], axis, 2), *hold).astype(F32)


def wide_sum_next(part, axis, hold=()):
    n = lax.axis_size(axis)
    part = part.reshape(n, part.shape[0] // n, part.shape[1])
    pieces = [pick(part, place(axis, d), 0) for d in range(n)]
    return exchange_sum(pieces, axis, hold).astype(BF)


def mm(left, right):
    return jnp.dot(left, right, preferred_element_type=F32)


def mm_last(left, right):
    return lax.dot_general(left, right, (((1,), (1,)), ((), ())), preferred_element_type=F32)


def normed_rows(piece):
    values = piece.astype(F32)
    factor = lax.rsqrt(jnp.mean(values * values, -1, keepdims=True) + epsilon)
    return values * factor, factor


def scale_rows(piece_refs, gain, scaled_ref):
    for n, ref in enumerate(piece_refs):
        for at in range(0, ref.shape[0], 32):
            normed, _ = normed_rows(ref[at : at + 32, :])
            rows = n * ref.shape[0] + at
            scaled_ref[rows : rows + 32, :] = (normed * gain).astype(BF)


def turned(block, cos, sin):
    a, b = block[: HD // 2], block[HD // 2 :]
    return jnp.concatenate([a * cos - b * sin, b * cos + a * sin], 0)


def keys_values_kernel(*refs):
    piece_refs, (w_ref, cos_ref, sin_ref, kv_ref, scaled_ref, gains_ref) = refs[:4], refs[4:]
    gains_ref[...] = w_ref[:, 128:].T[:8].astype(F32)
    scale_rows(piece_refs, gains_ref[0:1, :], scaled_ref)
    both = mm(scaled_ref[...], w_ref[:, :128]).T
    keys = turned(both[:HD], cos_ref[...], sin_ref[...])
    kv_ref[...] = jnp.concatenate([keys, both[HD:]], 0).T.astype(BF)


def queries_kernel(x_ref, w_ref, cos_ref, sin_ref, q_ref):
    for at in range(0, q_ref.shape[0], 256):
        piece = mm(x_ref[...], w_ref[:, at : at + 256]).T
        for sub in range(0, 256, HD):
            low = turned(piece[sub : sub + HD], cos_ref[...], sin_ref[...]).astype(BF)
            q_ref[at + sub : at + sub + HD, :] = low * 0.125


def to_inner(ref, out_ref):
    half = ref.shape[1] // 2
    for at in range(0, half, 128):
        low, high = ref[:, at : at + 128], ref[:, half + at : half + at + 128]
        out_ref[:, 2 * at : 2 * at + 128] = jnp.concatenate([low[:, :HD], high[:, :HD]], 1)
        out_ref[:, 2 * at + 128 : 2 * at + 256] = jnp.concatenate([low[:, HD:], high[:, HD:]], 1)


def pack_kernel(inputs_ref, cot_ref, again_ref, mgain_ref, k_ref, v_ref, g_ref, u_ref, d_ref,
                rows_ref, cots_ref, kv_ref, mlp_ref):
    to_inner(inputs_ref, rows_ref)
    to_inner(cot_ref, cots_ref)
    kv_ref[:, :128] = jnp.concatenate([k_ref[...], v_ref[...]], 1)
    gains = jnp.concatenate(
        [again_ref[...].astype(F32), mgain_ref[...].astype(F32), jnp.zeros((126, HD), F32)], 0
    )
    kv_ref[:, 128:] = gains.T.astype(BF)
    width = g_ref.shape[1]
    down = d_ref[...]
    whole_units = 128 * (width // 256)
    tail = 2 * whole_units
    for side in range(2):
        units = slice(side * whole_units, (side + 1) * whole_units)
        ends = slice(tail + 64 * side, tail + 64 * side + 64)
        mlp_ref[side, :, :whole_units] = g_ref[:, units]
        mlp_ref[side, :, whole_units:tail] = u_ref[:, units]
        mlp_ref[side, :, tail : tail + 128] = jnp.concatenate([g_ref[:, ends], u_ref[:, ends]], 1)
        mlp_ref[side, :, tail + 128 : tail + 128 + whole_units] = down[:, units]
        mlp_ref[side, :, tail + 128 + whole_units :] = jnp.concatenate(
            [down[:, ends], jnp.zeros_like(down[:, ends])], 1
        )


def finish_mlp_kernel(side_ref, pair_ref, other_ref, gate_ref, up_ref, down_ref):
    rows = pl.ds(pl.multiple_of(side_ref[0, 0] * HD, HD), HD)
    own, other = pair_ref[rows, :].astype(F32), other_ref[...].astype(F32)
    here = side_ref[0, 0] == 0
    halves = jnp.where(here, own, other), jnp.where(here, other, own)
    units = 128 * (gate_ref.shape[1] // 256)
    tail = 2 * units
    down = []
    for n, half in enumerate(halves):
        gate_ref[:, n * units : (n + 1) * units] = half[:, :units]
        up_ref[:, n * units : (n + 1) * units] = half[:, units:tail]
        down.append(half[:, tail + 128 : tail + 128 + units])
    ends = [half[:, tail : tail + 128] for half in halves]
    gate_ref[:, tail:] = jnp.concatenate([end[:, :64] for end in ends], 1)
    up_ref[:, tail:] = jnp.concatenate([end[:, 64:] for end in ends], 1)
    down += [half[:, tail + 128 + units : tail + 192 + units] for half in halves]
    for n in range(2):
        down_ref[:, n * units : (n + 1) * units] = down[n]
    down_ref[:, tail:] = jnp.concatenate(down[2:], 1)


def finish_attn_kernel(side_ref, pair_ref, other_ref, q_ref, k_ref, v_ref, o_ref):
    rows = pl.ds(pl.multiple_of(side_ref[0, 0] * HD, HD), HD)
    both = pair_ref[rows, :].astype(F32) + other_ref[...].astype(F32)
    width = q_ref.shape[1]
    q_ref[...] = both[:, :width]
    k_ref[...] = both[:, width : width + HD]
    v_ref[...] = both[:, width + HD : width + 2 * HD]
    o_ref[...] = both[:, width + 2 * HD :]


def add_pieces_kernel(one_ref, two_ref, *outs):
    for n, out in enumerate(outs):
        rows = slice(n * out.shape[0], (n + 1) * out.shape[0])
        out[...] = (one_ref[rows, :].astype(F32) + two_ref[rows, :].astype(F32)).astype(out.dtype)


def pair_pieces_kernel(odd_ref, one_ref, two_ref, own_ref, beside_ref, far_ref):
    size = own_ref.shape[0]
    back = 3 - 2 * odd_ref[0, 0]
    for out, at, step in (
        (own_ref, 0, 0), (beside_ref, 0, back), (beside_ref, size, 4 - back), (far_ref, 0, 2)
    ):
        rows = pl.ds(pl.multiple_of(step * size, size), size)
        value = one_ref[rows, :].astype(F32) + two_ref[rows, :].astype(F32)
        out[at : at + size, :] = value.astype(out.dtype)


def middle_kernel(base_ref, *refs):
    parts, (gain_ref, sum_ref, scaled_ref) = refs[:-3], refs[-3:]
    for at in range(0, base_ref.shape[0], 32):
        rows = slice(at, at + 32)
        value = base_ref[rows, :].astype(F32)
        for ref in parts:
            value = value + ref[rows, :].astype(F32)
        sum_ref[rows, :] = value
        normed, _ = normed_rows(value.astype(BF))
        scaled_ref[rows, :] = (normed * gain_ref[1:2, :]).astype(BF)


def middle_grad_kernel(base_ref, *refs):
    parts, (middle_ref, gain_ref, sum_ref, low_ref) = refs[:-4], refs[-4:]
    for at in range(0, base_ref.shape[0], 32):
        rows = slice(at, at + 32)
        value = parts[0][rows, :].astype(F32)
        for ref in parts[1:]:
            value = value + ref[rows, :].astype(F32)
        normed, factor = normed_rows(middle_ref[rows, :].astype(BF))
        value = value * gain_ref[1:2, :]
        inner = jnp.mean(value * normed, -1, keepdims=True)
        value = base_ref[rows, :].astype(F32) + factor * (value - normed * inner)
        sum_ref[rows, :] = value
        low_ref[rows, :] = value.astype(BF)


def cotangent_at(odd_ref, n):
    return (0, 3 - 2 * odd_ref[0, 0], 2, 1 + 2 * odd_ref[0, 0])[n % 4]


def hidden_kernel(width, odd_ref, *refs):
    (w_ref, hidden_ref, both_ref, x_ref, c_ref, gate_up_ref, down_ref, sems) = refs[10:]
    first = gate_up_ref.shape[1]
    copies = [
        pltpu.make_async_copy(w_ref.at[:, pl.ds(0, first)], gate_up_ref, sems.at[0]),
        pltpu.make_async_copy(w_ref.at[:, pl.ds(first, down_ref.shape[1])], down_ref, sems.at[1]),
    ]
    count = x_ref.shape[0] // 8
    for n in range(8):
        rows = pl.ds(n * count, count)
        copies.append(pltpu.make_async_copy(refs[n], x_ref.at[rows, :], sems.at[2 + n]))
        at = pl.ds(pl.multiple_of(cotangent_at(odd_ref, n) * count, count), count)
        copies.append(
            pltpu.make_async_copy(refs[8 + n // 4].at[at, :], c_ref.at[rows, :], sems.at[10 + n])
        )
    weights_up, weights_down, *pieces = copies
    xs, cots = pieces[::2], pieces[1::2]
    for copy in (*xs[:4], weights_up, *xs[4:], weights_down, *cots):
        copy.start()

    def units(gate, up, grad):
        sigmoid = 1.0 / (1.0 + jnp.exp(-gate))
        gated = gate * sigmoid
        return (
            (gated * up).astype(BF),
            (grad * up * sigmoid * (1.0 + gate * (1.0 - sigmoid))).astype(BF),
            (grad * gated).astype(BF),
        )

    half = 4 * count
    for part in range(2):
        rows = slice(part * half, (part + 1) * half)
        for copy in xs[4 * part : 4 * part + 4]:
            copy.wait()
        if part == 0:
            weights_up.wait()
        x = x_ref[rows, :]
        gate = mm(x, gate_up_ref[:, :width])
        up = mm(x, gate_up_ref[:, width : 2 * width])
        ends = mm(x, gate_up_ref[:, 2 * width :])
        for copy in cots[4 * part : 4 * part + 4]:
            copy.wait()
        if part == 0:
            weights_down.wait()
        c = c_ref[rows, :]
        value, dgate, dup = units(gate, up, mm(c, down_ref[:, :width]))
        hidden_ref[rows, :width] = value
        both_ref[rows, :width] = dgate
        both_ref[rows, width : 2 * width] = dup
        value, dgate, dup = units(ends[:, :64], ends[:, 64:], mm(c, down_ref[:, width:])[:, :64])
        hidden_ref[rows, width:] = jnp.concatenate([value, jnp.zeros_like(value)], 1)
        both_ref[rows, 2 * width :] = jnp.concatenate([dgate, dup], 1)


def sum_of_products(terms, refs):
    total = None
    for left, (low, high), right, (first, last) in terms:
        part = mm_last(refs[left][:, low:high], refs[right][:, first:last])
        total = part if total is None else total + part
    return total


def rows_grad_kernel(terms, count, gain_row, *refs):
    pieces, gain_ref, outs, sum_ref = refs[count : count + 4], refs[count + 4], refs[count + 5 : -1], refs[-1]
    own_ref, across_ref, cores_ref = outs
    size = own_ref.shape[0]
    outs = [own_ref, cores_ref.at[pl.ds(0, size), :], across_ref, cores_ref.at[pl.ds(size, size), :]]
    step = pl.program_id(0)
    tile = sum_ref.shape[1] // pl.num_programs(0)
    columns = pl.ds(pl.multiple_of(step * tile, tile), tile)
    sum_ref[:, columns] = sum_of_products(terms, refs) * gain_ref[gain_row : gain_row + 1, columns]

    @pl.when(step == pl.num_programs(0) - 1)
    def _():
        for n, ref in enumerate(pieces):
            for at in range(0, ref.shape[0], 32):
                normed, factor = normed_rows(ref[at : at + 32, :])
                scaled = sum_ref[n * ref.shape[0] + at : n * ref.shape[0] + at + 32, :]
                inner = jnp.mean(scaled * normed, -1, keepdims=True)
                outs[n][at : at + 32, :] = (factor * (scaled - normed * inner)).astype(BF)


def rows_out_kernel(terms, places, *refs):
    value = sum_of_products(terms, refs).astype(BF)
    outs = refs[len(refs) - len(places) :]
    size = value.shape[0] // sum(len(held) for held in places)
    for out, held in zip(outs, places):
        for n, piece in enumerate(held):
            out[n * size : (n + 1) * size, :] = value[piece * size : (piece + 1) * size]


def write_parts(outs, turned_of, axis, me, right, base):
    for d, out in enumerate(outs):
        index = (me + d) & 3
        if axis == "z":
            turned = turned_of(pl.multiple_of(index * 512, 512), 512)
        else:
            turned = jnp.concatenate(
                [turned_of(pl.multiple_of(z * 512 + index * 128, 128), 128) for z in range(4)], 0
            )
        out[:, base : base + right.shape[1]] = mm(turned, right).astype(BF)


def parts_kernel(axis, columns, count, me_ref, *refs):
    lefts, right_ref, outs = refs[:count], refs[count], refs[count + 1 :]

    def turned_of(at, size):
        return jnp.concatenate([left[:, pl.ds(at, size)] for left in lefts], 0).T

    write_parts(outs, turned_of, axis, me_ref[0, 0], right_ref[:, columns[0] : columns[1]], 0)


def last_parts_kernel(axis, cut, me_ref, left_ref, dq_ref, own_ref, one_ref, two_ref, three_ref,
                      cos_ref, sin_ref, *outs):
    half = HD // 2
    cos, sin = cos_ref[...], sin_ref[...]
    kv = own_ref[...]
    for ref in (one_ref, two_ref, three_ref):
        kv = kv + ref[...].astype(F32)
    kv = kv.T
    a, b = kv[:half], kv[half:HD]
    kv = jnp.concatenate([a * cos + b * sin, b * cos - a * sin, kv[HD:]], 0).T.astype(BF)
    outs[0][...] = kv
    right = jnp.concatenate([dq_ref[:, cut:], kv], 1)

    def turned_of(at, size):
        return left_ref[:, pl.ds(at, size)].T

    write_parts(outs[1:], turned_of, axis, me_ref[0, 0], right, 0)


def settle_kernel(base_ref, *refs):
    out_ref = refs[-1]
    width = base_ref.shape[1]

    def block(at):
        value = base_ref[:, at : at + 128].astype(F32)
        for ref in refs[:-1]:
            value = value + ref[:, at : at + 128].astype(F32)
        return value

    for n in range(width // 256):
        one, two = block(256 * n), block(256 * n + 128)
        low = jnp.concatenate([one[:, :HD], two[:, :HD]], 1)
        high = jnp.concatenate([one[:, HD:], two[:, HD:]], 1)
        out_ref[:, 128 * n : 128 * n + 128] = low.astype(out_ref.dtype)
        out_ref[:, width // 2 + 128 * n : width // 2 + 128 * n + 128] = high.astype(out_ref.dtype)


def fill_bias(bias_ref, me_ref, pos_ref, span, distances):
    step = 64
    quarter = span // 4
    me = me_ref[0, 0]
    at = lax.broadcasted_iota(jnp.int32, (1, span), 1)
    query = (((at // quarter) ^ me) * quarter) + (at & (quarter - 1))
    first = query - pos_ref[...]

    @pl.loop(0, span // step)
    def _(i):
        block = (i * step) // quarter
        start = (block ^ me) * quarter + i * step - block * quarter
        key = start + lax.broadcasted_iota(jnp.int32, (step, span), 0)
        for n, d in enumerate(distances):
            seen = (key - d * span <= query) & (key - d * span >= first)
            bias_ref[pl.ds(pl.multiple_of(n * span + i * step, step), step), :] = jnp.where(
                seen, 0.0, masked_fill
            ).astype(F32)


def attend_kernel(q_ref, *refs):
    blocks = len(refs) - 7
    kv_refs = refs[:blocks]
    me_ref, pos_ref, mix_ref, lse_ref, bias_ref, s_ref, vt_ref = refs[blocks:]
    span = q_ref.shape[1]
    fill_bias(bias_ref, me_ref, pos_ref, span, range(blocks))
    for d in range(blocks):
        vt_ref[:, d * span : (d + 1) * span] = kv_refs[d][...].T[HD:]

    @pl.loop(0, q_ref.shape[0] // 128)
    def _(pair):
        outs = []
        for sub in range(2):
            q = q_ref[pl.ds(pl.multiple_of(pair * 128 + sub * HD, HD), HD), :]
            top = None
            for d in range(blocks):
                rows = slice(d * span, (d + 1) * span)
                s = mm(kv_refs[d][:, :HD], q) + bias_ref[rows, :]
                s_ref[rows, :] = s
                high = jnp.max(s, 0, keepdims=True)
                top = high if top is None else jnp.maximum(top, high)
            total = jnp.zeros_like(top)
            out = jnp.zeros((HD, span), F32)
            for d in range(blocks):
                rows = slice(d * span, (d + 1) * span)
                p = jnp.exp(s_ref[rows, :] - top)
                total = total + jnp.sum(p, 0, keepdims=True)
                out = out + mm(vt_ref[:, rows], p.astype(BF))
            outs.append(out / total)
            lse_ref[pl.ds(pair * 2 + sub, 1), :] = top + jnp.log(total)
        mix_ref[:, pl.ds(pl.multiple_of(pair * 128, 128), 128)] = (
            jnp.concatenate(outs, 0).T.astype(BF)
        )


def attend_back_kernel(distances, first, last, q_ref, *refs):
    blocks = len(distances)
    refs = list(refs)

    def take(count):
        got, refs[:count] = refs[:count], []
        return got

    kv_refs = take(blocks)
    me_ref, pos_ref, lse_ref = take(3)
    if first:
        mix_ref, w_ref, *piece_refs = take(6)
    else:
        gt_ref, delta_ref, part_ref = take(3)
    if last:
        cos_ref, sin_ref = take(2)
        (dq_ref,) = take(1)
    else:
        (sum_ref,) = take(1)
    (dkv_ref,) = take(1)
    if first:
        gt_ref, delta_ref = take(2)
    bias_ref, v_ref, kt_ref, dk_ref, dv_ref = take(5)
    span = q_ref.shape[1]
    half = HD // 2
    heads = q_ref.shape[0] // HD
    fill_bias(bias_ref, me_ref, pos_ref, span, distances)
    for n in range(blocks):
        rows = slice(n * span, (n + 1) * span)
        both = kv_refs[n][...].T
        kt_ref[:, rows] = both[:HD]
        v_ref[rows, :] = both[HD:].T
    dk_ref[...] = jnp.zeros_like(dk_ref)
    dv_ref[...] = jnp.zeros_like(dv_ref)
    if first:
        rows_all = jnp.concatenate([ref[...] for ref in piece_refs], 0)
        for at in range(0, heads * HD, 256):
            grads = mm(rows_all, w_ref[:, heads * HD + at : heads * HD + at + 256]).astype(BF).T
            gt_ref[at : at + 256, :] = grads
        for at in range(0, heads * HD, 128):
            gt = gt_ref[at : at + 128, :]
            mt = mix_ref[:, at : at + 128].T
            prod = gt.astype(F32) * mt.astype(F32)
            for sub in range(2):
                h = at // HD + sub
                delta_ref[h : h + 1, :] = jnp.sum(prod[sub * HD : (sub + 1) * HD], 0, keepdims=True)

    @pl.loop(0, heads // 2)
    def _(pair):
        outs = []
        for sub in range(2):
            rows_h = pl.ds(pl.multiple_of(pair * 128 + sub * HD, HD), HD)
            q, g = q_ref[rows_h, :], gt_ref[rows_h, :]
            lse = lse_ref[pl.ds(pair * 2 + sub, 1), :]
            delta = delta_ref[pl.ds(pair * 2 + sub, 1), :]
            dq = jnp.zeros((HD, span), F32) if first else part_ref[rows_h, :]
            for n in range(blocks):
                rows = slice(n * span, (n + 1) * span)
                s = mm(kv_refs[n][:, :HD], q) + bias_ref[rows, :]
                p = jnp.exp(s - lse)
                ds = (p * (mm(v_ref[rows, :], g) - delta)).astype(BF)
                dv_ref[rows, :] += mm_last(p.astype(BF), g)
                dk_ref[rows, :] += mm_last(ds, q)
                dq = dq + mm(kt_ref[:, rows], ds)
            if last:
                dq = dq * 0.125
                a, b = dq[:half], dq[half:]
                cos, sin = cos_ref[...], sin_ref[...]
                outs += [a * cos + b * sin, b * cos - a * sin]
            else:
                sum_ref[rows_h, :] = dq
        if last:
            dq_ref[:, pl.ds(pl.multiple_of(pair * 128, 128), 128)] = (
                jnp.concatenate(outs, 0).T.astype(BF)
            )

    for n in range(blocks):
        rows = slice(n * span, (n + 1) * span)
        dkv_ref[rows, :] = jnp.concatenate([dk_ref[rows, :], dv_ref[rows, :]], 1).astype(dkv_ref.dtype)


def weight_grads_kernel(odd_ref, *refs):
    one_ref, two_ref, out_ref = refs[10:]
    count = refs[0].shape[0]

    def cotangent(n):
        at = pl.multiple_of(cotangent_at(odd_ref, n) * count, count)
        return refs[8 + n // 4][pl.ds(at, count), :]

    at = 0
    for lefts, ref in (
        ([left[...] for left in refs[:8]], one_ref), ([cotangent(n) for n in range(8)], two_ref)
    ):
        turned = jnp.concatenate(lefts, 0).T
        for c in range(0, ref.shape[1], 256):
            size = min(256, ref.shape[1] - c)
            out_ref[:, at + c : at + c + size] = mm(turned, ref[:, c : c + size]).astype(BF)
        at += ref.shape[1]


def params(mib):
    return pltpu.CompilerParams(vmem_limit_bytes=mib * MIB)


def whole(count):
    return [pl.BlockSpec(memory_space=pltpu.VMEM)] * count


def cost(products, moved):
    return pl.CostEstimate(flops=2 * products, bytes_accessed=moved, transcendentals=0)


def call(kernel, name, shapes, operands, scalars=0, products=0, mib=16):
    return pl.pallas_call(
        kernel,
        out_shape=tuple(jax.ShapeDtypeStruct(*shape) for shape in shapes),
        in_specs=scalar() * scalars + whole(len(operands) - scalars),
        out_specs=tuple(whole(len(shapes))),
        compiler_params=params(mib),
        cost_estimate=cost(products, 4 << 20),
        name=name,
    )(*operands)


def hidden_units(odd, pieces, cots, weights, width):
    count, d = pieces[0].shape
    span = 8 * count
    both, down = 2 * width + 128, width + 128
    return pl.pallas_call(
        functools.partial(hidden_kernel, width),
        out_shape=(jax.ShapeDtypeStruct((span, down), BF), jax.ShapeDtypeStruct((span, both), BF)),
        in_specs=scalar() + [pl.BlockSpec(memory_space=pl.ANY)] * 11,
        out_specs=tuple(whole(2)),
        scratch_shapes=[
            pltpu.VMEM((span, d), BF),
            pltpu.VMEM((span, d), BF),
            pltpu.VMEM((d, both), BF),
            pltpu.VMEM((d, down), BF),
            pltpu.SemaphoreType.DMA((18,)),
        ],
        compiler_params=params(56),
        cost_estimate=cost(3 * span * d * width, 6 * d * width),
        name="hidden_units",
    )(odd, *pieces, *cots, weights)


def feature_rows(weight, tile):
    if not isinstance(weight, tuple):
        return pl.BlockSpec((tile, weight.shape[1]), lambda i: (i, 0))
    return pl.BlockSpec((pl.Element(tile), pl.Element(weight[2])), lambda i: (i * tile, weight[1]))


def array_of(weight):
    return weight[0] if isinstance(weight, tuple) else weight


def fixed(array):
    return pl.BlockSpec(array.shape, lambda i: (0, 0))


def rows_grad(grads, weights, terms, pieces, gains, gain_row):
    span, d = 4 * pieces[0].shape[0], pieces[0].shape[1]
    tile = 512
    n = len(grads)
    terms = [(g, c, n + w, e) for g, c, w, e in terms]
    return pl.pallas_call(
        functools.partial(rows_grad_kernel, terms, n + len(weights), gain_row),
        grid=(d // tile,),
        out_shape=tuple(jax.ShapeDtypeStruct((span // n, d), BF) for n in (4, 4, 2)),
        in_specs=[fixed(g) for g in grads]
        + [feature_rows(w, tile) for w in weights]
        + [fixed(a) for a in (*pieces, gains)],
        out_specs=tuple(pl.BlockSpec((span // n, d), lambda i: (0, 0)) for n in (4, 4, 2)),
        scratch_shapes=[pltpu.VMEM((span, d), F32)],
        compiler_params=params(32),
        cost_estimate=cost(0, 0),
        name="rows_grad",
    )(*grads, *map(array_of, weights), *pieces, gains)


def rows_out(lefts, weights, terms, tile, places, mib):
    span, d = lefts[0].shape[0], array_of(weights[0]).shape[0]
    n = len(lefts)
    terms = [(g, c, n + w, e) for g, c, w, e in terms]
    size = span // sum(len(held) for held in places)
    return pl.pallas_call(
        functools.partial(rows_out_kernel, terms, places),
        grid=(d // tile,),
        out_shape=tuple(jax.ShapeDtypeStruct((len(held) * size, d), BF) for held in places),
        in_specs=[fixed(g) for g in lefts] + [feature_rows(w, tile) for w in weights],
        out_specs=tuple(pl.BlockSpec((len(held) * size, tile), lambda i: (0, i)) for held in places),
        compiler_params=params(mib),
        cost_estimate=cost(sum(span * d * (c[1] - c[0]) for _, c, _, _ in terms), 6 << 20),
        name="rows_out",
    )(*lefts, *map(array_of, weights))


def scalar():
    return [pl.BlockSpec(memory_space=pltpu.SMEM)]


def at_place(axis):
    return place(axis).astype(jnp.int32).reshape(1, 1)


def wide_parts(lefts, right, columns, axis):
    span, d = right.shape[0], lefts[0].shape[1]
    width = columns[1] - columns[0]
    return pl.pallas_call(
        functools.partial(parts_kernel, axis, columns, len(lefts)),
        out_shape=(jax.ShapeDtypeStruct((d // 4, width), BF),) * 4,
        in_specs=scalar() + whole(len(lefts) + 1),
        out_specs=tuple(whole(4)),
        compiler_params=params(20),
        cost_estimate=cost(span * d * width, 8 << 20),
        name="wide_parts",
    )(at_place(axis), *lefts, right)


def last_parts(left, dq, cut, own, arrived, cos, sin, axis):
    span, d = left.shape
    width = dq.shape[1] - cut + 2 * HD
    return pl.pallas_call(
        functools.partial(last_parts_kernel, axis, cut),
        out_shape=(jax.ShapeDtypeStruct((span, 2 * HD), BF),)
        + (jax.ShapeDtypeStruct((d // 4, width), BF),) * 4,
        in_specs=scalar() + whole(8),
        out_specs=tuple(whole(5)),
        compiler_params=params(20),
        cost_estimate=cost(0, 0),
        name="last_parts",
    )(at_place(axis), left, dq, own, *arrived, cos, sin)


def settle(base, parts, kind):
    return pl.pallas_call(
        settle_kernel,
        out_shape=jax.ShapeDtypeStruct(base.shape, kind),
        in_specs=whole(1 + len(parts)),
        out_specs=whole(1)[0],
        compiler_params=params(12),
        cost_estimate=cost(0, 4 << 20),
        name="settle",
    )(base, *parts)


def window_specs():
    return [pl.BlockSpec(memory_space=pltpu.SMEM)] + whole(1)


def attend(q, kvs, window):
    n = len(kvs)
    width, span = q.shape
    heads = width // HD
    return pl.pallas_call(
        attend_kernel,
        out_shape=(
            jax.ShapeDtypeStruct((span, width), BF),
            jax.ShapeDtypeStruct((heads, span), F32),
        ),
        in_specs=whole(n + 1) + window_specs(),
        out_specs=tuple(whole(2)),
        scratch_shapes=[
            pltpu.VMEM((n * span, span), F32),
            pltpu.VMEM((n * span, span), F32),
            pltpu.VMEM((HD, n * span), BF),
        ],
        compiler_params=params(32),
        cost_estimate=cost(30 * 580_000_000, 2 << 20),
        name="attend",
    )(q, *kvs, *window)


def attend_back(distances, q, kvs, window, lse, prepared, mixed=None, out=None, turn=None):
    n = len(kvs)
    width, span = q.shape
    heads = width // HD
    first, last = prepared is None, turn is not None
    operands = [q, *kvs, *window, lse]
    operands += [mixed, *out] if first else list(prepared)
    shapes = []
    if last:
        operands += turn
        shapes.append(jax.ShapeDtypeStruct((span, width), BF))
    else:
        shapes.append(jax.ShapeDtypeStruct((width, span), F32))
    shapes.append(jax.ShapeDtypeStruct((n * span, 2 * HD), F32 if last else BF))
    if first:
        shapes.append(jax.ShapeDtypeStruct((width, span), BF))
        shapes.append(jax.ShapeDtypeStruct((heads, span), F32))
    specs = whole(n + 1) + window_specs() + whole(len(operands) - n - 3)
    return pl.pallas_call(
        functools.partial(attend_back_kernel, distances, first, last),
        out_shape=tuple(shapes),
        in_specs=specs,
        out_specs=tuple(whole(len(shapes))),
        scratch_shapes=[
            pltpu.VMEM((n * span, span), F32),
            pltpu.VMEM((n * span, HD), BF),
            pltpu.VMEM((HD, n * span), BF),
            pltpu.VMEM((n * span, HD), F32),
            pltpu.VMEM((n * span, HD), F32),
        ],
        compiler_params=params(40),
        cost_estimate=cost(1000 * 580_000_000 if first else 0, 1 << 20),
        name="attend_back",
    )(*operands)


def weight_grads(odd, xs, cots, one, two):
    t, d = xs[0].shape
    tile = 256
    rows = pl.BlockSpec((t, tile), lambda i: (0, i))
    width = one.shape[1] + two.shape[1]
    return pl.pallas_call(
        weight_grads_kernel,
        grid=(d // tile,),
        out_shape=jax.ShapeDtypeStruct((d, width), BF),
        in_specs=scalar()
        + [rows] * 8
        + [pl.BlockSpec((4 * t, tile), lambda i: (0, i))] * 2
        + [fixed(one), fixed(two)],
        out_specs=pl.BlockSpec((tile, width), lambda i: (i, 0)),
        compiler_params=params(56),
        cost_estimate=cost(8 * t * d * width, 2 * d * width + 32 * t * d),
        name="weight_grads",
    )(odd, *xs, *cots, one, two)


def per_device(
    inputs,
    positions,
    attn_gain,
    query_weight,
    key_weight,
    value_weight,
    out_weight,
    mlp_gain,
    gate_weight,
    up_weight,
    down_weight,
    cotangent,
):
    width_q = query_weight.shape[1]
    width_k = key_weight.shape[1]
    hidden_width = gate_weight.shape[1]
    span = positions.shape[0]
    quarter = span // 4
    cut = 3 * width_q // 4
    d = inputs.shape[1]
    shard = query_weight.shape[0]
    side = place("yh").astype(jnp.int32).reshape(1, 1)

    units = 128 * (hidden_width // 256)
    both_width, down_width = 2 * units + 128, units + 128
    inputs, cotangent, shard_kv, shard_mlp = call(
        pack_kernel, "pack",
        [(inputs.shape, BF), (inputs.shape, BF), ((shard, 256), BF),
         ((2, shard, both_width + down_width), BF)],
        [inputs, cotangent, attn_gain[None], mlp_gain[None], key_weight, value_weight,
         gate_weight, up_weight, down_weight.T],
        mib=56,
    )
    shard_first = jnp.concatenate([query_weight, out_weight.T], 1)
    other_first, other_kv = swap(shard_first, "yh"), swap(shard_kv, "yh")
    pair_first = join_sides(shard_first, after(other_first, shard_kv))
    first_whole = lax.all_gather(pair_first, ("z", "x"), axis=0, tiled=True)
    pair_kv = join_sides(shard_kv, other_kv)
    along_kv = send_stage(pair_kv, "x")
    rows_in = gather_rows(after(inputs, other_kv))
    kv_whole = flat(stack_stage(send_stage(stack_stage(along_kv, "x", 0), "z"), "z", 0))

    me = (lax.axis_index("yl") * 2 + lax.axis_index("core")).astype(jnp.int32)
    blocked = jnp.arange(4, dtype=jnp.int32) ^ me
    positions = jnp.take(positions.reshape(4, quarter), blocked, axis=0, mode="clip").reshape(1, span)
    freqs = 10000.0 ** (-(jnp.arange(HD // 2, dtype=F32) * 2.0) / HD)
    angles = freqs[:, None] * positions.astype(F32)
    cos, sin = jnp.cos(angles), jnp.sin(angles)
    window = (me.reshape(1, 1), positions)

    kv_block, scaled_in, gains = call(
        keys_values_kernel, "keys_values",
        [((span, 2 * width_k), BF), ((span, d), BF), ((8, d), F32)],
        [*rows_in, kv_whole, cos, sin], products=span * d * 2 * width_k,
    )
    (queries,) = call(
        queries_kernel, "queries",
        [((width_q, span), BF)],
        [scaled_in, after(first_whole, kv_block), cos, sin], products=span * d * width_q,
    )
    blocks = [kv_block] + [shift(kv_block, "x", d) for d in range(1, SEQ_DEVS)]
    cot_yl = swap(after(cotangent, kv_block), "yl")
    cot_near = jnp.concatenate([cotangent, cot_yl], 0)
    cot_far = swap(cot_near, "yh")
    other_mlp = swap(after(pick(shard_mlp, place("yh", 1), 0), kv_block), "yh")
    mlp_pair = join_sides(pick(shard_mlp, place("yh"), 0), after(other_mlp, first_whole, blocks[1:], cot_yl))
    mlp_whole = lax.all_gather(mlp_pair, ("z", "x"), axis=0, tiled=True)
    odd = place("yl").astype(jnp.int32).reshape(1, 1)
    mixed, log_total = attend(queries, blocks, window)

    cotangents = jnp.concatenate([cot_near, after(cot_far, log_total)], 0)
    all_heads = (0, width_q)
    attn_rows = rows_out(
        [after(mixed, cotangents)], [(first_whole, width_q, width_q)], [(0, all_heads, 0, all_heads)],
        1024, [(0,), (2,), (1, 3)], 24,
    )
    cotangents = [cotangents, swap(cotangents, "core")]
    middle, scaled_mid = call(
        middle_kernel, "middle", [(inputs.shape, F32), (inputs.shape, BF)],
        [inputs, *scatter_rows(attn_rows), gains],
    )
    scaled_all = gather_eight(scaled_mid)
    hidden, grad_both = hidden_units(odd, scaled_all, cotangents, mlp_whole, units)
    mid_partial = rows_out(
        [grad_both], [(mlp_whole, 0, both_width)], [(0, (0, both_width), 0, (0, both_width))], 512, [(0, 1, 2, 3), (4, 5, 6, 7)], 56,
    )
    mid_own, mid_others = scatter_eight(*mid_partial)
    mid_arrived = send_back(mid_others)
    mlp_sum = weight_grads(
        odd, [after(scaled_all[0], mid_others), *scaled_all[1:]], cotangents, grad_both, hidden
    )
    mlp_rows = rows_out(
        [after(hidden, mlp_sum)], [(mlp_whole, both_width, down_width)],
        [(0, (0, down_width), 0, (0, down_width))], 512, [(0, 1, 2, 3), (4, 5, 6, 7)], 56,
    )
    grad_middle, grad_middle_low = call(
        middle_grad_kernel, "middle_grad", [(inputs.shape, F32), (inputs.shape, BF)],
        [cotangent, mid_own, *after(mid_arrived, mlp_rows), middle, gains],
    )
    rows_grad_middle = gather_rows(grad_middle_low)
    mlp_sum = lax.psum_scatter(mlp_sum, ("z", "x"), scatter_dimension=0, tiled=True)

    out_parts = wide_parts(rows_grad_middle, mixed, (0, width_q), "z")
    mlp_cores = swap(after(mlp_rows[1], grad_middle_low), "core")
    mlp_own, mlp_beside, mlp_far = call(
        pair_pieces_kernel, "pair_pieces",
        [(inputs.shape, F32), ((2 * quarter, d), BF), (inputs.shape, BF)],
        [odd, mlp_rows[0], mlp_cores], scalars=1,
    )
    query_part, far_grads, grad_turned, delta = attend_back(
        (1, 2, 3), queries, blocks[1:], window, log_total, None, after(mixed, out_parts, mlp_beside),
        [first_whole, *rows_grad_middle],
    )
    mlp_arrived = after(swap(after(mlp_beside, rows_grad_middle), "yl"), query_part)
    mlp_far = (mlp_far.astype(F32) + mlp_arrived[quarter:].astype(F32)).astype(BF)
    arriving = [
        shift(far_grads[(d - 1) * span : d * span], "x", -d) for d in range(1, SEQ_DEVS)
    ]
    out_arrived = [after(shift(out_parts[n], "z", n), query_part) for n in (1, 2, 3)]
    query_raw_grad, own_grads = attend_back(
        (0,), after(queries, mlp_far, out_arrived), blocks[:1], window, log_total, (grad_turned, delta, query_part), turn=[cos, sin]
    )

    out_sum = total(out_parts[0].astype(F32), out_arrived).astype(BF)
    output = settle(
        middle, [mlp_own, mlp_arrived[:quarter], after(swap(mlp_far, "yh"), query_raw_grad)], BF
    )
    a_parts = wide_parts([scaled_in], after(query_raw_grad, arriving), (0, cut), "x")
    a_arrived = [shift(a_parts[n], "x", n) for n in (2, 1, 3)]
    kv_raw_grad, *b_parts = last_parts(
        scaled_in, after(query_raw_grad, a_parts), cut, own_grads, arriving, cos, sin, "z"
    )
    b_arrived = [shift(b_parts[n], "z", n) for n in (2, 1, 3)]
    in_partial = rows_grad(
        [query_raw_grad, kv_raw_grad],
        [(first_whole, 0, width_q), kv_whole],
        [(0, all_heads, 0, all_heads), (1, (0, 2 * width_k), 1, (0, 2 * width_k))],
        rows_in, gains, 0,
    )
    in_own, in_across, in_cores = in_partial
    in_parts = scatter_rows((in_own, in_across, after(in_cores, a_arrived, b_arrived)))
    input_grad = settle(grad_middle, in_parts, F32)

    mlp_send = pick(mlp_sum.reshape(2, shard, -1), place("yh", 1), 0)
    a_sum = wide_sum_next(total(a_parts[0].astype(F32), a_arrived).astype(BF), "z")
    b_sum = total(b_parts[0].astype(F32), b_arrived).astype(BF)
    b_sum = wide_sum_next(jnp.concatenate([b_sum, out_sum], 1), "x", hold=[mlp_send])
    sides = jnp.concatenate([a_sum, b_sum], 1)
    other_sides = swap(pick(sides.reshape(2, shard, -1), place("yh", 1), 0), "yh")
    query_grad, key_grad, value_grad, out_grad = call(
        finish_attn_kernel, "finish_attn",
        [(query_weight.shape, F32), (key_weight.shape, F32), (value_weight.shape, F32),
         (out_weight.shape[::-1], F32)],
        [side, sides, other_sides], scalars=1,
    )
    gate_grad, up_grad, down_grad = call(
        finish_mlp_kernel, "finish_mlp",
        [(gate_weight.shape, F32), (up_weight.shape, F32), (down_weight.shape[::-1], F32)],
        [side, mlp_sum, swap(mlp_send, "yh")], scalars=1,
    )

    ends = width_q - cut
    attn_weights = jnp.concatenate([pair_first[:, :width_q], pair_kv[:, : 2 * width_k]], 1).astype(F32)
    gain_parts = jnp.stack(
        [
            jnp.sum(attn_weights * sides[:, : cut + ends + 2 * width_k].astype(F32), 1),
            jnp.sum(
                mlp_pair[:, :both_width].astype(F32) * mlp_sum[:, :both_width].astype(F32),
                1,
            ),
        ]
    )
    gain_parts = lax.psum(gain_parts, ("yh",) + TP)
    own_gains = pick(gain_parts.reshape(2, 2, shard), place("yh"), 1)
    return (
        output,
        input_grad,
        own_gains[0] / attn_gain.astype(F32),
        query_grad,
        key_grad,
        value_grad,
        out_grad.T,
        own_gains[1] / mlp_gain.astype(F32),
        gate_grad,
        up_grad,
        down_grad.T,
    )


def solution(mesh):
    split = Mesh(mesh.devices.reshape(2, 4, 4, 2, 2), WIDE + TP)
    rows = P(WIDE + TP, None)
    inward = P(WIDE, TP)
    outward = P(TP, WIDE)
    gain = P(WIDE)
    return jax.shard_map(
        per_device,
        mesh=split,
        in_specs=(
            rows, gain, gain, inward, inward, inward, outward, gain, inward, inward, outward, rows,
        ),
        out_specs=(
            rows, rows, gain, inward, inward, inward, outward, gain, inward, inward, outward,
        ),
        check_vma=False,
    )
```

```python
import functools

import jax
import jax.numpy as jnp
from jax import lax
from jax.experimental import pallas as pl
from jax.experimental.pallas import tpu as pltpu
from jax.sharding import Mesh, PartitionSpec as P

HEADS = 32
KV = 4
HD = 64
SEQ_DEVS = 4
WIDE = ("yh", "z", "x")
TP = ("yl", "core")
RING = ("yh", "yl")
BF = jnp.bfloat16
F32 = jnp.float32

epsilon = 1e-05
masked_fill = -1e30
MIB = 1024 * 1024


def after(value, *earlier):
    return lax.optimization_barrier((value, earlier))[0]


def shift(block, axis, distance):
    n = 4 if axis == RING else lax.axis_size(axis)
    return lax.ppermute(block, axis, [(i, (i + distance) % n) for i in range(n)])


def swap(block, axis):
    return shift(block, axis, 1)


def place(axis, step=0):
    n = lax.axis_size(axis)
    return ((lax.axis_index(axis) + (step + n)) & (n - 1)).astype(jnp.uint32)


def pick(array, index, dim):
    return lax.dynamic_index_in_dim(array, index, dim, keepdims=False)


def send_stage(block, axis):
    n = lax.axis_size(axis)
    return [block] + [shift(block, axis, d) for d in (1, n - 1, *range(2, n - 1))]


def stack_stage(arrived, axis, dim):
    n = len(arrived)
    block = arrived[0]
    out = jnp.zeros(block.shape[:dim] + (n,) + block.shape[dim:], block.dtype)
    for d, piece in zip((0, 1, n - 1, *range(2, n - 1)), arrived):
        out = lax.dynamic_update_index_in_dim(out, piece, place(axis, -d), dim)
    return out


def join_sides(shard, other):
    first = lax.axis_index("yh") == 0
    return jnp.concatenate([jnp.where(first, shard, other), jnp.where(first, other, shard)], 0)


def flat(blocks):
    return blocks.reshape(-1, blocks.shape[-1])


def gather_rows(rows):
    across = swap(rows, "yl")
    return [rows, swap(rows, "core"), across, swap(across, "core")]


def gather_eight(rows):
    near = [rows, shift(rows, RING, 1), shift(rows, RING, 2), shift(rows, RING, -1)]
    return near + [swap(piece, "core") for piece in near]


def scatter_eight(own_core, other_core):
    quarter, d = own_core.shape[0] // 4, own_core.shape[1]
    own, *others = call(
        add_pieces_kernel, "add_pieces",
        [((quarter, d), F32)] + [((quarter, d), BF)] * 3, [own_core, swap(other_core, "core")],
    )
    return own, others


def send_back(others):
    one, two, three = others
    return [shift(one, RING, -1), shift(three, RING, 1), shift(two, RING, 2)]


def scatter_rows(partial):
    own, across, cores = partial
    n = own.shape[0]
    arrived = swap(cores, "core")
    other = (across.astype(F32) + arrived[n:].astype(F32)).astype(BF)
    return [own, arrived[:n], swap(other, "yl")]


def total(first, parts):
    for part in parts:
        first = first + part.astype(F32)
    return first


def exchange_sum(parts, axis, hold=()):
    near = parts[0].astype(F32)
    for d in (1, 3):
        near = near + after(shift(parts[d], axis, d), *hold).astype(F32)
    return near + after(shift(parts[2], axis, 2), *hold).astype(F32)


def wide_sum_next(part, axis, hold=()):
    n = lax.axis_size(axis)
    part = part.reshape(n, part.shape[0] // n, part.shape[1])
    pieces = [pick(part, place(axis, d), 0) for d in range(n)]
    return exchange_sum(pieces, axis, hold).astype(BF)


def mm(left, right):
    return jnp.dot(left, right, preferred_element_type=F32)


def mm_last(left, right):
    return lax.dot_general(left, right, (((1,), (1,)), ((), ())), preferred_element_type=F32)


def normed_rows(piece):
    values = piece.astype(F32)
    factor = lax.rsqrt(jnp.mean(values * values, -1, keepdims=True) + epsilon)
    return values * factor, factor


def scale_rows(piece_refs, gain, scaled_ref):
    for n, ref in enumerate(piece_refs):
        for at in range(0, ref.shape[0], 32):
            normed, _ = normed_rows(ref[at : at + 32, :])
            rows = n * ref.shape[0] + at
            scaled_ref[rows : rows + 32, :] = (normed * gain).astype(BF)


def turned(block, cos, sin):
    a, b = block[: HD // 2], block[HD // 2 :]
    return jnp.concatenate([a * cos - b * sin, b * cos + a * sin], 0)


def keys_values_kernel(*refs):
    piece_refs, (w_ref, cos_ref, sin_ref, kv_ref, scaled_ref, gains_ref) = refs[:4], refs[4:]
    gains_ref[...] = w_ref[:, 128:].T[:8].astype(F32)
    scale_rows(piece_refs, gains_ref[0:1, :], scaled_ref)
    both = mm(scaled_ref[...], w_ref[:, :128]).T
    keys = turned(both[:HD], cos_ref[...], sin_ref[...])
    kv_ref[...] = jnp.concatenate([keys, both[HD:]], 0).T.astype(BF)


def queries_kernel(x_ref, w_ref, cos_ref, sin_ref, q_ref):
    for at in range(0, q_ref.shape[0], 256):
        piece = mm(x_ref[...], w_ref[:, at : at + 256]).T
        for sub in range(0, 256, HD):
            low = turned(piece[sub : sub + HD], cos_ref[...], sin_ref[...]).astype(BF)
            q_ref[at + sub : at + sub + HD, :] = low * 0.125


def to_inner(ref, out_ref):
    half = ref.shape[1] // 2
    for at in range(0, half, 128):
        low, high = ref[:, at : at + 128], ref[:, half + at : half + at + 128]
        out_ref[:, 2 * at : 2 * at + 128] = jnp.concatenate([low[:, :HD], high[:, :HD]], 1)
        out_ref[:, 2 * at + 128 : 2 * at + 256] = jnp.concatenate([low[:, HD:], high[:, HD:]], 1)


def pack_kernel(inputs_ref, cot_ref, again_ref, mgain_ref, k_ref, v_ref, g_ref, u_ref, d_ref,
                rows_ref, cots_ref, kv_ref, mlp_ref):
    to_inner(inputs_ref, rows_ref)
    to_inner(cot_ref, cots_ref)
    kv_ref[:, :128] = jnp.concatenate([k_ref[...], v_ref[...]], 1)
    gains = jnp.concatenate(
        [again_ref[...].astype(F32), mgain_ref[...].astype(F32), jnp.zeros((126, HD), F32)], 0
    )
    kv_ref[:, 128:] = gains.T.astype(BF)
    width = g_ref.shape[1]
    down = d_ref[...]
    whole_units = 128 * (width // 256)
    tail = 2 * whole_units
    for side in range(2):
        units = slice(side * whole_units, (side + 1) * whole_units)
        ends = slice(tail + 64 * side, tail + 64 * side + 64)
        mlp_ref[side, :, :whole_units] = g_ref[:, units]
        mlp_ref[side, :, whole_units:tail] = u_ref[:, units]
        mlp_ref[side, :, tail : tail + 128] = jnp.concatenate([g_ref[:, ends], u_ref[:, ends]], 1)
        mlp_ref[side, :, tail + 128 : tail + 128 + whole_units] = down[:, units]
        mlp_ref[side, :, tail + 128 + whole_units :] = jnp.concatenate(
            [down[:, ends], jnp.zeros_like(down[:, ends])], 1
        )


def finish_mlp_kernel(side_ref, pair_ref, other_ref, gate_ref, up_ref, down_ref):
    rows = pl.ds(pl.multiple_of(side_ref[0, 0] * HD, HD), HD)
    own, other = pair_ref[rows, :].astype(F32), other_ref[...].astype(F32)
    here = side_ref[0, 0] == 0
    halves = jnp.where(here, own, other), jnp.where(here, other, own)
    units = 128 * (gate_ref.shape[1] // 256)
    tail = 2 * units
    down = []
    for n, half in enumerate(halves):
        gate_ref[:, n * units : (n + 1) * units] = half[:, :units]
        up_ref[:, n * units : (n + 1) * units] = half[:, units:tail]
        down.append(half[:, tail + 128 : tail + 128 + units])
    ends = [half[:, tail : tail + 128] for half in halves]
    gate_ref[:, tail:] = jnp.concatenate([end[:, :64] for end in ends], 1)
    up_ref[:, tail:] = jnp.concatenate([end[:, 64:] for end in ends], 1)
    down += [half[:, tail + 128 + units : tail + 192 + units] for half in halves]
    for n in range(2):
        down_ref[:, n * units : (n + 1) * units] = down[n]
    down_ref[:, tail:] = jnp.concatenate(down[2:], 1)


def finish_attn_kernel(side_ref, pair_ref, other_ref, q_ref, k_ref, v_ref, o_ref):
    rows = pl.ds(pl.multiple_of(side_ref[0, 0] * HD, HD), HD)
    both = pair_ref[rows, :].astype(F32) + other_ref[...].astype(F32)
    width = q_ref.shape[1]
    q_ref[...] = both[:, :width]
    k_ref[...] = both[:, width : width + HD]
    v_ref[...] = both[:, width + HD : width + 2 * HD]
    o_ref[...] = both[:, width + 2 * HD :]


def add_pieces_kernel(one_ref, two_ref, *outs):
    for n, out in enumerate(outs):
        rows = slice(n * out.shape[0], (n + 1) * out.shape[0])
        out[...] = (one_ref[rows, :].astype(F32) + two_ref[rows, :].astype(F32)).astype(out.dtype)


def pair_pieces_kernel(odd_ref, one_ref, two_ref, own_ref, beside_ref, far_ref):
    size = own_ref.shape[0]
    back = 3 - 2 * odd_ref[0, 0]
    for out, at, step in (
        (own_ref, 0, 0), (beside_ref, 0, back), (beside_ref, size, 4 - back), (far_ref, 0, 2)
    ):
        rows = pl.ds(pl.multiple_of(step * size, size), size)
        value = one_ref[rows, :].astype(F32) + two_ref[rows, :].astype(F32)
        out[at : at + size, :] = value.astype(out.dtype)


def middle_kernel(base_ref, *refs):
    parts, (gain_ref, sum_ref, scaled_ref) = refs[:-3], refs[-3:]
    for at in range(0, base_ref.shape[0], 32):
        rows = slice(at, at + 32)
        value = base_ref[rows, :].astype(F32)
        for ref in parts:
            value = value + ref[rows, :].astype(F32)
        sum_ref[rows, :] = value
        normed, _ = normed_rows(value.astype(BF))
        scaled_ref[rows, :] = (normed * gain_ref[1:2, :]).astype(BF)


def middle_grad_kernel(base_ref, *refs):
    parts, (middle_ref, gain_ref, sum_ref, low_ref) = refs[:-4], refs[-4:]
    for at in range(0, base_ref.shape[0], 32):
        rows = slice(at, at + 32)
        value = parts[0][rows, :].astype(F32)
        for ref in parts[1:]:
            value = value + ref[rows, :].astype(F32)
        normed, factor = normed_rows(middle_ref[rows, :].astype(BF))
        value = value * gain_ref[1:2, :]
        inner = jnp.mean(value * normed, -1, keepdims=True)
        value = base_ref[rows, :].astype(F32) + factor * (value - normed * inner)
        sum_ref[rows, :] = value
        low_ref[rows, :] = value.astype(BF)


def cotangent_at(odd_ref, n):
    return (0, 3 - 2 * odd_ref[0, 0], 2, 1 + 2 * odd_ref[0, 0])[n % 4]


def hidden_kernel(width, odd_ref, *refs):
    (w_ref, hidden_ref, both_ref, x_ref, c_ref, gate_up_ref, down_ref, sems) = refs[10:]
    first = gate_up_ref.shape[1]
    copies = [
        pltpu.make_async_copy(w_ref.at[:, pl.ds(0, first)], gate_up_ref, sems.at[0]),
        pltpu.make_async_copy(w_ref.at[:, pl.ds(first, down_ref.shape[1])], down_ref, sems.at[1]),
    ]
    count = x_ref.shape[0] // 8
    for n in range(8):
        rows = pl.ds(n * count, count)
        copies.append(pltpu.make_async_copy(refs[n], x_ref.at[rows, :], sems.at[2 + n]))
        at = pl.ds(pl.multiple_of(cotangent_at(odd_ref, n) * count, count), count)
        copies.append(
            pltpu.make_async_copy(refs[8 + n // 4].at[at, :], c_ref.at[rows, :], sems.at[10 + n])
        )
    weights_up, weights_down, *pieces = copies
    xs, cots = pieces[::2], pieces[1::2]
    for copy in (*xs[:4], weights_up, *xs[4:], weights_down, *cots):
        copy.start()

    def units(gate, up, grad):
        sigmoid = 1.0 / (1.0 + jnp.exp(-gate))
        gated = gate * sigmoid
        return (
            (gated * up).astype(BF),
            (grad * up * sigmoid * (1.0 + gate * (1.0 - sigmoid))).astype(BF),
            (grad * gated).astype(BF),
        )

    half = 4 * count
    for part in range(2):
        rows = slice(part * half, (part + 1) * half)
        for copy in xs[4 * part : 4 * part + 4]:
            copy.wait()
        if part == 0:
            weights_up.wait()
        x = x_ref[rows, :]
        gate = mm(x, gate_up_ref[:, :width])
        up = mm(x, gate_up_ref[:, width : 2 * width])
        ends = mm(x, gate_up_ref[:, 2 * width :])
        for copy in cots[4 * part : 4 * part + 4]:
            copy.wait()
        if part == 0:
            weights_down.wait()
        c = c_ref[rows, :]
        value, dgate, dup = units(gate, up, mm(c, down_ref[:, :width]))
        hidden_ref[rows, :width] = value
        both_ref[rows, :width] = dgate
        both_ref[rows, width : 2 * width] = dup
        value, dgate, dup = units(ends[:, :64], ends[:, 64:], mm(c, down_ref[:, width:])[:, :64])
        hidden_ref[rows, width:] = jnp.concatenate([value, jnp.zeros_like(value)], 1)
        both_ref[rows, 2 * width :] = jnp.concatenate([dgate, dup], 1)


def sum_of_products(terms, refs):
    total = None
    for left, (low, high), right, (first, last) in terms:
        part = mm_last(refs[left][:, low:high], refs[right][:, first:last])
        total = part if total is None else total + part
    return total


def rows_grad_kernel(terms, count, gain_row, *refs):
    pieces, gain_ref, outs, sum_ref = refs[count : count + 4], refs[count + 4], refs[count + 5 : -1], refs[-1]
    own_ref, across_ref, cores_ref = outs
    size = own_ref.shape[0]
    outs = [own_ref, cores_ref.at[pl.ds(0, size), :], across_ref, cores_ref.at[pl.ds(size, size), :]]
    step = pl.program_id(0)
    tile = sum_ref.shape[1] // pl.num_programs(0)
    columns = pl.ds(pl.multiple_of(step * tile, tile), tile)
    sum_ref[:, columns] = sum_of_products(terms, refs) * gain_ref[gain_row : gain_row + 1, columns]

    @pl.when(step == pl.num_programs(0) - 1)
    def _():
        for n, ref in enumerate(pieces):
            for at in range(0, ref.shape[0], 32):
                normed, factor = normed_rows(ref[at : at + 32, :])
                scaled = sum_ref[n * ref.shape[0] + at : n * ref.shape[0] + at + 32, :]
                inner = jnp.mean(scaled * normed, -1, keepdims=True)
                outs[n][at : at + 32, :] = (factor * (scaled - normed * inner)).astype(BF)


def rows_out_kernel(terms, places, *refs):
    value = sum_of_products(terms, refs).astype(BF)
    outs = refs[len(refs) - len(places) :]
    size = value.shape[0] // sum(len(held) for held in places)
    for out, held in zip(outs, places):
        for n, piece in enumerate(held):
            out[n * size : (n + 1) * size, :] = value[piece * size : (piece + 1) * size]


def write_parts(outs, turned_of, axis, me, right, base):
    for d, out in enumerate(outs):
        index = (me + d) & 3
        if axis == "z":
            turned = turned_of(pl.multiple_of(index * 512, 512), 512)
        else:
            turned = jnp.concatenate(
                [turned_of(pl.multiple_of(z * 512 + index * 128, 128), 128) for z in range(4)], 0
            )
        out[:, base : base + right.shape[1]] = mm(turned, right).astype(BF)


def parts_kernel(axis, columns, count, me_ref, *refs):
    lefts, right_ref, outs = refs[:count], refs[count], refs[count + 1 :]

    def turned_of(at, size):
        return jnp.concatenate([left[:, pl.ds(at, size)] for left in lefts], 0).T

    write_parts(outs, turned_of, axis, me_ref[0, 0], right_ref[:, columns[0] : columns[1]], 0)


def last_parts_kernel(axis, cut, me_ref, left_ref, dq_ref, own_ref, one_ref, two_ref, three_ref,
                      cos_ref, sin_ref, *outs):
    half = HD // 2
    cos, sin = cos_ref[...], sin_ref[...]
    kv = own_ref[...]
    for ref in (one_ref, two_ref, three_ref):
        kv = kv + ref[...].astype(F32)
    kv = kv.T
    a, b = kv[:half], kv[half:HD]
    kv = jnp.concatenate([a * cos + b * sin, b * cos - a * sin, kv[HD:]], 0).T.astype(BF)
    outs[0][...] = kv
    right = jnp.concatenate([dq_ref[:, cut:], kv], 1)

    def turned_of(at, size):
        return left_ref[:, pl.ds(at, size)].T

    write_parts(outs[1:], turned_of, axis, me_ref[0, 0], right, 0)


def settle_kernel(base_ref, *refs):
    out_ref = refs[-1]
    width = base_ref.shape[1]

    def block(at):
        value = base_ref[:, at : at + 128].astype(F32)
        for ref in refs[:-1]:
            value = value + ref[:, at : at + 128].astype(F32)
        return value

    for n in range(width // 256):
        one, two = block(256 * n), block(256 * n + 128)
        low = jnp.concatenate([one[:, :HD], two[:, :HD]], 1)
        high = jnp.concatenate([one[:, HD:], two[:, HD:]], 1)
        out_ref[:, 128 * n : 128 * n + 128] = low.astype(out_ref.dtype)
        out_ref[:, width // 2 + 128 * n : width // 2 + 128 * n + 128] = high.astype(out_ref.dtype)


def fill_bias(bias_ref, me_ref, pos_ref, span, distances):
    step = 64
    quarter = span // 4
    me = me_ref[0, 0]
    at = lax.broadcasted_iota(jnp.int32, (1, span), 1)
    query = (((at // quarter) ^ me) * quarter) + (at & (quarter - 1))
    first = query - pos_ref[...]

    @pl.loop(0, span // step)
    def _(i):
        block = (i * step) // quarter
        start = (block ^ me) * quarter + i * step - block * quarter
        key = start + lax.broadcasted_iota(jnp.int32, (step, span), 0)
        for n, d in enumerate(distances):
            seen = (key - d * span <= query) & (key - d * span >= first)
            bias_ref[pl.ds(pl.multiple_of(n * span + i * step, step), step), :] = jnp.where(
                seen, 0.0, masked_fill
            ).astype(F32)


def attend_kernel(q_ref, *refs):
    blocks = len(refs) - 7
    kv_refs = refs[:blocks]
    me_ref, pos_ref, mix_ref, lse_ref, bias_ref, s_ref, vt_ref = refs[blocks:]
    span = q_ref.shape[1]
    fill_bias(bias_ref, me_ref, pos_ref, span, range(blocks))
    for d in range(blocks):
        vt_ref[:, d * span : (d + 1) * span] = kv_refs[d][...].T[HD:]

    @pl.loop(0, q_ref.shape[0] // 128)
    def _(pair):
        outs = []
        for sub in range(2):
            q = q_ref[pl.ds(pl.multiple_of(pair * 128 + sub * HD, HD), HD), :]
            top = None
            for d in range(blocks):
                rows = slice(d * span, (d + 1) * span)
                s = mm(kv_refs[d][:, :HD], q) + bias_ref[rows, :]
                s_ref[rows, :] = s
                high = jnp.max(s, 0, keepdims=True)
                top = high if top is None else jnp.maximum(top, high)
            total = jnp.zeros_like(top)
            out = jnp.zeros((HD, span), F32)
            for d in range(blocks):
                rows = slice(d * span, (d + 1) * span)
                p = jnp.exp(s_ref[rows, :] - top)
                total = total + jnp.sum(p, 0, keepdims=True)
                out = out + mm(vt_ref[:, rows], p.astype(BF))
            outs.append(out / total)
            lse_ref[pl.ds(pair * 2 + sub, 1), :] = top + jnp.log(total)
        mix_ref[:, pl.ds(pl.multiple_of(pair * 128, 128), 128)] = (
            jnp.concatenate(outs, 0).T.astype(BF)
        )


def attend_back_kernel(distances, first, last, q_ref, *refs):
    blocks = len(distances)
    refs = list(refs)

    def take(count):
        got, refs[:count] = refs[:count], []
        return got

    kv_refs = take(blocks)
    me_ref, pos_ref, lse_ref = take(3)
    if first:
        mix_ref, w_ref, *piece_refs = take(6)
    else:
        gt_ref, delta_ref, part_ref = take(3)
    if last:
        cos_ref, sin_ref = take(2)
        (dq_ref,) = take(1)
    else:
        (sum_ref,) = take(1)
    (dkv_ref,) = take(1)
    if first:
        gt_ref, delta_ref = take(2)
    bias_ref, v_ref, kt_ref, dk_ref, dv_ref = take(5)
    span = q_ref.shape[1]
    half = HD // 2
    heads = q_ref.shape[0] // HD
    fill_bias(bias_ref, me_ref, pos_ref, span, distances)
    for n in range(blocks):
        rows = slice(n * span, (n + 1) * span)
        both = kv_refs[n][...].T
        kt_ref[:, rows] = both[:HD]
        v_ref[rows, :] = both[HD:].T
    dk_ref[...] = jnp.zeros_like(dk_ref)
    dv_ref[...] = jnp.zeros_like(dv_ref)
    if first:
        rows_all = jnp.concatenate([ref[...] for ref in piece_refs], 0)
        for at in range(0, heads * HD, 256):
            grads = mm(rows_all, w_ref[:, heads * HD + at : heads * HD + at + 256]).astype(BF).T
            gt_ref[at : at + 256, :] = grads
        for at in range(0, heads * HD, 128):
            gt = gt_ref[at : at + 128, :]
            mt = mix_ref[:, at : at + 128].T
            prod = gt.astype(F32) * mt.astype(F32)
            for sub in range(2):
                h = at // HD + sub
                delta_ref[h : h + 1, :] = jnp.sum(prod[sub * HD : (sub + 1) * HD], 0, keepdims=True)

    @pl.loop(0, heads // 2)
    def _(pair):
        outs = []
        for sub in range(2):
            rows_h = pl.ds(pl.multiple_of(pair * 128 + sub * HD, HD), HD)
            q, g = q_ref[rows_h, :], gt_ref[rows_h, :]
            lse = lse_ref[pl.ds(pair * 2 + sub, 1), :]
            delta = delta_ref[pl.ds(pair * 2 + sub, 1), :]
            dq = jnp.zeros((HD, span), F32) if first else part_ref[rows_h, :]
            for n in range(blocks):
                rows = slice(n * span, (n + 1) * span)
                s = mm(kv_refs[n][:, :HD], q) + bias_ref[rows, :]
                p = jnp.exp(s - lse)
                ds = (p * (mm(v_ref[rows, :], g) - delta)).astype(BF)
                dv_ref[rows, :] += mm_last(p.astype(BF), g)
                dk_ref[rows, :] += mm_last(ds, q)
                dq = dq + mm(kt_ref[:, rows], ds)
            if last:
                dq = dq * 0.125
                a, b = dq[:half], dq[half:]
                cos, sin = cos_ref[...], sin_ref[...]
                outs += [a * cos + b * sin, b * cos - a * sin]
            else:
                sum_ref[rows_h, :] = dq
        if last:
            dq_ref[:, pl.ds(pl.multiple_of(pair * 128, 128), 128)] = (
                jnp.concatenate(outs, 0).T.astype(BF)
            )

    for n in range(blocks):
        rows = slice(n * span, (n + 1) * span)
        dkv_ref[rows, :] = jnp.concatenate([dk_ref[rows, :], dv_ref[rows, :]], 1).astype(dkv_ref.dtype)


def weight_grads_kernel(odd_ref, *refs):
    one_ref, two_ref, out_ref = refs[10:]
    count = refs[0].shape[0]

    def cotangent(n):
        at = pl.multiple_of(cotangent_at(odd_ref, n) * count, count)
        return refs[8 + n // 4][pl.ds(at, count), :]

    at = 0
    for lefts, ref in (
        ([left[...] for left in refs[:8]], one_ref), ([cotangent(n) for n in range(8)], two_ref)
    ):
        turned = jnp.concatenate(lefts, 0).T
        for c in range(0, ref.shape[1], 256):
            size = min(256, ref.shape[1] - c)
            out_ref[:, at + c : at + c + size] = mm(turned, ref[:, c : c + size]).astype(BF)
        at += ref.shape[1]


def params(mib):
    return pltpu.CompilerParams(vmem_limit_bytes=mib * MIB)


def whole(count):
    return [pl.BlockSpec(memory_space=pltpu.VMEM)] * count


def cost(products, moved):
    return pl.CostEstimate(flops=2 * products, bytes_accessed=moved, transcendentals=0)


def call(kernel, name, shapes, operands, scalars=0, products=0, mib=16):
    return pl.pallas_call(
        kernel,
        out_shape=tuple(jax.ShapeDtypeStruct(*shape) for shape in shapes),
        in_specs=scalar() * scalars + whole(len(operands) - scalars),
        out_specs=tuple(whole(len(shapes))),
        compiler_params=params(mib),
        cost_estimate=cost(products, 4 << 20),
        name=name,
    )(*operands)


def hidden_units(odd, pieces, cots, weights, width):
    count, d = pieces[0].shape
    span = 8 * count
    both, down = 2 * width + 128, width + 128
    return pl.pallas_call(
        functools.partial(hidden_kernel, width),
        out_shape=(jax.ShapeDtypeStruct((span, down), BF), jax.ShapeDtypeStruct((span, both), BF)),
        in_specs=scalar() + [pl.BlockSpec(memory_space=pl.ANY)] * 11,
        out_specs=tuple(whole(2)),
        scratch_shapes=[
            pltpu.VMEM((span, d), BF),
            pltpu.VMEM((span, d), BF),
            pltpu.VMEM((d, both), BF),
            pltpu.VMEM((d, down), BF),
            pltpu.SemaphoreType.DMA((18,)),
        ],
        compiler_params=params(56),
        cost_estimate=cost(3 * span * d * width, 6 * d * width),
        name="hidden_units",
    )(odd, *pieces, *cots, weights)


def feature_rows(weight, tile):
    if not isinstance(weight, tuple):
        return pl.BlockSpec((tile, weight.shape[1]), lambda i: (i, 0))
    return pl.BlockSpec((pl.Element(tile), pl.Element(weight[2])), lambda i: (i * tile, weight[1]))


def array_of(weight):
    return weight[0] if isinstance(weight, tuple) else weight


def fixed(array):
    return pl.BlockSpec(array.shape, lambda i: (0, 0))


def rows_grad(grads, weights, terms, pieces, gains, gain_row):
    span, d = 4 * pieces[0].shape[0], pieces[0].shape[1]
    tile = 512
    n = len(grads)
    terms = [(g, c, n + w, e) for g, c, w, e in terms]
    return pl.pallas_call(
        functools.partial(rows_grad_kernel, terms, n + len(weights), gain_row),
        grid=(d // tile,),
        out_shape=tuple(jax.ShapeDtypeStruct((span // n, d), BF) for n in (4, 4, 2)),
        in_specs=[fixed(g) for g in grads]
        + [feature_rows(w, tile) for w in weights]
        + [fixed(a) for a in (*pieces, gains)],
        out_specs=tuple(pl.BlockSpec((span // n, d), lambda i: (0, 0)) for n in (4, 4, 2)),
        scratch_shapes=[pltpu.VMEM((span, d), F32)],
        compiler_params=params(32),
        cost_estimate=cost(0, 0),
        name="rows_grad",
    )(*grads, *map(array_of, weights), *pieces, gains)


def rows_out(lefts, weights, terms, tile, places, mib):
    span, d = lefts[0].shape[0], array_of(weights[0]).shape[0]
    n = len(lefts)
    terms = [(g, c, n + w, e) for g, c, w, e in terms]
    size = span // sum(len(held) for held in places)
    return pl.pallas_call(
        functools.partial(rows_out_kernel, terms, places),
        grid=(d // tile,),
        out_shape=tuple(jax.ShapeDtypeStruct((len(held) * size, d), BF) for held in places),
        in_specs=[fixed(g) for g in lefts] + [feature_rows(w, tile) for w in weights],
        out_specs=tuple(pl.BlockSpec((len(held) * size, tile), lambda i: (0, i)) for held in places),
        compiler_params=params(mib),
        cost_estimate=cost(sum(span * d * (c[1] - c[0]) for _, c, _, _ in terms), 6 << 20),
        name="rows_out",
    )(*lefts, *map(array_of, weights))


def scalar():
    return [pl.BlockSpec(memory_space=pltpu.SMEM)]


def at_place(axis):
    return place(axis).astype(jnp.int32).reshape(1, 1)


def wide_parts(lefts, right, columns, axis):
    span, d = right.shape[0], lefts[0].shape[1]
    width = columns[1] - columns[0]
    return pl.pallas_call(
        functools.partial(parts_kernel, axis, columns, len(lefts)),
        out_shape=(jax.ShapeDtypeStruct((d // 4, width), BF),) * 4,
        in_specs=scalar() + whole(len(lefts) + 1),
        out_specs=tuple(whole(4)),
        compiler_params=params(20),
        cost_estimate=cost(span * d * width, 8 << 20),
        name="wide_parts",
    )(at_place(axis), *lefts, right)


def last_parts(left, dq, cut, own, arrived, cos, sin, axis):
    span, d = left.shape
    width = dq.shape[1] - cut + 2 * HD
    return pl.pallas_call(
        functools.partial(last_parts_kernel, axis, cut),
        out_shape=(jax.ShapeDtypeStruct((span, 2 * HD), BF),)
        + (jax.ShapeDtypeStruct((d // 4, width), BF),) * 4,
        in_specs=scalar() + whole(8),
        out_specs=tuple(whole(5)),
        compiler_params=params(20),
        cost_estimate=cost(0, 0),
        name="last_parts",
    )(at_place(axis), left, dq, own, *arrived, cos, sin)


def settle(base, parts, kind):
    return pl.pallas_call(
        settle_kernel,
        out_shape=jax.ShapeDtypeStruct(base.shape, kind),
        in_specs=whole(1 + len(parts)),
        out_specs=whole(1)[0],
        compiler_params=params(12),
        cost_estimate=cost(0, 4 << 20),
        name="settle",
    )(base, *parts)


def window_specs():
    return [pl.BlockSpec(memory_space=pltpu.SMEM)] + whole(1)


def attend(q, kvs, window):
    n = len(kvs)
    width, span = q.shape
    heads = width // HD
    return pl.pallas_call(
        attend_kernel,
        out_shape=(
            jax.ShapeDtypeStruct((span, width), BF),
            jax.ShapeDtypeStruct((heads, span), F32),
        ),
        in_specs=whole(n + 1) + window_specs(),
        out_specs=tuple(whole(2)),
        scratch_shapes=[
            pltpu.VMEM((n * span, span), F32),
            pltpu.VMEM((n * span, span), F32),
            pltpu.VMEM((HD, n * span), BF),
        ],
        compiler_params=params(32),
        cost_estimate=cost(30 * 580_000_000, 2 << 20),
        name="attend",
    )(q, *kvs, *window)


def attend_back(distances, q, kvs, window, lse, prepared, mixed=None, out=None, turn=None):
    n = len(kvs)
    width, span = q.shape
    heads = width // HD
    first, last = prepared is None, turn is not None
    operands = [q, *kvs, *window, lse]
    operands += [mixed, *out] if first else list(prepared)
    shapes = []
    if last:
        operands += turn
        shapes.append(jax.ShapeDtypeStruct((span, width), BF))
    else:
        shapes.append(jax.ShapeDtypeStruct((width, span), F32))
    shapes.append(jax.ShapeDtypeStruct((n * span, 2 * HD), F32 if last else BF))
    if first:
        shapes.append(jax.ShapeDtypeStruct((width, span), BF))
        shapes.append(jax.ShapeDtypeStruct((heads, span), F32))
    specs = whole(n + 1) + window_specs() + whole(len(operands) - n - 3)
    return pl.pallas_call(
        functools.partial(attend_back_kernel, distances, first, last),
        out_shape=tuple(shapes),
        in_specs=specs,
        out_specs=tuple(whole(len(shapes))),
        scratch_shapes=[
            pltpu.VMEM((n * span, span), F32),
            pltpu.VMEM((n * span, HD), BF),
            pltpu.VMEM((HD, n * span), BF),
            pltpu.VMEM((n * span, HD), F32),
            pltpu.VMEM((n * span, HD), F32),
        ],
        compiler_params=params(40),
        cost_estimate=cost(110 * 580_000_000 if first else 0, 1 << 20),
        name="attend_back",
    )(*operands)


def weight_grads(odd, xs, cots, one, two):
    t, d = xs[0].shape
    tile = 256
    rows = pl.BlockSpec((t, tile), lambda i: (0, i))
    width = one.shape[1] + two.shape[1]
    return pl.pallas_call(
        weight_grads_kernel,
        grid=(d // tile,),
        out_shape=jax.ShapeDtypeStruct((d, width), BF),
        in_specs=scalar()
        + [rows] * 8
        + [pl.BlockSpec((4 * t, tile), lambda i: (0, i))] * 2
        + [fixed(one), fixed(two)],
        out_specs=pl.BlockSpec((tile, width), lambda i: (i, 0)),
        compiler_params=params(56),
        cost_estimate=cost(8 * t * d * width, 2 * d * width + 32 * t * d),
        name="weight_grads",
    )(odd, *xs, *cots, one, two)


def per_device(
    inputs,
    positions,
    attn_gain,
    query_weight,
    key_weight,
    value_weight,
    out_weight,
    mlp_gain,
    gate_weight,
    up_weight,
    down_weight,
    cotangent,
):
    width_q = query_weight.shape[1]
    width_k = key_weight.shape[1]
    hidden_width = gate_weight.shape[1]
    span = positions.shape[0]
    quarter = span // 4
    cut = 3 * width_q // 4
    d = inputs.shape[1]
    shard = query_weight.shape[0]
    side = place("yh").astype(jnp.int32).reshape(1, 1)

    units = 128 * (hidden_width // 256)
    both_width, down_width = 2 * units + 128, units + 128
    inputs, cotangent, shard_kv, shard_mlp = call(
        pack_kernel, "pack",
        [(inputs.shape, BF), (inputs.shape, BF), ((shard, 256), BF),
         ((2, shard, both_width + down_width), BF)],
        [inputs, cotangent, attn_gain[None], mlp_gain[None], key_weight, value_weight,
         gate_weight, up_weight, down_weight.T],
        mib=56,
    )
    shard_first = jnp.concatenate([query_weight, out_weight.T], 1)
    other_first, other_kv = swap(shard_first, "yh"), swap(shard_kv, "yh")
    pair_first = join_sides(shard_first, after(other_first, shard_kv))
    first_whole = lax.all_gather(pair_first, ("z", "x"), axis=0, tiled=True)
    pair_kv = join_sides(shard_kv, other_kv)
    along_kv = send_stage(pair_kv, "x")
    rows_in = gather_rows(after(inputs, other_kv))
    kv_whole = flat(stack_stage(send_stage(stack_stage(along_kv, "x", 0), "z"), "z", 0))

    me = (lax.axis_index("yl") * 2 + lax.axis_index("core")).astype(jnp.int32)
    blocked = jnp.arange(4, dtype=jnp.int32) ^ me
    positions = jnp.take(positions.reshape(4, quarter), blocked, axis=0, mode="clip").reshape(1, span)
    freqs = 10000.0 ** (-(jnp.arange(HD // 2, dtype=F32) * 2.0) / HD)
    angles = freqs[:, None] * positions.astype(F32)
    cos, sin = jnp.cos(angles), jnp.sin(angles)
    window = (me.reshape(1, 1), positions)

    kv_block, scaled_in, gains = call(
        keys_values_kernel, "keys_values",
        [((span, 2 * width_k), BF), ((span, d), BF), ((8, d), F32)],
        [*rows_in, kv_whole, cos, sin], products=span * d * 2 * width_k,
    )
    (queries,) = call(
        queries_kernel, "queries",
        [((width_q, span), BF)],
        [scaled_in, after(first_whole, kv_block), cos, sin], products=span * d * width_q,
    )
    blocks = [kv_block] + [shift(kv_block, "x", d) for d in range(1, SEQ_DEVS)]
    cot_yl = swap(after(cotangent, kv_block), "yl")
    cot_near = jnp.concatenate([cotangent, cot_yl], 0)
    cot_far = swap(cot_near, "yh")
    other_mlp = swap(after(pick(shard_mlp, place("yh", 1), 0), kv_block), "yh")
    mlp_pair = join_sides(pick(shard_mlp, place("yh"), 0), after(other_mlp, first_whole, blocks[1:], cot_near))
    mlp_whole = lax.all_gather(mlp_pair, ("z", "x"), axis=0, tiled=True)
    odd = place("yl").astype(jnp.int32).reshape(1, 1)
    mixed, log_total = attend(queries, blocks, window)

    cot_far = after(cot_far, log_total)
    cotangents = jnp.concatenate([after(cot_near, log_total), cot_far], 0)
    all_heads = (0, width_q)
    attn_rows = rows_out(
        [after(mixed, cot_far)], [(first_whole, width_q, width_q)], [(0, all_heads, 0, all_heads)],
        1024, [(0,), (2,), (1, 3)], 24,
    )
    cotangents = [cotangents, swap(cotangents, "core")]
    middle, scaled_mid = call(
        middle_kernel, "middle", [(inputs.shape, F32), (inputs.shape, BF)],
        [inputs, *scatter_rows(attn_rows), gains],
    )
    scaled_all = gather_eight(scaled_mid)
    hidden, grad_both = hidden_units(odd, scaled_all, cotangents, mlp_whole, units)
    mid_partial = rows_out(
        [grad_both], [(mlp_whole, 0, both_width)], [(0, (0, both_width), 0, (0, both_width))], 512, [(0, 1, 2, 3), (4, 5, 6, 7)], 56,
    )
    mid_own, mid_others = scatter_eight(*mid_partial)
    mid_arrived = send_back(mid_others)
    mlp_sum = weight_grads(
        odd, [after(scaled_all[0], mid_others), *scaled_all[1:]], cotangents, grad_both, hidden
    )
    mlp_rows = rows_out(
        [after(hidden, mlp_sum)], [(mlp_whole, both_width, down_width)],
        [(0, (0, down_width), 0, (0, down_width))], 512, [(0, 1, 2, 3), (4, 5, 6, 7)], 56,
    )
    grad_middle, grad_middle_low = call(
        middle_grad_kernel, "middle_grad", [(inputs.shape, F32), (inputs.shape, BF)],
        [cotangent, mid_own, *after(mid_arrived, mlp_rows), middle, gains],
    )
    rows_grad_middle = gather_rows(grad_middle_low)
    mlp_sum = lax.psum_scatter(mlp_sum, ("z", "x"), scatter_dimension=0, tiled=True)

    out_parts = wide_parts(rows_grad_middle, mixed, (0, width_q), "z")
    mlp_cores = swap(after(mlp_rows[1], grad_middle_low), "core")
    mlp_own, mlp_beside, mlp_far = call(
        pair_pieces_kernel, "pair_pieces",
        [(inputs.shape, F32), ((2 * quarter, d), BF), (inputs.shape, BF)],
        [odd, mlp_rows[0], mlp_cores], scalars=1,
    )
    query_part, far_grads, grad_turned, delta = attend_back(
        (1, 2, 3), queries, blocks[1:], window, log_total, None, after(mixed, out_parts, mlp_beside),
        [first_whole, *rows_grad_middle],
    )
    mlp_arrived = after(swap(after(mlp_beside, rows_grad_middle), "yl"), query_part)
    mlp_far = (mlp_far.astype(F32) + mlp_arrived[quarter:].astype(F32)).astype(BF)
    arriving = [
        shift(far_grads[(d - 1) * span : d * span], "x", -d) for d in range(1, SEQ_DEVS)
    ]
    out_arrived = [shift(out_parts[n], "z", n) for n in (2, 1, 3)]
    query_raw_grad, own_grads = attend_back(
        (0,), after(queries, mlp_far), blocks[:1], window, log_total, (grad_turned, delta, query_part), turn=[cos, sin]
    )

    out_sum = total(out_parts[0].astype(F32), after(out_arrived, query_raw_grad)).astype(BF)
    output = settle(
        middle, [mlp_own, mlp_arrived[:quarter], after(swap(mlp_far, "yh"), query_raw_grad)], BF
    )
    a_parts = wide_parts([scaled_in], after(query_raw_grad, arriving, out_arrived), (0, cut), "x")
    a_arrived = [shift(a_parts[n], "x", n) for n in (2, 1, 3)]
    kv_raw_grad, *b_parts = last_parts(
        scaled_in, after(query_raw_grad, a_parts), cut, own_grads, arriving, cos, sin, "z"
    )
    b_arrived = [shift(b_parts[n], "z", n) for n in (2, 1, 3)]
    in_partial = rows_grad(
        [query_raw_grad, kv_raw_grad],
        [(first_whole, 0, width_q), kv_whole],
        [(0, all_heads, 0, all_heads), (1, (0, 2 * width_k), 1, (0, 2 * width_k))],
        rows_in, gains, 0,
    )
    in_own, in_across, in_cores = in_partial
    in_parts = scatter_rows((in_own, in_across, after(in_cores, a_arrived, b_arrived)))
    input_grad = settle(grad_middle, in_parts, F32)

    mlp_send = pick(mlp_sum.reshape(2, shard, -1), place("yh", 1), 0)
    a_sum = wide_sum_next(total(a_parts[0].astype(F32), a_arrived).astype(BF), "z")
    b_sum = total(b_parts[0].astype(F32), b_arrived).astype(BF)
    b_sum = wide_sum_next(jnp.concatenate([b_sum, out_sum], 1), "x", hold=[mlp_send])
    sides = jnp.concatenate([a_sum, b_sum], 1)
    other_sides = swap(pick(sides.reshape(2, shard, -1), place("yh", 1), 0), "yh")
    query_grad, key_grad, value_grad, out_grad = call(
        finish_attn_kernel, "finish_attn",
        [(query_weight.shape, F32), (key_weight.shape, F32), (value_weight.shape, F32),
         (out_weight.shape[::-1], F32)],
        [side, sides, other_sides], scalars=1,
    )
    gate_grad, up_grad, down_grad = call(
        finish_mlp_kernel, "finish_mlp",
        [(gate_weight.shape, F32), (up_weight.shape, F32), (down_weight.shape[::-1], F32)],
        [side, mlp_sum, swap(mlp_send, "yh")], scalars=1,
    )

    ends = width_q - cut
    attn_weights = jnp.concatenate([pair_first[:, :width_q], pair_kv[:, : 2 * width_k]], 1).astype(F32)
    gain_parts = jnp.stack(
        [
            jnp.sum(attn_weights * sides[:, : cut + ends + 2 * width_k].astype(F32), 1),
            jnp.sum(
                mlp_pair[:, :both_width].astype(F32) * mlp_sum[:, :both_width].astype(F32),
                1,
            ),
        ]
    )
    gain_parts = lax.psum(gain_parts, ("yh",) + TP)
    own_gains = pick(gain_parts.reshape(2, 2, shard), place("yh"), 1)
    return (
        output,
        input_grad,
        own_gains[0] / attn_gain.astype(F32),
        query_grad,
        key_grad,
        value_grad,
        out_grad.T,
        own_gains[1] / mlp_gain.astype(F32),
        gate_grad,
        up_grad,
        down_grad.T,
    )


def solution(mesh):
    split = Mesh(mesh.devices.reshape(2, 4, 4, 2, 2), WIDE + TP)
    rows = P(WIDE + TP, None)
    inward = P(WIDE, TP)
    outward = P(TP, WIDE)
    gain = P(WIDE)
    return jax.shard_map(
        per_device,
        mesh=split,
        in_specs=(
            rows, gain, gain, inward, inward, inward, outward, gain, inward, inward, outward, rows,
        ),
        out_specs=(
            rows, rows, gain, inward, inward, inward, outward, gain, inward, inward, outward,
        ),
        check_vma=False,
    )
```

```python
import functools

import jax
import jax.numpy as jnp
from jax import lax
from jax.experimental import pallas as pl
from jax.experimental.pallas import tpu as pltpu
from jax.sharding import Mesh, PartitionSpec as P

HEADS = 32
KV = 4
HD = 64
SEQ_DEVS = 4
WIDE = ("yh", "z", "x")
TP = ("yl", "core")
RING = ("yh", "yl")
BF = jnp.bfloat16
F32 = jnp.float32

epsilon = 1e-05
masked_fill = -1e30
MIB = 1024 * 1024


def after(value, *earlier):
    return lax.optimization_barrier((value, earlier))[0]


def shift(block, axis, distance):
    n = 4 if axis == RING else lax.axis_size(axis)
    return lax.ppermute(block, axis, [(i, (i + distance) % n) for i in range(n)])


def swap(block, axis):
    return shift(block, axis, 1)


def place(axis, step=0):
    n = lax.axis_size(axis)
    return ((lax.axis_index(axis) + (step + n)) & (n - 1)).astype(jnp.uint32)


def pick(array, index, dim):
    return lax.dynamic_index_in_dim(array, index, dim, keepdims=False)


def send_stage(block, axis):
    n = lax.axis_size(axis)
    return [block] + [shift(block, axis, d) for d in (1, n - 1, *range(2, n - 1))]


def stack_stage(arrived, axis, dim):
    n = len(arrived)
    block = arrived[0]
    out = jnp.zeros(block.shape[:dim] + (n,) + block.shape[dim:], block.dtype)
    for d, piece in zip((0, 1, n - 1, *range(2, n - 1)), arrived):
        out = lax.dynamic_update_index_in_dim(out, piece, place(axis, -d), dim)
    return out


def join_sides(shard, other):
    first = lax.axis_index("yh") == 0
    return jnp.concatenate([jnp.where(first, shard, other), jnp.where(first, other, shard)], 0)


def flat(blocks):
    return blocks.reshape(-1, blocks.shape[-1])


def gather_rows(rows):
    across = swap(rows, "yl")
    return [rows, swap(rows, "core"), across, swap(across, "core")]


def gather_eight(rows):
    near = [rows, shift(rows, RING, 1), shift(rows, RING, 2), shift(rows, RING, -1)]
    return near + [swap(piece, "core") for piece in near]


def scatter_eight(own_core, other_core):
    quarter, d = own_core.shape[0] // 4, own_core.shape[1]
    own, *others = call(
        add_pieces_kernel, "add_pieces",
        [((quarter, d), F32)] + [((quarter, d), BF)] * 3, [own_core, swap(other_core, "core")],
    )
    return own, others


def send_back(others):
    one, two, three = others
    return [shift(one, RING, -1), shift(three, RING, 1), shift(two, RING, 2)]


def scatter_rows(partial):
    own, across, cores = partial
    n = own.shape[0]
    arrived = swap(cores, "core")
    other = (across.astype(F32) + arrived[n:].astype(F32)).astype(BF)
    return [own, arrived[:n], swap(other, "yl")]


def total(first, parts):
    for part in parts:
        first = first + part.astype(F32)
    return first


def exchange_sum(parts, axis, hold=()):
    near = parts[0].astype(F32)
    for d in (1, 3):
        near = near + after(shift(parts[d], axis, d), *hold).astype(F32)
    return near + after(shift(parts[2], axis, 2), *hold).astype(F32)


def wide_sum_next(part, axis, hold=()):
    n = lax.axis_size(axis)
    part = part.reshape(n, part.shape[0] // n, part.shape[1])
    pieces = [pick(part, place(axis, d), 0) for d in range(n)]
    return exchange_sum(pieces, axis, hold).astype(BF)


def mm(left, right):
    return jnp.dot(left, right, preferred_element_type=F32)


def mm_last(left, right):
    return lax.dot_general(left, right, (((1,), (1,)), ((), ())), preferred_element_type=F32)


def normed_rows(piece):
    values = piece.astype(F32)
    factor = lax.rsqrt(jnp.mean(values * values, -1, keepdims=True) + epsilon)
    return values * factor, factor


def scale_rows(piece_refs, gain, scaled_ref):
    for n, ref in enumerate(piece_refs):
        for at in range(0, ref.shape[0], 32):
            normed, _ = normed_rows(ref[at : at + 32, :])
            rows = n * ref.shape[0] + at
            scaled_ref[rows : rows + 32, :] = (normed * gain).astype(BF)


def turned(block, cos, sin):
    a, b = block[: HD // 2], block[HD // 2 :]
    return jnp.concatenate([a * cos - b * sin, b * cos + a * sin], 0)


def keys_values_kernel(*refs):
    piece_refs, (w_ref, cos_ref, sin_ref, kv_ref, scaled_ref, gains_ref) = refs[:4], refs[4:]
    gains_ref[...] = w_ref[:, 128:].T[:8].astype(F32)
    scale_rows(piece_refs, gains_ref[0:1, :], scaled_ref)
    both = mm(scaled_ref[...], w_ref[:, :128]).T
    keys = turned(both[:HD], cos_ref[...], sin_ref[...])
    kv_ref[...] = jnp.concatenate([keys, both[HD:]], 0).T.astype(BF)


def queries_kernel(x_ref, w_ref, cos_ref, sin_ref, q_ref):
    for at in range(0, q_ref.shape[0], 256):
        piece = mm(x_ref[...], w_ref[:, at : at + 256]).T
        for sub in range(0, 256, HD):
            low = turned(piece[sub : sub + HD], cos_ref[...], sin_ref[...]).astype(BF)
            q_ref[at + sub : at + sub + HD, :] = low * 0.125


def to_inner(ref, out_ref):
    half = ref.shape[1] // 2
    for at in range(0, half, 128):
        low, high = ref[:, at : at + 128], ref[:, half + at : half + at + 128]
        out_ref[:, 2 * at : 2 * at + 128] = jnp.concatenate([low[:, :HD], high[:, :HD]], 1)
        out_ref[:, 2 * at + 128 : 2 * at + 256] = jnp.concatenate([low[:, HD:], high[:, HD:]], 1)


def pack_kernel(inputs_ref, cot_ref, again_ref, mgain_ref, k_ref, v_ref, g_ref, u_ref, d_ref,
                rows_ref, cots_ref, kv_ref, mlp_ref):
    to_inner(inputs_ref, rows_ref)
    to_inner(cot_ref, cots_ref)
    kv_ref[:, :128] = jnp.concatenate([k_ref[...], v_ref[...]], 1)
    gains = jnp.concatenate(
        [again_ref[...].astype(F32), mgain_ref[...].astype(F32), jnp.zeros((126, HD), F32)], 0
    )
    kv_ref[:, 128:] = gains.T.astype(BF)
    width = g_ref.shape[1]
    down = d_ref[...]
    whole_units = 128 * (width // 256)
    tail = 2 * whole_units
    for side in range(2):
        units = slice(side * whole_units, (side + 1) * whole_units)
        ends = slice(tail + 64 * side, tail + 64 * side + 64)
        mlp_ref[side, :, :whole_units] = g_ref[:, units]
        mlp_ref[side, :, whole_units:tail] = u_ref[:, units]
        mlp_ref[side, :, tail : tail + 128] = jnp.concatenate([g_ref[:, ends], u_ref[:, ends]], 1)
        mlp_ref[side, :, tail + 128 : tail + 128 + whole_units] = down[:, units]
        mlp_ref[side, :, tail + 128 + whole_units :] = jnp.concatenate(
            [down[:, ends], jnp.zeros_like(down[:, ends])], 1
        )


def finish_mlp_kernel(side_ref, pair_ref, other_ref, gate_ref, up_ref, down_ref):
    rows = pl.ds(pl.multiple_of(side_ref[0, 0] * HD, HD), HD)
    own, other = pair_ref[rows, :].astype(F32), other_ref[...].astype(F32)
    here = side_ref[0, 0] == 0
    halves = jnp.where(here, own, other), jnp.where(here, other, own)
    units = 128 * (gate_ref.shape[1] // 256)
    tail = 2 * units
    down = []
    for n, half in enumerate(halves):
        gate_ref[:, n * units : (n + 1) * units] = half[:, :units]
        up_ref[:, n * units : (n + 1) * units] = half[:, units:tail]
        down.append(half[:, tail + 128 : tail + 128 + units])
    ends = [half[:, tail : tail + 128] for half in halves]
    gate_ref[:, tail:] = jnp.concatenate([end[:, :64] for end in ends], 1)
    up_ref[:, tail:] = jnp.concatenate([end[:, 64:] for end in ends], 1)
    down += [half[:, tail + 128 + units : tail + 192 + units] for half in halves]
    for n in range(2):
        down_ref[:, n * units : (n + 1) * units] = down[n]
    down_ref[:, tail:] = jnp.concatenate(down[2:], 1)


def finish_attn_kernel(side_ref, pair_ref, other_ref, q_ref, k_ref, v_ref, o_ref):
    rows = pl.ds(pl.multiple_of(side_ref[0, 0] * HD, HD), HD)
    both = pair_ref[rows, :].astype(F32) + other_ref[...].astype(F32)
    width = q_ref.shape[1]
    q_ref[...] = both[:, :width]
    k_ref[...] = both[:, width : width + HD]
    v_ref[...] = both[:, width + HD : width + 2 * HD]
    o_ref[...] = both[:, width + 2 * HD :]


def add_pieces_kernel(one_ref, two_ref, *outs):
    for n, out in enumerate(outs):
        rows = slice(n * out.shape[0], (n + 1) * out.shape[0])
        out[...] = (one_ref[rows, :].astype(F32) + two_ref[rows, :].astype(F32)).astype(out.dtype)


def pair_pieces_kernel(odd_ref, one_ref, two_ref, own_ref, beside_ref, far_ref):
    size = own_ref.shape[0]
    back = 3 - 2 * odd_ref[0, 0]
    for out, at, step in (
        (own_ref, 0, 0), (beside_ref, 0, back), (beside_ref, size, 4 - back), (far_ref, 0, 2)
    ):
        rows = pl.ds(pl.multiple_of(step * size, size), size)
        value = one_ref[rows, :].astype(F32) + two_ref[rows, :].astype(F32)
        out[at : at + size, :] = value.astype(out.dtype)


def middle_kernel(base_ref, *refs):
    parts, (gain_ref, sum_ref, scaled_ref) = refs[:-3], refs[-3:]
    for at in range(0, base_ref.shape[0], 32):
        rows = slice(at, at + 32)
        value = base_ref[rows, :].astype(F32)
        for ref in parts:
            value = value + ref[rows, :].astype(F32)
        sum_ref[rows, :] = value
        normed, _ = normed_rows(value.astype(BF))
        scaled_ref[rows, :] = (normed * gain_ref[1:2, :]).astype(BF)


def middle_grad_kernel(base_ref, *refs):
    parts, (middle_ref, gain_ref, sum_ref, low_ref) = refs[:-4], refs[-4:]
    for at in range(0, base_ref.shape[0], 32):
        rows = slice(at, at + 32)
        value = parts[0][rows, :].astype(F32)
        for ref in parts[1:]:
            value = value + ref[rows, :].astype(F32)
        normed, factor = normed_rows(middle_ref[rows, :].astype(BF))
        value = value * gain_ref[1:2, :]
        inner = jnp.mean(value * normed, -1, keepdims=True)
        value = base_ref[rows, :].astype(F32) + factor * (value - normed * inner)
        sum_ref[rows, :] = value
        low_ref[rows, :] = value.astype(BF)


def cotangent_at(odd_ref, n):
    return (0, 3 - 2 * odd_ref[0, 0], 2, 1 + 2 * odd_ref[0, 0])[n % 4]


def hidden_kernel(width, odd_ref, *refs):
    (w_ref, hidden_ref, both_ref, x_ref, c_ref, gate_up_ref, down_ref, sems) = refs[10:]
    first = gate_up_ref.shape[1]
    copies = [
        pltpu.make_async_copy(w_ref.at[:, pl.ds(0, first)], gate_up_ref, sems.at[0]),
        pltpu.make_async_copy(w_ref.at[:, pl.ds(first, down_ref.shape[1])], down_ref, sems.at[1]),
    ]
    count = x_ref.shape[0] // 8
    for n in range(8):
        rows = pl.ds(n * count, count)
        copies.append(pltpu.make_async_copy(refs[n], x_ref.at[rows, :], sems.at[2 + n]))
        at = pl.ds(pl.multiple_of(cotangent_at(odd_ref, n) * count, count), count)
        copies.append(
            pltpu.make_async_copy(refs[8 + n // 4].at[at, :], c_ref.at[rows, :], sems.at[10 + n])
        )
    weights_up, weights_down, *pieces = copies
    xs, cots = pieces[::2], pieces[1::2]
    for copy in (*xs[:4], weights_up, *xs[4:], weights_down, *cots):
        copy.start()

    def units(gate, up, grad):
        sigmoid = 1.0 / (1.0 + jnp.exp(-gate))
        gated = gate * sigmoid
        return (
            (gated * up).astype(BF),
            (grad * up * sigmoid * (1.0 + gate * (1.0 - sigmoid))).astype(BF),
            (grad * gated).astype(BF),
        )

    half = 4 * count
    for part in range(2):
        rows = slice(part * half, (part + 1) * half)
        for copy in xs[4 * part : 4 * part + 4]:
            copy.wait()
        if part == 0:
            weights_up.wait()
        x = x_ref[rows, :]
        gate = mm(x, gate_up_ref[:, :width])
        up = mm(x, gate_up_ref[:, width : 2 * width])
        ends = mm(x, gate_up_ref[:, 2 * width :])
        for copy in cots[4 * part : 4 * part + 4]:
            copy.wait()
        if part == 0:
            weights_down.wait()
        c = c_ref[rows, :]
        value, dgate, dup = units(gate, up, mm(c, down_ref[:, :width]))
        hidden_ref[rows, :width] = value
        both_ref[rows, :width] = dgate
        both_ref[rows, width : 2 * width] = dup
        value, dgate, dup = units(ends[:, :64], ends[:, 64:], mm(c, down_ref[:, width:])[:, :64])
        hidden_ref[rows, width:] = jnp.concatenate([value, jnp.zeros_like(value)], 1)
        both_ref[rows, 2 * width :] = jnp.concatenate([dgate, dup], 1)


def sum_of_products(terms, refs):
    total = None
    for left, (low, high), right, (first, last) in terms:
        part = mm_last(refs[left][:, low:high], refs[right][:, first:last])
        total = part if total is None else total + part
    return total


def rows_grad_kernel(terms, count, gain_row, *refs):
    pieces, gain_ref, outs, sum_ref = refs[count : count + 4], refs[count + 4], refs[count + 5 : -1], refs[-1]
    own_ref, across_ref, cores_ref = outs
    size = own_ref.shape[0]
    outs = [own_ref, cores_ref.at[pl.ds(0, size), :], across_ref, cores_ref.at[pl.ds(size, size), :]]
    step = pl.program_id(0)
    tile = sum_ref.shape[1] // pl.num_programs(0)
    columns = pl.ds(pl.multiple_of(step * tile, tile), tile)
    sum_ref[:, columns] = sum_of_products(terms, refs) * gain_ref[gain_row : gain_row + 1, columns]

    @pl.when(step == pl.num_programs(0) - 1)
    def _():
        for n, ref in enumerate(pieces):
            for at in range(0, ref.shape[0], 32):
                normed, factor = normed_rows(ref[at : at + 32, :])
                scaled = sum_ref[n * ref.shape[0] + at : n * ref.shape[0] + at + 32, :]
                inner = jnp.mean(scaled * normed, -1, keepdims=True)
                outs[n][at : at + 32, :] = (factor * (scaled - normed * inner)).astype(BF)


def rows_out_kernel(terms, places, *refs):
    value = sum_of_products(terms, refs).astype(BF)
    outs = refs[len(refs) - len(places) :]
    size = value.shape[0] // sum(len(held) for held in places)
    for out, held in zip(outs, places):
        for n, piece in enumerate(held):
            out[n * size : (n + 1) * size, :] = value[piece * size : (piece + 1) * size]


def write_parts(outs, turned_of, axis, me, right, base):
    for d, out in enumerate(outs):
        index = (me + d) & 3
        if axis == "z":
            turned = turned_of(pl.multiple_of(index * 512, 512), 512)
        else:
            turned = jnp.concatenate(
                [turned_of(pl.multiple_of(z * 512 + index * 128, 128), 128) for z in range(4)], 0
            )
        out[:, base : base + right.shape[1]] = mm(turned, right).astype(BF)


def parts_kernel(axis, columns, count, me_ref, *refs):
    lefts, right_ref, outs = refs[:count], refs[count], refs[count + 1 :]

    def turned_of(at, size):
        return jnp.concatenate([left[:, pl.ds(at, size)] for left in lefts], 0).T

    write_parts(outs, turned_of, axis, me_ref[0, 0], right_ref[:, columns[0] : columns[1]], 0)


def last_parts_kernel(axis, cut, me_ref, left_ref, dq_ref, own_ref, one_ref, two_ref, three_ref,
                      cos_ref, sin_ref, *outs):
    half = HD // 2
    cos, sin = cos_ref[...], sin_ref[...]
    kv = own_ref[...]
    for ref in (one_ref, two_ref, three_ref):
        kv = kv + ref[...].astype(F32)
    kv = kv.T
    a, b = kv[:half], kv[half:HD]
    kv = jnp.concatenate([a * cos + b * sin, b * cos - a * sin, kv[HD:]], 0).T.astype(BF)
    outs[0][...] = kv
    right = jnp.concatenate([dq_ref[:, cut:], kv], 1)

    def turned_of(at, size):
        return left_ref[:, pl.ds(at, size)].T

    write_parts(outs[1:], turned_of, axis, me_ref[0, 0], right, 0)


def settle_kernel(base_ref, *refs):
    out_ref = refs[-1]
    width = base_ref.shape[1]

    def block(at):
        value = base_ref[:, at : at + 128].astype(F32)
        for ref in refs[:-1]:
            value = value + ref[:, at : at + 128].astype(F32)
        return value

    for n in range(width // 256):
        one, two = block(256 * n), block(256 * n + 128)
        low = jnp.concatenate([one[:, :HD], two[:, :HD]], 1)
        high = jnp.concatenate([one[:, HD:], two[:, HD:]], 1)
        out_ref[:, 128 * n : 128 * n + 128] = low.astype(out_ref.dtype)
        out_ref[:, width // 2 + 128 * n : width // 2 + 128 * n + 128] = high.astype(out_ref.dtype)


def fill_bias(bias_ref, me_ref, pos_ref, span, distances):
    step = 64
    quarter = span // 4
    me = me_ref[0, 0]
    at = lax.broadcasted_iota(jnp.int32, (1, span), 1)
    query = (((at // quarter) ^ me) * quarter) + (at & (quarter - 1))
    first = query - pos_ref[...]

    @pl.loop(0, span // step)
    def _(i):
        block = (i * step) // quarter
        start = (block ^ me) * quarter + i * step - block * quarter
        key = start + lax.broadcasted_iota(jnp.int32, (step, span), 0)
        for n, d in enumerate(distances):
            seen = (key - d * span <= query) & (key - d * span >= first)
            bias_ref[pl.ds(pl.multiple_of(n * span + i * step, step), step), :] = jnp.where(
                seen, 0.0, masked_fill
            ).astype(F32)


def attend_kernel(q_ref, *refs):
    blocks = len(refs) - 7
    kv_refs = refs[:blocks]
    me_ref, pos_ref, mix_ref, lse_ref, bias_ref, s_ref, vt_ref = refs[blocks:]
    span = q_ref.shape[1]
    fill_bias(bias_ref, me_ref, pos_ref, span, range(blocks))
    for d in range(blocks):
        vt_ref[:, d * span : (d + 1) * span] = kv_refs[d][...].T[HD:]

    @pl.loop(0, q_ref.shape[0] // 128)
    def _(pair):
        outs = []
        for sub in range(2):
            q = q_ref[pl.ds(pl.multiple_of(pair * 128 + sub * HD, HD), HD), :]
            top = None
            for d in range(blocks):
                rows = slice(d * span, (d + 1) * span)
                s = mm(kv_refs[d][:, :HD], q) + bias_ref[rows, :]
                s_ref[rows, :] = s
                high = jnp.max(s, 0, keepdims=True)
                top = high if top is None else jnp.maximum(top, high)
            total = jnp.zeros_like(top)
            out = jnp.zeros((HD, span), F32)
            for d in range(blocks):
                rows = slice(d * span, (d + 1) * span)
                p = jnp.exp(s_ref[rows, :] - top)
                total = total + jnp.sum(p, 0, keepdims=True)
                out = out + mm(vt_ref[:, rows], p.astype(BF))
            outs.append(out / total)
            lse_ref[pl.ds(pair * 2 + sub, 1), :] = top + jnp.log(total)
        mix_ref[:, pl.ds(pl.multiple_of(pair * 128, 128), 128)] = (
            jnp.concatenate(outs, 0).T.astype(BF)
        )


def attend_back_kernel(distances, first, last, q_ref, *refs):
    blocks = len(distances)
    refs = list(refs)

    def take(count):
        got, refs[:count] = refs[:count], []
        return got

    kv_refs = take(blocks)
    me_ref, pos_ref, lse_ref = take(3)
    if first:
        mix_ref, w_ref, *piece_refs = take(6)
    else:
        gt_ref, delta_ref, part_ref = take(3)
    if last:
        cos_ref, sin_ref = take(2)
        (dq_ref,) = take(1)
    else:
        (sum_ref,) = take(1)
    (dkv_ref,) = take(1)
    if first:
        gt_ref, delta_ref = take(2)
    bias_ref, v_ref, kt_ref, dk_ref, dv_ref = take(5)
    span = q_ref.shape[1]
    half = HD // 2
    heads = q_ref.shape[0] // HD
    fill_bias(bias_ref, me_ref, pos_ref, span, distances)
    for n in range(blocks):
        rows = slice(n * span, (n + 1) * span)
        both = kv_refs[n][...].T
        kt_ref[:, rows] = both[:HD]
        v_ref[rows, :] = both[HD:].T
    dk_ref[...] = jnp.zeros_like(dk_ref)
    dv_ref[...] = jnp.zeros_like(dv_ref)
    if first:
        rows_all = jnp.concatenate([ref[...] for ref in piece_refs], 0)
        for at in range(0, heads * HD, 256):
            grads = mm(rows_all, w_ref[:, heads * HD + at : heads * HD + at + 256]).astype(BF).T
            gt_ref[at : at + 256, :] = grads
        for at in range(0, heads * HD, 128):
            gt = gt_ref[at : at + 128, :]
            mt = mix_ref[:, at : at + 128].T
            prod = gt.astype(F32) * mt.astype(F32)
            for sub in range(2):
                h = at // HD + sub
                delta_ref[h : h + 1, :] = jnp.sum(prod[sub * HD : (sub + 1) * HD], 0, keepdims=True)

    @pl.loop(0, heads // 2)
    def _(pair):
        outs = []
        for sub in range(2):
            rows_h = pl.ds(pl.multiple_of(pair * 128 + sub * HD, HD), HD)
            q, g = q_ref[rows_h, :], gt_ref[rows_h, :]
            lse = lse_ref[pl.ds(pair * 2 + sub, 1), :]
            delta = delta_ref[pl.ds(pair * 2 + sub, 1), :]
            dq = jnp.zeros((HD, span), F32) if first else part_ref[rows_h, :]
            for n in range(blocks):
                rows = slice(n * span, (n + 1) * span)
                s = mm(kv_refs[n][:, :HD], q) + bias_ref[rows, :]
                p = jnp.exp(s - lse)
                ds = (p * (mm(v_ref[rows, :], g) - delta)).astype(BF)
                dv_ref[rows, :] += mm_last(p.astype(BF), g)
                dk_ref[rows, :] += mm_last(ds, q)
                dq = dq + mm(kt_ref[:, rows], ds)
            if last:
                dq = dq * 0.125
                a, b = dq[:half], dq[half:]
                cos, sin = cos_ref[...], sin_ref[...]
                outs += [a * cos + b * sin, b * cos - a * sin]
            else:
                sum_ref[rows_h, :] = dq
        if last:
            dq_ref[:, pl.ds(pl.multiple_of(pair * 128, 128), 128)] = (
                jnp.concatenate(outs, 0).T.astype(BF)
            )

    for n in range(blocks):
        rows = slice(n * span, (n + 1) * span)
        dkv_ref[rows, :] = jnp.concatenate([dk_ref[rows, :], dv_ref[rows, :]], 1).astype(dkv_ref.dtype)


def weight_grads_kernel(odd_ref, *refs):
    one_ref, two_ref, out_ref = refs[10:]
    count = refs[0].shape[0]

    def cotangent(n):
        at = pl.multiple_of(cotangent_at(odd_ref, n) * count, count)
        return refs[8 + n // 4][pl.ds(at, count), :]

    at = 0
    for lefts, ref in (
        ([left[...] for left in refs[:8]], one_ref), ([cotangent(n) for n in range(8)], two_ref)
    ):
        turned = jnp.concatenate(lefts, 0).T
        for c in range(0, ref.shape[1], 256):
            size = min(256, ref.shape[1] - c)
            out_ref[:, at + c : at + c + size] = mm(turned, ref[:, c : c + size]).astype(BF)
        at += ref.shape[1]


def params(mib):
    return pltpu.CompilerParams(vmem_limit_bytes=mib * MIB)


def whole(count):
    return [pl.BlockSpec(memory_space=pltpu.VMEM)] * count


def cost(products, moved):
    return pl.CostEstimate(flops=2 * products, bytes_accessed=moved, transcendentals=0)


def call(kernel, name, shapes, operands, scalars=0, products=0, mib=16):
    return pl.pallas_call(
        kernel,
        out_shape=tuple(jax.ShapeDtypeStruct(*shape) for shape in shapes),
        in_specs=scalar() * scalars + whole(len(operands) - scalars),
        out_specs=tuple(whole(len(shapes))),
        compiler_params=params(mib),
        cost_estimate=cost(products, 4 << 20),
        name=name,
    )(*operands)


def hidden_units(odd, pieces, cots, weights, width):
    count, d = pieces[0].shape
    span = 8 * count
    both, down = 2 * width + 128, width + 128
    return pl.pallas_call(
        functools.partial(hidden_kernel, width),
        out_shape=(jax.ShapeDtypeStruct((span, down), BF), jax.ShapeDtypeStruct((span, both), BF)),
        in_specs=scalar() + [pl.BlockSpec(memory_space=pl.ANY)] * 11,
        out_specs=tuple(whole(2)),
        scratch_shapes=[
            pltpu.VMEM((span, d), BF),
            pltpu.VMEM((span, d), BF),
            pltpu.VMEM((d, both), BF),
            pltpu.VMEM((d, down), BF),
            pltpu.SemaphoreType.DMA((18,)),
        ],
        compiler_params=params(56),
        cost_estimate=cost(3 * span * d * width, 6 * d * width),
        name="hidden_units",
    )(odd, *pieces, *cots, weights)


def feature_rows(weight, tile):
    if not isinstance(weight, tuple):
        return pl.BlockSpec((tile, weight.shape[1]), lambda i: (i, 0))
    return pl.BlockSpec((pl.Element(tile), pl.Element(weight[2])), lambda i: (i * tile, weight[1]))


def array_of(weight):
    return weight[0] if isinstance(weight, tuple) else weight


def fixed(array):
    return pl.BlockSpec(array.shape, lambda i: (0, 0))


def rows_grad(grads, weights, terms, pieces, gains, gain_row):
    span, d = 4 * pieces[0].shape[0], pieces[0].shape[1]
    tile = 512
    n = len(grads)
    terms = [(g, c, n + w, e) for g, c, w, e in terms]
    return pl.pallas_call(
        functools.partial(rows_grad_kernel, terms, n + len(weights), gain_row),
        grid=(d // tile,),
        out_shape=tuple(jax.ShapeDtypeStruct((span // n, d), BF) for n in (4, 4, 2)),
        in_specs=[fixed(g) for g in grads]
        + [feature_rows(w, tile) for w in weights]
        + [fixed(a) for a in (*pieces, gains)],
        out_specs=tuple(pl.BlockSpec((span // n, d), lambda i: (0, 0)) for n in (4, 4, 2)),
        scratch_shapes=[pltpu.VMEM((span, d), F32)],
        compiler_params=params(32),
        cost_estimate=cost(0, 0),
        name="rows_grad",
    )(*grads, *map(array_of, weights), *pieces, gains)


def rows_out(lefts, weights, terms, tile, places, mib, part=(0, 1)):
    span, d = lefts[0].shape[0] // part[1], array_of(weights[0]).shape[0]
    n = len(lefts)
    terms = [(g, c, n + w, e) for g, c, w, e in terms]
    size = span // sum(len(held) for held in places)
    return pl.pallas_call(
        functools.partial(rows_out_kernel, terms, places),
        grid=(d // tile,),
        out_shape=tuple(jax.ShapeDtypeStruct((len(held) * size, d), BF) for held in places),
        in_specs=[pl.BlockSpec((span, g.shape[1]), lambda i: (part[0], 0)) for g in lefts]
        + [feature_rows(w, tile) for w in weights],
        out_specs=tuple(pl.BlockSpec((len(held) * size, tile), lambda i: (0, i)) for held in places),
        compiler_params=params(mib),
        cost_estimate=cost(sum(span * d * (c[1] - c[0]) for _, c, _, _ in terms), 6 << 20),
        name="rows_out",
    )(*lefts, *map(array_of, weights))


def scalar():
    return [pl.BlockSpec(memory_space=pltpu.SMEM)]


def at_place(axis):
    return place(axis).astype(jnp.int32).reshape(1, 1)


def wide_parts(lefts, right, columns, axis):
    span, d = right.shape[0], lefts[0].shape[1]
    width = columns[1] - columns[0]
    return pl.pallas_call(
        functools.partial(parts_kernel, axis, columns, len(lefts)),
        out_shape=(jax.ShapeDtypeStruct((d // 4, width), BF),) * 4,
        in_specs=scalar() + whole(len(lefts) + 1),
        out_specs=tuple(whole(4)),
        compiler_params=params(20),
        cost_estimate=cost(span * d * width, 8 << 20),
        name="wide_parts",
    )(at_place(axis), *lefts, right)


def last_parts(left, dq, cut, own, arrived, cos, sin, axis):
    span, d = left.shape
    width = dq.shape[1] - cut + 2 * HD
    return pl.pallas_call(
        functools.partial(last_parts_kernel, axis, cut),
        out_shape=(jax.ShapeDtypeStruct((span, 2 * HD), BF),)
        + (jax.ShapeDtypeStruct((d // 4, width), BF),) * 4,
        in_specs=scalar() + whole(8),
        out_specs=tuple(whole(5)),
        compiler_params=params(20),
        cost_estimate=cost(0, 0),
        name="last_parts",
    )(at_place(axis), left, dq, own, *arrived, cos, sin)


def settle(base, parts, kind):
    return pl.pallas_call(
        settle_kernel,
        out_shape=jax.ShapeDtypeStruct(base.shape, kind),
        in_specs=whole(1 + len(parts)),
        out_specs=whole(1)[0],
        compiler_params=params(12),
        cost_estimate=cost(0, 4 << 20),
        name="settle",
    )(base, *parts)


def window_specs():
    return [pl.BlockSpec(memory_space=pltpu.SMEM)] + whole(1)


def attend(q, kvs, window):
    n = len(kvs)
    width, span = q.shape
    heads = width // HD
    return pl.pallas_call(
        attend_kernel,
        out_shape=(
            jax.ShapeDtypeStruct((span, width), BF),
            jax.ShapeDtypeStruct((heads, span), F32),
        ),
        in_specs=whole(n + 1) + window_specs(),
        out_specs=tuple(whole(2)),
        scratch_shapes=[
            pltpu.VMEM((n * span, span), F32),
            pltpu.VMEM((n * span, span), F32),
            pltpu.VMEM((HD, n * span), BF),
        ],
        compiler_params=params(32),
        cost_estimate=cost(5 * 580_000_000, 1 << 20),
        name="attend",
    )(q, *kvs, *window)


def attend_back(distances, q, kvs, window, lse, prepared, mixed=None, out=None, turn=None):
    n = len(kvs)
    width, span = q.shape
    heads = width // HD
    first, last = prepared is None, turn is not None
    operands = [q, *kvs, *window, lse]
    operands += [mixed, *out] if first else list(prepared)
    shapes = []
    if last:
        operands += turn
        shapes.append(jax.ShapeDtypeStruct((span, width), BF))
    else:
        shapes.append(jax.ShapeDtypeStruct((width, span), F32))
    shapes.append(jax.ShapeDtypeStruct((n * span, 2 * HD), F32 if last else BF))
    if first:
        shapes.append(jax.ShapeDtypeStruct((width, span), BF))
        shapes.append(jax.ShapeDtypeStruct((heads, span), F32))
    specs = whole(n + 1) + window_specs() + whole(len(operands) - n - 3)
    return pl.pallas_call(
        functools.partial(attend_back_kernel, distances, first, last),
        out_shape=tuple(shapes),
        in_specs=specs,
        out_specs=tuple(whole(len(shapes))),
        scratch_shapes=[
            pltpu.VMEM((n * span, span), F32),
            pltpu.VMEM((n * span, HD), BF),
            pltpu.VMEM((HD, n * span), BF),
            pltpu.VMEM((n * span, HD), F32),
            pltpu.VMEM((n * span, HD), F32),
        ],
        compiler_params=params(40),
        cost_estimate=cost(110 * 580_000_000 if first else 0, 1 << 20),
        name="attend_back",
    )(*operands)


def weight_grads(odd, xs, cots, one, two):
    t, d = xs[0].shape
    tile = 256
    rows = pl.BlockSpec((t, tile), lambda i: (0, i))
    width = one.shape[1] + two.shape[1]
    return pl.pallas_call(
        weight_grads_kernel,
        grid=(d // tile,),
        out_shape=jax.ShapeDtypeStruct((d, width), BF),
        in_specs=scalar()
        + [rows] * 8
        + [pl.BlockSpec((4 * t, tile), lambda i: (0, i))] * 2
        + [fixed(one), fixed(two)],
        out_specs=pl.BlockSpec((tile, width), lambda i: (i, 0)),
        compiler_params=params(56),
        cost_estimate=cost(8 * t * d * width, 2 * d * width + 32 * t * d),
        name="weight_grads",
    )(odd, *xs, *cots, one, two)


def per_device(
    inputs,
    positions,
    attn_gain,
    query_weight,
    key_weight,
    value_weight,
    out_weight,
    mlp_gain,
    gate_weight,
    up_weight,
    down_weight,
    cotangent,
):
    width_q = query_weight.shape[1]
    width_k = key_weight.shape[1]
    hidden_width = gate_weight.shape[1]
    span = positions.shape[0]
    quarter = span // 4
    cut = 3 * width_q // 4
    d = inputs.shape[1]
    shard = query_weight.shape[0]
    side = place("yh").astype(jnp.int32).reshape(1, 1)

    units = 128 * (hidden_width // 256)
    both_width, down_width = 2 * units + 128, units + 128
    inputs, cotangent, shard_kv, shard_mlp = call(
        pack_kernel, "pack",
        [(inputs.shape, BF), (inputs.shape, BF), ((shard, 256), BF),
         ((2, shard, both_width + down_width), BF)],
        [inputs, cotangent, attn_gain[None], mlp_gain[None], key_weight, value_weight,
         gate_weight, up_weight, down_weight.T],
        mib=56,
    )
    shard_first = jnp.concatenate([query_weight, out_weight.T], 1)
    other_first, other_kv = swap(shard_first, "yh"), swap(shard_kv, "yh")
    pair_first = join_sides(shard_first, other_first)
    first_whole = lax.all_gather(pair_first, ("z", "x"), axis=0, tiled=True)
    pair_kv = join_sides(shard_kv, other_kv)
    along_kv = send_stage(pair_kv, "x")
    rows_in = gather_rows(after(inputs, other_kv))
    kv_whole = flat(stack_stage(send_stage(stack_stage(along_kv, "x", 0), "z"), "z", 0))

    me = (lax.axis_index("yl") * 2 + lax.axis_index("core")).astype(jnp.int32)
    blocked = jnp.arange(4, dtype=jnp.int32) ^ me
    positions = jnp.take(positions.reshape(4, quarter), blocked, axis=0, mode="clip").reshape(1, span)
    freqs = 10000.0 ** (-(jnp.arange(HD // 2, dtype=F32) * 2.0) / HD)
    angles = freqs[:, None] * positions.astype(F32)
    cos, sin = jnp.cos(angles), jnp.sin(angles)
    window = (me.reshape(1, 1), positions)

    kv_block, scaled_in, gains = call(
        keys_values_kernel, "keys_values",
        [((span, 2 * width_k), BF), ((span, d), BF), ((8, d), F32)],
        [*rows_in, kv_whole, cos, sin], products=span * d * 2 * width_k,
    )
    (queries,) = call(
        queries_kernel, "queries",
        [((width_q, span), BF)],
        [scaled_in, after(first_whole, kv_block), cos, sin], products=span * d * width_q,
    )
    blocks = [kv_block] + [shift(kv_block, "x", d) for d in range(1, SEQ_DEVS)]
    cot_yl = swap(after(cotangent, kv_block), "yl")
    cot_near = jnp.concatenate([cotangent, cot_yl], 0)
    cot_far = swap(cot_near, "yh")
    other_mlp = swap(after(pick(shard_mlp, place("yh", 1), 0), kv_block), "yh")
    mlp_pair = join_sides(pick(shard_mlp, place("yh"), 0), after(other_mlp, first_whole, blocks[1:], cot_near))
    mlp_whole = lax.all_gather(mlp_pair, ("z", "x"), axis=0, tiled=True)
    odd = place("yl").astype(jnp.int32).reshape(1, 1)
    mixed, log_total = attend(queries, blocks, window)

    cot_far = after(cot_far, log_total)
    cotangents = jnp.concatenate([after(cot_near, log_total), cot_far], 0)
    all_heads = (0, width_q)
    attn_rows = rows_out(
        [after(mixed, cot_far)], [(first_whole, width_q, width_q)], [(0, all_heads, 0, all_heads)],
        1024, [(0,), (2,), (1, 3)], 24,
    )
    cotangents = [cotangents, swap(cotangents, "core")]
    middle, scaled_mid = call(
        middle_kernel, "middle", [(inputs.shape, F32), (inputs.shape, BF)],
        [inputs, *scatter_rows(attn_rows), gains],
    )
    scaled_all = gather_eight(scaled_mid)
    hidden, grad_both = hidden_units(odd, scaled_all, cotangents, mlp_whole, units)
    for_both = [(0, (0, both_width), 0, (0, both_width))]
    quarters = [(0, 1, 2, 3)]
    (mid_there,) = rows_out(
        [grad_both], [(mlp_whole, 0, both_width)], for_both, 512, quarters, 56, (1, 2)
    )
    (mid_here,) = rows_out(
        [after(grad_both, mid_there)], [(mlp_whole, 0, both_width)], for_both, 512, quarters, 56, (0, 2)
    )
    mid_own, mid_others = scatter_eight(mid_here, mid_there)
    mid_arrived = send_back(mid_others)
    mlp_sum = weight_grads(
        odd, [after(scaled_all[0], mid_others), *scaled_all[1:]], cotangents, grad_both, hidden
    )
    mlp_rows = rows_out(
        [after(hidden, mlp_sum)], [(mlp_whole, both_width, down_width)],
        [(0, (0, down_width), 0, (0, down_width))], 512, [(0, 1, 2, 3), (4, 5, 6, 7)], 56,
    )
    grad_middle, grad_middle_low = call(
        middle_grad_kernel, "middle_grad", [(inputs.shape, F32), (inputs.shape, BF)],
        [cotangent, mid_own, *after(mid_arrived, mlp_rows), middle, gains],
    )
    grad_across = swap(grad_middle_low, "yl")
    mlp_sum = lax.psum_scatter(mlp_sum, ("z", "x"), scatter_dimension=0, tiled=True)

    mlp_cores = swap(after(mlp_rows[1], grad_middle_low), "core")
    mlp_own, mlp_beside, mlp_far = call(
        pair_pieces_kernel, "pair_pieces",
        [(inputs.shape, F32), ((2 * quarter, d), BF), (inputs.shape, BF)],
        [odd, mlp_rows[0], mlp_cores], scalars=1,
    )
    rows_grad_middle = [
        grad_middle_low, swap(grad_middle_low, "core"), grad_across, swap(grad_across, "core")
    ]
    out_parts = wide_parts(rows_grad_middle, mixed, (0, width_q), "z")
    query_part, far_grads, grad_turned, delta = attend_back(
        (1, 2, 3), queries, blocks[1:], window, log_total, None, after(mixed, out_parts, mlp_beside),
        [first_whole, *rows_grad_middle],
    )
    mlp_arrived = after(swap(after(mlp_beside, rows_grad_middle), "yl"), query_part)
    mlp_far = (mlp_far.astype(F32) + mlp_arrived[quarter:].astype(F32)).astype(BF)
    arriving = [
        shift(far_grads[(d - 1) * span : d * span], "x", -d) for d in range(1, SEQ_DEVS)
    ]
    out_arrived = [shift(out_parts[n], "z", n) for n in (2, 1, 3)]
    query_raw_grad, own_grads = attend_back(
        (0,), after(queries, mlp_far), blocks[:1], window, log_total, (grad_turned, delta, query_part), turn=[cos, sin]
    )

    out_sum = total(out_parts[0].astype(F32), after(out_arrived, query_raw_grad)).astype(BF)
    output = settle(
        middle, [mlp_own, mlp_arrived[:quarter], after(swap(mlp_far, "yh"), query_raw_grad)], BF
    )
    a_parts = wide_parts([scaled_in], after(query_raw_grad, arriving, out_arrived), (0, cut), "x")
    a_arrived = [shift(a_parts[n], "x", n) for n in (2, 1, 3)]
    kv_raw_grad, *b_parts = last_parts(
        scaled_in, after(query_raw_grad, a_parts), cut, own_grads, arriving, cos, sin, "z"
    )
    b_arrived = [shift(b_parts[n], "z", n) for n in (2, 1, 3)]
    in_partial = rows_grad(
        [query_raw_grad, kv_raw_grad],
        [(first_whole, 0, width_q), kv_whole],
        [(0, all_heads, 0, all_heads), (1, (0, 2 * width_k), 1, (0, 2 * width_k))],
        rows_in, gains, 0,
    )
    in_own, in_across, in_cores = in_partial
    in_parts = scatter_rows((in_own, in_across, after(in_cores, a_arrived, b_arrived)))
    input_grad = settle(grad_middle, in_parts, F32)

    mlp_send = pick(mlp_sum.reshape(2, shard, -1), place("yh", 1), 0)
    a_sum = wide_sum_next(total(a_parts[0].astype(F32), a_arrived).astype(BF), "z")
    b_sum = total(b_parts[0].astype(F32), b_arrived).astype(BF)
    b_sum = wide_sum_next(jnp.concatenate([b_sum, out_sum], 1), "x", hold=[mlp_send])
    sides = jnp.concatenate([a_sum, b_sum], 1)
    other_sides = swap(pick(sides.reshape(2, shard, -1), place("yh", 1), 0), "yh")
    query_grad, key_grad, value_grad, out_grad = call(
        finish_attn_kernel, "finish_attn",
        [(query_weight.shape, F32), (key_weight.shape, F32), (value_weight.shape, F32),
         (out_weight.shape[::-1], F32)],
        [side, sides, other_sides], scalars=1,
    )
    gate_grad, up_grad, down_grad = call(
        finish_mlp_kernel, "finish_mlp",
        [(gate_weight.shape, F32), (up_weight.shape, F32), (down_weight.shape[::-1], F32)],
        [side, mlp_sum, swap(mlp_send, "yh")], scalars=1,
    )

    ends = width_q - cut
    attn_weights = jnp.concatenate([pair_first[:, :width_q], pair_kv[:, : 2 * width_k]], 1).astype(F32)
    gain_parts = jnp.stack(
        [
            jnp.sum(attn_weights * sides[:, : cut + ends + 2 * width_k].astype(F32), 1),
            jnp.sum(
                mlp_pair[:, :both_width].astype(F32) * mlp_sum[:, :both_width].astype(F32),
                1,
            ),
        ]
    )
    gain_parts = lax.psum(gain_parts, ("yh",) + TP)
    own_gains = pick(gain_parts.reshape(2, 2, shard), place("yh"), 1)
    return (
        output,
        input_grad,
        own_gains[0] / attn_gain.astype(F32),
        query_grad,
        key_grad,
        value_grad,
        out_grad.T,
        own_gains[1] / mlp_gain.astype(F32),
        gate_grad,
        up_grad,
        down_grad.T,
    )


def solution(mesh):
    split = Mesh(mesh.devices.reshape(2, 4, 4, 2, 2), WIDE + TP)
    rows = P(WIDE + TP, None)
    inward = P(WIDE, TP)
    outward = P(TP, WIDE)
    gain = P(WIDE)
    return jax.shard_map(
        per_device,
        mesh=split,
        in_specs=(
            rows, gain, gain, inward, inward, inward, outward, gain, inward, inward, outward, rows,
        ),
        out_specs=(
            rows, rows, gain, inward, inward, inward, outward, gain, inward, inward, outward,
        ),
        check_vma=False,
    )
```

```python
import functools

import jax
import jax.numpy as jnp
from jax import lax
from jax.experimental import pallas as pl
from jax.experimental.pallas import tpu as pltpu
from jax.sharding import Mesh, PartitionSpec as P

HEADS = 32
KV = 4
HD = 64
SEQ_DEVS = 4
WIDE = ("yh", "z", "x")
TP = ("yl", "core")
RING = ("yh", "yl")
BF = jnp.bfloat16
F32 = jnp.float32

epsilon = 1e-05
masked_fill = -1e30
MIB = 1024 * 1024


def after(value, *earlier):
    return lax.optimization_barrier((value, earlier))[0]


def shift(block, axis, distance):
    n = 4 if axis == RING else lax.axis_size(axis)
    return lax.ppermute(block, axis, [(i, (i + distance) % n) for i in range(n)])


def swap(block, axis):
    return shift(block, axis, 1)


def place(axis, step=0):
    n = lax.axis_size(axis)
    return ((lax.axis_index(axis) + (step + n)) & (n - 1)).astype(jnp.uint32)


def pick(array, index, dim):
    return lax.dynamic_index_in_dim(array, index, dim, keepdims=False)


def send_stage(block, axis):
    n = lax.axis_size(axis)
    return [block] + [shift(block, axis, d) for d in (1, n - 1, *range(2, n - 1))]


def stack_stage(arrived, axis, dim):
    n = len(arrived)
    block = arrived[0]
    out = jnp.zeros(block.shape[:dim] + (n,) + block.shape[dim:], block.dtype)
    for d, piece in zip((0, 1, n - 1, *range(2, n - 1)), arrived):
        out = lax.dynamic_update_index_in_dim(out, piece, place(axis, -d), dim)
    return out


def join_sides(shard, other):
    first = lax.axis_index("yh") == 0
    return jnp.concatenate([jnp.where(first, shard, other), jnp.where(first, other, shard)], 0)


def flat(blocks):
    return blocks.reshape(-1, blocks.shape[-1])


def gather_rows(rows):
    across = swap(rows, "yl")
    return [rows, swap(rows, "core"), across, swap(across, "core")]


def gather_eight(rows):
    near = [rows, shift(rows, RING, 1), shift(rows, RING, 2), shift(rows, RING, -1)]
    return near + [swap(piece, "core") for piece in near]


def scatter_eight(own_core, other_core):
    quarter, d = own_core.shape[0] // 4, own_core.shape[1]
    own, *others = call(
        add_pieces_kernel, "add_pieces",
        [((quarter, d), F32)] + [((quarter, d), BF)] * 3, [own_core, swap(other_core, "core")],
    )
    return own, others


def send_back(others):
    one, two, three = others
    return [shift(one, RING, -1), shift(three, RING, 1), shift(two, RING, 2)]


def scatter_rows(partial):
    own, across, cores = partial
    n = own.shape[0]
    arrived = swap(cores, "core")
    other = (across.astype(F32) + arrived[n:].astype(F32)).astype(BF)
    return [own, arrived[:n], swap(other, "yl")]


def total(first, parts):
    for part in parts:
        first = first + part.astype(F32)
    return first


def exchange_sum(parts, axis, hold=()):
    near = parts[0].astype(F32)
    for d in (1, 3):
        near = near + after(shift(parts[d], axis, d), *hold).astype(F32)
    return near + after(shift(parts[2], axis, 2), *hold).astype(F32)


def wide_sum_next(part, axis, hold=()):
    n = lax.axis_size(axis)
    part = part.reshape(n, part.shape[0] // n, part.shape[1])
    pieces = [pick(part, place(axis, d), 0) for d in range(n)]
    return exchange_sum(pieces, axis, hold).astype(BF)


def mm(left, right):
    return jnp.dot(left, right, preferred_element_type=F32)


def mm_last(left, right):
    return lax.dot_general(left, right, (((1,), (1,)), ((), ())), preferred_element_type=F32)


def normed_rows(piece):
    values = piece.astype(F32)
    factor = lax.rsqrt(jnp.mean(values * values, -1, keepdims=True) + epsilon)
    return values * factor, factor


def scale_rows(piece_refs, gain, scaled_ref):
    for n, ref in enumerate(piece_refs):
        for at in range(0, ref.shape[0], 32):
            normed, _ = normed_rows(ref[at : at + 32, :])
            rows = n * ref.shape[0] + at
            scaled_ref[rows : rows + 32, :] = (normed * gain).astype(BF)


def turned(block, cos, sin):
    a, b = block[: HD // 2], block[HD // 2 :]
    return jnp.concatenate([a * cos - b * sin, b * cos + a * sin], 0)


def keys_values_kernel(*refs):
    piece_refs, (w_ref, cos_ref, sin_ref, kv_ref, scaled_ref, gains_ref) = refs[:4], refs[4:]
    gains_ref[...] = w_ref[:, 128:].T[:8].astype(F32)
    scale_rows(piece_refs, gains_ref[0:1, :], scaled_ref)
    both = mm(scaled_ref[...], w_ref[:, :128]).T
    keys = turned(both[:HD], cos_ref[...], sin_ref[...])
    kv_ref[...] = jnp.concatenate([keys, both[HD:]], 0).T.astype(BF)


def queries_kernel(x_ref, w_ref, cos_ref, sin_ref, q_ref):
    for at in range(0, q_ref.shape[0], 256):
        piece = mm(x_ref[...], w_ref[:, at : at + 256]).T
        for sub in range(0, 256, HD):
            low = turned(piece[sub : sub + HD], cos_ref[...], sin_ref[...]).astype(BF)
            q_ref[at + sub : at + sub + HD, :] = low * 0.125


def to_inner(ref, out_ref):
    half = ref.shape[1] // 2
    for at in range(0, half, 128):
        low, high = ref[:, at : at + 128], ref[:, half + at : half + at + 128]
        out_ref[:, 2 * at : 2 * at + 128] = jnp.concatenate([low[:, :HD], high[:, :HD]], 1)
        out_ref[:, 2 * at + 128 : 2 * at + 256] = jnp.concatenate([low[:, HD:], high[:, HD:]], 1)


def pack_kernel(inputs_ref, cot_ref, again_ref, mgain_ref, k_ref, v_ref, g_ref, u_ref, d_ref,
                rows_ref, cots_ref, kv_ref, mlp_ref):
    to_inner(inputs_ref, rows_ref)
    to_inner(cot_ref, cots_ref)
    kv_ref[:, :128] = jnp.concatenate([k_ref[...], v_ref[...]], 1)
    gains = jnp.concatenate(
        [again_ref[...].astype(F32), mgain_ref[...].astype(F32), jnp.zeros((126, HD), F32)], 0
    )
    kv_ref[:, 128:] = gains.T.astype(BF)
    width = g_ref.shape[1]
    down = d_ref[...]
    whole_units = 128 * (width // 256)
    tail = 2 * whole_units
    for side in range(2):
        units = slice(side * whole_units, (side + 1) * whole_units)
        ends = slice(tail + 64 * side, tail + 64 * side + 64)
        mlp_ref[side, :, :whole_units] = g_ref[:, units]
        mlp_ref[side, :, whole_units:tail] = u_ref[:, units]
        mlp_ref[side, :, tail : tail + 128] = jnp.concatenate([g_ref[:, ends], u_ref[:, ends]], 1)
        mlp_ref[side, :, tail + 128 : tail + 128 + whole_units] = down[:, units]
        mlp_ref[side, :, tail + 128 + whole_units :] = jnp.concatenate(
            [down[:, ends], jnp.zeros_like(down[:, ends])], 1
        )


def finish_mlp_kernel(side_ref, pair_ref, other_ref, gate_ref, up_ref, down_ref):
    rows = pl.ds(pl.multiple_of(side_ref[0, 0] * HD, HD), HD)
    own, other = pair_ref[rows, :].astype(F32), other_ref[...].astype(F32)
    here = side_ref[0, 0] == 0
    halves = jnp.where(here, own, other), jnp.where(here, other, own)
    units = 128 * (gate_ref.shape[1] // 256)
    tail = 2 * units
    down = []
    for n, half in enumerate(halves):
        gate_ref[:, n * units : (n + 1) * units] = half[:, :units]
        up_ref[:, n * units : (n + 1) * units] = half[:, units:tail]
        down.append(half[:, tail + 128 : tail + 128 + units])
    ends = [half[:, tail : tail + 128] for half in halves]
    gate_ref[:, tail:] = jnp.concatenate([end[:, :64] for end in ends], 1)
    up_ref[:, tail:] = jnp.concatenate([end[:, 64:] for end in ends], 1)
    down += [half[:, tail + 128 + units : tail + 192 + units] for half in halves]
    for n in range(2):
        down_ref[:, n * units : (n + 1) * units] = down[n]
    down_ref[:, tail:] = jnp.concatenate(down[2:], 1)


def finish_attn_kernel(side_ref, pair_ref, other_ref, q_ref, k_ref, v_ref, o_ref):
    rows = pl.ds(pl.multiple_of(side_ref[0, 0] * HD, HD), HD)
    both = pair_ref[rows, :].astype(F32) + other_ref[...].astype(F32)
    width = q_ref.shape[1]
    q_ref[...] = both[:, :width]
    k_ref[...] = both[:, width : width + HD]
    v_ref[...] = both[:, width + HD : width + 2 * HD]
    o_ref[...] = both[:, width + 2 * HD :]


def add_pieces_kernel(one_ref, two_ref, *outs):
    for n, out in enumerate(outs):
        rows = slice(n * out.shape[0], (n + 1) * out.shape[0])
        out[...] = (one_ref[rows, :].astype(F32) + two_ref[rows, :].astype(F32)).astype(out.dtype)


def pair_pieces_kernel(odd_ref, one_ref, two_ref, own_ref, beside_ref, far_ref):
    size = own_ref.shape[0]
    back = 3 - 2 * odd_ref[0, 0]
    for out, at, step in (
        (own_ref, 0, 0), (beside_ref, 0, back), (beside_ref, size, 4 - back), (far_ref, 0, 2)
    ):
        rows = pl.ds(pl.multiple_of(step * size, size), size)
        value = one_ref[rows, :].astype(F32) + two_ref[rows, :].astype(F32)
        out[at : at + size, :] = value.astype(out.dtype)


def middle_kernel(base_ref, *refs):
    parts, (gain_ref, sum_ref, scaled_ref) = refs[:-3], refs[-3:]
    for at in range(0, base_ref.shape[0], 32):
        rows = slice(at, at + 32)
        value = base_ref[rows, :].astype(F32)
        for ref in parts:
            value = value + ref[rows, :].astype(F32)
        sum_ref[rows, :] = value
        normed, _ = normed_rows(value.astype(BF))
        scaled_ref[rows, :] = (normed * gain_ref[1:2, :]).astype(BF)


def middle_grad_kernel(base_ref, *refs):
    parts, (middle_ref, gain_ref, sum_ref, low_ref) = refs[:-4], refs[-4:]
    for at in range(0, base_ref.shape[0], 32):
        rows = slice(at, at + 32)
        value = parts[0][rows, :].astype(F32)
        for ref in parts[1:]:
            value = value + ref[rows, :].astype(F32)
        normed, factor = normed_rows(middle_ref[rows, :].astype(BF))
        value = value * gain_ref[1:2, :]
        inner = jnp.mean(value * normed, -1, keepdims=True)
        value = base_ref[rows, :].astype(F32) + factor * (value - normed * inner)
        sum_ref[rows, :] = value
        low_ref[rows, :] = value.astype(BF)


def cotangent_at(odd_ref, n):
    return (0, 3 - 2 * odd_ref[0, 0], 2, 1 + 2 * odd_ref[0, 0])[n % 4]


def hidden_kernel(width, odd_ref, *refs):
    (w_ref, hidden_ref, both_ref, x_ref, c_ref, gate_up_ref, down_ref, sems) = refs[10:]
    first = gate_up_ref.shape[1]
    copies = [
        pltpu.make_async_copy(w_ref.at[:, pl.ds(0, first)], gate_up_ref, sems.at[0]),
        pltpu.make_async_copy(w_ref.at[:, pl.ds(first, down_ref.shape[1])], down_ref, sems.at[1]),
    ]
    count = x_ref.shape[0] // 8
    for n in range(8):
        rows = pl.ds(n * count, count)
        copies.append(pltpu.make_async_copy(refs[n], x_ref.at[rows, :], sems.at[2 + n]))
        at = pl.ds(pl.multiple_of(cotangent_at(odd_ref, n) * count, count), count)
        copies.append(
            pltpu.make_async_copy(refs[8 + n // 4].at[at, :], c_ref.at[rows, :], sems.at[10 + n])
        )
    weights_up, weights_down, *pieces = copies
    xs, cots = pieces[::2], pieces[1::2]
    for copy in (*xs[:4], weights_up, *xs[4:], weights_down, *cots):
        copy.start()

    def units(gate, up, grad):
        sigmoid = 1.0 / (1.0 + jnp.exp(-gate))
        gated = gate * sigmoid
        return (
            (gated * up).astype(BF),
            (grad * up * sigmoid * (1.0 + gate * (1.0 - sigmoid))).astype(BF),
            (grad * gated).astype(BF),
        )

    half = 4 * count
    for part in range(2):
        rows = slice(part * half, (part + 1) * half)
        for copy in xs[4 * part : 4 * part + 4]:
            copy.wait()
        if part == 0:
            weights_up.wait()
        x = x_ref[rows, :]
        gate = mm(x, gate_up_ref[:, :width])
        up = mm(x, gate_up_ref[:, width : 2 * width])
        ends = mm(x, gate_up_ref[:, 2 * width :])
        for copy in cots[4 * part : 4 * part + 4]:
            copy.wait()
        if part == 0:
            weights_down.wait()
        c = c_ref[rows, :]
        value, dgate, dup = units(gate, up, mm(c, down_ref[:, :width]))
        hidden_ref[rows, :width] = value
        both_ref[rows, :width] = dgate
        both_ref[rows, width : 2 * width] = dup
        value, dgate, dup = units(ends[:, :64], ends[:, 64:], mm(c, down_ref[:, width:])[:, :64])
        hidden_ref[rows, width:] = jnp.concatenate([value, jnp.zeros_like(value)], 1)
        both_ref[rows, 2 * width :] = jnp.concatenate([dgate, dup], 1)


def sum_of_products(terms, refs):
    total = None
    for left, (low, high), right, (first, last) in terms:
        part = mm_last(refs[left][:, low:high], refs[right][:, first:last])
        total = part if total is None else total + part
    return total


def rows_grad_kernel(terms, count, gain_row, *refs):
    pieces, gain_ref, outs, sum_ref = refs[count : count + 4], refs[count + 4], refs[count + 5 : -1], refs[-1]
    own_ref, across_ref, cores_ref = outs
    size = own_ref.shape[0]
    outs = [own_ref, cores_ref.at[pl.ds(0, size), :], across_ref, cores_ref.at[pl.ds(size, size), :]]
    step = pl.program_id(0)
    tile = sum_ref.shape[1] // pl.num_programs(0)
    columns = pl.ds(pl.multiple_of(step * tile, tile), tile)
    sum_ref[:, columns] = sum_of_products(terms, refs) * gain_ref[gain_row : gain_row + 1, columns]

    @pl.when(step == pl.num_programs(0) - 1)
    def _():
        for n, ref in enumerate(pieces):
            for at in range(0, ref.shape[0], 32):
                normed, factor = normed_rows(ref[at : at + 32, :])
                scaled = sum_ref[n * ref.shape[0] + at : n * ref.shape[0] + at + 32, :]
                inner = jnp.mean(scaled * normed, -1, keepdims=True)
                outs[n][at : at + 32, :] = (factor * (scaled - normed * inner)).astype(BF)


def rows_out_kernel(terms, places, *refs):
    value = sum_of_products(terms, refs).astype(BF)
    outs = refs[len(refs) - len(places) :]
    size = value.shape[0] // sum(len(held) for held in places)
    for out, held in zip(outs, places):
        for n, piece in enumerate(held):
            out[n * size : (n + 1) * size, :] = value[piece * size : (piece + 1) * size]


def write_parts(outs, turned_of, axis, me, right, base):
    for d, out in enumerate(outs):
        index = (me + d) & 3
        if axis == "z":
            turned = turned_of(pl.multiple_of(index * 512, 512), 512)
        else:
            turned = jnp.concatenate(
                [turned_of(pl.multiple_of(z * 512 + index * 128, 128), 128) for z in range(4)], 0
            )
        out[:, base : base + right.shape[1]] = mm(turned, right).astype(BF)


def parts_kernel(axis, columns, count, me_ref, *refs):
    lefts, right_ref, outs = refs[:count], refs[count], refs[count + 1 :]

    def turned_of(at, size):
        return jnp.concatenate([left[:, pl.ds(at, size)] for left in lefts], 0).T

    write_parts(outs, turned_of, axis, me_ref[0, 0], right_ref[:, columns[0] : columns[1]], 0)


def last_parts_kernel(axis, cut, me_ref, left_ref, dq_ref, own_ref, one_ref, two_ref, three_ref,
                      cos_ref, sin_ref, *outs):
    half = HD // 2
    cos, sin = cos_ref[...], sin_ref[...]
    kv = own_ref[...]
    for ref in (one_ref, two_ref, three_ref):
        kv = kv + ref[...].astype(F32)
    kv = kv.T
    a, b = kv[:half], kv[half:HD]
    kv = jnp.concatenate([a * cos + b * sin, b * cos - a * sin, kv[HD:]], 0).T.astype(BF)
    outs[0][...] = kv
    right = jnp.concatenate([dq_ref[:, cut:], kv], 1)

    def turned_of(at, size):
        return left_ref[:, pl.ds(at, size)].T

    write_parts(outs[1:], turned_of, axis, me_ref[0, 0], right, 0)


def settle_kernel(base_ref, *refs):
    out_ref = refs[-1]
    width = base_ref.shape[1]

    def block(at):
        value = base_ref[:, at : at + 128].astype(F32)
        for ref in refs[:-1]:
            value = value + ref[:, at : at + 128].astype(F32)
        return value

    for n in range(width // 256):
        one, two = block(256 * n), block(256 * n + 128)
        low = jnp.concatenate([one[:, :HD], two[:, :HD]], 1)
        high = jnp.concatenate([one[:, HD:], two[:, HD:]], 1)
        out_ref[:, 128 * n : 128 * n + 128] = low.astype(out_ref.dtype)
        out_ref[:, width // 2 + 128 * n : width // 2 + 128 * n + 128] = high.astype(out_ref.dtype)


def fill_bias(bias_ref, me_ref, pos_ref, span, distances):
    step = 64
    quarter = span // 4
    me = me_ref[0, 0]
    at = lax.broadcasted_iota(jnp.int32, (1, span), 1)
    query = (((at // quarter) ^ me) * quarter) + (at & (quarter - 1))
    first = query - pos_ref[...]

    @pl.loop(0, span // step)
    def _(i):
        block = (i * step) // quarter
        start = (block ^ me) * quarter + i * step - block * quarter
        key = start + lax.broadcasted_iota(jnp.int32, (step, span), 0)
        for n, d in enumerate(distances):
            seen = (key - d * span <= query) & (key - d * span >= first)
            bias_ref[pl.ds(pl.multiple_of(n * span + i * step, step), step), :] = jnp.where(
                seen, 0.0, masked_fill
            ).astype(F32)


def attend_kernel(q_ref, *refs):
    blocks = len(refs) - 7
    kv_refs = refs[:blocks]
    me_ref, pos_ref, mix_ref, lse_ref, bias_ref, s_ref, vt_ref = refs[blocks:]
    span = q_ref.shape[1]
    fill_bias(bias_ref, me_ref, pos_ref, span, range(blocks))
    for d in range(blocks):
        vt_ref[:, d * span : (d + 1) * span] = kv_refs[d][...].T[HD:]

    @pl.loop(0, q_ref.shape[0] // 128)
    def _(pair):
        outs = []
        for sub in range(2):
            q = q_ref[pl.ds(pl.multiple_of(pair * 128 + sub * HD, HD), HD), :]
            top = None
            for d in range(blocks):
                rows = slice(d * span, (d + 1) * span)
                s = mm(kv_refs[d][:, :HD], q) + bias_ref[rows, :]
                s_ref[rows, :] = s
                high = jnp.max(s, 0, keepdims=True)
                top = high if top is None else jnp.maximum(top, high)
            total = jnp.zeros_like(top)
            out = jnp.zeros((HD, span), F32)
            for d in range(blocks):
                rows = slice(d * span, (d + 1) * span)
                p = jnp.exp(s_ref[rows, :] - top)
                total = total + jnp.sum(p, 0, keepdims=True)
                out = out + mm(vt_ref[:, rows], p.astype(BF))
            outs.append(out / total)
            lse_ref[pl.ds(pair * 2 + sub, 1), :] = top + jnp.log(total)
        mix_ref[:, pl.ds(pl.multiple_of(pair * 128, 128), 128)] = (
            jnp.concatenate(outs, 0).T.astype(BF)
        )


def attend_back_kernel(distances, first, last, q_ref, *refs):
    blocks = len(distances)
    refs = list(refs)

    def take(count):
        got, refs[:count] = refs[:count], []
        return got

    kv_refs = take(blocks)
    me_ref, pos_ref, lse_ref = take(3)
    if first:
        mix_ref, w_ref, *piece_refs = take(6)
    else:
        gt_ref, delta_ref, part_ref = take(3)
    if last:
        cos_ref, sin_ref = take(2)
        (dq_ref,) = take(1)
    else:
        (sum_ref,) = take(1)
    (dkv_ref,) = take(1)
    if first:
        gt_ref, delta_ref = take(2)
    bias_ref, v_ref, kt_ref, dk_ref, dv_ref = take(5)
    span = q_ref.shape[1]
    half = HD // 2
    heads = q_ref.shape[0] // HD
    fill_bias(bias_ref, me_ref, pos_ref, span, distances)
    for n in range(blocks):
        rows = slice(n * span, (n + 1) * span)
        both = kv_refs[n][...].T
        kt_ref[:, rows] = both[:HD]
        v_ref[rows, :] = both[HD:].T
    dk_ref[...] = jnp.zeros_like(dk_ref)
    dv_ref[...] = jnp.zeros_like(dv_ref)
    if first:
        rows_all = jnp.concatenate([ref[...] for ref in piece_refs], 0)
        for at in range(0, heads * HD, 256):
            grads = mm(rows_all, w_ref[:, heads * HD + at : heads * HD + at + 256]).astype(BF).T
            gt_ref[at : at + 256, :] = grads
        for at in range(0, heads * HD, 128):
            gt = gt_ref[at : at + 128, :]
            mt = mix_ref[:, at : at + 128].T
            prod = gt.astype(F32) * mt.astype(F32)
            for sub in range(2):
                h = at // HD + sub
                delta_ref[h : h + 1, :] = jnp.sum(prod[sub * HD : (sub + 1) * HD], 0, keepdims=True)

    @pl.loop(0, heads // 2)
    def _(pair):
        outs = []
        for sub in range(2):
            rows_h = pl.ds(pl.multiple_of(pair * 128 + sub * HD, HD), HD)
            q, g = q_ref[rows_h, :], gt_ref[rows_h, :]
            lse = lse_ref[pl.ds(pair * 2 + sub, 1), :]
            delta = delta_ref[pl.ds(pair * 2 + sub, 1), :]
            dq = jnp.zeros((HD, span), F32) if first else part_ref[rows_h, :]
            for n in range(blocks):
                rows = slice(n * span, (n + 1) * span)
                s = mm(kv_refs[n][:, :HD], q) + bias_ref[rows, :]
                p = jnp.exp(s - lse)
                ds = (p * (mm(v_ref[rows, :], g) - delta)).astype(BF)
                dv_ref[rows, :] += mm_last(p.astype(BF), g)
                dk_ref[rows, :] += mm_last(ds, q)
                dq = dq + mm(kt_ref[:, rows], ds)
            if last:
                dq = dq * 0.125
                a, b = dq[:half], dq[half:]
                cos, sin = cos_ref[...], sin_ref[...]
                outs += [a * cos + b * sin, b * cos - a * sin]
            else:
                sum_ref[rows_h, :] = dq
        if last:
            dq_ref[:, pl.ds(pl.multiple_of(pair * 128, 128), 128)] = (
                jnp.concatenate(outs, 0).T.astype(BF)
            )

    for n in range(blocks):
        rows = slice(n * span, (n + 1) * span)
        dkv_ref[rows, :] = jnp.concatenate([dk_ref[rows, :], dv_ref[rows, :]], 1).astype(dkv_ref.dtype)


def weight_grads_kernel(odd_ref, *refs):
    one_ref, two_ref, out_ref = refs[10:]
    count = refs[0].shape[0]

    def cotangent(n):
        at = pl.multiple_of(cotangent_at(odd_ref, n) * count, count)
        return refs[8 + n // 4][pl.ds(at, count), :]

    at = 0
    for lefts, ref in (
        ([left[...] for left in refs[:8]], one_ref), ([cotangent(n) for n in range(8)], two_ref)
    ):
        turned = jnp.concatenate(lefts, 0).T
        for c in range(0, ref.shape[1], 256):
            size = min(256, ref.shape[1] - c)
            out_ref[:, at + c : at + c + size] = mm(turned, ref[:, c : c + size]).astype(BF)
        at += ref.shape[1]


def params(mib):
    return pltpu.CompilerParams(vmem_limit_bytes=mib * MIB)


def whole(count):
    return [pl.BlockSpec(memory_space=pltpu.VMEM)] * count


def cost(products, moved):
    return pl.CostEstimate(flops=2 * products, bytes_accessed=moved, transcendentals=0)


def call(kernel, name, shapes, operands, scalars=0, products=0, mib=16):
    return pl.pallas_call(
        kernel,
        out_shape=tuple(jax.ShapeDtypeStruct(*shape) for shape in shapes),
        in_specs=scalar() * scalars + whole(len(operands) - scalars),
        out_specs=tuple(whole(len(shapes))),
        compiler_params=params(mib),
        cost_estimate=cost(products, 4 << 20),
        name=name,
    )(*operands)


def hidden_units(odd, pieces, cots, weights, width):
    count, d = pieces[0].shape
    span = 8 * count
    both, down = 2 * width + 128, width + 128
    return pl.pallas_call(
        functools.partial(hidden_kernel, width),
        out_shape=(jax.ShapeDtypeStruct((span, down), BF), jax.ShapeDtypeStruct((span, both), BF)),
        in_specs=scalar() + [pl.BlockSpec(memory_space=pl.ANY)] * 11,
        out_specs=tuple(whole(2)),
        scratch_shapes=[
            pltpu.VMEM((span, d), BF),
            pltpu.VMEM((span, d), BF),
            pltpu.VMEM((d, both), BF),
            pltpu.VMEM((d, down), BF),
            pltpu.SemaphoreType.DMA((18,)),
        ],
        compiler_params=params(56),
        cost_estimate=cost(3 * span * d * width, 6 * d * width),
        name="hidden_units",
    )(odd, *pieces, *cots, weights)


def feature_rows(weight, tile):
    if not isinstance(weight, tuple):
        return pl.BlockSpec((tile, weight.shape[1]), lambda i: (i, 0))
    return pl.BlockSpec((pl.Element(tile), pl.Element(weight[2])), lambda i: (i * tile, weight[1]))


def array_of(weight):
    return weight[0] if isinstance(weight, tuple) else weight


def fixed(array):
    return pl.BlockSpec(array.shape, lambda i: (0, 0))


def rows_grad(grads, weights, terms, pieces, gains, gain_row):
    span, d = 4 * pieces[0].shape[0], pieces[0].shape[1]
    tile = 512
    n = len(grads)
    terms = [(g, c, n + w, e) for g, c, w, e in terms]
    return pl.pallas_call(
        functools.partial(rows_grad_kernel, terms, n + len(weights), gain_row),
        grid=(d // tile,),
        out_shape=tuple(jax.ShapeDtypeStruct((span // n, d), BF) for n in (4, 4, 2)),
        in_specs=[fixed(g) for g in grads]
        + [feature_rows(w, tile) for w in weights]
        + [fixed(a) for a in (*pieces, gains)],
        out_specs=tuple(pl.BlockSpec((span // n, d), lambda i: (0, 0)) for n in (4, 4, 2)),
        scratch_shapes=[pltpu.VMEM((span, d), F32)],
        compiler_params=params(32),
        cost_estimate=cost(0, 0),
        name="rows_grad",
    )(*grads, *map(array_of, weights), *pieces, gains)


def rows_out(lefts, weights, terms, tile, places, mib, part=(0, 1)):
    span, d = lefts[0].shape[0] // part[1], array_of(weights[0]).shape[0]
    n = len(lefts)
    terms = [(g, c, n + w, e) for g, c, w, e in terms]
    size = span // sum(len(held) for held in places)
    return pl.pallas_call(
        functools.partial(rows_out_kernel, terms, places),
        grid=(d // tile,),
        out_shape=tuple(jax.ShapeDtypeStruct((len(held) * size, d), BF) for held in places),
        in_specs=[pl.BlockSpec((span, g.shape[1]), lambda i: (part[0], 0)) for g in lefts]
        + [feature_rows(w, tile) for w in weights],
        out_specs=tuple(pl.BlockSpec((len(held) * size, tile), lambda i: (0, i)) for held in places),
        compiler_params=params(mib),
        cost_estimate=cost(sum(span * d * (c[1] - c[0]) for _, c, _, _ in terms), 6 << 20),
        name="rows_out",
    )(*lefts, *map(array_of, weights))


def scalar():
    return [pl.BlockSpec(memory_space=pltpu.SMEM)]


def at_place(axis):
    return place(axis).astype(jnp.int32).reshape(1, 1)


def wide_parts(lefts, right, columns, axis):
    span, d = right.shape[0], lefts[0].shape[1]
    width = columns[1] - columns[0]
    return pl.pallas_call(
        functools.partial(parts_kernel, axis, columns, len(lefts)),
        out_shape=(jax.ShapeDtypeStruct((d // 4, width), BF),) * 4,
        in_specs=scalar() + whole(len(lefts) + 1),
        out_specs=tuple(whole(4)),
        compiler_params=params(20),
        cost_estimate=cost(span * d * width, 8 << 20),
        name="wide_parts",
    )(at_place(axis), *lefts, right)


def last_parts(left, dq, cut, own, arrived, cos, sin, axis):
    span, d = left.shape
    width = dq.shape[1] - cut + 2 * HD
    return pl.pallas_call(
        functools.partial(last_parts_kernel, axis, cut),
        out_shape=(jax.ShapeDtypeStruct((span, 2 * HD), BF),)
        + (jax.ShapeDtypeStruct((d // 4, width), BF),) * 4,
        in_specs=scalar() + whole(8),
        out_specs=tuple(whole(5)),
        compiler_params=params(20),
        cost_estimate=cost(0, 0),
        name="last_parts",
    )(at_place(axis), left, dq, own, *arrived, cos, sin)


def settle(base, parts, kind):
    return pl.pallas_call(
        settle_kernel,
        out_shape=jax.ShapeDtypeStruct(base.shape, kind),
        in_specs=whole(1 + len(parts)),
        out_specs=whole(1)[0],
        compiler_params=params(12),
        cost_estimate=cost(0, 4 << 20),
        name="settle",
    )(base, *parts)


def window_specs():
    return [pl.BlockSpec(memory_space=pltpu.SMEM)] + whole(1)


def attend(q, kvs, window):
    n = len(kvs)
    width, span = q.shape
    heads = width // HD
    return pl.pallas_call(
        attend_kernel,
        out_shape=(
            jax.ShapeDtypeStruct((span, width), BF),
            jax.ShapeDtypeStruct((heads, span), F32),
        ),
        in_specs=whole(n + 1) + window_specs(),
        out_specs=tuple(whole(2)),
        scratch_shapes=[
            pltpu.VMEM((n * span, span), F32),
            pltpu.VMEM((n * span, span), F32),
            pltpu.VMEM((HD, n * span), BF),
        ],
        compiler_params=params(32),
        cost_estimate=cost(5 * 580_000_000, 1 << 20),
        name="attend",
    )(q, *kvs, *window)


def attend_back(distances, q, kvs, window, lse, prepared, mixed=None, out=None, turn=None):
    n = len(kvs)
    width, span = q.shape
    heads = width // HD
    first, last = prepared is None, turn is not None
    operands = [q, *kvs, *window, lse]
    operands += [mixed, *out] if first else list(prepared)
    shapes = []
    if last:
        operands += turn
        shapes.append(jax.ShapeDtypeStruct((span, width), BF))
    else:
        shapes.append(jax.ShapeDtypeStruct((width, span), F32))
    shapes.append(jax.ShapeDtypeStruct((n * span, 2 * HD), F32 if last else BF))
    if first:
        shapes.append(jax.ShapeDtypeStruct((width, span), BF))
        shapes.append(jax.ShapeDtypeStruct((heads, span), F32))
    specs = whole(n + 1) + window_specs() + whole(len(operands) - n - 3)
    return pl.pallas_call(
        functools.partial(attend_back_kernel, distances, first, last),
        out_shape=tuple(shapes),
        in_specs=specs,
        out_specs=tuple(whole(len(shapes))),
        scratch_shapes=[
            pltpu.VMEM((n * span, span), F32),
            pltpu.VMEM((n * span, HD), BF),
            pltpu.VMEM((HD, n * span), BF),
            pltpu.VMEM((n * span, HD), F32),
            pltpu.VMEM((n * span, HD), F32),
        ],
        compiler_params=params(40),
        cost_estimate=cost(120 * 580_000_000 if first else 0, 1 << 20),
        name="attend_back",
    )(*operands)


def weight_grads(odd, xs, cots, one, two):
    t, d = xs[0].shape
    tile = 512
    rows = pl.BlockSpec((t, tile), lambda i: (0, i))
    width = one.shape[1] + two.shape[1]
    return pl.pallas_call(
        weight_grads_kernel,
        grid=(d // tile,),
        out_shape=jax.ShapeDtypeStruct((d, width), BF),
        in_specs=scalar()
        + [rows] * 8
        + [pl.BlockSpec((4 * t, tile), lambda i: (0, i))] * 2
        + [fixed(one), fixed(two)],
        out_specs=pl.BlockSpec((tile, width), lambda i: (i, 0)),
        compiler_params=params(56),
        cost_estimate=cost(8 * t * d * width, 2 * d * width + 32 * t * d),
        name="weight_grads",
    )(odd, *xs, *cots, one, two)


def per_device(
    inputs,
    positions,
    attn_gain,
    query_weight,
    key_weight,
    value_weight,
    out_weight,
    mlp_gain,
    gate_weight,
    up_weight,
    down_weight,
    cotangent,
):
    width_q = query_weight.shape[1]
    width_k = key_weight.shape[1]
    hidden_width = gate_weight.shape[1]
    span = positions.shape[0]
    quarter = span // 4
    cut = 3 * width_q // 4
    d = inputs.shape[1]
    shard = query_weight.shape[0]
    side = place("yh").astype(jnp.int32).reshape(1, 1)

    units = 128 * (hidden_width // 256)
    both_width, down_width = 2 * units + 128, units + 128
    inputs, cotangent, shard_kv, shard_mlp = call(
        pack_kernel, "pack",
        [(inputs.shape, BF), (inputs.shape, BF), ((shard, 256), BF),
         ((2, shard, both_width + down_width), BF)],
        [inputs, cotangent, attn_gain[None], mlp_gain[None], key_weight, value_weight,
         gate_weight, up_weight, down_weight.T],
        mib=56,
    )
    shard_first = jnp.concatenate([query_weight, out_weight.T], 1)
    other_first, other_kv = swap(shard_first, "yh"), swap(shard_kv, "yh")
    pair_first = join_sides(shard_first, other_first)
    first_whole = lax.all_gather(pair_first, ("z", "x"), axis=0, tiled=True)
    pair_kv = join_sides(shard_kv, other_kv)
    along_kv = send_stage(pair_kv, "x")
    rows_in = gather_rows(after(inputs, other_kv))
    kv_whole = flat(stack_stage(send_stage(stack_stage(along_kv, "x", 0), "z"), "z", 0))

    me = (lax.axis_index("yl") * 2 + lax.axis_index("core")).astype(jnp.int32)
    blocked = jnp.arange(4, dtype=jnp.int32) ^ me
    positions = jnp.take(positions.reshape(4, quarter), blocked, axis=0, mode="clip").reshape(1, span)
    freqs = 10000.0 ** (-(jnp.arange(HD // 2, dtype=F32) * 2.0) / HD)
    angles = freqs[:, None] * positions.astype(F32)
    cos, sin = jnp.cos(angles), jnp.sin(angles)
    window = (me.reshape(1, 1), positions)

    kv_block, scaled_in, gains = call(
        keys_values_kernel, "keys_values",
        [((span, 2 * width_k), BF), ((span, d), BF), ((8, d), F32)],
        [*rows_in, kv_whole, cos, sin], products=span * d * 2 * width_k,
    )
    (queries,) = call(
        queries_kernel, "queries",
        [((width_q, span), BF)],
        [scaled_in, after(first_whole, kv_block), cos, sin], products=span * d * width_q,
    )
    blocks = [kv_block] + [shift(kv_block, "x", d) for d in range(1, SEQ_DEVS)]
    cot_yl = swap(after(cotangent, kv_block), "yl")
    cot_near = jnp.concatenate([cotangent, cot_yl], 0)
    cot_far = swap(cot_near, "yh")
    other_mlp = swap(after(pick(shard_mlp, place("yh", 1), 0), kv_block), "yh")
    mlp_pair = join_sides(pick(shard_mlp, place("yh"), 0), other_mlp)
    mlp_whole = lax.all_gather(
        after(mlp_pair, first_whole, blocks[1:], cot_near), ("z", "x"), axis=0, tiled=True
    )
    odd = place("yl").astype(jnp.int32).reshape(1, 1)
    mixed, log_total = attend(queries, blocks, window)

    cot_far = after(cot_far, log_total)
    cotangents = jnp.concatenate([after(cot_near, log_total), cot_far], 0)
    all_heads = (0, width_q)
    attn_rows = rows_out(
        [after(mixed, cot_far)], [(first_whole, width_q, width_q)], [(0, all_heads, 0, all_heads)],
        1024, [(0,), (2,), (1, 3)], 24,
    )
    cotangents = [cotangents, swap(cotangents, "core")]
    middle, scaled_mid = call(
        middle_kernel, "middle", [(inputs.shape, F32), (inputs.shape, BF)],
        [inputs, *scatter_rows(attn_rows), gains],
    )
    scaled_all = gather_eight(scaled_mid)
    hidden, grad_both = hidden_units(odd, scaled_all, cotangents, mlp_whole, units)
    for_both = [(0, (0, both_width), 0, (0, both_width))]
    quarters = [(0, 1, 2, 3)]
    (mid_there,) = rows_out(
        [grad_both], [(mlp_whole, 0, both_width)], for_both, 512, quarters, 56, (1, 2)
    )
    (mid_here,) = rows_out(
        [after(grad_both, mid_there)], [(mlp_whole, 0, both_width)], for_both, 512, quarters, 56, (0, 2)
    )
    mid_own, mid_others = scatter_eight(mid_here, mid_there)
    mid_arrived = send_back(mid_others)
    mlp_sum = weight_grads(
        odd, [after(scaled_all[0], mid_others), *scaled_all[1:]], cotangents, grad_both, hidden
    )
    mlp_rows = rows_out(
        [after(hidden, mlp_sum)], [(mlp_whole, both_width, down_width)],
        [(0, (0, down_width), 0, (0, down_width))], 512, [(0, 1, 2, 3), (4, 5, 6, 7)], 56,
    )
    grad_middle, grad_middle_low = call(
        middle_grad_kernel, "middle_grad", [(inputs.shape, F32), (inputs.shape, BF)],
        [cotangent, mid_own, *after(mid_arrived, mlp_rows), middle, gains],
    )
    grad_across = swap(grad_middle_low, "yl")
    mlp_sum = lax.psum_scatter(mlp_sum, ("z", "x"), scatter_dimension=0, tiled=True)

    mlp_cores = swap(after(mlp_rows[1], grad_middle_low), "core")
    mlp_own, mlp_beside, mlp_far = call(
        pair_pieces_kernel, "pair_pieces",
        [(inputs.shape, F32), ((2 * quarter, d), BF), (inputs.shape, BF)],
        [odd, mlp_rows[0], mlp_cores], scalars=1,
    )
    rows_grad_middle = [
        grad_middle_low, swap(grad_middle_low, "core"), grad_across, swap(grad_across, "core")
    ]
    out_parts = wide_parts(rows_grad_middle, mixed, (0, width_q), "z")
    query_part, far_grads, grad_turned, delta = attend_back(
        (1, 2, 3), queries, blocks[1:], window, log_total, None, after(mixed, out_parts, mlp_beside),
        [first_whole, *rows_grad_middle],
    )
    mlp_arrived = after(swap(after(mlp_beside, rows_grad_middle), "yl"), query_part)
    mlp_far = (mlp_far.astype(F32) + mlp_arrived[quarter:].astype(F32)).astype(BF)
    arriving = [
        shift(far_grads[(d - 1) * span : d * span], "x", -d) for d in range(1, SEQ_DEVS)
    ]
    out_arrived = [shift(out_parts[n], "z", n) for n in (2, 1, 3)]
    query_raw_grad, own_grads = attend_back(
        (0,), queries, blocks[:1], window, log_total, (grad_turned, delta, query_part), turn=[cos, sin]
    )

    out_sum = total(out_parts[0].astype(F32), after(out_arrived, query_raw_grad)).astype(BF)
    mlp_across = swap(mlp_far, "yh")
    a_parts = wide_parts([scaled_in], after(query_raw_grad, arriving, out_arrived, mlp_arrived), (0, cut), "x")
    a_arrived = [shift(a_parts[n], "x", n) for n in (2, 1, 3)]
    kv_raw_grad, *b_parts = last_parts(
        scaled_in, after(query_raw_grad, a_parts), cut, own_grads, arriving, cos, sin, "z"
    )
    b_arrived = [shift(b_parts[n], "z", n) for n in (2, 1, 3)]
    in_partial = rows_grad(
        [query_raw_grad, kv_raw_grad],
        [(first_whole, 0, width_q), kv_whole],
        [(0, all_heads, 0, all_heads), (1, (0, 2 * width_k), 1, (0, 2 * width_k))],
        rows_in, gains, 0,
    )
    in_own, in_across, in_cores = in_partial
    in_parts = scatter_rows((in_own, in_across, after(in_cores, a_arrived, b_arrived)))

    mlp_there = swap(pick(mlp_sum.reshape(2, shard, -1), place("yh", 1), 0), "yh")
    a_sum = wide_sum_next(total(a_parts[0].astype(F32), a_arrived).astype(BF), "z")
    b_sum = total(b_parts[0].astype(F32), b_arrived).astype(BF)
    b_sum = wide_sum_next(jnp.concatenate([b_sum, out_sum], 1), "x", hold=[mlp_there, mlp_across])
    sides = jnp.concatenate([a_sum, b_sum], 1)
    other_sides = swap(pick(sides.reshape(2, shard, -1), place("yh", 1), 0), "yh")
    output = settle(middle, [mlp_own, mlp_arrived[:quarter], after(mlp_across, sides)], BF)
    input_grad = settle(grad_middle, in_parts[:2] + [after(in_parts[2], sides)], F32)
    query_grad, key_grad, value_grad, out_grad = call(
        finish_attn_kernel, "finish_attn",
        [(query_weight.shape, F32), (key_weight.shape, F32), (value_weight.shape, F32),
         (out_weight.shape[::-1], F32)],
        [side, sides, other_sides], scalars=1,
    )
    gate_grad, up_grad, down_grad = call(
        finish_mlp_kernel, "finish_mlp",
        [(gate_weight.shape, F32), (up_weight.shape, F32), (down_weight.shape[::-1], F32)],
        [side, mlp_sum, mlp_there], scalars=1,
    )

    ends = width_q - cut
    attn_weights = jnp.concatenate([pair_first[:, :width_q], pair_kv[:, : 2 * width_k]], 1).astype(F32)
    gain_parts = jnp.stack(
        [
            jnp.sum(attn_weights * sides[:, : cut + ends + 2 * width_k].astype(F32), 1),
            jnp.sum(
                mlp_pair[:, :both_width].astype(F32) * mlp_sum[:, :both_width].astype(F32),
                1,
            ),
        ]
    )
    gain_parts = lax.psum(gain_parts, ("yh",) + TP)
    own_gains = pick(gain_parts.reshape(2, 2, shard), place("yh"), 1)
    return (
        output,
        input_grad,
        own_gains[0] / attn_gain.astype(F32),
        query_grad,
        key_grad,
        value_grad,
        out_grad.T,
        own_gains[1] / mlp_gain.astype(F32),
        gate_grad,
        up_grad,
        down_grad.T,
    )


def solution(mesh):
    split = Mesh(mesh.devices.reshape(2, 4, 4, 2, 2), WIDE + TP)
    rows = P(WIDE + TP, None)
    inward = P(WIDE, TP)
    outward = P(TP, WIDE)
    gain = P(WIDE)
    return jax.shard_map(
        per_device,
        mesh=split,
        in_specs=(
            rows, gain, gain, inward, inward, inward, outward, gain, inward, inward, outward, rows,
        ),
        out_specs=(
            rows, rows, gain, inward, inward, inward, outward, gain, inward, inward, outward,
        ),
        check_vma=False,
    )
```

```python
import functools

import jax
import jax.numpy as jnp
from jax import lax
from jax.experimental import pallas as pl
from jax.experimental.pallas import tpu as pltpu
from jax.sharding import Mesh, PartitionSpec as P

HEADS = 32
KV = 4
HD = 64
SEQ_DEVS = 4
WIDE = ("yh", "z", "x")
TP = ("yl", "core")
RING = ("yh", "yl")
BF = jnp.bfloat16
F32 = jnp.float32

epsilon = 1e-05
masked_fill = -1e30
MIB = 1024 * 1024


def after(value, *earlier):
    return lax.optimization_barrier((value, earlier))[0]


def shift(block, axis, distance):
    n = 4 if axis == RING else lax.axis_size(axis)
    return lax.ppermute(block, axis, [(i, (i + distance) % n) for i in range(n)])


def swap(block, axis):
    return shift(block, axis, 1)


def place(axis, step=0):
    n = lax.axis_size(axis)
    return ((lax.axis_index(axis) + (step + n)) & (n - 1)).astype(jnp.uint32)


def pick(array, index, dim):
    return lax.dynamic_index_in_dim(array, index, dim, keepdims=False)


def send_stage(block, axis):
    n = lax.axis_size(axis)
    return [block] + [shift(block, axis, d) for d in (1, n - 1, *range(2, n - 1))]


def stack_stage(arrived, axis, dim):
    n = len(arrived)
    block = arrived[0]
    out = jnp.zeros(block.shape[:dim] + (n,) + block.shape[dim:], block.dtype)
    for d, piece in zip((0, 1, n - 1, *range(2, n - 1)), arrived):
        out = lax.dynamic_update_index_in_dim(out, piece, place(axis, -d), dim)
    return out


def join_sides(shard, other):
    first = lax.axis_index("yh") == 0
    return jnp.concatenate([jnp.where(first, shard, other), jnp.where(first, other, shard)], 0)


def flat(blocks):
    return blocks.reshape(-1, blocks.shape[-1])


def gather_rows(rows):
    across = swap(rows, "yl")
    return [rows, swap(rows, "core"), across, swap(across, "core")]


def gather_eight(rows):
    near = [rows, shift(rows, RING, 1), shift(rows, RING, 2), shift(rows, RING, -1)]
    return near + [swap(piece, "core") for piece in near]


def scatter_eight(own_core, other_core):
    quarter, d = own_core.shape[0] // 4, own_core.shape[1]
    own, *others = call(
        add_pieces_kernel, "add_pieces",
        [((quarter, d), F32)] + [((quarter, d), BF)] * 3, [own_core, swap(other_core, "core")],
    )
    return own, others


def send_back(others):
    one, two, three = others
    return [shift(one, RING, -1), shift(three, RING, 1), shift(two, RING, 2)]


def scatter_rows(partial):
    own, across, cores = partial
    n = own.shape[0]
    arrived = swap(cores, "core")
    other = (across.astype(F32) + arrived[n:].astype(F32)).astype(BF)
    return [own, arrived[:n], swap(other, "yl")]


def total(first, parts):
    for part in parts:
        first = first + part.astype(F32)
    return first


def exchange_sum(parts, axis, hold=()):
    near = parts[0].astype(F32)
    for d in (1, 3):
        near = near + after(shift(parts[d], axis, d), *hold).astype(F32)
    return near + after(shift(parts[2], axis, 2), *hold).astype(F32)


def wide_sum_next(part, axis, hold=()):
    n = lax.axis_size(axis)
    part = part.reshape(n, part.shape[0] // n, part.shape[1])
    pieces = [pick(part, place(axis, d), 0) for d in range(n)]
    return exchange_sum(pieces, axis, hold).astype(BF)


def mm(left, right):
    return jnp.dot(left, right, preferred_element_type=F32)


def mm_last(left, right):
    return lax.dot_general(left, right, (((1,), (1,)), ((), ())), preferred_element_type=F32)


def normed_rows(piece):
    values = piece.astype(F32)
    factor = lax.rsqrt(jnp.mean(values * values, -1, keepdims=True) + epsilon)
    return values * factor, factor


def scale_rows(piece_refs, gain, scaled_ref):
    for n, ref in enumerate(piece_refs):
        for at in range(0, ref.shape[0], 32):
            normed, _ = normed_rows(ref[at : at + 32, :])
            rows = n * ref.shape[0] + at
            scaled_ref[rows : rows + 32, :] = (normed * gain).astype(BF)


def turned(block, cos, sin):
    a, b = block[: HD // 2], block[HD // 2 :]
    return jnp.concatenate([a * cos - b * sin, b * cos + a * sin], 0)


def keys_values_kernel(*refs):
    piece_refs, (w_ref, cos_ref, sin_ref, kv_ref, scaled_ref, gains_ref) = refs[:4], refs[4:]
    gains_ref[...] = w_ref[:, 128:].T[:8].astype(F32)
    scale_rows(piece_refs, gains_ref[0:1, :], scaled_ref)
    both = mm(scaled_ref[...], w_ref[:, :128]).T
    keys = turned(both[:HD], cos_ref[...], sin_ref[...])
    kv_ref[...] = jnp.concatenate([keys, both[HD:]], 0).T.astype(BF)


def queries_kernel(x_ref, w_ref, cos_ref, sin_ref, q_ref):
    for at in range(0, q_ref.shape[0], 256):
        piece = mm(x_ref[...], w_ref[:, at : at + 256]).T
        for sub in range(0, 256, HD):
            low = turned(piece[sub : sub + HD], cos_ref[...], sin_ref[...]).astype(BF)
            q_ref[at + sub : at + sub + HD, :] = low * 0.125


def to_inner(ref, out_ref):
    half = ref.shape[1] // 2
    for at in range(0, half, 128):
        low, high = ref[:, at : at + 128], ref[:, half + at : half + at + 128]
        out_ref[:, 2 * at : 2 * at + 128] = jnp.concatenate([low[:, :HD], high[:, :HD]], 1)
        out_ref[:, 2 * at + 128 : 2 * at + 256] = jnp.concatenate([low[:, HD:], high[:, HD:]], 1)


def pack_kernel(inputs_ref, cot_ref, again_ref, mgain_ref, k_ref, v_ref, g_ref, u_ref, d_ref,
                rows_ref, cots_ref, kv_ref, mlp_ref):
    to_inner(inputs_ref, rows_ref)
    to_inner(cot_ref, cots_ref)
    kv_ref[:, :128] = jnp.concatenate([k_ref[...], v_ref[...]], 1)
    gains = jnp.concatenate(
        [again_ref[...].astype(F32), mgain_ref[...].astype(F32), jnp.zeros((126, HD), F32)], 0
    )
    kv_ref[:, 128:] = gains.T.astype(BF)
    width = g_ref.shape[1]
    down = d_ref[...]
    whole_units = 128 * (width // 256)
    tail = 2 * whole_units
    for side in range(2):
        units = slice(side * whole_units, (side + 1) * whole_units)
        ends = slice(tail + 64 * side, tail + 64 * side + 64)
        mlp_ref[side, :, :whole_units] = g_ref[:, units]
        mlp_ref[side, :, whole_units:tail] = u_ref[:, units]
        mlp_ref[side, :, tail : tail + 128] = jnp.concatenate([g_ref[:, ends], u_ref[:, ends]], 1)
        mlp_ref[side, :, tail + 128 : tail + 128 + whole_units] = down[:, units]
        mlp_ref[side, :, tail + 128 + whole_units :] = jnp.concatenate(
            [down[:, ends], jnp.zeros_like(down[:, ends])], 1
        )


def finish_mlp_kernel(side_ref, pair_ref, other_ref, gate_ref, up_ref, down_ref):
    rows = pl.ds(pl.multiple_of(side_ref[0, 0] * HD, HD), HD)
    own, other = pair_ref[rows, :].astype(F32), other_ref[...].astype(F32)
    here = side_ref[0, 0] == 0
    halves = jnp.where(here, own, other), jnp.where(here, other, own)
    units = 128 * (gate_ref.shape[1] // 256)
    tail = 2 * units
    down = []
    for n, half in enumerate(halves):
        gate_ref[:, n * units : (n + 1) * units] = half[:, :units]
        up_ref[:, n * units : (n + 1) * units] = half[:, units:tail]
        down.append(half[:, tail + 128 : tail + 128 + units])
    ends = [half[:, tail : tail + 128] for half in halves]
    gate_ref[:, tail:] = jnp.concatenate([end[:, :64] for end in ends], 1)
    up_ref[:, tail:] = jnp.concatenate([end[:, 64:] for end in ends], 1)
    down += [half[:, tail + 128 + units : tail + 192 + units] for half in halves]
    for n in range(2):
        down_ref[:, n * units : (n + 1) * units] = down[n]
    down_ref[:, tail:] = jnp.concatenate(down[2:], 1)


def finish_attn_kernel(side_ref, pair_ref, other_ref, q_ref, k_ref, v_ref, o_ref):
    rows = pl.ds(pl.multiple_of(side_ref[0, 0] * HD, HD), HD)
    both = pair_ref[rows, :].astype(F32) + other_ref[:, : pair_ref.shape[1]].astype(F32)
    width = q_ref.shape[1]
    q_ref[...] = both[:, :width]
    k_ref[...] = both[:, width : width + HD]
    v_ref[...] = both[:, width + HD : width + 2 * HD]
    o_ref[...] = both[:, width + 2 * HD :]


def add_pieces_kernel(one_ref, two_ref, *outs):
    for n, out in enumerate(outs):
        rows = slice(n * out.shape[0], (n + 1) * out.shape[0])
        out[...] = (one_ref[rows, :].astype(F32) + two_ref[rows, :].astype(F32)).astype(out.dtype)


def pair_pieces_kernel(odd_ref, one_ref, two_ref, own_ref, beside_ref, far_ref):
    size = own_ref.shape[0]
    back = 3 - 2 * odd_ref[0, 0]
    for out, at, step in (
        (own_ref, 0, 0), (beside_ref, 0, back), (beside_ref, size, 4 - back), (far_ref, 0, 2)
    ):
        rows = pl.ds(pl.multiple_of(step * size, size), size)
        value = one_ref[rows, :].astype(F32) + two_ref[rows, :].astype(F32)
        out[at : at + size, :] = value.astype(out.dtype)


def middle_kernel(base_ref, *refs):
    parts, (gain_ref, sum_ref, scaled_ref) = refs[:-3], refs[-3:]
    for at in range(0, base_ref.shape[0], 32):
        rows = slice(at, at + 32)
        value = base_ref[rows, :].astype(F32)
        for ref in parts:
            value = value + ref[rows, :].astype(F32)
        sum_ref[rows, :] = value
        normed, _ = normed_rows(value.astype(BF))
        scaled_ref[rows, :] = (normed * gain_ref[1:2, :]).astype(BF)


def middle_grad_kernel(base_ref, *refs):
    parts, (middle_ref, gain_ref, sum_ref, low_ref) = refs[:-4], refs[-4:]
    for at in range(0, base_ref.shape[0], 32):
        rows = slice(at, at + 32)
        value = parts[0][rows, :].astype(F32)
        for ref in parts[1:]:
            value = value + ref[rows, :].astype(F32)
        normed, factor = normed_rows(middle_ref[rows, :].astype(BF))
        value = value * gain_ref[1:2, :]
        inner = jnp.mean(value * normed, -1, keepdims=True)
        value = base_ref[rows, :].astype(F32) + factor * (value - normed * inner)
        sum_ref[rows, :] = value
        low_ref[rows, :] = value.astype(BF)


def cotangent_at(odd_ref, n):
    return (0, 3 - 2 * odd_ref[0, 0], 2, 1 + 2 * odd_ref[0, 0])[n % 4]


def hidden_kernel(width, odd_ref, *refs):
    (w_ref, hidden_ref, both_ref, x_ref, c_ref, gate_up_ref, down_ref, sems) = refs[10:]
    first = gate_up_ref.shape[1]
    copies = [
        pltpu.make_async_copy(w_ref.at[:, pl.ds(0, first)], gate_up_ref, sems.at[0]),
        pltpu.make_async_copy(w_ref.at[:, pl.ds(first, down_ref.shape[1])], down_ref, sems.at[1]),
    ]
    count = x_ref.shape[0] // 8
    for n in range(8):
        rows = pl.ds(n * count, count)
        copies.append(pltpu.make_async_copy(refs[n], x_ref.at[rows, :], sems.at[2 + n]))
        at = pl.ds(pl.multiple_of(cotangent_at(odd_ref, n) * count, count), count)
        copies.append(
            pltpu.make_async_copy(refs[8 + n // 4].at[at, :], c_ref.at[rows, :], sems.at[10 + n])
        )
    weights_up, weights_down, *pieces = copies
    xs, cots = pieces[::2], pieces[1::2]
    for copy in (*xs[:4], weights_up, *xs[4:], weights_down, *cots):
        copy.start()

    def units(gate, up, grad):
        sigmoid = 1.0 / (1.0 + jnp.exp(-gate))
        gated = gate * sigmoid
        return (
            (gated * up).astype(BF),
            (grad * up * sigmoid * (1.0 + gate * (1.0 - sigmoid))).astype(BF),
            (grad * gated).astype(BF),
        )

    half = 4 * count
    for part in range(2):
        rows = slice(part * half, (part + 1) * half)
        for copy in xs[4 * part : 4 * part + 4]:
            copy.wait()
        if part == 0:
            weights_up.wait()
        x = x_ref[rows, :]
        gate = mm(x, gate_up_ref[:, :width])
        up = mm(x, gate_up_ref[:, width : 2 * width])
        ends = mm(x, gate_up_ref[:, 2 * width :])
        for copy in cots[4 * part : 4 * part + 4]:
            copy.wait()
        if part == 0:
            weights_down.wait()
        c = c_ref[rows, :]
        value, dgate, dup = units(gate, up, mm(c, down_ref[:, :width]))
        hidden_ref[rows, :width] = value
        both_ref[rows, :width] = dgate
        both_ref[rows, width : 2 * width] = dup
        value, dgate, dup = units(ends[:, :64], ends[:, 64:], mm(c, down_ref[:, width:])[:, :64])
        hidden_ref[rows, width:] = jnp.concatenate([value, jnp.zeros_like(value)], 1)
        both_ref[rows, 2 * width :] = jnp.concatenate([dgate, dup], 1)


def sum_of_products(terms, refs):
    total = None
    for left, (low, high), right, (first, last) in terms:
        part = mm_last(refs[left][:, low:high], refs[right][:, first:last])
        total = part if total is None else total + part
    return total


def rows_grad_kernel(terms, count, gain_row, *refs):
    pieces, gain_ref, outs, sum_ref = refs[count : count + 4], refs[count + 4], refs[count + 5 : -1], refs[-1]
    own_ref, across_ref, cores_ref = outs
    size = own_ref.shape[0]
    outs = [own_ref, cores_ref.at[pl.ds(0, size), :], across_ref, cores_ref.at[pl.ds(size, size), :]]
    step = pl.program_id(0)
    tile = sum_ref.shape[1] // pl.num_programs(0)
    columns = pl.ds(pl.multiple_of(step * tile, tile), tile)
    sum_ref[:, columns] = sum_of_products(terms, refs) * gain_ref[gain_row : gain_row + 1, columns]

    @pl.when(step == pl.num_programs(0) - 1)
    def _():
        for n, ref in enumerate(pieces):
            for at in range(0, ref.shape[0], 32):
                normed, factor = normed_rows(ref[at : at + 32, :])
                scaled = sum_ref[n * ref.shape[0] + at : n * ref.shape[0] + at + 32, :]
                inner = jnp.mean(scaled * normed, -1, keepdims=True)
                outs[n][at : at + 32, :] = (factor * (scaled - normed * inner)).astype(BF)


def rows_out_kernel(terms, places, *refs):
    value = sum_of_products(terms, refs).astype(BF)
    outs = refs[len(refs) - len(places) :]
    size = value.shape[0] // sum(len(held) for held in places)
    for out, held in zip(outs, places):
        for n, piece in enumerate(held):
            out[n * size : (n + 1) * size, :] = value[piece * size : (piece + 1) * size]


def write_parts(outs, turned_of, axis, me, right, base):
    for d, out in enumerate(outs):
        index = (me + d) & 3
        if axis == "z":
            turned = turned_of(pl.multiple_of(index * 512, 512), 512)
        else:
            turned = jnp.concatenate(
                [turned_of(pl.multiple_of(z * 512 + index * 128, 128), 128) for z in range(4)], 0
            )
        out[:, base : base + right.shape[1]] = mm(turned, right).astype(BF)


def parts_kernel(axis, columns, count, me_ref, *refs):
    lefts, right_ref, outs = refs[:count], refs[count], refs[count + 1 :]

    def turned_of(at, size):
        return jnp.concatenate([left[:, pl.ds(at, size)] for left in lefts], 0).T

    write_parts(outs, turned_of, axis, me_ref[0, 0], right_ref[:, columns[0] : columns[1]], 0)


def last_parts_kernel(axis, cut, me_ref, left_ref, dq_ref, own_ref, one_ref, two_ref, three_ref,
                      cos_ref, sin_ref, *outs):
    half = HD // 2
    cos, sin = cos_ref[...], sin_ref[...]
    kv = own_ref[...]
    for ref in (one_ref, two_ref, three_ref):
        kv = kv + ref[...].astype(F32)
    kv = kv.T
    a, b = kv[:half], kv[half:HD]
    kv = jnp.concatenate([a * cos + b * sin, b * cos - a * sin, kv[HD:]], 0).T.astype(BF)
    outs[0][...] = kv
    right = jnp.concatenate([dq_ref[:, cut:], kv], 1)

    def turned_of(at, size):
        return left_ref[:, pl.ds(at, size)].T

    write_parts(outs[1:], turned_of, axis, me_ref[0, 0], right, 0)


def settle_kernel(base_ref, *refs):
    out_ref = refs[-1]
    width = base_ref.shape[1]

    def block(at):
        value = base_ref[:, at : at + 128].astype(F32)
        for ref in refs[:-1]:
            value = value + ref[:, at : at + 128].astype(F32)
        return value

    for n in range(width // 256):
        one, two = block(256 * n), block(256 * n + 128)
        low = jnp.concatenate([one[:, :HD], two[:, :HD]], 1)
        high = jnp.concatenate([one[:, HD:], two[:, HD:]], 1)
        out_ref[:, 128 * n : 128 * n + 128] = low.astype(out_ref.dtype)
        out_ref[:, width // 2 + 128 * n : width // 2 + 128 * n + 128] = high.astype(out_ref.dtype)


def fill_bias(bias_ref, me_ref, pos_ref, span, distances):
    step = 64
    quarter = span // 4
    me = me_ref[0, 0]
    at = lax.broadcasted_iota(jnp.int32, (1, span), 1)
    query = (((at // quarter) ^ me) * quarter) + (at & (quarter - 1))
    first = query - pos_ref[...]

    @pl.loop(0, span // step)
    def _(i):
        block = (i * step) // quarter
        start = (block ^ me) * quarter + i * step - block * quarter
        key = start + lax.broadcasted_iota(jnp.int32, (step, span), 0)
        for n, d in enumerate(distances):
            seen = (key - d * span <= query) & (key - d * span >= first)
            bias_ref[pl.ds(pl.multiple_of(n * span + i * step, step), step), :] = jnp.where(
                seen, 0.0, masked_fill
            ).astype(F32)


def attend_kernel(q_ref, *refs):
    blocks = len(refs) - 7
    kv_refs = refs[:blocks]
    me_ref, pos_ref, mix_ref, lse_ref, bias_ref, s_ref, vt_ref = refs[blocks:]
    span = q_ref.shape[1]
    fill_bias(bias_ref, me_ref, pos_ref, span, range(blocks))
    for d in range(blocks):
        vt_ref[:, d * span : (d + 1) * span] = kv_refs[d][...].T[HD:]

    @pl.loop(0, q_ref.shape[0] // 128)
    def _(pair):
        outs = []
        for sub in range(2):
            q = q_ref[pl.ds(pl.multiple_of(pair * 128 + sub * HD, HD), HD), :]
            top = None
            for d in range(blocks):
                rows = slice(d * span, (d + 1) * span)
                s = mm(kv_refs[d][:, :HD], q) + bias_ref[rows, :]
                s_ref[rows, :] = s
                high = jnp.max(s, 0, keepdims=True)
                top = high if top is None else jnp.maximum(top, high)
            total = jnp.zeros_like(top)
            out = jnp.zeros((HD, span), F32)
            for d in range(blocks):
                rows = slice(d * span, (d + 1) * span)
                p = jnp.exp(s_ref[rows, :] - top)
                total = total + jnp.sum(p, 0, keepdims=True)
                out = out + mm(vt_ref[:, rows], p.astype(BF))
            outs.append(out / total)
            lse_ref[pl.ds(pair * 2 + sub, 1), :] = top + jnp.log(total)
        mix_ref[:, pl.ds(pl.multiple_of(pair * 128, 128), 128)] = (
            jnp.concatenate(outs, 0).T.astype(BF)
        )


def attend_back_kernel(distances, first, last, q_ref, *refs):
    blocks = len(distances)
    refs = list(refs)

    def take(count):
        got, refs[:count] = refs[:count], []
        return got

    kv_refs = take(blocks)
    me_ref, pos_ref, lse_ref = take(3)
    if first:
        mix_ref, w_ref, *piece_refs = take(6)
    else:
        gt_ref, delta_ref, part_ref = take(3)
    if last:
        cos_ref, sin_ref = take(2)
        (dq_ref,) = take(1)
    else:
        (sum_ref,) = take(1)
    (dkv_ref,) = take(1)
    if first:
        gt_ref, delta_ref = take(2)
    bias_ref, v_ref, kt_ref, dk_ref, dv_ref = take(5)
    span = q_ref.shape[1]
    half = HD // 2
    heads = q_ref.shape[0] // HD
    fill_bias(bias_ref, me_ref, pos_ref, span, distances)
    for n in range(blocks):
        rows = slice(n * span, (n + 1) * span)
        both = kv_refs[n][...].T
        kt_ref[:, rows] = both[:HD]
        v_ref[rows, :] = both[HD:].T
    dk_ref[...] = jnp.zeros_like(dk_ref)
    dv_ref[...] = jnp.zeros_like(dv_ref)
    if first:
        rows_all = jnp.concatenate([ref[...] for ref in piece_refs], 0)
        for at in range(0, heads * HD, 256):
            grads = mm(rows_all, w_ref[:, heads * HD + at : heads * HD + at + 256]).astype(BF).T
            gt_ref[at : at + 256, :] = grads
        for at in range(0, heads * HD, 128):
            gt = gt_ref[at : at + 128, :]
            mt = mix_ref[:, at : at + 128].T
            prod = gt.astype(F32) * mt.astype(F32)
            for sub in range(2):
                h = at // HD + sub
                delta_ref[h : h + 1, :] = jnp.sum(prod[sub * HD : (sub + 1) * HD], 0, keepdims=True)

    @pl.loop(0, heads // 2)
    def _(pair):
        outs = []
        for sub in range(2):
            rows_h = pl.ds(pl.multiple_of(pair * 128 + sub * HD, HD), HD)
            q, g = q_ref[rows_h, :], gt_ref[rows_h, :]
            lse = lse_ref[pl.ds(pair * 2 + sub, 1), :]
            delta = delta_ref[pl.ds(pair * 2 + sub, 1), :]
            dq = jnp.zeros((HD, span), F32) if first else part_ref[rows_h, :]
            for n in range(blocks):
                rows = slice(n * span, (n + 1) * span)
                s = mm(kv_refs[n][:, :HD], q) + bias_ref[rows, :]
                p = jnp.exp(s - lse)
                ds = (p * (mm(v_ref[rows, :], g) - delta)).astype(BF)
                dv_ref[rows, :] += mm_last(p.astype(BF), g)
                dk_ref[rows, :] += mm_last(ds, q)
                dq = dq + mm(kt_ref[:, rows], ds)
            if last:
                dq = dq * 0.125
                a, b = dq[:half], dq[half:]
                cos, sin = cos_ref[...], sin_ref[...]
                outs += [a * cos + b * sin, b * cos - a * sin]
            else:
                sum_ref[rows_h, :] = dq
        if last:
            dq_ref[:, pl.ds(pl.multiple_of(pair * 128, 128), 128)] = (
                jnp.concatenate(outs, 0).T.astype(BF)
            )

    for n in range(blocks):
        rows = slice(n * span, (n + 1) * span)
        dkv_ref[rows, :] = jnp.concatenate([dk_ref[rows, :], dv_ref[rows, :]], 1).astype(dkv_ref.dtype)


def weight_grads_kernel(odd_ref, *refs):
    one_ref, two_ref, out_ref = refs[10:]
    count = refs[0].shape[0]

    def cotangent(n):
        at = pl.multiple_of(cotangent_at(odd_ref, n) * count, count)
        return refs[8 + n // 4][pl.ds(at, count), :]

    at = 0
    for lefts, ref in (
        ([left[...] for left in refs[:8]], one_ref), ([cotangent(n) for n in range(8)], two_ref)
    ):
        turned = jnp.concatenate(lefts, 0).T
        for c in range(0, ref.shape[1], 256):
            size = min(256, ref.shape[1] - c)
            out_ref[:, at + c : at + c + size] = mm(turned, ref[:, c : c + size]).astype(BF)
        at += ref.shape[1]


def params(mib):
    return pltpu.CompilerParams(vmem_limit_bytes=mib * MIB)


def whole(count):
    return [pl.BlockSpec(memory_space=pltpu.VMEM)] * count


def cost(products, moved):
    return pl.CostEstimate(flops=2 * products, bytes_accessed=moved, transcendentals=0)


def call(kernel, name, shapes, operands, scalars=0, products=0, mib=16):
    return pl.pallas_call(
        kernel,
        out_shape=tuple(jax.ShapeDtypeStruct(*shape) for shape in shapes),
        in_specs=scalar() * scalars + whole(len(operands) - scalars),
        out_specs=tuple(whole(len(shapes))),
        compiler_params=params(mib),
        cost_estimate=cost(products, 4 << 20),
        name=name,
    )(*operands)


def hidden_units(odd, pieces, cots, weights, width):
    count, d = pieces[0].shape
    span = 8 * count
    both, down = 2 * width + 128, width + 128
    return pl.pallas_call(
        functools.partial(hidden_kernel, width),
        out_shape=(jax.ShapeDtypeStruct((span, down), BF), jax.ShapeDtypeStruct((span, both), BF)),
        in_specs=scalar() + [pl.BlockSpec(memory_space=pl.ANY)] * 11,
        out_specs=tuple(whole(2)),
        scratch_shapes=[
            pltpu.VMEM((span, d), BF),
            pltpu.VMEM((span, d), BF),
            pltpu.VMEM((d, both), BF),
            pltpu.VMEM((d, down), BF),
            pltpu.SemaphoreType.DMA((18,)),
        ],
        compiler_params=params(56),
        cost_estimate=cost(3 * span * d * width, 6 * d * width),
        name="hidden_units",
    )(odd, *pieces, *cots, weights)


def feature_rows(weight, tile):
    if not isinstance(weight, tuple):
        return pl.BlockSpec((tile, weight.shape[1]), lambda i: (i, 0))
    return pl.BlockSpec((pl.Element(tile), pl.Element(weight[2])), lambda i: (i * tile, weight[1]))


def array_of(weight):
    return weight[0] if isinstance(weight, tuple) else weight


def fixed(array):
    return pl.BlockSpec(array.shape, lambda i: (0, 0))


def rows_grad(grads, weights, terms, pieces, gains, gain_row):
    span, d = 4 * pieces[0].shape[0], pieces[0].shape[1]
    tile = 512
    n = len(grads)
    terms = [(g, c, n + w, e) for g, c, w, e in terms]
    return pl.pallas_call(
        functools.partial(rows_grad_kernel, terms, n + len(weights), gain_row),
        grid=(d // tile,),
        out_shape=tuple(jax.ShapeDtypeStruct((span // n, d), BF) for n in (4, 4, 2)),
        in_specs=[fixed(g) for g in grads]
        + [feature_rows(w, tile) for w in weights]
        + [fixed(a) for a in (*pieces, gains)],
        out_specs=tuple(pl.BlockSpec((span // n, d), lambda i: (0, 0)) for n in (4, 4, 2)),
        scratch_shapes=[pltpu.VMEM((span, d), F32)],
        compiler_params=params(32),
        cost_estimate=cost(0, 0),
        name="rows_grad",
    )(*grads, *map(array_of, weights), *pieces, gains)


def rows_out(lefts, weights, terms, tile, places, mib, part=(0, 1)):
    span, d = lefts[0].shape[0] // part[1], array_of(weights[0]).shape[0]
    n = len(lefts)
    terms = [(g, c, n + w, e) for g, c, w, e in terms]
    size = span // sum(len(held) for held in places)
    return pl.pallas_call(
        functools.partial(rows_out_kernel, terms, places),
        grid=(d // tile,),
        out_shape=tuple(jax.ShapeDtypeStruct((len(held) * size, d), BF) for held in places),
        in_specs=[pl.BlockSpec((span, g.shape[1]), lambda i: (part[0], 0)) for g in lefts]
        + [feature_rows(w, tile) for w in weights],
        out_specs=tuple(pl.BlockSpec((len(held) * size, tile), lambda i: (0, i)) for held in places),
        compiler_params=params(mib),
        cost_estimate=cost(sum(span * d * (c[1] - c[0]) for _, c, _, _ in terms), 6 << 20),
        name="rows_out",
    )(*lefts, *map(array_of, weights))


def scalar():
    return [pl.BlockSpec(memory_space=pltpu.SMEM)]


def at_place(axis):
    return place(axis).astype(jnp.int32).reshape(1, 1)


def wide_parts(lefts, right, columns, axis):
    span, d = right.shape[0], lefts[0].shape[1]
    width = columns[1] - columns[0]
    return pl.pallas_call(
        functools.partial(parts_kernel, axis, columns, len(lefts)),
        out_shape=(jax.ShapeDtypeStruct((d // 4, width), BF),) * 4,
        in_specs=scalar() + whole(len(lefts) + 1),
        out_specs=tuple(whole(4)),
        compiler_params=params(20),
        cost_estimate=cost(span * d * width, 8 << 20),
        name="wide_parts",
    )(at_place(axis), *lefts, right)


def last_parts(left, dq, cut, own, arrived, cos, sin, axis):
    span, d = left.shape
    width = dq.shape[1] - cut + 2 * HD
    return pl.pallas_call(
        functools.partial(last_parts_kernel, axis, cut),
        out_shape=(jax.ShapeDtypeStruct((span, 2 * HD), BF),)
        + (jax.ShapeDtypeStruct((d // 4, width), BF),) * 4,
        in_specs=scalar() + whole(8),
        out_specs=tuple(whole(5)),
        compiler_params=params(20),
        cost_estimate=cost(0, 0),
        name="last_parts",
    )(at_place(axis), left, dq, own, *arrived, cos, sin)


def settle(base, parts, kind):
    return pl.pallas_call(
        settle_kernel,
        out_shape=jax.ShapeDtypeStruct(base.shape, kind),
        in_specs=whole(1 + len(parts)),
        out_specs=whole(1)[0],
        compiler_params=params(12),
        cost_estimate=cost(0, 4 << 20),
        name="settle",
    )(base, *parts)


def window_specs():
    return [pl.BlockSpec(memory_space=pltpu.SMEM)] + whole(1)


def attend(q, kvs, window):
    n = len(kvs)
    width, span = q.shape
    heads = width // HD
    return pl.pallas_call(
        attend_kernel,
        out_shape=(
            jax.ShapeDtypeStruct((span, width), BF),
            jax.ShapeDtypeStruct((heads, span), F32),
        ),
        in_specs=whole(n + 1) + window_specs(),
        out_specs=tuple(whole(2)),
        scratch_shapes=[
            pltpu.VMEM((n * span, span), F32),
            pltpu.VMEM((n * span, span), F32),
            pltpu.VMEM((HD, n * span), BF),
        ],
        compiler_params=params(32),
        cost_estimate=cost(5 * 580_000_000, 1 << 20),
        name="attend",
    )(q, *kvs, *window)


def attend_back(distances, q, kvs, window, lse, prepared, mixed=None, out=None, turn=None):
    n = len(kvs)
    width, span = q.shape
    heads = width // HD
    first, last = prepared is None, turn is not None
    operands = [q, *kvs, *window, lse]
    operands += [mixed, *out] if first else list(prepared)
    shapes = []
    if last:
        operands += turn
        shapes.append(jax.ShapeDtypeStruct((span, width), BF))
    else:
        shapes.append(jax.ShapeDtypeStruct((width, span), F32))
    shapes.append(jax.ShapeDtypeStruct((n * span, 2 * HD), F32 if last else BF))
    if first:
        shapes.append(jax.ShapeDtypeStruct((width, span), BF))
        shapes.append(jax.ShapeDtypeStruct((heads, span), F32))
    specs = whole(n + 1) + window_specs() + whole(len(operands) - n - 3)
    return pl.pallas_call(
        functools.partial(attend_back_kernel, distances, first, last),
        out_shape=tuple(shapes),
        in_specs=specs,
        out_specs=tuple(whole(len(shapes))),
        scratch_shapes=[
            pltpu.VMEM((n * span, span), F32),
            pltpu.VMEM((n * span, HD), BF),
            pltpu.VMEM((HD, n * span), BF),
            pltpu.VMEM((n * span, HD), F32),
            pltpu.VMEM((n * span, HD), F32),
        ],
        compiler_params=params(40),
        cost_estimate=cost(114 * 580_000_000 if first else 0, 1 << 20),
        name="attend_back",
    )(*operands)


def weight_grads(odd, xs, cots, one, two):
    t, d = xs[0].shape
    tile = 512
    rows = pl.BlockSpec((t, tile), lambda i: (0, i))
    width = one.shape[1] + two.shape[1]
    return pl.pallas_call(
        weight_grads_kernel,
        grid=(d // tile,),
        out_shape=jax.ShapeDtypeStruct((d, width), BF),
        in_specs=scalar()
        + [rows] * 8
        + [pl.BlockSpec((4 * t, tile), lambda i: (0, i))] * 2
        + [fixed(one), fixed(two)],
        out_specs=pl.BlockSpec((tile, width), lambda i: (i, 0)),
        compiler_params=params(56),
        cost_estimate=cost(8 * t * d * width, 2 * d * width + 32 * t * d),
        name="weight_grads",
    )(odd, *xs, *cots, one, two)


def per_device(
    inputs,
    positions,
    attn_gain,
    query_weight,
    key_weight,
    value_weight,
    out_weight,
    mlp_gain,
    gate_weight,
    up_weight,
    down_weight,
    cotangent,
):
    width_q = query_weight.shape[1]
    width_k = key_weight.shape[1]
    hidden_width = gate_weight.shape[1]
    span = positions.shape[0]
    quarter = span // 4
    cut = 3 * width_q // 4
    d = inputs.shape[1]
    shard = query_weight.shape[0]
    side = place("yh").astype(jnp.int32).reshape(1, 1)

    units = 128 * (hidden_width // 256)
    both_width, down_width = 2 * units + 128, units + 128
    inputs, cotangent, shard_kv, shard_mlp = call(
        pack_kernel, "pack",
        [(inputs.shape, BF), (inputs.shape, BF), ((shard, 256), BF),
         ((2, shard, both_width + down_width), BF)],
        [inputs, cotangent, attn_gain[None], mlp_gain[None], key_weight, value_weight,
         gate_weight, up_weight, down_weight.T],
        mib=56,
    )
    shard_first = jnp.concatenate([query_weight, out_weight.T], 1)
    other_first, other_kv = swap(shard_first, "yh"), swap(shard_kv, "yh")
    pair_first = join_sides(shard_first, other_first)
    first_whole = lax.all_gather(pair_first, ("z", "x"), axis=0, tiled=True)
    pair_kv = join_sides(shard_kv, other_kv)
    along_kv = send_stage(pair_kv, "x")
    rows_in = gather_rows(after(inputs, other_kv))
    kv_whole = flat(stack_stage(send_stage(stack_stage(along_kv, "x", 0), "z"), "z", 0))

    me = (lax.axis_index("yl") * 2 + lax.axis_index("core")).astype(jnp.int32)
    blocked = jnp.arange(4, dtype=jnp.int32) ^ me
    positions = jnp.take(positions.reshape(4, quarter), blocked, axis=0, mode="clip").reshape(1, span)
    freqs = 10000.0 ** (-(jnp.arange(HD // 2, dtype=F32) * 2.0) / HD)
    angles = freqs[:, None] * positions.astype(F32)
    cos, sin = jnp.cos(angles), jnp.sin(angles)
    window = (me.reshape(1, 1), positions)

    kv_block, scaled_in, gains = call(
        keys_values_kernel, "keys_values",
        [((span, 2 * width_k), BF), ((span, d), BF), ((8, d), F32)],
        [*rows_in, kv_whole, cos, sin], products=span * d * 2 * width_k,
    )
    (queries,) = call(
        queries_kernel, "queries",
        [((width_q, span), BF)],
        [scaled_in, after(first_whole, kv_block), cos, sin], products=span * d * width_q,
    )
    blocks = [kv_block] + [shift(kv_block, "x", d) for d in range(1, SEQ_DEVS)]
    cot_yl = swap(after(cotangent, kv_block), "yl")
    cot_near = jnp.concatenate([cotangent, cot_yl], 0)
    cot_far = swap(cot_near, "yh")
    other_mlp = swap(after(pick(shard_mlp, place("yh", 1), 0), kv_block), "yh")
    mlp_pair = join_sides(pick(shard_mlp, place("yh"), 0), other_mlp)
    mlp_whole = lax.all_gather(
        after(mlp_pair, first_whole, blocks[1:], cot_near), ("z", "x"), axis=0, tiled=True
    )
    odd = place("yl").astype(jnp.int32).reshape(1, 1)
    mixed, log_total = attend(queries, blocks, window)

    cot_far = after(cot_far, log_total)
    cotangents = jnp.concatenate([after(cot_near, log_total), cot_far], 0)
    all_heads = (0, width_q)
    attn_rows = rows_out(
        [after(mixed, cot_far)], [(first_whole, width_q, width_q)], [(0, all_heads, 0, all_heads)],
        1024, [(0,), (2,), (1, 3)], 24,
    )
    cotangents = [cotangents, swap(cotangents, "core")]
    middle, scaled_mid = call(
        middle_kernel, "middle", [(inputs.shape, F32), (inputs.shape, BF)],
        [inputs, *scatter_rows(attn_rows), gains],
    )
    scaled_all = gather_eight(scaled_mid)
    hidden, grad_both = hidden_units(odd, scaled_all, cotangents, mlp_whole, units)
    for_both = [(0, (0, both_width), 0, (0, both_width))]
    quarters = [(0, 1, 2, 3)]
    (mid_there,) = rows_out(
        [grad_both], [(mlp_whole, 0, both_width)], for_both, 512, quarters, 56, (1, 2)
    )
    (mid_here,) = rows_out(
        [after(grad_both, mid_there)], [(mlp_whole, 0, both_width)], for_both, 512, quarters, 56, (0, 2)
    )
    mid_own, mid_others = scatter_eight(mid_here, mid_there)
    mid_arrived = send_back(mid_others)
    mlp_sum = weight_grads(
        odd, [after(scaled_all[0], mid_others), *scaled_all[1:]], cotangents, grad_both, hidden
    )
    mlp_rows = rows_out(
        [after(hidden, mlp_sum)], [(mlp_whole, both_width, down_width)],
        [(0, (0, down_width), 0, (0, down_width))], 512, [(0, 1, 2, 3), (4, 5, 6, 7)], 56,
    )
    grad_middle, grad_middle_low = call(
        middle_grad_kernel, "middle_grad", [(inputs.shape, F32), (inputs.shape, BF)],
        [cotangent, mid_own, *after(mid_arrived, mlp_rows), middle, gains],
    )
    grad_across = swap(grad_middle_low, "yl")
    mlp_sum = lax.psum_scatter(mlp_sum, ("z", "x"), scatter_dimension=0, tiled=True)

    mlp_cores = swap(after(mlp_rows[1], grad_middle_low), "core")
    mlp_own, mlp_beside, mlp_far = call(
        pair_pieces_kernel, "pair_pieces",
        [(inputs.shape, F32), ((2 * quarter, d), BF), (inputs.shape, BF)],
        [odd, mlp_rows[0], mlp_cores], scalars=1,
    )
    rows_grad_middle = [
        grad_middle_low, swap(grad_middle_low, "core"), grad_across, swap(grad_across, "core")
    ]
    out_parts = wide_parts(rows_grad_middle, mixed, (0, width_q), "z")
    query_part, far_grads, grad_turned, delta = attend_back(
        (1, 2, 3), queries, blocks[1:], window, log_total, None, after(mixed, out_parts, mlp_beside),
        [first_whole, *rows_grad_middle],
    )
    mlp_arrived = after(swap(after(mlp_beside, rows_grad_middle), "yl"), query_part)
    mlp_far = (mlp_far.astype(F32) + mlp_arrived[quarter:].astype(F32)).astype(BF)
    arriving = [
        shift(far_grads[(d - 1) * span : d * span], "x", -d) for d in range(1, SEQ_DEVS)
    ]
    out_arrived = [shift(out_parts[n], "z", n) for n in (2, 1, 3)]
    query_raw_grad, own_grads = attend_back(
        (0,), after(queries, mlp_far), blocks[:1], window, log_total, (grad_turned, delta, query_part), turn=[cos, sin]
    )

    out_sum = total(out_parts[0].astype(F32), after(out_arrived, query_raw_grad)).astype(BF)
    mlp_across = swap(mlp_far, "yh")
    a_parts = wide_parts([scaled_in], after(query_raw_grad, arriving, out_arrived), (0, cut), "x")
    a_arrived = [shift(a_parts[n], "x", n) for n in (2, 1, 3)]
    kv_raw_grad, *b_parts = last_parts(
        scaled_in, after(query_raw_grad, a_parts), cut, own_grads, arriving, cos, sin, "z"
    )
    b_arrived = [shift(b_parts[n], "z", n) for n in (2, 1, 3)]
    in_partial = rows_grad(
        [query_raw_grad, kv_raw_grad],
        [(first_whole, 0, width_q), kv_whole],
        [(0, all_heads, 0, all_heads), (1, (0, 2 * width_k), 1, (0, 2 * width_k))],
        rows_in, gains, 0,
    )
    in_own, in_across, in_cores = in_partial
    in_parts = scatter_rows((in_own, in_across, after(in_cores, a_arrived, b_arrived)))

    mlp_there = swap(pick(mlp_sum.reshape(2, shard, -1), place("yh", 1), 0), "yh")
    a_sum = wide_sum_next(total(a_parts[0].astype(F32), a_arrived).astype(BF), "z")
    b_sum = total(b_parts[0].astype(F32), b_arrived).astype(BF)
    b_sum = wide_sum_next(jnp.concatenate([b_sum, out_sum], 1), "x", hold=[mlp_there, mlp_across])
    sides = jnp.concatenate([a_sum, b_sum], 1)

    attn_weights = jnp.concatenate([pair_first[:, :width_q], pair_kv[:, : 2 * width_k]], 1).astype(F32)
    gain_parts = jnp.stack(
        [
            jnp.sum(attn_weights * sides[:, : width_q + 2 * width_k].astype(F32), 1),
            jnp.sum(
                mlp_pair[:, :both_width].astype(F32) * mlp_sum[:, :both_width].astype(F32), 1
            ),
        ],
        1,
    )
    sent = jnp.concatenate([sides, jnp.pad(gain_parts.astype(BF), ((0, 0), (0, 126)))], 1)
    other_sides = swap(pick(sent.reshape(2, shard, -1), place("yh", 1), 0), "yh")
    output = settle(middle, [mlp_own, mlp_arrived[:quarter], after(mlp_across, sides)], BF)
    input_grad = settle(grad_middle, in_parts[:2] + [after(in_parts[2], sides)], F32)
    query_grad, key_grad, value_grad, out_grad = call(
        finish_attn_kernel, "finish_attn",
        [(query_weight.shape, F32), (key_weight.shape, F32), (value_weight.shape, F32),
         (out_weight.shape[::-1], F32)],
        [side, sides, other_sides], scalars=1,
    )
    gate_grad, up_grad, down_grad = call(
        finish_mlp_kernel, "finish_mlp",
        [(gate_weight.shape, F32), (up_weight.shape, F32), (down_weight.shape[::-1], F32)],
        [side, mlp_sum, mlp_there], scalars=1,
    )

    own_gains = pick(gain_parts.reshape(2, shard, 2), place("yh"), 0)
    own_gains = own_gains + other_sides[:, sides.shape[1] : sides.shape[1] + 2].astype(F32)
    own_gains = lax.psum(own_gains.T, TP)
    return (
        output,
        input_grad,
        own_gains[0] / attn_gain.astype(F32),
        query_grad,
        key_grad,
        value_grad,
        out_grad.T,
        own_gains[1] / mlp_gain.astype(F32),
        gate_grad,
        up_grad,
        down_grad.T,
    )


def solution(mesh):
    split = Mesh(mesh.devices.reshape(2, 4, 4, 2, 2), WIDE + TP)
    rows = P(WIDE + TP, None)
    inward = P(WIDE, TP)
    outward = P(TP, WIDE)
    gain = P(WIDE)
    return jax.shard_map(
        per_device,
        mesh=split,
        in_specs=(
            rows, gain, gain, inward, inward, inward, outward, gain, inward, inward, outward, rows,
        ),
        out_specs=(
            rows, rows, gain, inward, inward, inward, outward, gain, inward, inward, outward,
        ),
        check_vma=False,
    )
```
